512 devices in a mesh: gx: 8 (over z), gy: 4 (over y_lo, core), gz: 16 (over x, y_hi).
Axes of the slice: x: 4, y: 8 (y_hi: 4, y_lo: 2; y = y_hi * 2 + y_lo), z: 8, core: 2. Of those that a mesh axis runs over, the one named last changes fastest.
Arguments:
- right_side: float32 [128, 64, 2048], P('gx', 'gy', 'gz'), may hold values from -6 to 6
- iterate: float32 [128, 64, 2048], P('gx', 'gy', 'gz'), may hold values from -3 to 3
- phase_map: int32 [128, 64, 2048], P('gx', 'gy', 'gz'), may hold values from 0 to 3
- phase_coef: float32 [4], replicated, may hold values from 0.5 to 8
Outputs:
- updated: float32 [128, 64, 2048], P('gx', 'gy', 'gz')
The draws below stay inside these ranges and needn't reach their ends.
All inputs are finite; a program needn't handle non-finite values.
Results may differ from the reference program's by a relative error of at most 0.0001.
Values sent between devices are 32-bit elements; how exact they have to be, the bound alone decides.
No kernel may reach another device: no remote copies, remote signals or barrier semaphores. Data moves between devices by JAX's collectives and lax.ppermute only.
A program may use at most 64 MiB of HBM per device.

```python
import math
import jax
import jax.numpy as jnp

PHASES = 4
LEVELS = 5
SWEEPS1 = 3
SWEEPS2 = 3
SWEEPS3 = 4
NX = 128
NY = 64
NZ = 2048


def place_ends(drawn, rng, low, high):
    place = [jax.random.randint(jax.random.fold_in(rng, axis), (), 0, length) for axis, length in enumerate(drawn.shape)]
    longest = drawn.shape.index(max(drawn.shape))
    next_to = place[:longest] + [(place[longest] + 1) % drawn.shape[longest]] + place[longest + 1:]
    return drawn.at[tuple(place)].set(low).at[tuple(next_to)].set(high)


def block_scale(rng, dims, cuts, low, largest):
    loudness, own = 1.0, jax.random.fold_in(rng, 6)
    for axis_at, shards_of in cuts:
        steps = jnp.exp(jax.random.uniform(jax.random.fold_in(own, axis_at), (shards_of,), jnp.float32, low / len(cuts), largest / len(cuts)))
        loudness = loudness * jnp.repeat(steps, dims[axis_at] // shards_of).reshape([-1 if axis == axis_at else 1 for axis in range(len(dims))])
    return loudness


def bell_draw(own_key, extent, spread, reach, cuts=(), dtype=jnp.bfloat16):
    entries = spread * jax.random.normal(own_key, extent, jnp.float32)
    if cuts:
        entries = entries * block_scale(own_key, extent, cuts, -0.22, 0.18)
    return jnp.clip(entries, -reach, reach).astype(dtype)


def setup_inputs(seed: int = 0) -> dict:
    key_of = jax.random.split(jax.random.key(seed), 5)
    return {
        "right_side": bell_draw(key_of[0], (NX, NY, NZ), 1.0, 6.0, ((0, 8), (1, 4), (2, 16)), jnp.float32),
        "iterate": bell_draw(key_of[1], (NX, NY, NZ), 0.5, 3.0, ((0, 8), (1, 4), (2, 16)), jnp.float32),
        "phase_map": place_ends(jax.random.randint(key_of[2], (NX, NY, NZ), 0, PHASES), jax.random.fold_in(key_of[2], 1), 0, PHASES - 1).astype(jnp.int32),
        "phase_coef": jnp.clip(jnp.exp(jax.random.uniform(key_of[3], (PHASES,), jnp.float32, math.log(0.5), math.log(8.0))), 0.5, 8.0),
    }


OMEGA = 2.0 / 3.0
OFFSETS = [(step_x, step_y, step_z) for step_x in (-1, 0, 1) for step_y in (-1, 0, 1) for step_z in (-1, 0, 1) if (step_x, step_y, step_z) != (0, 0, 0)]


def offset_weight(offset):
    return 2.0 ** (1 - (abs(offset[0]) + abs(offset[1]) + abs(offset[2])))


def window(padded, offset):
    ext_x = padded.shape[0] - 2
    ext_y = padded.shape[1] - 2
    ext_z = padded.shape[2] - 2
    return padded[1 + offset[0]:1 + offset[0] + ext_x, 1 + offset[1]:1 + offset[1] + ext_y, 1 + offset[2]:1 + offset[2] + ext_z]


def stencil_diag(coef_pad):
    centre = window(coef_pad, (0, 0, 0))
    summed = jnp.zeros(centre.shape, jnp.float32)
    for offset in OFFSETS:
        summed = summed + offset_weight(offset) * 0.5 * (centre + window(coef_pad, offset))
    return summed


def apply_stencil(coef_pad, field_pad):
    centre = window(coef_pad, (0, 0, 0))
    middle = window(field_pad, (0, 0, 0))
    summed = jnp.zeros(centre.shape, jnp.float32)
    for offset in OFFSETS:
        summed = summed + offset_weight(offset) * 0.5 * (centre + window(coef_pad, offset)) * (middle - window(field_pad, offset))
    return summed


def coarsen(field):
    ext_x, ext_y, ext_z = field.shape
    return field.reshape(ext_x // 2, 2, ext_y // 2, 2, ext_z // 2, 2).sum(axis=(1, 3, 5))


def refine(field):
    return jnp.repeat(jnp.repeat(jnp.repeat(field, 2, axis=0), 2, axis=1), 2, axis=2)


def smooth(residual, coefficient, sweeps):
    coef_pad = jnp.pad(coefficient, 1)
    diagonal = stencil_diag(coef_pad)
    correction = OMEGA * residual / diagonal
    for sweep_index in range(sweeps - 1):
        correction = correction + OMEGA * (residual - apply_stencil(coef_pad, jnp.pad(correction, 1))) / diagonal
    return correction


def lookup(phase_map, phase_coef):
    coefficient = jnp.zeros(phase_map.shape, jnp.float32)
    for phase_index in range(PHASES):
        coefficient = coefficient + jnp.where(phase_map == phase_index, phase_coef[phase_index], 0.0)
    return coefficient


def reference(right_side, iterate, phase_map, phase_coef):
    coefficient = lookup(phase_map, phase_coef)
    residual = right_side - apply_stencil(jnp.pad(coefficient, 1), jnp.pad(iterate, 1))
    level_res = residual
    level_coef = coefficient
    corrections = []
    for level_index in range(LEVELS):
        if level_index == 0:
            sweeps = SWEEPS1
        elif level_index == 1:
            sweeps = SWEEPS2
        else:
            sweeps = SWEEPS3
        corrections.append(smooth(level_res, level_coef, sweeps))
        if level_index + 1 < LEVELS:
            level_res = 0.5 * coarsen(level_res)
            level_coef = 0.125 * coarsen(level_coef)
    summed = corrections[-1]
    for level_index in range(LEVELS - 2, -1, -1):
        summed = corrections[level_index] + refine(summed)
    return iterate + summed
```

```python
import jax
import jax.numpy as jnp
from jax import lax
from jax.experimental import pallas as pl
from jax.experimental.pallas import tpu as pltpu
from jax.sharding import PartitionSpec as P

HALO = (6, 5, 4)
ROWS = (0, 6, 11, 15)
OMEGA = 2.0 / 3.0
F32 = jnp.float32
BF16 = jnp.bfloat16


def iota(shape, dim):
    return lax.broadcasted_iota(jnp.int32, shape, dim)


def ones_where(cond, scale=1.0):
    return jnp.where(cond, F32(scale), F32(0.0)).astype(BF16)


def split3(x):
    high = x.astype(BF16)
    rest = x - high.astype(F32)
    middle = rest.astype(BF16)
    low = (rest - middle.astype(F32)).astype(BF16)
    return high, middle, low


def select_rows(pattern, x):
    parts = [jnp.dot(pattern, part, preferred_element_type=F32) for part in split3(x)]
    return parts[0] + (parts[1] + parts[2])


def select_lanes(x, pattern):
    parts = [jnp.dot(part, pattern, preferred_element_type=F32) for part in split3(x)]
    return parts[0] + (parts[1] + parts[2])


def band(x, axis):
    x = x + pltpu.roll(x, 1, axis)
    return x + pltpu.roll(x, x.shape[axis] - 1, axis)


def band_yz(x):
    return band(band(x, x.ndim - 1), x.ndim - 2)


def band_x(x):
    up = jnp.concatenate([x[1:], x[:1]], axis=0)
    down = jnp.concatenate([x[-1:], x[:-1]], axis=0)
    return (up + down) + 2.0 * x


def damped_inverse(coef, diagonal):
    inside = coef > 0.0
    return jnp.where(inside, OMEGA / jnp.where(inside, diagonal, 1.0), 0.0)


def relax(corr, inverse, residual, coef, tu_corr, tu_product):
    return corr * (1.0 / 3.0) + inverse * (residual - 2.0 * (coef * corr) + 0.125 * (coef * tu_corr + tu_product))


def smooth_small(residual, coef, sweeps):
    inverse = damped_inverse(coef, 6.0 * coef + 0.125 * band_x(band_yz(coef)))
    corr = inverse * residual
    for _ in range(sweeps - 1):
        corr = relax(corr, inverse, residual, coef, band_x(band_yz(corr)), band_x(band_yz(coef * corr)))
    return corr


def pack_y(table, phase, iterate, right, coef, to_up, to_down):
    p = phase[...]
    k = jnp.zeros(p.shape, F32)
    for index in range(4):
        k = jnp.where(p == index, table[index], k)
    coef[...] = k
    for field, ref in enumerate((coef, iterate, right)):
        h, a, b = HALO[field], ROWS[field], ROWS[field + 1]
        to_up[:, a:b, :] = ref[:, 16 - h : 16, :]
        to_down[:, a:b, :] = ref[:, 0:h, :]
    to_up[:, 15:16, :] = jnp.zeros((16, 1, 128), F32)
    to_down[:, 15:16, :] = jnp.zeros((16, 1, 128), F32)


def pack_x(coef, iterate, right, from_down, from_up, ext, to_up, to_down):
    for field, ref in enumerate((coef, iterate, right)):
        h, a, b = HALO[field], ROWS[field], ROWS[field + 1]
        ext[field, :, 0:16, :] = ref[...]
        ext[field, :, 16 : 16 + h, :] = from_up[:, a:b, :]
        ext[field, :, 16 + h : 32 - h, :] = jnp.zeros((16, 16 - 2 * h, 128), F32)
        ext[field, :, 32 - h : 32, :] = from_down[:, a:b, :]
        to_up[a:b] = ext[field, 16 - h : 16]
        to_down[a:b] = ext[field, 0:h]


def pack_z(ext, from_down, from_up, full, to_up, to_down):
    up = jnp.zeros((16, 896), F32)
    down = jnp.zeros((16, 896), F32)
    row = iota((16, 128), 0)
    lane = iota((16, 128), 1)
    contract = (((1,), (1,)), ((), ()))
    for field in range(3):
        h, a, b = HALO[field], ROWS[field], ROWS[field + 1]
        if h < 6:
            full[field, 0 : 6 - h] = jnp.zeros((6 - h, 32, 128), F32)
            full[field, 22 + h : 28] = jnp.zeros((6 - h, 32, 128), F32)
        full[field, 6 - h : 6] = from_down[a:b]
        full[field, 6:22] = ext[field]
        full[field, 22 : 22 + h] = from_up[a:b]
        mine = (row >= a) & (row < b)
        pick_up = ones_where(mine & (lane == row - a + 128 - h))
        pick_down = ones_where(mine & (lane == row - a))
        for part in split3(full[field].reshape(896, 128)):
            up = up + lax.dot_general(pick_up, part, contract, preferred_element_type=F32)
            down = down + lax.dot_general(pick_down, part, contract, preferred_element_type=F32)
    to_up[...] = up
    to_down[...] = down


def fine_residual(full, from_down, from_up, coef, res, inv, own, to_up, to_down, field, yz_k, yz_v, yz_kv):
    halo = jnp.concatenate([from_up[...], from_down[...]], axis=0).T
    row = iota((32, 128), 0)
    lane = iota((32, 128), 1)
    for index in range(3):
        h, a, b = HALO[index], ROWS[index], ROWS[index + 1]
        upper = (row >= a) & (row < b) & (lane == row - a)
        lower = (row >= 16 + a) & (row < 16 + b) & (lane == row - 16 - a + 128 - h)
        tile = select_lanes(halo, ones_where(upper | lower)).reshape(28, 32, 128)
        target = coef if index == 0 else field.at[index - 1]
        target[:, :, 0:128] = full[index]
        target[:, :, 128:256] = tile

    def bands(x, carry):
        k = coef[x]
        v = field[0, x]
        yz_k[x] = band_yz(k)
        yz_v[x] = band_yz(v)
        yz_kv[x] = band_yz(k * v)
        return carry

    lax.fori_loop(0, 28, bands, 0, unroll=2)
    for x in (0, 1, 26, 27):
        res[x] = jnp.zeros((32, 256), F32)
        inv[x] = jnp.zeros((32, 256), F32)

    def over_x(ref, x):
        return (ref[x - 1] + ref[x + 1]) + 2.0 * ref[x]

    def cells(x, carry):
        k = coef[x]
        v = field[0, x]
        diagonal = 6.0 * k + 0.125 * over_x(yz_k, x)
        applied = v * diagonal + 2.0 * (k * v) - 0.125 * (k * over_x(yz_v, x) + over_x(yz_kv, x))
        res[x] = field[1, x] - applied
        inv[x] = damped_inverse(k, diagonal)
        return carry

    lax.fori_loop(2, 26, cells, 0, unroll=2)

    row = iota((16, 512), 0)
    cell = iota((16, 512), 1)
    block = ones_where((row == (cell >> 7) * 4 + ((cell & 31) >> 2)) & ((cell & 31) < 16))
    both = jnp.concatenate([res[6:22, :, 0:128].reshape(512, 128), coef[6:22, :, 0:128].reshape(512, 128)], axis=1)
    sums = select_rows(block, both)
    source = iota((256, 128), 0)
    lane = iota((256, 128), 1)
    coarse = (source & 127) >> 2
    base = (source >> 7) * 64
    scale = jnp.where(source < 128, F32(0.25), F32(1.0 / 64.0))
    for ref, place in (
        (own, lane == base + 16 + coarse),
        (to_up, (lane == base + coarse - 16) & (coarse >= 16)),
        (to_down, (lane == base + 48 + coarse) & (coarse < 16)),
    ):
        ref[...] = select_lanes(sums, jnp.where(place, scale, 0.0).astype(BF16))


def fine_smooth(coef, res, inv, iterate, base, corr, corr_next, yz_c, yz_kc, pairs, narrow, spread):
    def over_x(ref, x):
        return (ref[x - 1] + ref[x + 1]) + 2.0 * ref[x]

    def first(x, carry):
        c = inv[x] * res[x]
        corr[x] = c
        yz_c[x] = band_yz(c)
        yz_kc[x] = band_yz(coef[x] * c)
        return carry

    lax.fori_loop(4, 24, first, 0, unroll=2)

    def second(x, carry):
        corr_next[x] = relax(corr[x], inv[x], res[x], coef[x], over_x(yz_c, x), over_x(yz_kc, x))
        return carry

    lax.fori_loop(5, 23, second, 0, unroll=2)

    def second_bands(x, carry):
        c = corr_next[x]
        yz_c[x] = band_yz(c)
        yz_kc[x] = band_yz(coef[x] * c)
        return carry

    lax.fori_loop(5, 23, second_bands, 0, unroll=2)

    lane = iota((256, 128), 0)
    halves = ones_where((lane >> 1) == iota((256, 128), 1))

    def coarse(ref, scale):
        def pair(x, carry):
            pairs[pl.ds(pl.multiple_of(32 * x, 32), 32), :] = ref[2 * x] + ref[2 * x + 1]
            return carry

        lax.fori_loop(0, 14, pair, 0, unroll=2)
        narrow[...] = select_lanes(pairs[...], halves)
        summed = narrow[pl.ds(0, 224, stride=2), :] + narrow[pl.ds(1, 224, stride=2), :]
        return (scale * summed).reshape(14, 16, 128)

    corr_two = smooth_small(coarse(res, 0.5), coarse(coef, 0.125), 3)
    doubled = ones_where(iota((128, 128), 0) == (iota((128, 128), 1) >> 1))
    wide = select_lanes(corr_two[3:11].reshape(128, 128), doubled).reshape(8, 16, 128)
    rows = wide[:, 0:8, :].reshape(64, 128)
    spread[pl.ds(0, 64, stride=2), :] = rows
    spread[pl.ds(1, 64, stride=2), :] = rows

    def third(x, carry):
        c = relax(
            corr_next[x, 0:16, 0:128],
            inv[x, 0:16, 0:128],
            res[x, 0:16, 0:128],
            coef[x, 0:16, 0:128],
            (yz_c[x - 1, 0:16, 0:128] + yz_c[x + 1, 0:16, 0:128]) + 2.0 * yz_c[x, 0:16, 0:128],
            (yz_kc[x - 1, 0:16, 0:128] + yz_kc[x + 1, 0:16, 0:128]) + 2.0 * yz_kc[x, 0:16, 0:128],
        )
        block = x - 6
        base[block] = iterate[block] + (c + spread[pl.ds(pl.multiple_of(16 * (block // 2), 16), 16), :])
        return carry

    lax.fori_loop(6, 22, third, 0, unroll=2)


def coarse_levels(place, plane, base, out):
    row = iota((192, 512), 0)
    cell = iota((192, 512), 1)
    cell_x = (cell >> 6) * 4 + ((cell >> 2) & 3)
    cell_y = ((cell >> 4) & 3) * 4 + (cell & 3)
    parts = split3(plane[...])
    windows = []
    for level in range(3):
        at_x = place[0] * (4 >> level) - 4 + (row >> 4)
        at_y = place[1] * (4 >> level) - 4 + (row & 15)
        pattern = ones_where(((cell_x >> level) == at_x) & ((cell_y >> level) == at_y))
        found = [jnp.dot(pattern, part, preferred_element_type=F32) for part in parts]
        windows.append(found[0] + (found[1] + found[2]))
    source = iota((128, 128), 0)
    lane = iota((128, 128), 1)
    residual = jnp.zeros((192, 128), F32)
    coef = jnp.zeros((192, 128), F32)
    for level, start in enumerate((0, 64, 96)):
        parts = split3(windows[level])
        target = start + ((source & 63) >> level)
        to_res = ones_where((source < 64) & (lane == target), 0.5**level)
        to_coef = ones_where((source >= 64) & (lane == target), 0.125**level)
        for part in parts:
            residual = residual + jnp.dot(part, to_res, preferred_element_type=F32)
            coef = coef + jnp.dot(part, to_coef, preferred_element_type=F32)
    corr = smooth_small(residual.reshape(12, 16, 128), coef.reshape(12, 16, 128), 4)
    mine = corr[4:8].reshape(64, 128)
    total = base[...].reshape(256, 128)
    row = iota((256, 64), 0)
    found = iota((256, 64), 1)
    for level, start in enumerate((16, 72, 100)):
        shift = 2 + level
        spread = ones_where(source == start + (lane >> shift))
        at = ((row >> 4) >> shift) * 16 + 4 + ((row & 15) >> shift)
        total = total + select_rows(ones_where(found == at), select_lanes(mine, spread))
    out[...] = total.reshape(16, 16, 128)


VMEM = pl.BlockSpec(memory_space=pltpu.VMEM)
SMEM = pl.BlockSpec(memory_space=pltpu.SMEM)


def call(kernel, outs, ins, scratch=(), scalars=0, flops=1000000):
    specs = [SMEM] * scalars + [VMEM] * (len(ins) - scalars)
    moved = 4 * sum(x.size for x in ins)
    return pl.pallas_call(
        kernel,
        out_shape=[jax.ShapeDtypeStruct(shape, F32) for shape in outs],
        in_specs=specs,
        out_specs=[VMEM] * len(outs),
        scratch_shapes=[pltpu.VMEM(shape, F32) for shape in scratch],
        compiler_params=pltpu.CompilerParams(vmem_limit_bytes=32 * 1024 * 1024),
        cost_estimate=pl.CostEstimate(flops=flops, bytes_accessed=moved, transcendentals=0),
        name=kernel.__name__,
    )(*ins)


def swap(axis, to_up, to_down):
    count = lax.axis_size(axis)
    up = [(i, i + 1) for i in range(count - 1)]
    down = [(i + 1, i) for i in range(count - 1)]
    return lax.ppermute(to_up, axis, up), lax.ppermute(to_down, axis, down)


def on_device(right, iterate, phase, table):
    block = (16, 16, 128)
    coef, to_up, to_down = call(pack_y, [block] * 3, [table, phase, iterate, right], scalars=1)
    from_down, from_up = swap("gy", to_up, to_down)
    ext, to_up, to_down = call(
        pack_x,
        [(3, 16, 32, 128), (15, 32, 128), (15, 32, 128)],
        [coef, iterate, right, from_down, from_up],
    )
    from_down, from_up = swap("gx", to_up, to_down)
    full, to_up, to_down = call(pack_z, [(3, 28, 32, 128), (16, 896), (16, 896)], [ext, from_down, from_up])
    from_down, from_up = swap("gz", to_up, to_down)
    wide = (28, 32, 256)
    coef, res, inv, own, to_up, to_down = call(
        fine_residual,
        [wide, wide, wide, (16, 128), (16, 128), (16, 128)],
        [full, from_down, from_up],
        scratch=[(2, *wide), wide, wide, wide],
        flops=30000000,
    )
    from_down, from_up = swap("gz", to_up, to_down)
    (base,) = call(
        fine_smooth,
        [block],
        [coef, res, inv, iterate],
        scratch=[wide, wide, wide, wide, (448, 256), (448, 128), (128, 128)],
        flops=30000000,
    )
    mine = own + from_down + from_up
    planes = lax.axis_size("gx") * lax.axis_size("gy")
    plane = lax.all_to_all(jnp.broadcast_to(mine[None], (planes, 16, 128)), ("gx", "gy"), 0, 0, tiled=True)
    place = jnp.stack([lax.axis_index("gx"), lax.axis_index("gy")]).astype(jnp.int32)
    (out,) = call(coarse_levels, [block], [place, plane.reshape(planes * 16, 128), base], scalars=1, flops=30000000)
    return out


def solution(mesh):
    placed = (P("gx", "gy", "gz"), P("gx", "gy", "gz"), P("gx", "gy", "gz"), P())
    return jax.shard_map(on_device, mesh=mesh, in_specs=placed, out_specs=P("gx", "gy", "gz"), check_vma=False)
```

```python
import jax
import jax.numpy as jnp
from jax import lax
from jax.experimental import pallas as pl
from jax.experimental.pallas import tpu as pltpu
from jax.sharding import PartitionSpec as P

HALO = (6, 5, 4)
ROWS = (0, 6, 11, 15)
OMEGA = 2.0 / 3.0
F32 = jnp.float32
BF16 = jnp.bfloat16


def iota(shape, dim):
    return lax.broadcasted_iota(jnp.int32, shape, dim)


def ones_where(cond, scale=1.0):
    return jnp.where(cond, F32(scale), F32(0.0)).astype(BF16)


def split3(x):
    high = x.astype(BF16)
    rest = x - high.astype(F32)
    middle = rest.astype(BF16)
    low = (rest - middle.astype(F32)).astype(BF16)
    return high, middle, low


def select_rows(pattern, x):
    parts = [jnp.dot(pattern, part, preferred_element_type=F32) for part in split3(x)]
    return parts[0] + (parts[1] + parts[2])


def select_lanes(x, pattern):
    parts = [jnp.dot(part, pattern, preferred_element_type=F32) for part in split3(x)]
    return parts[0] + (parts[1] + parts[2])


def band(x, axis):
    x = x + pltpu.roll(x, 1, axis)
    return x + pltpu.roll(x, x.shape[axis] - 1, axis)


def band_yz(x):
    return band(band(x, x.ndim - 1), x.ndim - 2)


def band_x(x):
    up = jnp.concatenate([x[1:], x[:1]], axis=0)
    down = jnp.concatenate([x[-1:], x[:-1]], axis=0)
    return (up + down) + 2.0 * x


def damped_inverse(coef, diagonal):
    inside = coef > 0.0
    return jnp.where(inside, OMEGA / jnp.where(inside, diagonal, 1.0), 0.0)


def relax(corr, inverse, residual, coef, tu_corr, tu_product):
    return corr * (1.0 / 3.0) + inverse * (residual - 2.0 * (coef * corr) + 0.125 * (coef * tu_corr + tu_product))


def smooth_small(residual, coef, sweeps):
    inverse = damped_inverse(coef, 6.0 * coef + 0.125 * band_x(band_yz(coef)))
    corr = inverse * residual
    for _ in range(sweeps - 1):
        corr = relax(corr, inverse, residual, coef, band_x(band_yz(corr)), band_x(band_yz(coef * corr)))
    return corr


def lookup(phase, values):
    k = jnp.zeros(phase.shape, F32)
    for index in range(4):
        k = jnp.where(phase == index, values[index], k)
    return k


def send_x(table, phase, iterate, right, to_up, to_down, values, upper, lower, sems):
    copies = [
        pltpu.make_async_copy(table, values, sems.at[0]),
        pltpu.make_async_copy(phase.at[10:16], upper, sems.at[1]),
        pltpu.make_async_copy(phase.at[0:6], lower, sems.at[2]),
        pltpu.make_async_copy(iterate.at[11:16], to_up.at[6:11], sems.at[3]),
        pltpu.make_async_copy(iterate.at[0:5], to_down.at[6:11], sems.at[4]),
        pltpu.make_async_copy(right.at[12:16], to_up.at[11:15], sems.at[5]),
        pltpu.make_async_copy(right.at[0:4], to_down.at[11:15], sems.at[6]),
    ]
    for copy in copies:
        copy.start()
    for copy in copies:
        copy.wait()
    to_up[0:6] = lookup(upper[...], values)
    to_down[0:6] = lookup(lower[...], values)


def keep_fields(table, phase, iterate, right, fields, values, phases, sems):
    copies = [
        pltpu.make_async_copy(table, values, sems.at[0]),
        pltpu.make_async_copy(phase, phases, sems.at[1]),
        pltpu.make_async_copy(iterate, fields.at[1], sems.at[2]),
        pltpu.make_async_copy(right, fields.at[2], sems.at[3]),
    ]
    for copy in copies:
        copy.start()
    for copy in copies:
        copy.wait()
    fields[0] = lookup(phases[...], values)


def pack_y(fields, from_down, from_up, ext, to_up, to_down):
    for field in range(3):
        h, a, b = HALO[field], ROWS[field], ROWS[field + 1]
        if h < 6:
            ext[field, 0 : 6 - h] = jnp.zeros((6 - h, 16, 128), F32)
            ext[field, 22 + h : 28] = jnp.zeros((6 - h, 16, 128), F32)
        ext[field, 6 - h : 6] = from_down[a:b]
        ext[field, 6:22] = fields[field]
        ext[field, 22 : 22 + h] = from_up[a:b]
        to_up[:, a:b, :] = ext[field, :, 16 - h : 16, :]
        to_down[:, a:b, :] = ext[field, :, 0:h, :]
    to_up[:, 15:16, :] = jnp.zeros((28, 1, 128), F32)
    to_down[:, 15:16, :] = jnp.zeros((28, 1, 128), F32)


def pack_z(ext, from_down, from_up, full, to_up, to_down):
    for field in range(3):
        h, a, b = HALO[field], ROWS[field], ROWS[field + 1]
        full[field, :, 0:16, :] = ext[field]
        full[field, :, 16 : 16 + h, :] = from_up[:, a:b, :]
        full[field, :, 16 + h : 32 - h, :] = jnp.zeros((28, 16 - 2 * h, 128), F32)
        full[field, :, 32 - h : 32, :] = from_down[:, a:b, :]
    lane = iota((32, 128), 1)
    for group in range(4):
        up = jnp.zeros((32, 128), F32)
        down = jnp.zeros((32, 128), F32)
        for x in range(8 * group, min(8 * group + 8, 28)):
            first = 16 * (x - 8 * group)
            for field in range(3):
                h, a, b = HALO[field], ROWS[field], ROWS[field + 1]
                cells = full[field, x]
                mine = (lane >= first + a) & (lane < first + b)
                up = jnp.where(mine, pltpu.roll(cells, (first + a + h) % 128, 1), up)
                down = jnp.where(mine, rolled(cells, first + a), down)
        to_up[:, 128 * group : 128 * group + 128] = up
        to_down[:, 128 * group : 128 * group + 128] = down


def rolled(x, shift):
    shift = shift % x.shape[1]
    return pltpu.roll(x, shift, 1) if shift else x


def bands_xy(full, xy, bands):
    def in_y(x, carry):
        k = full[0, x]
        v = full[1, x]
        bands[0, x] = band(k, 0)
        bands[1, x] = band(v, 0)
        bands[2, x] = band(k * v, 0)
        return carry

    lax.fori_loop(0, 28, in_y, 0, unroll=2)

    def in_x(x, carry):
        for field in range(3):
            xy[field, x] = (bands[field, x - 1] + bands[field, x + 1]) + 2.0 * bands[field, x]
        return carry

    lax.fori_loop(1, 27, in_x, 0, unroll=2)
    for field in range(3):
        for x in (0, 27):
            xy[field, x] = jnp.zeros((32, 128), F32)


def own_residual(full, xy, from_down, from_up, own, to_up, to_down, quads):
    def edge(cells, shift):
        k = cells
        v = pltpu.roll(cells, 512 - shift, 1)
        found = []
        for f in (k, v, k * v):
            f = band(f, 0)
            f = f + pltpu.roll(f, 16, 1)
            found.append(f + pltpu.roll(f, 512 - 16, 1))
        return found

    below = edge(from_down[...], 5)
    above = edge(from_up[...], 6)
    lane = iota((16, 128), 1)
    sums = [None, None]
    for x in range(6, 22):
        group, first = 128 * (x // 8), 16 * (x % 8)
        tu = []
        for field in range(3):
            cells = xy[field, x, 0:16, :]
            left = rolled(below[field][0:16, group : group + 128], -first - 5)
            after = rolled(above[field][0:16, group : group + 128], 127 - first)
            left = jnp.where(lane == 0, left, pltpu.roll(cells, 1, 1))
            after = jnp.where(lane == 127, after, pltpu.roll(cells, 127, 1))
            tu.append((left + after) + 2.0 * cells)
        k = full[0, x, 0:16, :]
        v = full[1, x, 0:16, :]
        diagonal = 6.0 * k + 0.125 * tu[0]
        res = full[2, x, 0:16, :] - (v * diagonal + 2.0 * (k * v) - 0.125 * (k * tu[1] + tu[2]))
        for at, f in enumerate((res, k)):
            sums[at] = f if (x - 6) % 4 == 0 else sums[at] + f
        if (x - 6) % 4 == 3:
            for at in range(2):
                f = sums[at] + pltpu.roll(sums[at], 15, 0)
                f = f + pltpu.roll(f, 14, 0)
                start = 64 * at + 16 * ((x - 6) // 4)
                quads[start : start + 16, :] = f
    sums = jnp.concatenate([quads[pl.ds(0, 16, stride=4), :], quads[pl.ds(64, 16, stride=4), :]], axis=1)
    source = iota((256, 128), 0)
    lane = iota((256, 128), 1)
    coarse = (source & 127) >> 2
    base = (source >> 7) * 64
    scale = jnp.where(source < 128, F32(0.25), F32(1.0 / 64.0))
    for ref, place in (
        (own, lane == base + 16 + coarse),
        (to_up, (lane == base + coarse - 16) & (coarse >= 16)),
        (to_down, (lane == base + 48 + coarse) & (coarse < 16)),
    ):
        ref[...] = select_lanes(sums, jnp.where(place, scale, 0.0).astype(BF16))


def fine_level(
    full, xy, from_down, from_up, base, res_two, coef_two, coef, side, res, inv, corr, corr_next, yz_c, yz_kc, pairs, narrow
):
    lane = iota((32, 128), 1)
    for x in range(28):
        group, first = 128 * (x // 8), 16 * (x % 8)
        up = from_up[:, group : group + 128]
        down = from_down[:, group : group + 128]
        tiles = []
        for field in range(3):
            h, a = HALO[field], ROWS[field]
            tile = jnp.where(lane >= 128 - h, rolled(down, 128 - h - first - a), 0.0)
            tiles.append(jnp.where(lane < h, rolled(up, -first - a), tile))
        coef[x, :, 0:128] = full[0, x]
        coef[x, :, 128:256] = tiles[0]
        side[0, x] = tiles[1]
        side[1, x] = tiles[2]
        corr[x, :, 0:128] = band(tiles[0], 0)
        corr[x, :, 128:256] = band(tiles[1], 0)
        corr_next[x, :, 0:128] = band(tiles[0] * tiles[1], 0)

    for x in (0, 1, 26, 27):
        res[x] = jnp.zeros((32, 256), F32)

    def over_x(ref, x):
        return (ref[x - 1] + ref[x + 1]) + 2.0 * ref[x]

    def cells(x, carry):
        sides = over_x(corr, x)
        product = (corr_next[x - 1, :, 0:128] + corr_next[x + 1, :, 0:128]) + 2.0 * corr_next[x, :, 0:128]
        tu_k = band(jnp.concatenate([xy[0, x], sides[:, 0:128]], axis=1), 1)
        tu_v = band(jnp.concatenate([xy[1, x], sides[:, 128:256]], axis=1), 1)
        tu_kv = band(jnp.concatenate([xy[2, x], product], axis=1), 1)
        k = coef[x]
        v = jnp.concatenate([full[1, x], side[0, x]], axis=1)
        diagonal = 6.0 * k + 0.125 * tu_k
        applied = v * diagonal + 2.0 * (k * v) - 0.125 * (k * tu_v + tu_kv)
        res[x] = jnp.concatenate([full[2, x], side[1, x]], axis=1) - applied
        inv[x] = damped_inverse(k, diagonal)
        return carry

    lax.fori_loop(2, 26, cells, 0, unroll=2)

    def first_sweep(x, carry):
        c = inv[x] * res[x]
        corr[x] = c
        yz_c[x] = band_yz(c)
        yz_kc[x] = band_yz(coef[x] * c)
        return carry

    lax.fori_loop(4, 24, first_sweep, 0, unroll=2)

    def second(x, carry):
        corr_next[x] = relax(corr[x], inv[x], res[x], coef[x], over_x(yz_c, x), over_x(yz_kc, x))
        return carry

    lax.fori_loop(5, 23, second, 0, unroll=2)

    def second_bands(x, carry):
        c = corr_next[x]
        yz_c[x] = band_yz(c)
        yz_kc[x] = band_yz(coef[x] * c)
        return carry

    lax.fori_loop(5, 23, second_bands, 0, unroll=2)

    def third(x, carry):
        c = relax(
            corr_next[x, 0:16, 0:128],
            inv[x, 0:16, 0:128],
            res[x, 0:16, 0:128],
            coef[x, 0:16, 0:128],
            (yz_c[x - 1, 0:16, 0:128] + yz_c[x + 1, 0:16, 0:128]) + 2.0 * yz_c[x, 0:16, 0:128],
            (yz_kc[x - 1, 0:16, 0:128] + yz_kc[x + 1, 0:16, 0:128]) + 2.0 * yz_kc[x, 0:16, 0:128],
        )
        base[x - 6] = full[1, x, 0:16, :] + c
        return carry

    lax.fori_loop(6, 22, third, 0, unroll=2)

    halves = ones_where((iota((256, 128), 0) >> 1) == iota((256, 128), 1))
    for ref, scale, out in ((res, 0.5, res_two), (coef, 0.125, coef_two)):

        def pair(x, carry):
            pairs[pl.ds(pl.multiple_of(32 * x, 32), 32), :] = ref[2 * x] + ref[2 * x + 1]
            return carry

        lax.fori_loop(0, 14, pair, 0, unroll=2)
        narrow[...] = select_lanes(pairs[...], halves)
        summed = narrow[pl.ds(0, 224, stride=2), :] + narrow[pl.ds(1, 224, stride=2), :]
        out[...] = (scale * summed).reshape(14, 16, 128)


def second_level(res_two, coef_two, base, out, spread):
    corr_two = smooth_small(res_two[...], coef_two[...], 3)
    doubled = ones_where(iota((128, 128), 0) == (iota((128, 128), 1) >> 1))
    wide = select_lanes(corr_two[3:11].reshape(128, 128), doubled).reshape(8, 16, 128)
    rows = wide[:, 0:8, :].reshape(64, 128)
    spread[pl.ds(0, 64, stride=2), :] = rows
    spread[pl.ds(1, 64, stride=2), :] = rows
    for x in range(16):
        start = 16 * (x // 2)
        out[x] = base[x] + spread[start : start + 16, :]


def coarse_levels(place, plane, base, out):
    row = iota((192, 512), 0)
    cell = iota((192, 512), 1)
    cell_x = (cell >> 6) * 4 + ((cell >> 2) & 3)
    cell_y = ((cell >> 4) & 3) * 4 + (cell & 3)
    parts = split3(plane[...])
    windows = []
    for level in range(3):
        at_x = place[0] * (4 >> level) - 4 + (row >> 4)
        at_y = place[1] * (4 >> level) - 4 + (row & 15)
        pattern = ones_where(((cell_x >> level) == at_x) & ((cell_y >> level) == at_y))
        found = [jnp.dot(pattern, part, preferred_element_type=F32) for part in parts]
        windows.append(found[0] + (found[1] + found[2]))
    source = iota((128, 128), 0)
    lane = iota((128, 128), 1)
    residual = jnp.zeros((192, 128), F32)
    coef = jnp.zeros((192, 128), F32)
    for level, start in enumerate((0, 64, 96)):
        parts = split3(windows[level])
        target = start + ((source & 63) >> level)
        to_res = ones_where((source < 64) & (lane == target), 0.5**level)
        to_coef = ones_where((source >= 64) & (lane == target), 0.125**level)
        for part in parts:
            residual = residual + jnp.dot(part, to_res, preferred_element_type=F32)
            coef = coef + jnp.dot(part, to_coef, preferred_element_type=F32)
    corr = smooth_small(residual.reshape(12, 16, 128), coef.reshape(12, 16, 128), 4)
    mine = corr[4:8].reshape(64, 128)
    total = base[...].reshape(256, 128)
    row = iota((256, 64), 0)
    found = iota((256, 64), 1)
    for level, start in enumerate((16, 72, 100)):
        shift = 2 + level
        spread = ones_where(source == start + (lane >> shift))
        at = ((row >> 4) >> shift) * 16 + 4 + ((row & 15) >> shift)
        total = total + select_rows(ones_where(found == at), select_lanes(mine, spread))
    out[...] = total.reshape(16, 16, 128)


VMEM = pl.BlockSpec(memory_space=pltpu.VMEM)
SMEM = pl.BlockSpec(memory_space=pltpu.SMEM)
HBM = pl.BlockSpec(memory_space=pltpu.HBM)


def call(kernel, outs, ins, scratch=(), first=VMEM, rest=VMEM, flops=1000000, grant=32):
    moved = 4 * sum(x.size for x in ins)
    return pl.pallas_call(
        kernel,
        out_shape=[jax.ShapeDtypeStruct(shape, F32) for shape in outs],
        in_specs=[first] + [rest] * (len(ins) - 1),
        out_specs=[VMEM] * len(outs),
        scratch_shapes=[pltpu.VMEM(shape, F32) if isinstance(shape, tuple) else shape for shape in scratch],
        compiler_params=pltpu.CompilerParams(vmem_limit_bytes=grant * 1024 * 1024),
        cost_estimate=pl.CostEstimate(flops=flops, bytes_accessed=moved, transcendentals=0),
        name=kernel.__name__,
    )(*ins)


def swap(axis, to_up, to_down):
    count = lax.axis_size(axis)
    up = [(i, i + 1) for i in range(count - 1)]
    down = [(i + 1, i) for i in range(count - 1)]
    return lax.ppermute(to_up, axis, up), lax.ppermute(to_down, axis, down)


def on_device(right, iterate, phase, table):
    block = (16, 16, 128)
    inputs = [table, phase, iterate, right]
    values = pltpu.SMEM((4,), F32)
    to_up, to_down = call(
        send_x,
        [(15, 16, 128)] * 2,
        inputs,
        scratch=[values, pltpu.VMEM((6, 16, 128), jnp.int32), pltpu.VMEM((6, 16, 128), jnp.int32), pltpu.SemaphoreType.DMA((7,))],
        first=HBM,
        rest=HBM,
        grant=60,
    )
    from_down, from_up = swap("gx", to_up, to_down)
    (fields,) = call(
        keep_fields,
        [(3, *block)],
        inputs,
        scratch=[values, pltpu.VMEM(block, jnp.int32), pltpu.SemaphoreType.DMA((4,))],
        first=HBM,
        rest=HBM,
    )
    ext, to_up, to_down = call(pack_y, [(3, 28, 16, 128), (28, 16, 128), (28, 16, 128)], [fields, from_down, from_up])
    from_down, from_up = swap("gy", to_up, to_down)
    planes = (3, 28, 32, 128)
    full, to_up, to_down = call(pack_z, [planes, (32, 512), (32, 512)], [ext, from_down, from_up])
    from_down, from_up = swap("gz", to_up, to_down)
    (xy,) = call(bands_xy, [planes], [full], scratch=[planes], flops=30000000)
    z_sides = [from_down, from_up]
    own, to_up, to_down = call(own_residual, [(16, 128)] * 3, [full, xy, *z_sides], scratch=[(128, 128)])
    from_down, from_up = swap("gz", to_up, to_down)
    wide = (28, 32, 256)
    base, res_two, coef_two = call(
        fine_level,
        [block, (14, 16, 128), (14, 16, 128)],
        [full, xy, *z_sides],
        scratch=[wide, (2, 28, 32, 128), wide, wide, wide, wide, wide, wide, (448, 256), (448, 128)],
        flops=60000000,
    )
    own, from_down, from_up, base, res_two, coef_two = lax.optimization_barrier(
        (own, from_down, from_up, base, res_two, coef_two)
    )
    mine = own + from_down + from_up
    chunks = lax.axis_size("gx") * lax.axis_size("gy")
    plane = lax.all_to_all(jnp.broadcast_to(mine[None], (chunks, 16, 128)), ("gx", "gy"), 0, 0, tiled=True)
    (base,) = call(second_level, [block], [res_two, coef_two, base], scratch=[(128, 128)], flops=30000000)
    place = jnp.stack([lax.axis_index("gx"), lax.axis_index("gy")]).astype(jnp.int32)
    (out,) = call(coarse_levels, [block], [place, plane.reshape(chunks * 16, 128), base], first=SMEM, flops=30000000)
    return out


def solution(mesh):
    placed = (P("gx", "gy", "gz"), P("gx", "gy", "gz"), P("gx", "gy", "gz"), P())
    return jax.shard_map(on_device, mesh=mesh, in_specs=placed, out_specs=P("gx", "gy", "gz"), check_vma=False)
```

```python
import jax
import jax.numpy as jnp
from jax import lax
from jax.experimental import pallas as pl
from jax.experimental.pallas import tpu as pltpu
from jax.sharding import PartitionSpec as P

HALO = (6, 5, 4)
ROWS = (0, 6, 11, 15)
OMEGA = 2.0 / 3.0
F32 = jnp.float32
BF16 = jnp.bfloat16


def iota(shape, dim):
    return lax.broadcasted_iota(jnp.int32, shape, dim)


def ones_where(cond, scale=1.0):
    return jnp.where(cond, F32(scale), F32(0.0)).astype(BF16)


def split3(x):
    high = x.astype(BF16)
    rest = x - high.astype(F32)
    middle = rest.astype(BF16)
    low = (rest - middle.astype(F32)).astype(BF16)
    return high, middle, low


def select_rows(pattern, x):
    parts = [jnp.dot(pattern, part, preferred_element_type=F32) for part in split3(x)]
    return parts[0] + (parts[1] + parts[2])


def select_lanes(x, pattern):
    parts = [jnp.dot(part, pattern, preferred_element_type=F32) for part in split3(x)]
    return parts[0] + (parts[1] + parts[2])


def band(x, axis):
    x = x + pltpu.roll(x, 1, axis)
    return x + pltpu.roll(x, x.shape[axis] - 1, axis)


def band_yz(x):
    return band(band(x, x.ndim - 1), x.ndim - 2)


def band_x(x):
    up = jnp.concatenate([x[1:], x[:1]], axis=0)
    down = jnp.concatenate([x[-1:], x[:-1]], axis=0)
    return (up + down) + 2.0 * x


def damped_inverse(coef, diagonal):
    inside = coef > 0.0
    return jnp.where(inside, OMEGA / jnp.where(inside, diagonal, 1.0), 0.0)


def relax(corr, inverse, residual, coef, tu_corr, tu_product):
    return corr * (1.0 / 3.0) + inverse * (residual - 2.0 * (coef * corr) + 0.125 * (coef * tu_corr + tu_product))


def smooth_small(residual, coef, sweeps):
    inverse = damped_inverse(coef, 6.0 * coef + 0.125 * band_x(band_yz(coef)))
    corr = inverse * residual
    for _ in range(sweeps - 1):
        corr = relax(corr, inverse, residual, coef, band_x(band_yz(corr)), band_x(band_yz(coef * corr)))
    return corr


def lookup(phase, values):
    k = jnp.zeros(phase.shape, F32)
    for index in range(4):
        k = jnp.where(phase == index, values[index], k)
    return k


def send_x(table, phase, iterate, right, to_up, to_down, values, upper, lower, sems):
    copies = [
        pltpu.make_async_copy(table, values, sems.at[0]),
        pltpu.make_async_copy(phase.at[10:16], upper, sems.at[1]),
        pltpu.make_async_copy(phase.at[0:6], lower, sems.at[2]),
        pltpu.make_async_copy(iterate.at[11:16], to_up.at[6:11], sems.at[3]),
        pltpu.make_async_copy(iterate.at[0:5], to_down.at[6:11], sems.at[4]),
        pltpu.make_async_copy(right.at[12:16], to_up.at[11:15], sems.at[5]),
        pltpu.make_async_copy(right.at[0:4], to_down.at[11:15], sems.at[6]),
    ]
    for copy in copies:
        copy.start()
    for copy in copies:
        copy.wait()
    to_up[0:6] = lookup(upper[...], values)
    to_down[0:6] = lookup(lower[...], values)


def keep_fields(table, phase, iterate, right, fields, values, phases, sems):
    copies = [
        pltpu.make_async_copy(table, values, sems.at[0]),
        pltpu.make_async_copy(phase, phases, sems.at[1]),
        pltpu.make_async_copy(iterate, fields.at[1], sems.at[2]),
        pltpu.make_async_copy(right, fields.at[2], sems.at[3]),
    ]
    for copy in copies:
        copy.start()
    for copy in copies:
        copy.wait()
    fields[0] = lookup(phases[...], values)


def pack_y(fields, from_down, from_up, ext, to_up, to_down):
    for field in range(3):
        h, a, b = HALO[field], ROWS[field], ROWS[field + 1]
        if h < 6:
            ext[field, 0 : 6 - h] = jnp.zeros((6 - h, 16, 128), F32)
            ext[field, 22 + h : 28] = jnp.zeros((6 - h, 16, 128), F32)
        ext[field, 6 - h : 6] = from_down[a:b]
        ext[field, 6:22] = fields[field]
        ext[field, 22 : 22 + h] = from_up[a:b]
        to_up[:, a:b, :] = ext[field, :, 16 - h : 16, :]
        to_down[:, a:b, :] = ext[field, :, 0:h, :]
    to_up[:, 15:16, :] = jnp.zeros((28, 1, 128), F32)
    to_down[:, 15:16, :] = jnp.zeros((28, 1, 128), F32)


def pack_z(ext, from_down, from_up, full, to_up, to_down):
    for field in range(3):
        h, a, b = HALO[field], ROWS[field], ROWS[field + 1]
        full[field, :, 0:16, :] = ext[field]
        full[field, :, 16 : 16 + h, :] = from_up[:, a:b, :]
        full[field, :, 16 + h : 32 - h, :] = jnp.zeros((28, 16 - 2 * h, 128), F32)
        full[field, :, 32 - h : 32, :] = from_down[:, a:b, :]
    lane = iota((32, 128), 1)
    for group in range(4):
        up = jnp.zeros((32, 128), F32)
        down = jnp.zeros((32, 128), F32)
        for x in range(8 * group, min(8 * group + 8, 28)):
            first = 16 * (x - 8 * group)
            for field in range(3):
                h, a, b = HALO[field], ROWS[field], ROWS[field + 1]
                cells = full[field, x]
                mine = (lane >= first + a) & (lane < first + b)
                up = jnp.where(mine, pltpu.roll(cells, (first + a + h) % 128, 1), up)
                down = jnp.where(mine, rolled(cells, first + a), down)
        to_up[:, 128 * group : 128 * group + 128] = up
        to_down[:, 128 * group : 128 * group + 128] = down


def rolled(x, shift):
    shift = shift % x.shape[1]
    return pltpu.roll(x, shift, 1) if shift else x


def bands_xy(full, xy, bands):
    def in_y(x, carry):
        k = full[0, x]
        v = full[1, x]
        bands[0, x] = band(k, 0)
        bands[1, x] = band(v, 0)
        bands[2, x] = band(k * v, 0)
        return carry

    lax.fori_loop(0, 28, in_y, 0, unroll=2)

    def in_x(x, carry):
        for field in range(3):
            xy[field, x] = (bands[field, x - 1] + bands[field, x + 1]) + 2.0 * bands[field, x]
        return carry

    lax.fori_loop(1, 27, in_x, 0, unroll=2)
    for field in range(3):
        for x in (0, 27):
            xy[field, x] = jnp.zeros((32, 128), F32)


def own_residual(full, xy, from_down, from_up, own, to_up, to_down, quads):
    def edge(cells, shift):
        k = cells
        v = pltpu.roll(cells, 512 - shift, 1)
        found = []
        for f in (k, v, k * v):
            f = band(f, 0)
            f = f + pltpu.roll(f, 16, 1)
            found.append(f + pltpu.roll(f, 512 - 16, 1))
        return found

    below = edge(from_down[...], 5)
    above = edge(from_up[...], 6)
    lane = iota((16, 128), 1)
    sums = [None, None]
    for x in range(6, 22):
        group, first = 128 * (x // 8), 16 * (x % 8)
        tu = []
        for field in range(3):
            cells = xy[field, x, 0:16, :]
            left = rolled(below[field][0:16, group : group + 128], -first - 5)
            after = rolled(above[field][0:16, group : group + 128], 127 - first)
            left = jnp.where(lane == 0, left, pltpu.roll(cells, 1, 1))
            after = jnp.where(lane == 127, after, pltpu.roll(cells, 127, 1))
            tu.append((left + after) + 2.0 * cells)
        k = full[0, x, 0:16, :]
        v = full[1, x, 0:16, :]
        diagonal = 6.0 * k + 0.125 * tu[0]
        res = full[2, x, 0:16, :] - (v * diagonal + 2.0 * (k * v) - 0.125 * (k * tu[1] + tu[2]))
        for at, f in enumerate((res, k)):
            sums[at] = f if (x - 6) % 4 == 0 else sums[at] + f
        if (x - 6) % 4 == 3:
            for at in range(2):
                f = sums[at] + pltpu.roll(sums[at], 15, 0)
                f = f + pltpu.roll(f, 14, 0)
                start = 64 * at + 16 * ((x - 6) // 4)
                quads[start : start + 16, :] = f
    sums = jnp.concatenate([quads[pl.ds(0, 16, stride=4), :], quads[pl.ds(64, 16, stride=4), :]], axis=1)
    source = iota((256, 128), 0)
    lane = iota((256, 128), 1)
    coarse = (source & 127) >> 2
    base = (source >> 7) * 64
    scale = jnp.where(source < 128, F32(0.25), F32(1.0 / 64.0))
    for ref, place in (
        (own, lane == base + 16 + coarse),
        (to_up, (lane == base + coarse - 16) & (coarse >= 16)),
        (to_down, (lane == base + 48 + coarse) & (coarse < 16)),
    ):
        ref[...] = select_lanes(sums, jnp.where(place, scale, 0.0).astype(BF16))


def fine_level(
    full, xy, from_down, from_up, base, res_two, coef_two, coef, side, res, inv, corr, corr_next, yz_c, yz_kc, pairs, narrow
):
    lane = iota((32, 128), 1)
    for x in range(28):
        group, first = 128 * (x // 8), 16 * (x % 8)
        up = from_up[:, group : group + 128]
        down = from_down[:, group : group + 128]
        tiles = []
        for field in range(3):
            h, a = HALO[field], ROWS[field]
            tile = jnp.where(lane >= 128 - h, rolled(down, 128 - h - first - a), 0.0)
            tiles.append(jnp.where(lane < h, rolled(up, -first - a), tile))
        coef[x, :, 0:128] = full[0, x]
        coef[x, :, 128:256] = tiles[0]
        side[0, x] = tiles[1]
        side[1, x] = tiles[2]
        corr[x, :, 0:128] = band(tiles[0], 0)
        corr[x, :, 128:256] = band(tiles[1], 0)
        corr_next[x, :, 0:128] = band(tiles[0] * tiles[1], 0)

    for x in (0, 1, 26, 27):
        res[x] = jnp.zeros((32, 256), F32)

    def over_x(ref, x):
        return (ref[x - 1] + ref[x + 1]) + 2.0 * ref[x]

    def cells(x, carry):
        sides = over_x(corr, x)
        product = (corr_next[x - 1, :, 0:128] + corr_next[x + 1, :, 0:128]) + 2.0 * corr_next[x, :, 0:128]
        tu_k = band(jnp.concatenate([xy[0, x], sides[:, 0:128]], axis=1), 1)
        tu_v = band(jnp.concatenate([xy[1, x], sides[:, 128:256]], axis=1), 1)
        tu_kv = band(jnp.concatenate([xy[2, x], product], axis=1), 1)
        k = coef[x]
        v = jnp.concatenate([full[1, x], side[0, x]], axis=1)
        diagonal = 6.0 * k + 0.125 * tu_k
        applied = v * diagonal + 2.0 * (k * v) - 0.125 * (k * tu_v + tu_kv)
        res[x] = jnp.concatenate([full[2, x], side[1, x]], axis=1) - applied
        inv[x] = damped_inverse(k, diagonal)
        return carry

    lax.fori_loop(2, 26, cells, 0, unroll=2)

    def first_sweep(x, carry):
        c = inv[x] * res[x]
        corr[x] = c
        yz_c[x] = band_yz(c)
        yz_kc[x] = band_yz(coef[x] * c)
        return carry

    lax.fori_loop(4, 24, first_sweep, 0, unroll=2)

    def second(x, carry):
        corr_next[x] = relax(corr[x], inv[x], res[x], coef[x], over_x(yz_c, x), over_x(yz_kc, x))
        return carry

    lax.fori_loop(5, 23, second, 0, unroll=2)

    def second_bands(x, carry):
        c = corr_next[x]
        yz_c[x] = band_yz(c)
        yz_kc[x] = band_yz(coef[x] * c)
        return carry

    lax.fori_loop(5, 23, second_bands, 0, unroll=2)

    def third(x, carry):
        c = relax(
            corr_next[x, 0:16, 0:128],
            inv[x, 0:16, 0:128],
            res[x, 0:16, 0:128],
            coef[x, 0:16, 0:128],
            (yz_c[x - 1, 0:16, 0:128] + yz_c[x + 1, 0:16, 0:128]) + 2.0 * yz_c[x, 0:16, 0:128],
            (yz_kc[x - 1, 0:16, 0:128] + yz_kc[x + 1, 0:16, 0:128]) + 2.0 * yz_kc[x, 0:16, 0:128],
        )
        base[x - 6] = full[1, x, 0:16, :] + c
        return carry

    lax.fori_loop(6, 22, third, 0, unroll=2)

    halves = ones_where((iota((256, 128), 0) >> 1) == iota((256, 128), 1))
    for ref, scale, out in ((res, 0.5, res_two), (coef, 0.125, coef_two)):

        def pair(x, carry):
            pairs[pl.ds(pl.multiple_of(32 * x, 32), 32), :] = ref[2 * x] + ref[2 * x + 1]
            return carry

        lax.fori_loop(0, 14, pair, 0, unroll=2)
        narrow[...] = select_lanes(pairs[...], halves)
        summed = narrow[pl.ds(0, 224, stride=2), :] + narrow[pl.ds(1, 224, stride=2), :]
        out[...] = (scale * summed).reshape(14, 16, 128)


def second_level(res_two, coef_two, base, out, spread):
    corr_two = smooth_small(res_two[...], coef_two[...], 3)
    doubled = ones_where(iota((128, 128), 0) == (iota((128, 128), 1) >> 1))
    wide = select_lanes(corr_two[3:11].reshape(128, 128), doubled).reshape(8, 16, 128)
    rows = wide[:, 0:8, :].reshape(64, 128)
    spread[pl.ds(0, 64, stride=2), :] = rows
    spread[pl.ds(1, 64, stride=2), :] = rows
    for x in range(16):
        start = 16 * (x // 2)
        out[x] = base[x] + spread[start : start + 16, :]


def coarse_levels(place, plane, base, out):
    row = iota((192, 512), 0)
    cell = iota((192, 512), 1)
    cell_x = (cell >> 6) * 4 + ((cell >> 2) & 3)
    cell_y = ((cell >> 4) & 3) * 4 + (cell & 3)
    parts = split3(plane[...])
    windows = []
    for level in range(3):
        at_x = place[0] * (4 >> level) - 4 + (row >> 4)
        at_y = place[1] * (4 >> level) - 4 + (row & 15)
        pattern = ones_where(((cell_x >> level) == at_x) & ((cell_y >> level) == at_y))
        found = [jnp.dot(pattern, part, preferred_element_type=F32) for part in parts]
        windows.append(found[0] + (found[1] + found[2]))
    source = iota((128, 128), 0)
    lane = iota((128, 128), 1)
    residual = jnp.zeros((192, 128), F32)
    coef = jnp.zeros((192, 128), F32)
    for level, start in enumerate((0, 64, 96)):
        parts = split3(windows[level])
        target = start + ((source & 63) >> level)
        to_res = ones_where((source < 64) & (lane == target), 0.5**level)
        to_coef = ones_where((source >= 64) & (lane == target), 0.125**level)
        for part in parts:
            residual = residual + jnp.dot(part, to_res, preferred_element_type=F32)
            coef = coef + jnp.dot(part, to_coef, preferred_element_type=F32)
    corr = smooth_small(residual.reshape(12, 16, 128), coef.reshape(12, 16, 128), 4)
    mine = corr[4:8].reshape(64, 128)
    total = base[...].reshape(256, 128)
    row = iota((256, 64), 0)
    found = iota((256, 64), 1)
    for level, start in enumerate((16, 72, 100)):
        shift = 2 + level
        spread = ones_where(source == start + (lane >> shift))
        at = ((row >> 4) >> shift) * 16 + 4 + ((row & 15) >> shift)
        total = total + select_rows(ones_where(found == at), select_lanes(mine, spread))
    out[...] = total.reshape(16, 16, 128)


VMEM = pl.BlockSpec(memory_space=pltpu.VMEM)
SMEM = pl.BlockSpec(memory_space=pltpu.SMEM)
HBM = pl.BlockSpec(memory_space=pltpu.HBM)


def call(kernel, outs, ins, scratch=(), first=VMEM, rest=VMEM, flops=1000000, grant=32):
    moved = 4 * sum(x.size for x in ins)
    return pl.pallas_call(
        kernel,
        out_shape=[jax.ShapeDtypeStruct(shape, F32) for shape in outs],
        in_specs=[first] + [rest] * (len(ins) - 1),
        out_specs=[VMEM] * len(outs),
        scratch_shapes=[pltpu.VMEM(shape, F32) if isinstance(shape, tuple) else shape for shape in scratch],
        compiler_params=pltpu.CompilerParams(vmem_limit_bytes=grant * 1024 * 1024),
        cost_estimate=pl.CostEstimate(flops=flops, bytes_accessed=moved, transcendentals=0),
        name=kernel.__name__,
    )(*ins)


def swap(axis, to_up, to_down):
    count = lax.axis_size(axis)
    up = [(i, i + 1) for i in range(count - 1)]
    down = [(i + 1, i) for i in range(count - 1)]
    return lax.ppermute(to_up, axis, up), lax.ppermute(to_down, axis, down)


def on_device(right, iterate, phase, table):
    block = (16, 16, 128)
    inputs = [table, phase, iterate, right]
    values = pltpu.SMEM((4,), F32)
    to_up, to_down = call(
        send_x,
        [(15, 16, 128)] * 2,
        inputs,
        scratch=[values, pltpu.VMEM((6, 16, 128), jnp.int32), pltpu.VMEM((6, 16, 128), jnp.int32), pltpu.SemaphoreType.DMA((7,))],
        first=HBM,
        rest=HBM,
        grant=60,
    )
    from_down, from_up = swap("gx", to_up, to_down)
    (fields,) = call(
        keep_fields,
        [(3, *block)],
        inputs,
        scratch=[values, pltpu.VMEM(block, jnp.int32), pltpu.SemaphoreType.DMA((4,))],
        first=HBM,
        rest=HBM,
    )
    ext, to_up, to_down = call(pack_y, [(3, 28, 16, 128), (28, 16, 128), (28, 16, 128)], [fields, from_down, from_up])
    from_down, from_up = swap("gy", to_up, to_down)
    planes = (3, 28, 32, 128)
    full, to_up, to_down = call(pack_z, [planes, (32, 512), (32, 512)], [ext, from_down, from_up])
    from_down, from_up = swap("gz", to_up, to_down)
    (xy,) = call(bands_xy, [planes], [full], scratch=[planes], flops=30000000)
    z_sides = [from_down, from_up]
    own, to_up, to_down = call(own_residual, [(16, 128)] * 3, [full, xy, *z_sides], scratch=[(128, 128)])
    from_down, from_up = swap("gz", to_up, to_down)
    wide = (28, 32, 256)
    base, res_two, coef_two = call(
        fine_level,
        [block, (14, 16, 128), (14, 16, 128)],
        [full, xy, *z_sides],
        scratch=[wide, (2, 28, 32, 128), wide, wide, wide, wide, wide, wide, (448, 256), (448, 128)],
        flops=60000000,
    )
    (base,) = call(second_level, [block], [res_two, coef_two, base], scratch=[(128, 128)], flops=30000000)
    place = jnp.stack([lax.axis_index("gx"), lax.axis_index("gy")]).astype(jnp.int32)
    own, from_down, from_up, base, place = lax.optimization_barrier((own, from_down, from_up, base, place))
    mine = own + from_down + from_up
    chunks = lax.axis_size("gx") * lax.axis_size("gy")
    plane = lax.all_to_all(jnp.broadcast_to(mine[None], (chunks, 16, 128)), ("gx", "gy"), 0, 0, tiled=True)
    (out,) = call(coarse_levels, [block], [place, plane.reshape(chunks * 16, 128), base], first=SMEM, flops=30000000)
    return out


def solution(mesh):
    placed = (P("gx", "gy", "gz"), P("gx", "gy", "gz"), P("gx", "gy", "gz"), P())
    return jax.shard_map(on_device, mesh=mesh, in_specs=placed, out_specs=P("gx", "gy", "gz"), check_vma=False)
```

```python
import jax
import jax.numpy as jnp
from jax import lax
from jax.experimental import pallas as pl
from jax.experimental.pallas import tpu as pltpu
from jax.sharding import PartitionSpec as P

HALO = (6, 5, 4)
ROWS = (0, 6, 11, 15)
OMEGA = 2.0 / 3.0
F32 = jnp.float32
BF16 = jnp.bfloat16


def iota(shape, dim):
    return lax.broadcasted_iota(jnp.int32, shape, dim)


def ones_where(cond, scale=1.0):
    return jnp.where(cond, F32(scale), F32(0.0)).astype(BF16)


def split3(x):
    high = x.astype(BF16)
    rest = x - high.astype(F32)
    middle = rest.astype(BF16)
    low = (rest - middle.astype(F32)).astype(BF16)
    return high, middle, low


def select_rows(pattern, x):
    parts = [jnp.dot(pattern, part, preferred_element_type=F32) for part in split3(x)]
    return parts[0] + (parts[1] + parts[2])


def select_lanes(x, pattern):
    parts = [jnp.dot(part, pattern, preferred_element_type=F32) for part in split3(x)]
    return parts[0] + (parts[1] + parts[2])


def band(x, axis):
    x = x + pltpu.roll(x, 1, axis)
    return x + pltpu.roll(x, x.shape[axis] - 1, axis)


def band_yz(x):
    return band(band(x, x.ndim - 1), x.ndim - 2)


def band_x(x):
    up = jnp.concatenate([x[1:], x[:1]], axis=0)
    down = jnp.concatenate([x[-1:], x[:-1]], axis=0)
    return (up + down) + 2.0 * x


def damped_inverse(coef, diagonal):
    inside = coef > 0.0
    return jnp.where(inside, OMEGA / jnp.where(inside, diagonal, 1.0), 0.0)


def relax(corr, inverse, residual, coef, tu_corr, tu_product):
    return corr * (1.0 / 3.0) + inverse * (residual - 2.0 * (coef * corr) + 0.125 * (coef * tu_corr + tu_product))


def smooth_small(residual, coef, sweeps):
    inverse = damped_inverse(coef, 6.0 * coef + 0.125 * band_x(band_yz(coef)))
    corr = inverse * residual
    for _ in range(sweeps - 1):
        corr = relax(corr, inverse, residual, coef, band_x(band_yz(corr)), band_x(band_yz(coef * corr)))
    return corr


def lookup(phase, values):
    k = jnp.zeros(phase.shape, F32)
    for index in range(4):
        k = jnp.where(phase == index, values[index], k)
    return k


def send_x(table, phase, iterate, right, fields, to_up, to_down, values, phases, sems):
    copies = [
        pltpu.make_async_copy(table, values, sems.at[0]),
        pltpu.make_async_copy(phase, phases, sems.at[1]),
        pltpu.make_async_copy(iterate, fields.at[1], sems.at[2]),
        pltpu.make_async_copy(right, fields.at[2], sems.at[3]),
    ]
    for copy in copies:
        copy.start()
    for copy in copies:
        copy.wait()
    p = phases[...]
    k = jnp.zeros(p.shape, F32)
    for index in range(4):
        k = jnp.where(p == index, values[index], k)
    fields[0] = k
    for field in range(3):
        h, a, b = HALO[field], ROWS[field], ROWS[field + 1]
        to_up[a:b] = fields[field, 16 - h : 16]
        to_down[a:b] = fields[field, 0:h]


def pack_y(fields, from_down, from_up, ext, to_up, to_down):
    for field in range(3):
        h, a, b = HALO[field], ROWS[field], ROWS[field + 1]
        if h < 6:
            ext[field, 0 : 6 - h] = jnp.zeros((6 - h, 16, 128), F32)
            ext[field, 22 + h : 28] = jnp.zeros((6 - h, 16, 128), F32)
        ext[field, 6 - h : 6] = from_down[a:b]
        ext[field, 6:22] = fields[field]
        ext[field, 22 : 22 + h] = from_up[a:b]
        to_up[:, a:b, :] = ext[field, :, 16 - h : 16, :]
        to_down[:, a:b, :] = ext[field, :, 0:h, :]
    to_up[:, 15:16, :] = jnp.zeros((28, 1, 128), F32)
    to_down[:, 15:16, :] = jnp.zeros((28, 1, 128), F32)


def pack_z(ext, from_down, from_up, full, to_up, to_down):
    for field in range(3):
        h, a, b = HALO[field], ROWS[field], ROWS[field + 1]
        full[field, :, 0:16, :] = ext[field]
        full[field, :, 16 : 16 + h, :] = from_up[:, a:b, :]
        full[field, :, 16 + h : 32 - h, :] = jnp.zeros((28, 16 - 2 * h, 128), F32)
        full[field, :, 32 - h : 32, :] = from_down[:, a:b, :]
    lane = iota((32, 128), 1)
    for group in range(4):
        up = jnp.zeros((32, 128), F32)
        down = jnp.zeros((32, 128), F32)
        for x in range(8 * group, min(8 * group + 8, 28)):
            first = 16 * (x - 8 * group)
            for field in range(3):
                h, a, b = HALO[field], ROWS[field], ROWS[field + 1]
                cells = full[field, x]
                mine = (lane >= first + a) & (lane < first + b)
                up = jnp.where(mine, pltpu.roll(cells, (first + a + h) % 128, 1), up)
                down = jnp.where(mine, rolled(cells, first + a), down)
        to_up[:, 128 * group : 128 * group + 128] = up
        to_down[:, 128 * group : 128 * group + 128] = down


def rolled(x, shift):
    shift = shift % x.shape[1]
    return pltpu.roll(x, shift, 1) if shift else x


def bands_xy(place, full, xy, patterns, bands):
    row = iota((192, 512), 0)
    cell = iota((192, 512), 1)
    cell_x = (cell >> 6) * 4 + ((cell >> 2) & 3)
    cell_y = ((cell >> 4) & 3) * 4 + (cell & 3)
    for level in range(3):
        at_x = place[0] * (4 >> level) - 4 + (row >> 4)
        at_y = place[1] * (4 >> level) - 4 + (row & 15)
        found = ((cell_x >> level) == at_x) & ((cell_y >> level) == at_y)
        patterns[192 * level : 192 * level + 192, :] = ones_where(found)

    def in_y(x, carry):
        k = full[0, x]
        v = full[1, x]
        bands[0, x] = band(k, 0)
        bands[1, x] = band(v, 0)
        bands[2, x] = band(k * v, 0)
        return carry

    lax.fori_loop(0, 28, in_y, 0, unroll=2)

    def in_x(x, carry):
        for field in range(3):
            xy[field, x] = (bands[field, x - 1] + bands[field, x + 1]) + 2.0 * bands[field, x]
        return carry

    lax.fori_loop(1, 27, in_x, 0, unroll=2)
    for field in range(3):
        for x in (0, 27):
            xy[field, x] = jnp.zeros((32, 128), F32)


def own_residual(full, xy, from_down, from_up, own, to_up, to_down, quads):
    def edge(cells, shift):
        k = cells
        v = pltpu.roll(cells, 512 - shift, 1)
        found = []
        for f in (k, v, k * v):
            f = band(f, 0)
            f = f + pltpu.roll(f, 16, 1)
            found.append(f + pltpu.roll(f, 512 - 16, 1))
        return found

    below = edge(from_down[...], 5)
    above = edge(from_up[...], 6)
    lane = iota((16, 128), 1)
    sums = [None, None]
    for x in range(6, 22):
        group, first = 128 * (x // 8), 16 * (x % 8)
        tu = []
        for field in range(3):
            cells = xy[field, x, 0:16, :]
            left = rolled(below[field][0:16, group : group + 128], -first - 5)
            after = rolled(above[field][0:16, group : group + 128], 127 - first)
            left = jnp.where(lane == 0, left, pltpu.roll(cells, 1, 1))
            after = jnp.where(lane == 127, after, pltpu.roll(cells, 127, 1))
            tu.append((left + after) + 2.0 * cells)
        k = full[0, x, 0:16, :]
        v = full[1, x, 0:16, :]
        diagonal = 6.0 * k + 0.125 * tu[0]
        res = full[2, x, 0:16, :] - (v * diagonal + 2.0 * (k * v) - 0.125 * (k * tu[1] + tu[2]))
        for at, f in enumerate((res, k)):
            sums[at] = f if (x - 6) % 4 == 0 else sums[at] + f
        if (x - 6) % 4 == 3:
            for at in range(2):
                f = sums[at] + pltpu.roll(sums[at], 15, 0)
                f = f + pltpu.roll(f, 14, 0)
                start = 64 * at + 16 * ((x - 6) // 4)
                quads[start : start + 16, :] = f
    sums = jnp.concatenate([quads[pl.ds(0, 16, stride=4), :], quads[pl.ds(64, 16, stride=4), :]], axis=1)
    source = iota((256, 128), 0)
    lane = iota((256, 128), 1)
    coarse = (source & 127) >> 2
    base = (source >> 7) * 64
    scale = jnp.where(source < 128, F32(0.25), F32(1.0 / 64.0))
    for ref, place in (
        (own, lane == base + 16 + coarse),
        (to_up, (lane == base + coarse - 16) & (coarse >= 16)),
        (to_down, (lane == base + 48 + coarse) & (coarse < 16)),
    ):
        ref[...] = select_lanes(sums, jnp.where(place, scale, 0.0).astype(BF16))


def fine_residual(full, xy, from_down, from_up, coef, res, inv, side, sides_kv, product):
    lane = iota((32, 128), 1)
    for x in range(28):
        group, first = 128 * (x // 8), 16 * (x % 8)
        up = from_up[:, group : group + 128]
        down = from_down[:, group : group + 128]
        tiles = []
        for field in range(3):
            h, a = HALO[field], ROWS[field]
            tile = jnp.where(lane >= 128 - h, rolled(down, 128 - h - first - a), 0.0)
            tiles.append(jnp.where(lane < h, rolled(up, -first - a), tile))
        coef[x, :, 0:128] = full[0, x]
        coef[x, :, 128:256] = tiles[0]
        side[0, x] = tiles[1]
        side[1, x] = tiles[2]
        sides_kv[x, :, 0:128] = band(tiles[0], 0)
        sides_kv[x, :, 128:256] = band(tiles[1], 0)
        product[x] = band(tiles[0] * tiles[1], 0)

    for x in (0, 1, 26, 27):
        res[x] = jnp.zeros((32, 256), F32)

    def over_x(ref, x):
        return (ref[x - 1] + ref[x + 1]) + 2.0 * ref[x]

    def cells(x, carry):
        sides = over_x(sides_kv, x)
        tu_k = band(jnp.concatenate([xy[0, x], sides[:, 0:128]], axis=1), 1)
        tu_v = band(jnp.concatenate([xy[1, x], sides[:, 128:256]], axis=1), 1)
        tu_kv = band(jnp.concatenate([xy[2, x], over_x(product, x)], axis=1), 1)
        k = coef[x]
        v = jnp.concatenate([full[1, x], side[0, x]], axis=1)
        diagonal = 6.0 * k + 0.125 * tu_k
        applied = v * diagonal + 2.0 * (k * v) - 0.125 * (k * tu_v + tu_kv)
        res[x] = jnp.concatenate([full[2, x], side[1, x]], axis=1) - applied
        inv[x] = damped_inverse(k, diagonal)
        return carry

    lax.fori_loop(2, 26, cells, 0, unroll=2)


def fine_sweeps(full, coef, res, inv, base, corr, corr_next, yz_c, yz_kc, pairs, narrow, spread):
    def over_x(ref, x):
        return (ref[x - 1] + ref[x + 1]) + 2.0 * ref[x]

    def first_sweep(x, carry):
        c = inv[x] * res[x]
        corr[x] = c
        yz_c[x] = band_yz(c)
        yz_kc[x] = band_yz(coef[x] * c)
        return carry

    lax.fori_loop(4, 24, first_sweep, 0, unroll=2)

    def second(x, carry):
        corr_next[x] = relax(corr[x], inv[x], res[x], coef[x], over_x(yz_c, x), over_x(yz_kc, x))
        return carry

    lax.fori_loop(5, 23, second, 0, unroll=2)

    def second_bands(x, carry):
        c = corr_next[x]
        yz_c[x] = band_yz(c)
        yz_kc[x] = band_yz(coef[x] * c)
        return carry

    lax.fori_loop(5, 23, second_bands, 0, unroll=2)

    halves = ones_where((iota((256, 128), 0) >> 1) == iota((256, 128), 1))

    def coarse(ref, scale):
        def pair(x, carry):
            pairs[pl.ds(pl.multiple_of(32 * x, 32), 32), :] = ref[2 * x] + ref[2 * x + 1]
            return carry

        lax.fori_loop(0, 14, pair, 0, unroll=2)
        narrow[...] = select_lanes(pairs[...], halves)
        summed = narrow[pl.ds(0, 224, stride=2), :] + narrow[pl.ds(1, 224, stride=2), :]
        return (scale * summed).reshape(14, 16, 128)

    corr_two = smooth_small(coarse(res, 0.5), coarse(coef, 0.125), 3)
    doubled = ones_where(iota((128, 128), 0) == (iota((128, 128), 1) >> 1))
    wide = select_lanes(corr_two[3:11].reshape(128, 128), doubled).reshape(8, 16, 128)
    rows = wide[:, 0:8, :].reshape(64, 128)
    spread[pl.ds(0, 64, stride=2), :] = rows
    spread[pl.ds(1, 64, stride=2), :] = rows

    def third(x, carry):
        c = relax(
            corr_next[x, 0:16, 0:128],
            inv[x, 0:16, 0:128],
            res[x, 0:16, 0:128],
            coef[x, 0:16, 0:128],
            (yz_c[x - 1, 0:16, 0:128] + yz_c[x + 1, 0:16, 0:128]) + 2.0 * yz_c[x, 0:16, 0:128],
            (yz_kc[x - 1, 0:16, 0:128] + yz_kc[x + 1, 0:16, 0:128]) + 2.0 * yz_kc[x, 0:16, 0:128],
        )
        block = x - 6
        base[block] = full[1, x, 0:16, :] + (c + spread[pl.ds(pl.multiple_of(16 * (block // 2), 16), 16), :])
        return carry

    lax.fori_loop(6, 22, third, 0, unroll=2)


def coarse_levels(patterns, plane, base, out):
    found = jnp.dot(patterns[...], jnp.concatenate(split3(plane[...]), axis=1), preferred_element_type=F32)
    found = found[:, 0:128] + (found[:, 128:256] + found[:, 256:384])
    windows = jnp.concatenate([found[192 * level : 192 * level + 192, :] for level in range(3)], axis=1)
    source = iota((384, 256), 0)
    lane = iota((384, 256), 1)
    level = source >> 7
    is_coef = (source >> 6) & 1
    start = jnp.where(level == 0, 0, jnp.where(level == 1, 64, 96))
    scale = jnp.where(is_coef == 1, jnp.where(level == 0, 1.0, jnp.where(level == 1, 0.125, 0.125**2)), 1.0)
    scale = jnp.where(is_coef == 0, jnp.where(level == 0, 1.0, jnp.where(level == 1, 0.5, 0.25)), scale)
    at = is_coef * 128 + start + ((source & 63) >> level)
    both = select_lanes(windows, jnp.where(lane == at, scale, 0.0).astype(BF16))
    corr = smooth_small(both[:, 0:128].reshape(12, 16, 128), both[:, 128:256].reshape(12, 16, 128), 4)
    source = iota((128, 384), 0)
    lane = iota((128, 384), 1)
    level = lane >> 7
    start = jnp.where(level == 0, 16, jnp.where(level == 1, 72, 100))
    wide = select_lanes(corr[4:8].reshape(64, 128), ones_where(source == start + ((lane & 127) >> (level + 2))))
    wide = jnp.concatenate([wide[:, 128 * level : 128 * level + 128] for level in range(3)], axis=0)
    row = iota((256, 192), 0)
    found = iota((256, 192), 1)
    shift = (found >> 6) + 2
    at = ((row >> 4) >> shift) * 16 + 4 + ((row & 15) >> shift)
    out[...] = base[...] + select_rows(ones_where((found & 63) == at), wide).reshape(16, 16, 128)


VMEM = pl.BlockSpec(memory_space=pltpu.VMEM)
SMEM = pl.BlockSpec(memory_space=pltpu.SMEM)
HBM = pl.BlockSpec(memory_space=pltpu.HBM)


def call(kernel, outs, ins, scratch=(), first=VMEM, rest=VMEM, flops=1000000, grant=32):
    moved = 4 * sum(x.size for x in ins)
    return pl.pallas_call(
        kernel,
        out_shape=[out if isinstance(out, jax.ShapeDtypeStruct) else jax.ShapeDtypeStruct(out, F32) for out in outs],
        in_specs=[first] + [rest] * (len(ins) - 1),
        out_specs=[VMEM] * len(outs),
        scratch_shapes=[pltpu.VMEM(shape, F32) if isinstance(shape, tuple) else shape for shape in scratch],
        compiler_params=pltpu.CompilerParams(vmem_limit_bytes=grant * 1024 * 1024),
        cost_estimate=pl.CostEstimate(flops=flops, bytes_accessed=moved, transcendentals=0),
        name=kernel.__name__,
    )(*ins)


def swap(axis, to_up, to_down):
    count = lax.axis_size(axis)
    up = [(i, i + 1) for i in range(count - 1)]
    down = [(i + 1, i) for i in range(count - 1)]
    return lax.ppermute(to_up, axis, up), lax.ppermute(to_down, axis, down)


def on_device(right, iterate, phase, table):
    block = (16, 16, 128)
    fields, to_up, to_down = call(
        send_x,
        [(3, *block), (15, 16, 128), (15, 16, 128)],
        [table, phase, iterate, right],
        scratch=[pltpu.SMEM((4,), F32), pltpu.VMEM(block, jnp.int32), pltpu.SemaphoreType.DMA((4,))],
        first=HBM,
        rest=HBM,
        grant=60,
    )
    from_down, from_up = swap("gx", to_up, to_down)
    ext, to_up, to_down = call(pack_y, [(3, 28, 16, 128), (28, 16, 128), (28, 16, 128)], [fields, from_down, from_up])
    from_down, from_up = swap("gy", to_up, to_down)
    planes = (3, 28, 32, 128)
    full, to_up, to_down = call(pack_z, [planes, (32, 512), (32, 512)], [ext, from_down, from_up])
    from_down, from_up = swap("gz", to_up, to_down)
    place = jnp.stack([lax.axis_index("gx"), lax.axis_index("gy")]).astype(jnp.int32)
    xy, patterns = call(
        bands_xy,
        [planes, jax.ShapeDtypeStruct((576, 512), BF16)],
        [place, full],
        scratch=[planes],
        first=SMEM,
        flops=30000000,
    )
    z_sides = [from_down, from_up]
    own, to_up, to_down = call(own_residual, [(16, 128)] * 3, [full, xy, *z_sides], scratch=[(128, 128)])
    from_down, from_up = swap("gz", to_up, to_down)
    mine = own + from_down + from_up
    chunks = lax.axis_size("gx") * lax.axis_size("gy")
    plane = lax.all_to_all(jnp.broadcast_to(mine[None], (chunks, 16, 128)), ("gx", "gy"), 0, 0, tiled=True)
    wide = (28, 32, 256)
    coef, res, inv = call(
        fine_residual,
        [wide] * 3,
        [full, xy, *z_sides],
        scratch=[(2, 28, 32, 128), wide, (28, 32, 128)],
        flops=30000000,
    )
    (base,) = call(
        fine_sweeps,
        [block],
        [full, coef, res, inv],
        scratch=[wide, wide, wide, wide, (448, 256), (448, 128), (128, 128)],
        flops=60000000,
    )
    (out,) = call(coarse_levels, [block], [patterns, plane.reshape(chunks * 16, 128), base], flops=30000000)
    return out


def solution(mesh):
    placed = (P("gx", "gy", "gz"), P("gx", "gy", "gz"), P("gx", "gy", "gz"), P())
    return jax.shard_map(on_device, mesh=mesh, in_specs=placed, out_specs=P("gx", "gy", "gz"), check_vma=False)
```

```python
import jax
import jax.numpy as jnp
from jax import lax
from jax.experimental import pallas as pl
from jax.experimental.pallas import tpu as pltpu
from jax.sharding import PartitionSpec as P

HALO = (6, 5, 4)
ROWS = (0, 6, 11, 15)
OMEGA = 2.0 / 3.0
F32 = jnp.float32
BF16 = jnp.bfloat16


def iota(shape, dim):
    return lax.broadcasted_iota(jnp.int32, shape, dim)


def ones_where(cond, scale=1.0):
    return jnp.where(cond, F32(scale), F32(0.0)).astype(BF16)


def split3(x):
    high = x.astype(BF16)
    rest = x - high.astype(F32)
    middle = rest.astype(BF16)
    low = (rest - middle.astype(F32)).astype(BF16)
    return high, middle, low


def select_rows(pattern, x):
    parts = [jnp.dot(pattern, part, preferred_element_type=F32) for part in split3(x)]
    return parts[0] + (parts[1] + parts[2])


def select_lanes(x, pattern):
    parts = [jnp.dot(part, pattern, preferred_element_type=F32) for part in split3(x)]
    return parts[0] + (parts[1] + parts[2])


def band(x, axis):
    x = x + pltpu.roll(x, 1, axis)
    return x + pltpu.roll(x, x.shape[axis] - 1, axis)


def band_yz(x):
    return band(band(x, x.ndim - 1), x.ndim - 2)


def band_x(x):
    up = jnp.concatenate([x[1:], x[:1]], axis=0)
    down = jnp.concatenate([x[-1:], x[:-1]], axis=0)
    return (up + down) + 2.0 * x


def damped_inverse(coef, diagonal):
    inside = coef > 0.0
    return jnp.where(inside, OMEGA / jnp.where(inside, diagonal, 1.0), 0.0)


def relax(corr, inverse, residual, coef, tu_corr, tu_product):
    return corr * (1.0 / 3.0) + inverse * (residual - 2.0 * (coef * corr) + 0.125 * (coef * tu_corr + tu_product))


def smooth_small(residual, coef, sweeps):
    inverse = damped_inverse(coef, 6.0 * coef + 0.125 * band_x(band_yz(coef)))
    corr = inverse * residual
    for _ in range(sweeps - 1):
        corr = relax(corr, inverse, residual, coef, band_x(band_yz(corr)), band_x(band_yz(coef * corr)))
    return corr


def lookup(phase, values):
    k = jnp.zeros(phase.shape, F32)
    for index in range(4):
        k = jnp.where(phase == index, values[index], k)
    return k


def send_x(table, phase, iterate, right, fields, to_up, to_down, values, phases, sems):
    copies = [
        pltpu.make_async_copy(table, values, sems.at[0]),
        pltpu.make_async_copy(phase, phases, sems.at[1]),
        pltpu.make_async_copy(iterate, fields.at[1], sems.at[2]),
        pltpu.make_async_copy(right, fields.at[2], sems.at[3]),
    ]
    for copy in copies:
        copy.start()
    for copy in copies:
        copy.wait()
    p = phases[...]
    k = jnp.zeros(p.shape, F32)
    for index in range(4):
        k = jnp.where(p == index, values[index], k)
    fields[0] = k
    for field in range(3):
        h, a, b = HALO[field], ROWS[field], ROWS[field + 1]
        to_up[a:b] = fields[field, 16 - h : 16]
        to_down[a:b] = fields[field, 0:h]


def pack_y(fields, from_down, from_up, ext, to_up, to_down):
    for field in range(3):
        h, a, b = HALO[field], ROWS[field], ROWS[field + 1]
        if h < 6:
            ext[field, 0 : 6 - h] = jnp.zeros((6 - h, 16, 128), F32)
            ext[field, 22 + h : 28] = jnp.zeros((6 - h, 16, 128), F32)
        ext[field, 6 - h : 6] = from_down[a:b]
        ext[field, 6:22] = fields[field]
        ext[field, 22 : 22 + h] = from_up[a:b]
        to_up[:, a:b, :] = ext[field, :, 16 - h : 16, :]
        to_down[:, a:b, :] = ext[field, :, 0:h, :]
    to_up[:, 15:16, :] = jnp.zeros((28, 1, 128), F32)
    to_down[:, 15:16, :] = jnp.zeros((28, 1, 128), F32)


def add_quads(quads, sums, x):
    if (x - 6) % 4 == 3:
        for at, f in enumerate(sums):
            f = f + pltpu.roll(f, 15, 0)
            f = f + pltpu.roll(f, 14, 0)
            for tile in range(f.shape[1] // 128):
                start = 64 * (at * (f.shape[1] // 128) + tile) + 16 * ((x - 6) // 4)
                quads[start : start + 16, :] = f[:, 128 * tile : 128 * tile + 128]


def read_quads(quads):
    count = quads.shape[0] // 64
    return jnp.concatenate([quads[pl.ds(64 * at, 16, stride=4), :] for at in range(count)], axis=1)


def pack_z(ext, from_down, from_up, full, to_up, to_down, quads):
    for field in range(3):
        h, a, b = HALO[field], ROWS[field], ROWS[field + 1]
        full[field, :, 0:16, :] = ext[field]
        full[field, :, 16 : 16 + h, :] = from_up[:, a:b, :]
        full[field, :, 16 + h : 32 - h, :] = jnp.zeros((28, 16 - 2 * h, 128), F32)
        full[field, :, 32 - h : 32, :] = from_down[:, a:b, :]
    in_y = {}
    sums = [None, None]
    for x in range(5, 23):
        k = full[0, x]
        v = full[1, x]
        in_y[x] = [band(f, 0)[0:16, :] for f in (k, v, k * v)]
        x = x - 1
        if x < 6:
            continue
        tu = [band((low + high) + 2.0 * f, 1) for low, f, high in zip(in_y.pop(x - 1), in_y[x], in_y[x + 1])]
        k = full[0, x, 0:16, :]
        v = full[1, x, 0:16, :]
        diagonal = 6.0 * k + 0.125 * tu[0]
        res = full[2, x, 0:16, :] - (v * diagonal + 2.0 * (k * v) - 0.125 * (k * tu[1] + tu[2]))
        sums = [f if (x - 6) % 4 == 0 else total + f for total, f in zip(sums, (res, k))]
        add_quads(quads, sums, x)
    source = iota((256, 128), 0)
    lane = iota((256, 128), 1)
    coarse = (source & 127) >> 2
    base = 64 + (source >> 7) * 16
    scale = jnp.where(source < 128, F32(0.25), F32(1.0 / 64.0))
    upper = (lane == base + coarse - 16) & (coarse >= 16) & (coarse <= 30)
    lower = (lane == base + coarse) & (coarse >= 1) & (coarse <= 15)
    place = jnp.concatenate([jnp.where(upper, scale, 0.0), jnp.where(lower, scale, 0.0)], axis=1).astype(BF16)
    level3 = select_lanes(read_quads(quads), place)
    lane = iota((32, 128), 1)
    for group in range(4):
        up = jnp.zeros((32, 128), F32)
        down = jnp.zeros((32, 128), F32)
        for x in range(8 * group, min(8 * group + 8, 28)):
            first = 16 * (x - 8 * group)
            for field in range(3):
                h, a, b = HALO[field], ROWS[field], ROWS[field + 1]
                cells = full[field, x]
                mine = (lane >= first + a) & (lane < first + b)
                up = jnp.where(mine, pltpu.roll(cells, (first + a + h) % 128, 1), up)
                down = jnp.where(mine, rolled(cells, first + a), down)
        to_up[:, 128 * group : 128 * group + 128] = up
        to_down[:, 128 * group : 128 * group + 128] = down
    to_up[0:16, 384:512] += level3[:, 0:128]
    to_down[0:16, 384:512] += level3[:, 128:256]


def rolled(x, shift):
    shift = shift % x.shape[1]
    return pltpu.roll(x, shift, 1) if shift else x


def bands_xy(place, full, xy, patterns, bands):
    row = iota((192, 512), 0)
    cell = iota((192, 512), 1)
    cell_x = (cell >> 6) * 4 + ((cell >> 2) & 3)
    cell_y = ((cell >> 4) & 3) * 4 + (cell & 3)
    for level in range(3):
        at_x = place[0] * (4 >> level) - 4 + (row >> 4)
        at_y = place[1] * (4 >> level) - 4 + (row & 15)
        found = ((cell_x >> level) == at_x) & ((cell_y >> level) == at_y)
        patterns[192 * level : 192 * level + 192, :] = ones_where(found)

    def in_y(x, carry):
        k = full[0, x]
        v = full[1, x]
        bands[0, x] = band(k, 0)
        bands[1, x] = band(v, 0)
        bands[2, x] = band(k * v, 0)
        return carry

    lax.fori_loop(0, 28, in_y, 0, unroll=2)

    def in_x(x, carry):
        for field in range(3):
            xy[field, x] = (bands[field, x - 1] + bands[field, x + 1]) + 2.0 * bands[field, x]
        return carry

    lax.fori_loop(1, 27, in_x, 0, unroll=2)
    for field in range(3):
        for x in (0, 27):
            xy[field, x] = jnp.zeros((32, 128), F32)


def own_residual(full, xy, from_down, from_up, chunks, quads):
    def edge(cells, shift_v, shift_right):
        k = cells
        v = pltpu.roll(cells, 512 - shift_v, 1)
        found = [k, v, pltpu.roll(cells, 512 - shift_right, 1)]
        for f in (k, v, k * v):
            f = band(f, 0)
            f = f + pltpu.roll(f, 16, 1)
            found.append(f + pltpu.roll(f, 512 - 16, 1))
        return [f[0:16, :] for f in found]

    below = edge(from_down[...], 5, 9)
    above = edge(from_up[...], 6, 11)
    lane = iota((16, 128), 1)
    sums = [None, None]
    for x in range(6, 22):
        group, first = 128 * (x // 8), 16 * (x % 8)
        beyond = []
        for low, high in zip(below, above):
            tile = jnp.where(lane >= 122, rolled(low[:, group : group + 128], 122 - first), 0.0)
            beyond.append(jnp.where(lane < 6, rolled(high[:, group : group + 128], -first), tile))
        k, v, right = [jnp.concatenate([full[at, x, 0:16, :], beyond[at]], axis=1) for at in range(3)]
        tu = [band(jnp.concatenate([xy[at, x, 0:16, :], beyond[3 + at]], axis=1), 1) for at in range(3)]
        diagonal = 6.0 * k + 0.125 * tu[0]
        res = right - (v * diagonal + 2.0 * (k * v) - 0.125 * (k * tu[1] + tu[2]))
        sums = [f if (x - 6) % 4 == 0 else total + f for total, f in zip(sums, (res, k))]
        add_quads(quads, sums, x)
    source = iota((512, 128), 0)
    lane = iota((512, 128), 1)
    cell = source & 255
    coarse = jnp.where(cell < 132, cell >> 2, -1)
    used = (cell < 132) | (cell >= 252)
    scale = jnp.where(source < 256, F32(0.25), F32(1.0 / 64.0))
    place = jnp.where(used & (lane == (source >> 8) * 64 + 16 + coarse), scale, 0.0).astype(BF16)
    mine = select_lanes(read_quads(quads), place)
    lane = iota((16, 128), 1)
    low = from_down[0:16, 384:512]
    high = from_up[0:16, 384:512]
    mine = jnp.where(lane < 15, pltpu.roll(low, 64, 1), mine)
    mine = jnp.where((lane >= 64) & (lane < 79), pltpu.roll(low, 112, 1), mine)
    mine = jnp.where((lane >= 49) & (lane < 64), pltpu.roll(high, 112, 1), mine)
    mine = jnp.where(lane >= 113, pltpu.roll(high, 32, 1), mine)
    chunks[...] = jnp.broadcast_to(mine[None], chunks.shape)


def fine_residual(full, xy, from_down, from_up, coef, res, inv, side, sides_kv, product):
    lane = iota((32, 128), 1)
    for x in range(28):
        group, first = 128 * (x // 8), 16 * (x % 8)
        up = from_up[:, group : group + 128]
        down = from_down[:, group : group + 128]
        tiles = []
        for field in range(3):
            h, a = HALO[field], ROWS[field]
            tile = jnp.where(lane >= 128 - h, rolled(down, 128 - h - first - a), 0.0)
            tiles.append(jnp.where(lane < h, rolled(up, -first - a), tile))
        coef[x, :, 0:128] = full[0, x]
        coef[x, :, 128:256] = tiles[0]
        side[0, x] = tiles[1]
        side[1, x] = tiles[2]
        sides_kv[x, :, 0:128] = band(tiles[0], 0)
        sides_kv[x, :, 128:256] = band(tiles[1], 0)
        product[x] = band(tiles[0] * tiles[1], 0)

    for x in (0, 1, 26, 27):
        res[x] = jnp.zeros((32, 256), F32)

    def over_x(ref, x):
        return (ref[x - 1] + ref[x + 1]) + 2.0 * ref[x]

    def cells(x, carry):
        sides = over_x(sides_kv, x)
        tu_k = band(jnp.concatenate([xy[0, x], sides[:, 0:128]], axis=1), 1)
        tu_v = band(jnp.concatenate([xy[1, x], sides[:, 128:256]], axis=1), 1)
        tu_kv = band(jnp.concatenate([xy[2, x], over_x(product, x)], axis=1), 1)
        k = coef[x]
        v = jnp.concatenate([full[1, x], side[0, x]], axis=1)
        diagonal = 6.0 * k + 0.125 * tu_k
        applied = v * diagonal + 2.0 * (k * v) - 0.125 * (k * tu_v + tu_kv)
        res[x] = jnp.concatenate([full[2, x], side[1, x]], axis=1) - applied
        inv[x] = damped_inverse(k, diagonal)
        return carry

    lax.fori_loop(2, 26, cells, 0, unroll=2)


def fine_sweeps(full, coef, res, inv, base, corr, corr_next, yz_c, yz_kc, pairs, narrow, spread):
    def over_x(ref, x):
        return (ref[x - 1] + ref[x + 1]) + 2.0 * ref[x]

    def first_sweep(x, carry):
        c = inv[x] * res[x]
        corr[x] = c
        yz_c[x] = band_yz(c)
        yz_kc[x] = band_yz(coef[x] * c)
        return carry

    lax.fori_loop(4, 24, first_sweep, 0, unroll=2)

    def second(x, carry):
        corr_next[x] = relax(corr[x], inv[x], res[x], coef[x], over_x(yz_c, x), over_x(yz_kc, x))
        return carry

    lax.fori_loop(5, 23, second, 0, unroll=2)

    def second_bands(x, carry):
        c = corr_next[x]
        yz_c[x] = band_yz(c)
        yz_kc[x] = band_yz(coef[x] * c)
        return carry

    lax.fori_loop(5, 23, second_bands, 0, unroll=2)

    halves = ones_where((iota((256, 128), 0) >> 1) == iota((256, 128), 1))

    def coarse(ref, scale):
        def pair(x, carry):
            pairs[pl.ds(pl.multiple_of(32 * x, 32), 32), :] = ref[2 * x] + ref[2 * x + 1]
            return carry

        lax.fori_loop(0, 14, pair, 0, unroll=2)
        narrow[...] = select_lanes(pairs[...], halves)
        summed = narrow[pl.ds(0, 224, stride=2), :] + narrow[pl.ds(1, 224, stride=2), :]
        return (scale * summed).reshape(14, 16, 128)

    corr_two = smooth_small(coarse(res, 0.5), coarse(coef, 0.125), 3)
    doubled = ones_where(iota((128, 128), 0) == (iota((128, 128), 1) >> 1))
    wide = select_lanes(corr_two[3:11].reshape(128, 128), doubled).reshape(8, 16, 128)
    rows = wide[:, 0:8, :].reshape(64, 128)
    spread[pl.ds(0, 64, stride=2), :] = rows
    spread[pl.ds(1, 64, stride=2), :] = rows

    def third(x, carry):
        c = relax(
            corr_next[x, 0:16, 0:128],
            inv[x, 0:16, 0:128],
            res[x, 0:16, 0:128],
            coef[x, 0:16, 0:128],
            (yz_c[x - 1, 0:16, 0:128] + yz_c[x + 1, 0:16, 0:128]) + 2.0 * yz_c[x, 0:16, 0:128],
            (yz_kc[x - 1, 0:16, 0:128] + yz_kc[x + 1, 0:16, 0:128]) + 2.0 * yz_kc[x, 0:16, 0:128],
        )
        block = x - 6
        base[block] = full[1, x, 0:16, :] + (c + spread[pl.ds(pl.multiple_of(16 * (block // 2), 16), 16), :])
        return carry

    lax.fori_loop(6, 22, third, 0, unroll=2)


def coarse_levels(patterns, plane, base, out):
    found = jnp.dot(patterns[...], jnp.concatenate(split3(plane[...]), axis=1), preferred_element_type=F32)
    found = found[:, 0:128] + (found[:, 128:256] + found[:, 256:384])
    windows = jnp.concatenate([found[192 * level : 192 * level + 192, :] for level in range(3)], axis=1)
    source = iota((384, 256), 0)
    lane = iota((384, 256), 1)
    level = source >> 7
    is_coef = (source >> 6) & 1
    start = jnp.where(level == 0, 0, jnp.where(level == 1, 64, 96))
    scale = jnp.where(is_coef == 1, jnp.where(level == 0, 1.0, jnp.where(level == 1, 0.125, 0.125**2)), 1.0)
    scale = jnp.where(is_coef == 0, jnp.where(level == 0, 1.0, jnp.where(level == 1, 0.5, 0.25)), scale)
    at = is_coef * 128 + start + ((source & 63) >> level)
    both = select_lanes(windows, jnp.where(lane == at, scale, 0.0).astype(BF16))
    corr = smooth_small(both[:, 0:128].reshape(12, 16, 128), both[:, 128:256].reshape(12, 16, 128), 4)
    source = iota((128, 384), 0)
    lane = iota((128, 384), 1)
    level = lane >> 7
    start = jnp.where(level == 0, 16, jnp.where(level == 1, 72, 100))
    wide = select_lanes(corr[4:8].reshape(64, 128), ones_where(source == start + ((lane & 127) >> (level + 2))))
    wide = jnp.concatenate([wide[:, 128 * level : 128 * level + 128] for level in range(3)], axis=0)
    row = iota((256, 192), 0)
    found = iota((256, 192), 1)
    shift = (found >> 6) + 2
    at = ((row >> 4) >> shift) * 16 + 4 + ((row & 15) >> shift)
    out[...] = base[...] + select_rows(ones_where((found & 63) == at), wide).reshape(16, 16, 128)


VMEM = pl.BlockSpec(memory_space=pltpu.VMEM)
SMEM = pl.BlockSpec(memory_space=pltpu.SMEM)
HBM = pl.BlockSpec(memory_space=pltpu.HBM)


def call(kernel, outs, ins, scratch=(), first=VMEM, rest=VMEM, flops=1000000, grant=32):
    moved = 4 * sum(x.size for x in ins)
    return pl.pallas_call(
        kernel,
        out_shape=[out if isinstance(out, jax.ShapeDtypeStruct) else jax.ShapeDtypeStruct(out, F32) for out in outs],
        in_specs=[first] + [rest] * (len(ins) - 1),
        out_specs=[VMEM] * len(outs),
        scratch_shapes=[pltpu.VMEM(shape, F32) if isinstance(shape, tuple) else shape for shape in scratch],
        compiler_params=pltpu.CompilerParams(vmem_limit_bytes=grant * 1024 * 1024),
        cost_estimate=pl.CostEstimate(flops=flops, bytes_accessed=moved, transcendentals=0),
        name=kernel.__name__,
    )(*ins)


def swap(axis, to_up, to_down):
    count = lax.axis_size(axis)
    up = [(i, i + 1) for i in range(count - 1)]
    down = [(i + 1, i) for i in range(count - 1)]
    return lax.ppermute(to_up, axis, up), lax.ppermute(to_down, axis, down)


def on_device(right, iterate, phase, table):
    block = (16, 16, 128)
    fields, to_up, to_down = call(
        send_x,
        [(3, *block), (15, 16, 128), (15, 16, 128)],
        [table, phase, iterate, right],
        scratch=[pltpu.SMEM((4,), F32), pltpu.VMEM(block, jnp.int32), pltpu.SemaphoreType.DMA((4,))],
        first=HBM,
        rest=HBM,
        grant=60,
    )
    from_down, from_up = swap("gx", to_up, to_down)
    ext, to_up, to_down = call(pack_y, [(3, 28, 16, 128), (28, 16, 128), (28, 16, 128)], [fields, from_down, from_up])
    from_down, from_up = swap("gy", to_up, to_down)
    planes = (3, 28, 32, 128)
    full, to_up, to_down = call(
        pack_z, [planes, (32, 512), (32, 512)], [ext, from_down, from_up], scratch=[(128, 128)]
    )
    from_down, from_up = swap("gz", to_up, to_down)
    place = jnp.stack([lax.axis_index("gx"), lax.axis_index("gy")]).astype(jnp.int32)
    xy, patterns = call(
        bands_xy,
        [planes, jax.ShapeDtypeStruct((576, 512), BF16)],
        [place, full],
        scratch=[planes],
        first=SMEM,
        flops=30000000,
    )
    z_sides = [from_down, from_up]
    count = lax.axis_size("gx") * lax.axis_size("gy")
    (chunks,) = call(own_residual, [(count, 16, 128)], [full, xy, *z_sides], scratch=[(256, 128)])
    plane = lax.all_to_all(chunks, ("gx", "gy"), 0, 0, tiled=True)
    wide = (28, 32, 256)
    coef, res, inv = call(
        fine_residual,
        [wide] * 3,
        [full, xy, *z_sides],
        scratch=[(2, 28, 32, 128), wide, (28, 32, 128)],
        flops=30000000,
    )
    (base,) = call(
        fine_sweeps,
        [block],
        [full, coef, res, inv],
        scratch=[wide, wide, wide, wide, (448, 256), (448, 128), (128, 128)],
        flops=60000000,
    )
    (out,) = call(coarse_levels, [block], [patterns, plane.reshape(count * 16, 128), base], flops=30000000)
    return out


def solution(mesh):
    placed = (P("gx", "gy", "gz"), P("gx", "gy", "gz"), P("gx", "gy", "gz"), P())
    return jax.shard_map(on_device, mesh=mesh, in_specs=placed, out_specs=P("gx", "gy", "gz"), check_vma=False)
```

```python
import jax
import jax.numpy as jnp
from jax import lax
from jax.experimental import pallas as pl
from jax.experimental.pallas import tpu as pltpu
from jax.sharding import PartitionSpec as P

HALO = (6, 5, 4)
ROWS = (0, 6, 11, 15)
OMEGA = 2.0 / 3.0
F32 = jnp.float32
BF16 = jnp.bfloat16


def iota(shape, dim):
    return lax.broadcasted_iota(jnp.int32, shape, dim)


def ones_where(cond, scale=1.0):
    return jnp.where(cond, F32(scale), F32(0.0)).astype(BF16)


def split3(x):
    high = x.astype(BF16)
    rest = x - high.astype(F32)
    middle = rest.astype(BF16)
    low = (rest - middle.astype(F32)).astype(BF16)
    return high, middle, low


def select_rows(pattern, x):
    parts = [jnp.dot(pattern, part, preferred_element_type=F32) for part in split3(x)]
    return parts[0] + (parts[1] + parts[2])


def select_lanes(x, pattern):
    parts = [jnp.dot(part, pattern, preferred_element_type=F32) for part in split3(x)]
    return parts[0] + (parts[1] + parts[2])


def band(x, axis):
    x = x + pltpu.roll(x, 1, axis)
    return x + pltpu.roll(x, x.shape[axis] - 1, axis)


def band_yz(x):
    return band(band(x, x.ndim - 1), x.ndim - 2)


def band_x(x):
    up = jnp.concatenate([x[1:], x[:1]], axis=0)
    down = jnp.concatenate([x[-1:], x[:-1]], axis=0)
    return (up + down) + 2.0 * x


def damped_inverse(coef, diagonal):
    inside = coef > 0.0
    return jnp.where(inside, OMEGA / jnp.where(inside, diagonal, 1.0), 0.0)


def relax(corr, inverse, residual, coef, tu_corr, tu_product):
    return corr * (1.0 / 3.0) + inverse * (residual - 2.0 * (coef * corr) + 0.125 * (coef * tu_corr + tu_product))


def smooth_small(residual, coef, sweeps):
    inverse = damped_inverse(coef, 6.0 * coef + 0.125 * band_x(band_yz(coef)))
    corr = inverse * residual
    for _ in range(sweeps - 1):
        corr = relax(corr, inverse, residual, coef, band_x(band_yz(corr)), band_x(band_yz(coef * corr)))
    return corr


def lookup(phase, values):
    k = jnp.zeros(phase.shape, F32)
    for index in range(4):
        k = jnp.where(phase == index, values[index], k)
    return k


def send_x(table, phase, iterate, right, fields, to_up, to_down, values, phases, sems):
    copies = [
        pltpu.make_async_copy(table, values, sems.at[0]),
        pltpu.make_async_copy(phase, phases, sems.at[1]),
        pltpu.make_async_copy(iterate, fields.at[1], sems.at[2]),
        pltpu.make_async_copy(right, fields.at[2], sems.at[3]),
    ]
    for copy in copies:
        copy.start()
    for copy in copies:
        copy.wait()
    p = phases[...]
    k = jnp.zeros(p.shape, F32)
    for index in range(4):
        k = jnp.where(p == index, values[index], k)
    fields[0] = k
    for field in range(3):
        h, a, b = HALO[field], ROWS[field], ROWS[field + 1]
        to_up[a:b] = fields[field, 16 - h : 16]
        to_down[a:b] = fields[field, 0:h]


def pack_y(fields, from_down, from_up, ext, to_up, to_down):
    for field in range(3):
        h, a, b = HALO[field], ROWS[field], ROWS[field + 1]
        if h < 6:
            ext[field, 0 : 6 - h] = jnp.zeros((6 - h, 16, 128), F32)
            ext[field, 22 + h : 28] = jnp.zeros((6 - h, 16, 128), F32)
        ext[field, 6 - h : 6] = from_down[a:b]
        ext[field, 6:22] = fields[field]
        ext[field, 22 : 22 + h] = from_up[a:b]
        to_up[:, a:b, :] = ext[field, :, 16 - h : 16, :]
        to_down[:, a:b, :] = ext[field, :, 0:h, :]
    to_up[:, 15:16, :] = jnp.zeros((28, 1, 128), F32)
    to_down[:, 15:16, :] = jnp.zeros((28, 1, 128), F32)


def sum_quads(quads, q, sums):
    for at, f in enumerate(sums):
        f = f + pltpu.roll(f, 15, 0)
        f = f + pltpu.roll(f, 14, 0)
        for tile in range(f.shape[1] // 128):
            start = 64 * (at * (f.shape[1] // 128) + tile) + 16 * q
            quads[pl.ds(pl.multiple_of(start, 16), 16), :] = f[:, 128 * tile : 128 * tile + 128]


def read_quads(quads):
    count = quads.shape[0] // 64
    return jnp.concatenate([quads[pl.ds(64 * at, 16, stride=4), :] for at in range(count)], axis=1)


def pack_z(ext, from_down, from_up, full, to_up, to_down, inner, in_y, quads):
    for field in range(3):
        h, a, b = HALO[field], ROWS[field], ROWS[field + 1]
        full[field, :, 0:16, :] = ext[field]
        full[field, :, 16 : 16 + h, :] = from_up[:, a:b, :]
        full[field, :, 16 + h : 32 - h, :] = jnp.zeros((28, 16 - 2 * h, 128), F32)
        full[field, :, 32 - h : 32, :] = from_down[:, a:b, :]

    def bands_y(x, carry):
        k = full[0, x]
        v = full[1, x]
        for at, f in enumerate((k, v, k * v)):
            in_y[at, x] = band(f, 0)[0:16, :]
        return carry

    lax.fori_loop(5, 23, bands_y, 0, unroll=2)

    def quad(q, carry):
        sums = [None, None]
        for j in range(4):
            x = 6 + 4 * q + j
            tu = [band((in_y[at, x - 1] + in_y[at, x + 1]) + 2.0 * in_y[at, x], 1) for at in range(3)]
            k = full[0, x, 0:16, :]
            v = full[1, x, 0:16, :]
            diagonal = 6.0 * k + 0.125 * tu[0]
            res = full[2, x, 0:16, :] - (v * diagonal + 2.0 * (k * v) - 0.125 * (k * tu[1] + tu[2]))
            sums = [f if j == 0 else total + f for total, f in zip(sums, (res, k))]
        sum_quads(quads, q, sums)
        return carry

    lax.fori_loop(0, 4, quad, 0)
    source = iota((256, 128), 0)
    lane = iota((256, 128), 1)
    coarse = (source & 127) >> 2
    base = 64 + (source >> 7) * 16
    scale = jnp.where(source < 128, F32(0.25), F32(1.0 / 64.0))
    upper = (lane == base + coarse - 16) & (coarse >= 16) & (coarse <= 30)
    lower = (lane == base + coarse) & (coarse >= 1) & (coarse <= 15)
    stay = (lane == (source >> 7) * 64 + 16 + coarse) & (coarse >= 1) & (coarse <= 30)
    place = jnp.concatenate([jnp.where(found, scale, 0.0) for found in (upper, lower, stay)], axis=1).astype(BF16)
    level3 = select_lanes(read_quads(quads), place)
    inner[...] = level3[:, 256:384]
    lane = iota((32, 128), 1)

    for group in range(4):
        up = jnp.zeros((32, 128), F32)
        down = jnp.zeros((32, 128), F32)
        for x in range(8 * group, min(8 * group + 8, 28)):
            first = 16 * (x - 8 * group)
            for field in range(3):
                h, a, b = HALO[field], ROWS[field], ROWS[field + 1]
                cells = full[field, x]
                mine = (lane >= first + a) & (lane < first + b)
                up = jnp.where(mine, pltpu.roll(cells, (first + a + h) % 128, 1), up)
                down = jnp.where(mine, rolled(cells, first + a), down)
        to_up[:, 128 * group : 128 * group + 128] = up
        to_down[:, 128 * group : 128 * group + 128] = down
    to_up[0:16, 384:512] += level3[:, 0:128]
    to_down[0:16, 384:512] += level3[:, 128:256]


def rolled(x, shift):
    shift = shift % x.shape[1]
    return pltpu.roll(x, shift, 1) if shift else x


def bands_xy(place, full, xy, patterns, bands):
    row = iota((192, 512), 0)
    cell = iota((192, 512), 1)
    cell_x = (cell >> 6) * 4 + ((cell >> 2) & 3)
    cell_y = ((cell >> 4) & 3) * 4 + (cell & 3)
    for level in range(3):
        at_x = place[0] * (4 >> level) - 4 + (row >> 4)
        at_y = place[1] * (4 >> level) - 4 + (row & 15)
        found = ((cell_x >> level) == at_x) & ((cell_y >> level) == at_y)
        patterns[192 * level : 192 * level + 192, :] = ones_where(found)

    def in_y(x, carry):
        k = full[0, x]
        v = full[1, x]
        bands[0, x] = band(k, 0)
        bands[1, x] = band(v, 0)
        bands[2, x] = band(k * v, 0)
        return carry

    lax.fori_loop(0, 28, in_y, 0, unroll=2)

    def in_x(x, carry):
        for field in range(3):
            xy[field, x] = (bands[field, x - 1] + bands[field, x + 1]) + 2.0 * bands[field, x]
        return carry

    lax.fori_loop(1, 27, in_x, 0, unroll=2)
    for field in range(3):
        for x in (0, 27):
            xy[field, x] = jnp.zeros((32, 128), F32)


def end_cells(lower_k, lower_v, lower_right, upper_k, upper_v, upper_right):
    position = iota((32, 512), 1) & 15
    k = jnp.where(position < 6, lower_k, jnp.where(position < 12, upper_k, 0.0))
    v = jnp.where(position < 6, lower_v, upper_v)
    right = jnp.where(position < 6, lower_right, upper_right)[0:16, :]
    tu = []
    for f in (k, v, k * v):
        f = band(f, 0)[0:16, :]
        f = f + pltpu.roll(f, 16, 1)
        tu.append(band(f + pltpu.roll(f, 512 - 16, 1), 1))
    k, v = k[0:16, :], v[0:16, :]
    diagonal = 6.0 * k + 0.125 * tu[0]
    return right - (v * diagonal + 2.0 * (k * v) - 0.125 * (k * tu[1] + tu[2])), k


def own_cells(sent_up, sent_down, from_down, from_up, inner, chunks, quads):
    def moved(f, shift):
        return pltpu.roll(f, shift % 512, 1)

    low, first, last, high = from_down[...], sent_down[...], sent_up[...], from_up[...]
    found = [
        end_cells(low, moved(low, -5), moved(low, -9), moved(first, 6), first, moved(first, -5)),
        end_cells(last, moved(last, -5), moved(last, -9), moved(high, 6), high, moved(high, -5)),
    ]
    rows = []
    for f in (found[0][0], found[1][0], found[0][1], found[1][1]):
        f = f[:, 0:384]
        f = f + pltpu.roll(f, 15, 0)
        rows.append(f + pltpu.roll(f, 14, 0))
    source = iota((384, 128), 0)
    x = (source >> 4) - 6
    z = (source & 15) - 2
    place = (x >= 0) & (x < 16) & (z >= 0) & (z < 8) & (iota((384, 128), 1) == (x >> 2) * 32 + (z >> 2))
    ends = select_lanes(jnp.concatenate(rows, axis=0), ones_where(place))
    ends = [0.25 * ends[0:16], 0.25 * ends[16:32], ends[32:48] / 64.0, ends[48:64] / 64.0]
    for q in range(4):
        for at in range(4):
            start = 64 * at + 16 * q
            quads[start : start + 16, :] = rolled(ends[at], -32 * q)
    lane = iota((16, 128), 1)
    mine = inner[...]
    for at, target in enumerate((15, 47, 79, 111)):
        cells = pltpu.roll(quads[pl.ds(64 * at, 16, stride=4), :], target, 1)
        mine = jnp.where((lane == target) | (lane == target + 1), cells, mine)
    low = from_down[0:16, 384:512]
    high = from_up[0:16, 384:512]
    mine = jnp.where(lane < 15, pltpu.roll(low, 64, 1), mine)
    mine = jnp.where((lane >= 64) & (lane < 79), pltpu.roll(low, 112, 1), mine)
    mine = jnp.where((lane >= 49) & (lane < 64), pltpu.roll(high, 112, 1), mine)
    mine = jnp.where(lane >= 113, pltpu.roll(high, 32, 1), mine)
    chunks[...] = jnp.broadcast_to(mine[None], chunks.shape)


def fine_residual(full, xy, from_down, from_up, coef, res, inv, side, sides_kv, product):
    lane = iota((32, 128), 1)

    for x in range(28):
        group, first = 128 * (x // 8), 16 * (x % 8)
        up = from_up[:, group : group + 128]
        down = from_down[:, group : group + 128]
        tiles = []
        for field in range(3):
            h, a = HALO[field], ROWS[field]
            tile = jnp.where(lane >= 128 - h, rolled(down, 128 - h - first - a), 0.0)
            tiles.append(jnp.where(lane < h, rolled(up, -first - a), tile))
        coef[x, :, 0:128] = full[0, x]
        coef[x, :, 128:256] = tiles[0]
        side[0, x] = tiles[1]
        side[1, x] = tiles[2]
        sides_kv[x, :, 0:128] = band(tiles[0], 0)
        sides_kv[x, :, 128:256] = band(tiles[1], 0)
        product[x] = band(tiles[0] * tiles[1], 0)

    for x in (0, 1, 26, 27):
        res[x] = jnp.zeros((32, 256), F32)

    def over_x(ref, x):
        return (ref[x - 1] + ref[x + 1]) + 2.0 * ref[x]

    def cells(x, carry):
        sides = over_x(sides_kv, x)
        tu_k = band(jnp.concatenate([xy[0, x], sides[:, 0:128]], axis=1), 1)
        tu_v = band(jnp.concatenate([xy[1, x], sides[:, 128:256]], axis=1), 1)
        tu_kv = band(jnp.concatenate([xy[2, x], over_x(product, x)], axis=1), 1)
        k = coef[x]
        v = jnp.concatenate([full[1, x], side[0, x]], axis=1)
        diagonal = 6.0 * k + 0.125 * tu_k
        applied = v * diagonal + 2.0 * (k * v) - 0.125 * (k * tu_v + tu_kv)
        res[x] = jnp.concatenate([full[2, x], side[1, x]], axis=1) - applied
        inv[x] = damped_inverse(k, diagonal)
        return carry

    lax.fori_loop(2, 26, cells, 0, unroll=2)


def fine_sweeps(full, coef, res, inv, base, corr, corr_next, yz_c, yz_kc, pairs, narrow, spread):
    def over_x(ref, x):
        return (ref[x - 1] + ref[x + 1]) + 2.0 * ref[x]

    def first_sweep(x, carry):
        c = inv[x] * res[x]
        corr[x] = c
        yz_c[x] = band_yz(c)
        yz_kc[x] = band_yz(coef[x] * c)
        return carry

    lax.fori_loop(4, 24, first_sweep, 0, unroll=2)

    def second(x, carry):
        corr_next[x] = relax(corr[x], inv[x], res[x], coef[x], over_x(yz_c, x), over_x(yz_kc, x))
        return carry

    lax.fori_loop(5, 23, second, 0, unroll=2)

    def second_bands(x, carry):
        c = corr_next[x]
        yz_c[x] = band_yz(c)
        yz_kc[x] = band_yz(coef[x] * c)
        return carry

    lax.fori_loop(5, 23, second_bands, 0, unroll=2)

    halves = ones_where((iota((256, 128), 0) >> 1) == iota((256, 128), 1))

    def coarse(ref, scale):
        def pair(x, carry):
            pairs[pl.ds(pl.multiple_of(32 * x, 32), 32), :] = ref[2 * x] + ref[2 * x + 1]
            return carry

        lax.fori_loop(0, 14, pair, 0, unroll=2)
        narrow[...] = select_lanes(pairs[...], halves)
        summed = narrow[pl.ds(0, 224, stride=2), :] + narrow[pl.ds(1, 224, stride=2), :]
        return (scale * summed).reshape(14, 16, 128)

    corr_two = smooth_small(coarse(res, 0.5), coarse(coef, 0.125), 3)
    doubled = ones_where(iota((128, 128), 0) == (iota((128, 128), 1) >> 1))
    wide = select_lanes(corr_two[3:11].reshape(128, 128), doubled).reshape(8, 16, 128)
    rows = wide[:, 0:8, :].reshape(64, 128)
    spread[pl.ds(0, 64, stride=2), :] = rows
    spread[pl.ds(1, 64, stride=2), :] = rows

    def third(x, carry):
        c = relax(
            corr_next[x, 0:16, 0:128],
            inv[x, 0:16, 0:128],
            res[x, 0:16, 0:128],
            coef[x, 0:16, 0:128],
            (yz_c[x - 1, 0:16, 0:128] + yz_c[x + 1, 0:16, 0:128]) + 2.0 * yz_c[x, 0:16, 0:128],
            (yz_kc[x - 1, 0:16, 0:128] + yz_kc[x + 1, 0:16, 0:128]) + 2.0 * yz_kc[x, 0:16, 0:128],
        )
        block = x - 6
        base[block] = full[1, x, 0:16, :] + (c + spread[pl.ds(pl.multiple_of(16 * (block // 2), 16), 16), :])
        return carry

    lax.fori_loop(6, 22, third, 0, unroll=2)


def coarse_levels(patterns, plane, base, out):
    found = jnp.dot(patterns[...], jnp.concatenate(split3(plane[...]), axis=1), preferred_element_type=F32)
    found = found[:, 0:128] + (found[:, 128:256] + found[:, 256:384])
    windows = jnp.concatenate([found[192 * level : 192 * level + 192, :] for level in range(3)], axis=1)
    source = iota((384, 256), 0)
    lane = iota((384, 256), 1)
    level = source >> 7
    is_coef = (source >> 6) & 1
    start = jnp.where(level == 0, 0, jnp.where(level == 1, 64, 96))
    scale = jnp.where(is_coef == 1, jnp.where(level == 0, 1.0, jnp.where(level == 1, 0.125, 0.125**2)), 1.0)
    scale = jnp.where(is_coef == 0, jnp.where(level == 0, 1.0, jnp.where(level == 1, 0.5, 0.25)), scale)
    at = is_coef * 128 + start + ((source & 63) >> level)
    both = select_lanes(windows, jnp.where(lane == at, scale, 0.0).astype(BF16))
    corr = smooth_small(both[:, 0:128].reshape(12, 16, 128), both[:, 128:256].reshape(12, 16, 128), 4)
    source = iota((128, 384), 0)
    lane = iota((128, 384), 1)
    level = lane >> 7
    start = jnp.where(level == 0, 16, jnp.where(level == 1, 72, 100))
    wide = select_lanes(corr[4:8].reshape(64, 128), ones_where(source == start + ((lane & 127) >> (level + 2))))
    wide = jnp.concatenate([wide[:, 128 * level : 128 * level + 128] for level in range(3)], axis=0)
    row = iota((256, 192), 0)
    found = iota((256, 192), 1)
    shift = (found >> 6) + 2
    at = ((row >> 4) >> shift) * 16 + 4 + ((row & 15) >> shift)
    out[...] = base[...] + select_rows(ones_where((found & 63) == at), wide).reshape(16, 16, 128)


VMEM = pl.BlockSpec(memory_space=pltpu.VMEM)
SMEM = pl.BlockSpec(memory_space=pltpu.SMEM)
HBM = pl.BlockSpec(memory_space=pltpu.HBM)


def call(kernel, outs, ins, scratch=(), first=VMEM, rest=VMEM, flops=1000000, grant=32):
    moved = 4 * sum(x.size for x in ins)
    return pl.pallas_call(
        kernel,
        out_shape=[out if isinstance(out, jax.ShapeDtypeStruct) else jax.ShapeDtypeStruct(out, F32) for out in outs],
        in_specs=[first] + [rest] * (len(ins) - 1),
        out_specs=[VMEM] * len(outs),
        scratch_shapes=[pltpu.VMEM(shape, F32) if isinstance(shape, tuple) else shape for shape in scratch],
        compiler_params=pltpu.CompilerParams(vmem_limit_bytes=grant * 1024 * 1024),
        cost_estimate=pl.CostEstimate(flops=flops, bytes_accessed=moved, transcendentals=0),
        name=kernel.__name__,
    )(*ins)


def swap(axis, to_up, to_down):
    count = lax.axis_size(axis)
    up = [(i, i + 1) for i in range(count - 1)]
    down = [(i + 1, i) for i in range(count - 1)]
    return lax.ppermute(to_up, axis, up), lax.ppermute(to_down, axis, down)


def on_device(right, iterate, phase, table):
    block = (16, 16, 128)
    fields, to_up, to_down = call(
        send_x,
        [(3, *block), (15, 16, 128), (15, 16, 128)],
        [table, phase, iterate, right],
        scratch=[pltpu.SMEM((4,), F32), pltpu.VMEM(block, jnp.int32), pltpu.SemaphoreType.DMA((4,))],
        first=HBM,
        rest=HBM,
        grant=60,
    )
    from_down, from_up = swap("gx", to_up, to_down)
    ext, to_up, to_down = call(pack_y, [(3, 28, 16, 128), (28, 16, 128), (28, 16, 128)], [fields, from_down, from_up])
    from_down, from_up = swap("gy", to_up, to_down)
    planes = (3, 28, 32, 128)
    full, to_up, to_down, inner = call(
        pack_z,
        [planes, (32, 512), (32, 512), (16, 128)],
        [ext, from_down, from_up],
        scratch=[(3, 28, 16, 128), (128, 128)],
    )
    from_down, from_up = swap("gz", to_up, to_down)
    place = jnp.stack([lax.axis_index("gx"), lax.axis_index("gy")]).astype(jnp.int32)
    xy, patterns = call(
        bands_xy,
        [planes, jax.ShapeDtypeStruct((576, 512), BF16)],
        [place, full],
        scratch=[planes],
        first=SMEM,
        flops=30000000,
    )
    z_sides = [from_down, from_up]
    count = lax.axis_size("gx") * lax.axis_size("gy")
    (chunks,) = call(own_cells, [(count, 16, 128)], [to_up, to_down, *z_sides, inner], scratch=[(256, 128)])
    plane = lax.all_to_all(chunks, ("gx", "gy"), 0, 0, tiled=True)
    wide = (28, 32, 256)
    coef, res, inv = call(
        fine_residual,
        [wide] * 3,
        [full, xy, *z_sides],
        scratch=[(2, 28, 32, 128), wide, (28, 32, 128)],
        flops=30000000,
    )
    (base,) = call(
        fine_sweeps,
        [block],
        [full, coef, res, inv],
        scratch=[wide, wide, wide, wide, (448, 256), (448, 128), (128, 128)],
        flops=60000000,
    )
    (out,) = call(coarse_levels, [block], [patterns, plane.reshape(count * 16, 128), base], flops=30000000)
    return out


def solution(mesh):
    placed = (P("gx", "gy", "gz"), P("gx", "gy", "gz"), P("gx", "gy", "gz"), P())
    return jax.shard_map(on_device, mesh=mesh, in_specs=placed, out_specs=P("gx", "gy", "gz"), check_vma=False)
```

```python
import jax
import jax.numpy as jnp
from jax import lax
from jax.experimental import pallas as pl
from jax.experimental.pallas import tpu as pltpu
from jax.sharding import PartitionSpec as P

HALO = (6, 5, 4)
ROWS = (0, 6, 11, 15)
OMEGA = 2.0 / 3.0
F32 = jnp.float32
BF16 = jnp.bfloat16


def iota(shape, dim):
    return lax.broadcasted_iota(jnp.int32, shape, dim)


def ones_where(cond, scale=1.0):
    return jnp.where(cond, F32(scale), F32(0.0)).astype(BF16)


def split3(x):
    high = x.astype(BF16)
    rest = x - high.astype(F32)
    middle = rest.astype(BF16)
    low = (rest - middle.astype(F32)).astype(BF16)
    return high, middle, low


def select_rows(pattern, x):
    parts = [jnp.dot(pattern, part, preferred_element_type=F32) for part in split3(x)]
    return parts[0] + (parts[1] + parts[2])


def select_lanes(x, pattern):
    parts = [jnp.dot(part, pattern, preferred_element_type=F32) for part in split3(x)]
    return parts[0] + (parts[1] + parts[2])


def band(x, axis):
    x = x + pltpu.roll(x, 1, axis)
    return x + pltpu.roll(x, x.shape[axis] - 1, axis)


def band_yz(x):
    return band(band(x, x.ndim - 1), x.ndim - 2)


def band_x(x):
    up = jnp.concatenate([x[1:], x[:1]], axis=0)
    down = jnp.concatenate([x[-1:], x[:-1]], axis=0)
    return (up + down) + 2.0 * x


def damped_inverse(coef, diagonal):
    inside = coef > 0.0
    return jnp.where(inside, OMEGA / jnp.where(inside, diagonal, 1.0), 0.0)


def relax(corr, inverse, residual, coef, tu_corr, tu_product):
    return corr * (1.0 / 3.0) + inverse * (residual - 2.0 * (coef * corr) + 0.125 * (coef * tu_corr + tu_product))


def smooth_small(residual, coef, sweeps):
    inverse = damped_inverse(coef, 6.0 * coef + 0.125 * band_x(band_yz(coef)))
    corr = inverse * residual
    for _ in range(sweeps - 1):
        corr = relax(corr, inverse, residual, coef, band_x(band_yz(corr)), band_x(band_yz(coef * corr)))
    return corr


def lookup(phase, values):
    k = jnp.zeros(phase.shape, F32)
    for index in range(4):
        k = jnp.where(phase == index, values[index], k)
    return k


def send_x(table, phase, iterate, right, fields, to_up, to_down, values, phases, sems):
    copies = [
        pltpu.make_async_copy(table, values, sems.at[0]),
        pltpu.make_async_copy(phase, phases, sems.at[1]),
        pltpu.make_async_copy(iterate, fields.at[1], sems.at[2]),
        pltpu.make_async_copy(right, fields.at[2], sems.at[3]),
    ]
    for copy in copies:
        copy.start()
    for copy in copies:
        copy.wait()
    p = phases[...]
    k = jnp.zeros(p.shape, F32)
    for index in range(4):
        k = jnp.where(p == index, values[index], k)
    fields[0] = k
    for field in range(3):
        h, a, b = HALO[field], ROWS[field], ROWS[field + 1]
        to_up[a:b] = fields[field, 16 - h : 16]
        to_down[a:b] = fields[field, 0:h]


def hold(fields, held):
    held[...] = fields[...]


def pack_y(fields, from_down, from_up, ext, to_up, to_down):
    for field in range(3):
        h, a, b = HALO[field], ROWS[field], ROWS[field + 1]
        if h < 6:
            ext[field, 0 : 6 - h] = jnp.zeros((6 - h, 16, 128), F32)
            ext[field, 22 + h : 28] = jnp.zeros((6 - h, 16, 128), F32)
        ext[field, 6 - h : 6] = from_down[a:b]
        ext[field, 6:22] = fields[field]
        ext[field, 22 : 22 + h] = from_up[a:b]
        to_up[:, a:b, :] = ext[field, :, 16 - h : 16, :]
        to_down[:, a:b, :] = ext[field, :, 0:h, :]
    to_up[:, 15:16, :] = jnp.zeros((28, 1, 128), F32)
    to_down[:, 15:16, :] = jnp.zeros((28, 1, 128), F32)


def sum_quads(quads, q, sums):
    for at, f in enumerate(sums):
        f = f + pltpu.roll(f, 15, 0)
        f = f + pltpu.roll(f, 14, 0)
        for tile in range(f.shape[1] // 128):
            start = 64 * (at * (f.shape[1] // 128) + tile) + 16 * q
            quads[pl.ds(pl.multiple_of(start, 16), 16), :] = f[:, 128 * tile : 128 * tile + 128]


def read_quads(quads):
    count = quads.shape[0] // 64
    return jnp.concatenate([quads[pl.ds(64 * at, 16, stride=4), :] for at in range(count)], axis=1)


def pack_z(ext, from_down, from_up, full, to_up, to_down, inner, in_y, quads):
    for field in range(3):
        h, a, b = HALO[field], ROWS[field], ROWS[field + 1]
        full[field, :, 0:16, :] = ext[field]
        full[field, :, 16 : 16 + h, :] = from_up[:, a:b, :]
        full[field, :, 16 + h : 32 - h, :] = jnp.zeros((28, 16 - 2 * h, 128), F32)
        full[field, :, 32 - h : 32, :] = from_down[:, a:b, :]

    def bands_y(x, carry):
        k = full[0, x]
        v = full[1, x]
        for at, f in enumerate((k, v, k * v)):
            in_y[at, x] = band(f, 0)[0:16, :]
        return carry

    lax.fori_loop(5, 23, bands_y, 0, unroll=2)

    def quad(q, carry):
        sums = [None, None]
        for j in range(4):
            x = 6 + 4 * q + j
            tu = [band((in_y[at, x - 1] + in_y[at, x + 1]) + 2.0 * in_y[at, x], 1) for at in range(3)]
            k = full[0, x, 0:16, :]
            v = full[1, x, 0:16, :]
            diagonal = 6.0 * k + 0.125 * tu[0]
            res = full[2, x, 0:16, :] - (v * diagonal + 2.0 * (k * v) - 0.125 * (k * tu[1] + tu[2]))
            sums = [f if j == 0 else total + f for total, f in zip(sums, (res, k))]
        sum_quads(quads, q, sums)
        return carry

    lax.fori_loop(0, 4, quad, 0)
    source = iota((256, 128), 0)
    lane = iota((256, 128), 1)
    coarse = (source & 127) >> 2
    base = 64 + (source >> 7) * 16
    scale = jnp.where(source < 128, F32(0.25), F32(1.0 / 64.0))
    upper = (lane == base + coarse - 16) & (coarse >= 16) & (coarse <= 30)
    lower = (lane == base + coarse) & (coarse >= 1) & (coarse <= 15)
    stay = (lane == (source >> 7) * 64 + 16 + coarse) & (coarse >= 1) & (coarse <= 30)
    place = jnp.concatenate([jnp.where(found, scale, 0.0) for found in (upper, lower, stay)], axis=1).astype(BF16)
    level3 = select_lanes(read_quads(quads), place)
    inner[...] = level3[:, 256:384]
    lane = iota((32, 128), 1)

    for group in range(4):
        up = jnp.zeros((32, 128), F32)
        down = jnp.zeros((32, 128), F32)
        for x in range(8 * group, min(8 * group + 8, 28)):
            first = 16 * (x - 8 * group)
            for field in range(3):
                h, a, b = HALO[field], ROWS[field], ROWS[field + 1]
                cells = full[field, x]
                mine = (lane >= first + a) & (lane < first + b)
                up = jnp.where(mine, pltpu.roll(cells, (first + a + h) % 128, 1), up)
                down = jnp.where(mine, rolled(cells, first + a), down)
        to_up[:, 128 * group : 128 * group + 128] = up
        to_down[:, 128 * group : 128 * group + 128] = down
    to_up[0:16, 384:512] += level3[:, 0:128]
    to_down[0:16, 384:512] += level3[:, 128:256]


def rolled(x, shift):
    shift = shift % x.shape[1]
    return pltpu.roll(x, shift, 1) if shift else x


def bands_xy(place, full, xy, patterns, bands):
    row = iota((192, 512), 0)
    cell = iota((192, 512), 1)
    cell_x = (cell >> 6) * 4 + ((cell >> 2) & 3)
    cell_y = ((cell >> 4) & 3) * 4 + (cell & 3)
    for level in range(3):
        at_x = place[0] * (4 >> level) - 4 + (row >> 4)
        at_y = place[1] * (4 >> level) - 4 + (row & 15)
        found = ((cell_x >> level) == at_x) & ((cell_y >> level) == at_y)
        patterns[192 * level : 192 * level + 192, :] = ones_where(found)

    def in_y(x, carry):
        k = full[0, x]
        v = full[1, x]
        bands[0, x] = band(k, 0)
        bands[1, x] = band(v, 0)
        bands[2, x] = band(k * v, 0)
        return carry

    lax.fori_loop(0, 28, in_y, 0, unroll=2)

    def in_x(x, carry):
        for field in range(3):
            xy[field, x] = (bands[field, x - 1] + bands[field, x + 1]) + 2.0 * bands[field, x]
        return carry

    lax.fori_loop(1, 27, in_x, 0, unroll=2)
    for field in range(3):
        for x in (0, 27):
            xy[field, x] = jnp.zeros((32, 128), F32)


def end_cells(lower_k, lower_v, lower_right, upper_k, upper_v, upper_right):
    position = iota((32, 512), 1) & 15
    k = jnp.where(position < 6, lower_k, jnp.where(position < 12, upper_k, 0.0))
    v = jnp.where(position < 6, lower_v, upper_v)
    right = jnp.where(position < 6, lower_right, upper_right)[0:16, :]
    tu = []
    for f in (k, v, k * v):
        f = band(f, 0)[0:16, :]
        f = f + pltpu.roll(f, 16, 1)
        tu.append(band(f + pltpu.roll(f, 512 - 16, 1), 1))
    k, v = k[0:16, :], v[0:16, :]
    diagonal = 6.0 * k + 0.125 * tu[0]
    return right - (v * diagonal + 2.0 * (k * v) - 0.125 * (k * tu[1] + tu[2])), k


def own_cells(sent_up, sent_down, from_down, from_up, inner, chunks, quads):
    def moved(f, shift):
        return pltpu.roll(f, shift % 512, 1)

    low, first, last, high = from_down[...], sent_down[...], sent_up[...], from_up[...]
    found = [
        end_cells(low, moved(low, -5), moved(low, -9), moved(first, 6), first, moved(first, -5)),
        end_cells(last, moved(last, -5), moved(last, -9), moved(high, 6), high, moved(high, -5)),
    ]
    rows = []
    for f in (found[0][0], found[1][0], found[0][1], found[1][1]):
        f = f[:, 0:384]
        f = f + pltpu.roll(f, 15, 0)
        rows.append(f + pltpu.roll(f, 14, 0))
    source = iota((384, 128), 0)
    x = (source >> 4) - 6
    z = (source & 15) - 2
    place = (x >= 0) & (x < 16) & (z >= 0) & (z < 8) & (iota((384, 128), 1) == (x >> 2) * 32 + (z >> 2))
    ends = select_lanes(jnp.concatenate(rows, axis=0), ones_where(place))
    ends = [0.25 * ends[0:16], 0.25 * ends[16:32], ends[32:48] / 64.0, ends[48:64] / 64.0]
    for q in range(4):
        for at in range(4):
            start = 64 * at + 16 * q
            quads[start : start + 16, :] = rolled(ends[at], -32 * q)
    lane = iota((16, 128), 1)
    mine = inner[...]
    for at, target in enumerate((15, 47, 79, 111)):
        cells = pltpu.roll(quads[pl.ds(64 * at, 16, stride=4), :], target, 1)
        mine = jnp.where((lane == target) | (lane == target + 1), cells, mine)
    low = from_down[0:16, 384:512]
    high = from_up[0:16, 384:512]
    mine = jnp.where(lane < 15, pltpu.roll(low, 64, 1), mine)
    mine = jnp.where((lane >= 64) & (lane < 79), pltpu.roll(low, 112, 1), mine)
    mine = jnp.where((lane >= 49) & (lane < 64), pltpu.roll(high, 112, 1), mine)
    mine = jnp.where(lane >= 113, pltpu.roll(high, 32, 1), mine)
    chunks[...] = jnp.broadcast_to(mine[None], chunks.shape)


def fine_residual(full, xy, from_down, from_up, coef, res, inv, side, sides_kv, product):
    lane = iota((32, 128), 1)

    for x in range(28):
        group, first = 128 * (x // 8), 16 * (x % 8)
        up = from_up[:, group : group + 128]
        down = from_down[:, group : group + 128]
        tiles = []
        for field in range(3):
            h, a = HALO[field], ROWS[field]
            tile = jnp.where(lane >= 128 - h, rolled(down, 128 - h - first - a), 0.0)
            tiles.append(jnp.where(lane < h, rolled(up, -first - a), tile))
        coef[x, :, 0:128] = full[0, x]
        coef[x, :, 128:256] = tiles[0]
        side[0, x] = tiles[1]
        side[1, x] = tiles[2]
        sides_kv[x, :, 0:128] = band(tiles[0], 0)
        sides_kv[x, :, 128:256] = band(tiles[1], 0)
        product[x] = band(tiles[0] * tiles[1], 0)

    for x in (0, 1, 26, 27):
        res[x] = jnp.zeros((32, 256), F32)

    def over_x(ref, x):
        return (ref[x - 1] + ref[x + 1]) + 2.0 * ref[x]

    def cells(x, carry):
        sides = over_x(sides_kv, x)
        tu_k = band(jnp.concatenate([xy[0, x], sides[:, 0:128]], axis=1), 1)
        tu_v = band(jnp.concatenate([xy[1, x], sides[:, 128:256]], axis=1), 1)
        tu_kv = band(jnp.concatenate([xy[2, x], over_x(product, x)], axis=1), 1)
        k = coef[x]
        v = jnp.concatenate([full[1, x], side[0, x]], axis=1)
        diagonal = 6.0 * k + 0.125 * tu_k
        applied = v * diagonal + 2.0 * (k * v) - 0.125 * (k * tu_v + tu_kv)
        res[x] = jnp.concatenate([full[2, x], side[1, x]], axis=1) - applied
        inv[x] = damped_inverse(k, diagonal)
        return carry

    lax.fori_loop(2, 26, cells, 0, unroll=2)


def fine_sweeps(full, coef, res, inv, base, corr, corr_next, yz_c, yz_kc, pairs, narrow, spread):
    def over_x(ref, x):
        return (ref[x - 1] + ref[x + 1]) + 2.0 * ref[x]

    def first_sweep(x, carry):
        c = inv[x] * res[x]
        corr[x] = c
        yz_c[x] = band_yz(c)
        yz_kc[x] = band_yz(coef[x] * c)
        return carry

    lax.fori_loop(4, 24, first_sweep, 0, unroll=2)

    def second(x, carry):
        corr_next[x] = relax(corr[x], inv[x], res[x], coef[x], over_x(yz_c, x), over_x(yz_kc, x))
        return carry

    lax.fori_loop(5, 23, second, 0, unroll=2)

    def second_bands(x, carry):
        c = corr_next[x]
        yz_c[x] = band_yz(c)
        yz_kc[x] = band_yz(coef[x] * c)
        return carry

    lax.fori_loop(5, 23, second_bands, 0, unroll=2)

    halves = ones_where((iota((256, 128), 0) >> 1) == iota((256, 128), 1))

    def coarse(ref, scale):
        def pair(x, carry):
            pairs[pl.ds(pl.multiple_of(32 * x, 32), 32), :] = ref[2 * x] + ref[2 * x + 1]
            return carry

        lax.fori_loop(0, 14, pair, 0, unroll=2)
        narrow[...] = select_lanes(pairs[...], halves)
        summed = narrow[pl.ds(0, 224, stride=2), :] + narrow[pl.ds(1, 224, stride=2), :]
        return (scale * summed).reshape(14, 16, 128)

    corr_two = smooth_small(coarse(res, 0.5), coarse(coef, 0.125), 3)
    doubled = ones_where(iota((128, 128), 0) == (iota((128, 128), 1) >> 1))
    wide = select_lanes(corr_two[3:11].reshape(128, 128), doubled).reshape(8, 16, 128)
    rows = wide[:, 0:8, :].reshape(64, 128)
    spread[pl.ds(0, 64, stride=2), :] = rows
    spread[pl.ds(1, 64, stride=2), :] = rows

    def third(x, carry):
        c = relax(
            corr_next[x, 0:16, 0:128],
            inv[x, 0:16, 0:128],
            res[x, 0:16, 0:128],
            coef[x, 0:16, 0:128],
            (yz_c[x - 1, 0:16, 0:128] + yz_c[x + 1, 0:16, 0:128]) + 2.0 * yz_c[x, 0:16, 0:128],
            (yz_kc[x - 1, 0:16, 0:128] + yz_kc[x + 1, 0:16, 0:128]) + 2.0 * yz_kc[x, 0:16, 0:128],
        )
        block = x - 6
        base[block] = full[1, x, 0:16, :] + (c + spread[pl.ds(pl.multiple_of(16 * (block // 2), 16), 16), :])
        return carry

    lax.fori_loop(6, 22, third, 0, unroll=2)


def coarse_levels(patterns, plane, base, out):
    found = jnp.dot(patterns[...], jnp.concatenate(split3(plane[...]), axis=1), preferred_element_type=F32)
    found = found[:, 0:128] + (found[:, 128:256] + found[:, 256:384])
    windows = jnp.concatenate([found[192 * level : 192 * level + 192, :] for level in range(3)], axis=1)
    source = iota((384, 256), 0)
    lane = iota((384, 256), 1)
    level = source >> 7
    is_coef = (source >> 6) & 1
    start = jnp.where(level == 0, 0, jnp.where(level == 1, 64, 96))
    scale = jnp.where(is_coef == 1, jnp.where(level == 0, 1.0, jnp.where(level == 1, 0.125, 0.125**2)), 1.0)
    scale = jnp.where(is_coef == 0, jnp.where(level == 0, 1.0, jnp.where(level == 1, 0.5, 0.25)), scale)
    at = is_coef * 128 + start + ((source & 63) >> level)
    both = select_lanes(windows, jnp.where(lane == at, scale, 0.0).astype(BF16))
    corr = smooth_small(both[:, 0:128].reshape(12, 16, 128), both[:, 128:256].reshape(12, 16, 128), 4)
    source = iota((128, 384), 0)
    lane = iota((128, 384), 1)
    level = lane >> 7
    start = jnp.where(level == 0, 16, jnp.where(level == 1, 72, 100))
    wide = select_lanes(corr[4:8].reshape(64, 128), ones_where(source == start + ((lane & 127) >> (level + 2))))
    wide = jnp.concatenate([wide[:, 128 * level : 128 * level + 128] for level in range(3)], axis=0)
    row = iota((256, 192), 0)
    found = iota((256, 192), 1)
    shift = (found >> 6) + 2
    at = ((row >> 4) >> shift) * 16 + 4 + ((row & 15) >> shift)
    out[...] = base[...] + select_rows(ones_where((found & 63) == at), wide).reshape(16, 16, 128)


VMEM = pl.BlockSpec(memory_space=pltpu.VMEM)
SMEM = pl.BlockSpec(memory_space=pltpu.SMEM)
HBM = pl.BlockSpec(memory_space=pltpu.HBM)


def call(kernel, outs, ins, scratch=(), first=VMEM, rest=VMEM, flops=1000000, grant=32):
    moved = 4 * sum(x.size for x in ins)
    return pl.pallas_call(
        kernel,
        out_shape=[out if isinstance(out, jax.ShapeDtypeStruct) else jax.ShapeDtypeStruct(out, F32) for out in outs],
        in_specs=[first] + [rest] * (len(ins) - 1),
        out_specs=[VMEM] * len(outs),
        scratch_shapes=[pltpu.VMEM(shape, F32) if isinstance(shape, tuple) else shape for shape in scratch],
        compiler_params=pltpu.CompilerParams(vmem_limit_bytes=grant * 1024 * 1024),
        cost_estimate=pl.CostEstimate(flops=flops, bytes_accessed=moved, transcendentals=0),
        name=kernel.__name__,
    )(*ins)


def swap(axis, to_up, to_down):
    count = lax.axis_size(axis)
    up = [(i, i + 1) for i in range(count - 1)]
    down = [(i + 1, i) for i in range(count - 1)]
    return lax.ppermute(to_up, axis, up), lax.ppermute(to_down, axis, down)


def on_device(right, iterate, phase, table):
    block = (16, 16, 128)
    fields, to_up, to_down = call(
        send_x,
        [(3, *block), (15, 16, 128), (15, 16, 128)],
        [table, phase, iterate, right],
        scratch=[pltpu.SMEM((4,), F32), pltpu.VMEM(block, jnp.int32), pltpu.SemaphoreType.DMA((4,))],
        first=HBM,
        rest=HBM,
        grant=60,
    )
    from_down, from_up = swap("gx", to_up, to_down)
    (held,) = call(hold, [(3, *block)], [fields], flops=30000000)
    from_down, from_up, fields = lax.optimization_barrier((from_down, from_up, held))
    ext, to_up, to_down = call(pack_y, [(3, 28, 16, 128), (28, 16, 128), (28, 16, 128)], [fields, from_down, from_up])
    from_down, from_up = swap("gy", to_up, to_down)
    planes = (3, 28, 32, 128)
    full, to_up, to_down, inner = call(
        pack_z,
        [planes, (32, 512), (32, 512), (16, 128)],
        [ext, from_down, from_up],
        scratch=[(3, 28, 16, 128), (128, 128)],
    )
    from_down, from_up = swap("gz", to_up, to_down)
    place = jnp.stack([lax.axis_index("gx"), lax.axis_index("gy")]).astype(jnp.int32)
    xy, patterns = call(
        bands_xy,
        [planes, jax.ShapeDtypeStruct((576, 512), BF16)],
        [place, full],
        scratch=[planes],
        first=SMEM,
        flops=30000000,
    )
    from_down, from_up, xy, patterns = lax.optimization_barrier((from_down, from_up, xy, patterns))
    z_sides = [from_down, from_up]
    count = lax.axis_size("gx") * lax.axis_size("gy")
    (chunks,) = call(own_cells, [(count, 16, 128)], [to_up, to_down, *z_sides, inner], scratch=[(256, 128)])
    plane = lax.all_to_all(chunks, ("gx", "gy"), 0, 0, tiled=True)
    wide = (28, 32, 256)
    coef, res, inv = call(
        fine_residual,
        [wide] * 3,
        [full, xy, *z_sides],
        scratch=[(2, 28, 32, 128), wide, (28, 32, 128)],
        flops=30000000,
    )
    (base,) = call(
        fine_sweeps,
        [block],
        [full, coef, res, inv],
        scratch=[wide, wide, wide, wide, (448, 256), (448, 128), (128, 128)],
        flops=60000000,
    )
    (out,) = call(coarse_levels, [block], [patterns, plane.reshape(count * 16, 128), base], flops=30000000)
    return out


def solution(mesh):
    placed = (P("gx", "gy", "gz"), P("gx", "gy", "gz"), P("gx", "gy", "gz"), P())
    return jax.shard_map(on_device, mesh=mesh, in_specs=placed, out_specs=P("gx", "gy", "gz"), check_vma=False)
```

```python
import jax
import jax.numpy as jnp
from jax import lax
from jax.experimental import pallas as pl
from jax.experimental.pallas import tpu as pltpu
from jax.sharding import PartitionSpec as P

HALO = (6, 5, 4)
ROWS = (0, 6, 11, 15)
OMEGA = 2.0 / 3.0
F32 = jnp.float32
BF16 = jnp.bfloat16


def iota(shape, dim):
    return lax.broadcasted_iota(jnp.int32, shape, dim)


def ones_where(cond, scale=1.0):
    return jnp.where(cond, F32(scale), F32(0.0)).astype(BF16)


def split(x):
    high = x.astype(BF16)
    return high, (x - high.astype(F32)).astype(BF16)


def select_rows(pattern, x):
    high, low = [jnp.dot(pattern, part, preferred_element_type=F32) for part in split(x)]
    return high + low


def select_lanes(x, pattern):
    high, low = [jnp.dot(part, pattern, preferred_element_type=F32) for part in split(x)]
    return high + low


def band_matrix(size):
    apart = jnp.abs(iota((size, size), 0) - iota((size, size), 1))
    return jnp.where(apart == 0, 2.0, jnp.where((apart == 1) | (apart == size - 1), 1.0, 0.0)).astype(BF16)


def band_z(fields, matrix):
    shape = fields[0].shape
    rows = fields[0].size // shape[-1]
    found = select_lanes(jnp.concatenate([f.reshape(rows, shape[-1]) for f in fields], axis=0), matrix)
    return [found[rows * at : rows * at + rows].reshape(shape) for at in range(len(fields))]


def band(x, axis):
    x = x + pltpu.roll(x, 1, axis)
    return x + pltpu.roll(x, x.shape[axis] - 1, axis)


def band_yz(x):
    return band(band(x, x.ndim - 1), x.ndim - 2)


def band_x(x):
    up = jnp.concatenate([x[1:], x[:1]], axis=0)
    down = jnp.concatenate([x[-1:], x[:-1]], axis=0)
    return (up + down) + 2.0 * x


def damped_inverse(coef, diagonal):
    inside = coef > 0.0
    return jnp.where(inside, OMEGA / jnp.where(inside, diagonal, 1.0), 0.0)


def relax(corr, inverse, residual, coef, tu_corr, tu_product):
    return corr * (1.0 / 3.0) + inverse * (residual - 2.0 * (coef * corr) + 0.125 * (coef * tu_corr + tu_product))


def smooth_small(residual, coef, sweeps):
    matrix = band_matrix(coef.shape[-1])
    inverse = damped_inverse(coef, 6.0 * coef + 0.125 * band_z([band_x(band(coef, 1))], matrix)[0])
    corr = inverse * residual
    for _ in range(sweeps - 1):
        tu = band_z([band_x(band(f, 1)) for f in (corr, coef * corr)], matrix)
        corr = relax(corr, inverse, residual, coef, *tu)
    return corr


def send_x(table, phase, iterate, right, fields, to_up, to_down, values, phases, sems):
    copies = [
        pltpu.make_async_copy(table, values, sems.at[0]),
        pltpu.make_async_copy(phase, phases, sems.at[1]),
        pltpu.make_async_copy(iterate, fields.at[1], sems.at[2]),
        pltpu.make_async_copy(right, fields.at[2], sems.at[3]),
    ]
    for copy in copies:
        copy.start()
    for copy in copies:
        copy.wait()
    p = phases[...]
    k = jnp.zeros(p.shape, F32)
    for index in range(4):
        k = jnp.where(p == index, values[index], k)
    fields[0] = k
    for field in range(3):
        h, a, b = HALO[field], ROWS[field], ROWS[field + 1]
        to_up[a:b] = fields[field, 16 - h : 16]
        to_down[a:b] = fields[field, 0:h]


def hold(fields, held):
    held[...] = fields[...]


def pack_y(fields, from_down, from_up, ext, to_up, to_down):
    for field in range(3):
        h, a, b = HALO[field], ROWS[field], ROWS[field + 1]
        if h < 6:
            ext[field, 0 : 6 - h] = jnp.zeros((6 - h, 16, 128), F32)
            ext[field, 22 + h : 28] = jnp.zeros((6 - h, 16, 128), F32)
        ext[field, 6 - h : 6] = from_down[a:b]
        ext[field, 6:22] = fields[field]
        ext[field, 22 : 22 + h] = from_up[a:b]
        to_up[:, a:b, :] = ext[field, :, 16 - h : 16, :]
        to_down[:, a:b, :] = ext[field, :, 0:h, :]
    to_up[:, 15:16, :] = jnp.zeros((28, 1, 128), F32)
    to_down[:, 15:16, :] = jnp.zeros((28, 1, 128), F32)


def sum_quads(quads, q, sums):
    for at, f in enumerate(sums):
        f = f + pltpu.roll(f, 15, 0)
        f = f + pltpu.roll(f, 14, 0)
        for tile in range(f.shape[1] // 128):
            start = 64 * (at * (f.shape[1] // 128) + tile) + 16 * q
            quads[pl.ds(pl.multiple_of(start, 16), 16), :] = f[:, 128 * tile : 128 * tile + 128]


def read_quads(quads):
    count = quads.shape[0] // 64
    return jnp.concatenate([quads[pl.ds(64 * at, 16, stride=4), :] for at in range(count)], axis=1)


def pack_z(ext, from_down, from_up, full, to_up, to_down, inner, in_y, quads):
    for field in range(3):
        h, a, b = HALO[field], ROWS[field], ROWS[field + 1]
        full[field, :, 0:16, :] = ext[field]
        full[field, :, 16 : 16 + h, :] = from_up[:, a:b, :]
        full[field, :, 16 + h : 32 - h, :] = jnp.zeros((28, 16 - 2 * h, 128), F32)
        full[field, :, 32 - h : 32, :] = from_down[:, a:b, :]

    def bands_y(x, carry):
        k = full[0, x]
        v = full[1, x]
        for at, f in enumerate((k, v, k * v)):
            in_y[at, x] = band(f, 0)[0:16, :]
        return carry

    lax.fori_loop(5, 23, bands_y, 0, unroll=2)

    matrix = band_matrix(128)

    def quad(q, carry):
        sums = [None, None]
        xs = [6 + 4 * q + j for j in range(4)]
        all_tu = band_z(
            [(in_y[at, x - 1] + in_y[at, x + 1]) + 2.0 * in_y[at, x] for x in xs for at in range(3)], matrix
        )
        for j, x in enumerate(xs):
            tu = all_tu[3 * j : 3 * j + 3]
            k = full[0, x, 0:16, :]
            v = full[1, x, 0:16, :]
            diagonal = 6.0 * k + 0.125 * tu[0]
            res = full[2, x, 0:16, :] - (v * diagonal + 2.0 * (k * v) - 0.125 * (k * tu[1] + tu[2]))
            sums = [f if j == 0 else total + f for total, f in zip(sums, (res, k))]
        sum_quads(quads, q, sums)
        return carry

    lax.fori_loop(0, 4, quad, 0)
    source = iota((256, 128), 0)
    lane = iota((256, 128), 1)
    coarse = (source & 127) >> 2
    base = 64 + (source >> 7) * 16
    scale = jnp.where(source < 128, F32(0.25), F32(1.0 / 64.0))
    upper = (lane == base + coarse - 16) & (coarse >= 16) & (coarse <= 30)
    lower = (lane == base + coarse) & (coarse >= 1) & (coarse <= 15)
    stay = (lane == (source >> 7) * 64 + 16 + coarse) & (coarse >= 1) & (coarse <= 30)
    place = jnp.concatenate([jnp.where(found, scale, 0.0) for found in (upper, lower, stay)], axis=1).astype(BF16)
    level3 = select_lanes(read_quads(quads), place)
    inner[...] = level3[:, 256:384]
    lane = iota((32, 128), 1)

    for group in range(4):
        up = jnp.zeros((32, 128), F32)
        down = jnp.zeros((32, 128), F32)
        for x in range(8 * group, min(8 * group + 8, 28)):
            first = 16 * (x - 8 * group)
            for field in range(3):
                h, a, b = HALO[field], ROWS[field], ROWS[field + 1]
                cells = full[field, x]
                mine = (lane >= first + a) & (lane < first + b)
                up = jnp.where(mine, pltpu.roll(cells, (first + a + h) % 128, 1), up)
                down = jnp.where(mine, rolled(cells, first + a), down)
        to_up[:, 128 * group : 128 * group + 128] = up
        to_down[:, 128 * group : 128 * group + 128] = down
    to_up[0:16, 384:512] += level3[:, 0:128]
    to_down[0:16, 384:512] += level3[:, 128:256]


def rolled(x, shift):
    shift = shift % x.shape[1]
    return pltpu.roll(x, shift, 1) if shift else x


def bands_xy(place, full, xy, tables, bands):
    row = iota((192, 512), 0)
    cell = iota((192, 512), 1)
    cell_x = (cell >> 6) * 4 + ((cell >> 2) & 3)
    cell_y = ((cell >> 4) & 3) * 4 + (cell & 3)
    for level in range(3):
        at_x = place[0] * (4 >> level) - 4 + (row >> 4)
        at_y = place[1] * (4 >> level) - 4 + (row & 15)
        found = ((cell_x >> level) == at_x) & ((cell_y >> level) == at_y)
        tables[192 * level : 192 * level + 192, :] = ones_where(found)
    source = iota((128, 256), 0)
    lane = iota((128, 256), 1)
    is_coef = source >> 6
    for level, start in enumerate((0, 64, 96)):
        scale = jnp.where(is_coef == 1, F32(0.125**level), F32(0.5**level))
        found = lane == is_coef * 128 + start + ((source & 63) >> level)
        at = 576 + 128 * level
        tables[at : at + 128, 0:256] = jnp.where(found, scale, 0.0).astype(BF16)
    source = iota((128, 128), 0)
    lane = iota((128, 128), 1)
    row = iota((256, 64), 0)
    found = iota((256, 64), 1)
    for level, start in enumerate((16, 72, 100)):
        shift = level + 2
        tables[960:1088, 128 * level : 128 * level + 128] = ones_where(source == start + (lane >> shift))
        at = ((row >> 4) >> shift) * 16 + 4 + ((row & 15) >> shift)
        tables[1088:1344, 64 * level : 64 * level + 64] = ones_where(found == at)

    def in_y(x, carry):
        k = full[0, x]
        v = full[1, x]
        bands[0, x] = band(k, 0)
        bands[1, x] = band(v, 0)
        bands[2, x] = band(k * v, 0)
        return carry

    lax.fori_loop(0, 28, in_y, 0, unroll=2)

    def in_x(x, carry):
        for field in range(3):
            xy[field, x] = (bands[field, x - 1] + bands[field, x + 1]) + 2.0 * bands[field, x]
        return carry

    lax.fori_loop(1, 27, in_x, 0, unroll=2)
    for field in range(3):
        for x in (0, 27):
            xy[field, x] = jnp.zeros((32, 128), F32)


def end_cells(lower_k, lower_v, lower_right, upper_k, upper_v, upper_right):
    position = iota((32, 512), 1) & 15
    k = jnp.where(position < 6, lower_k, jnp.where(position < 12, upper_k, 0.0))
    v = jnp.where(position < 6, lower_v, upper_v)
    right = jnp.where(position < 6, lower_right, upper_right)[0:16, :]
    tu = []
    for f in (k, v, k * v):
        f = band(f, 0)[0:16, :]
        f = f + pltpu.roll(f, 16, 1)
        tu.append(band(f + pltpu.roll(f, 512 - 16, 1), 1))
    k, v = k[0:16, :], v[0:16, :]
    diagonal = 6.0 * k + 0.125 * tu[0]
    return right - (v * diagonal + 2.0 * (k * v) - 0.125 * (k * tu[1] + tu[2])), k


def own_cells(sent_up, sent_down, from_down, from_up, inner, chunks, quads):
    def moved(f, shift):
        return pltpu.roll(f, shift % 512, 1)

    low, first, last, high = from_down[...], sent_down[...], sent_up[...], from_up[...]
    found = [
        end_cells(low, moved(low, -5), moved(low, -9), moved(first, 6), first, moved(first, -5)),
        end_cells(last, moved(last, -5), moved(last, -9), moved(high, 6), high, moved(high, -5)),
    ]
    rows = []
    for f in (found[0][0], found[1][0], found[0][1], found[1][1]):
        f = f[:, 0:384]
        f = f + pltpu.roll(f, 15, 0)
        rows.append(f + pltpu.roll(f, 14, 0))
    source = iota((384, 128), 0)
    x = (source >> 4) - 6
    z = (source & 15) - 2
    place = (x >= 0) & (x < 16) & (z >= 0) & (z < 8) & (iota((384, 128), 1) == (x >> 2) * 32 + (z >> 2))
    ends = select_lanes(jnp.concatenate(rows, axis=0), ones_where(place))
    ends = [0.25 * ends[0:16], 0.25 * ends[16:32], ends[32:48] / 64.0, ends[48:64] / 64.0]
    for q in range(4):
        for at in range(4):
            start = 64 * at + 16 * q
            quads[start : start + 16, :] = rolled(ends[at], -32 * q)
    lane = iota((16, 128), 1)
    mine = inner[...]
    for at, target in enumerate((15, 47, 79, 111)):
        cells = pltpu.roll(quads[pl.ds(64 * at, 16, stride=4), :], target, 1)
        mine = jnp.where((lane == target) | (lane == target + 1), cells, mine)
    low = from_down[0:16, 384:512]
    high = from_up[0:16, 384:512]
    mine = jnp.where(lane < 15, pltpu.roll(low, 64, 1), mine)
    mine = jnp.where((lane >= 64) & (lane < 79), pltpu.roll(low, 112, 1), mine)
    mine = jnp.where((lane >= 49) & (lane < 64), pltpu.roll(high, 112, 1), mine)
    mine = jnp.where(lane >= 113, pltpu.roll(high, 32, 1), mine)
    chunks[...] = jnp.broadcast_to(mine[None], chunks.shape)


def fine_residual(full, xy, from_down, from_up, coef, res, inv, side, sides_kv, product):
    lane = iota((32, 128), 1)

    for x in range(28):
        group, first = 128 * (x // 8), 16 * (x % 8)
        up = from_up[:, group : group + 128]
        down = from_down[:, group : group + 128]
        tiles = []
        for field in range(3):
            h, a = HALO[field], ROWS[field]
            tile = jnp.where(lane >= 128 - h, rolled(down, 128 - h - first - a), 0.0)
            tiles.append(jnp.where(lane < h, rolled(up, -first - a), tile))
        coef[x, :, 0:128] = full[0, x]
        coef[x, :, 128:256] = tiles[0]
        side[0, x] = tiles[1]
        side[1, x] = tiles[2]
        sides_kv[x, :, 0:128] = band(tiles[0], 0)
        sides_kv[x, :, 128:256] = band(tiles[1], 0)
        product[x] = band(tiles[0] * tiles[1], 0)

    for x in (0, 1, 26, 27):
        res[x] = jnp.zeros((32, 256), F32)

    def over_x(ref, x):
        return (ref[x - 1] + ref[x + 1]) + 2.0 * ref[x]

    matrix = band_matrix(256)

    def cells(step, carry):
        xs = [2 + 8 * step + j for j in range(8)]
        wanted = []
        for x in xs:
            sides = over_x(sides_kv, x)
            wanted += [
                jnp.concatenate([xy[0, x], sides[:, 0:128]], axis=1),
                jnp.concatenate([xy[1, x], sides[:, 128:256]], axis=1),
                jnp.concatenate([xy[2, x], over_x(product, x)], axis=1),
            ]
        found = band_z(wanted, matrix)
        for j, x in enumerate(xs):
            tu_k, tu_v, tu_kv = found[3 * j : 3 * j + 3]
            k = coef[x]
            v = jnp.concatenate([full[1, x], side[0, x]], axis=1)
            diagonal = 6.0 * k + 0.125 * tu_k
            applied = v * diagonal + 2.0 * (k * v) - 0.125 * (k * tu_v + tu_kv)
            res[x] = jnp.concatenate([full[2, x], side[1, x]], axis=1) - applied
            inv[x] = damped_inverse(k, diagonal)
        return carry

    lax.fori_loop(0, 3, cells, 0)


def fine_sweeps(full, coef, res, inv, base, corr, corr_next, yz_c, yz_kc, pairs, spread):
    def over_x(ref, x):
        return (ref[x - 1] + ref[x + 1]) + 2.0 * ref[x]

    matrix = band_matrix(256)

    def bands_of(xs, ref):
        wanted = []
        for x in xs:
            c = ref[x]
            wanted += [band(c, 0), band(coef[x] * c, 0)]
        found = band_z(wanted, matrix)
        for j, x in enumerate(xs):
            yz_c[x] = found[2 * j]
            yz_kc[x] = found[2 * j + 1]

    def first_sweep(step, carry):
        xs = [4 + 4 * step + j for j in range(4)]
        for x in xs:
            corr[x] = inv[x] * res[x]
        bands_of(xs, corr)
        return carry

    lax.fori_loop(0, 5, first_sweep, 0)

    def second(x, carry):
        corr_next[x] = relax(corr[x], inv[x], res[x], coef[x], over_x(yz_c, x), over_x(yz_kc, x))
        return carry

    lax.fori_loop(5, 23, second, 0, unroll=3)

    def second_bands(step, carry):
        bands_of([5 + 3 * step + j for j in range(3)], corr_next)
        return carry

    lax.fori_loop(0, 6, second_bands, 0)

    halves = ones_where((iota((256, 128), 0) >> 1) == iota((256, 128), 1))

    def pair(x, carry):
        for at, ref in enumerate((res, coef)):
            f = ref[2 * x] + ref[2 * x + 1]
            for tile in range(2):
                place = pl.ds(pl.multiple_of(448 * at + 32 * x, 32), 32)
                pairs[tile, place, :] = f[:, 128 * tile : 128 * tile + 128]
        return carry

    lax.fori_loop(0, 14, pair, 0, unroll=2)
    sums = [pairs[tile, pl.ds(0, 448, stride=2), :] + pairs[tile, pl.ds(1, 448, stride=2), :] for tile in range(2)]
    sums = select_lanes(jnp.concatenate(sums, axis=1), halves).reshape(2, 14, 16, 128)
    corr_two = smooth_small(0.5 * sums[0], 0.125 * sums[1], 3)
    doubled = ones_where(iota((128, 128), 0) == (iota((128, 128), 1) >> 1))
    wide = select_lanes(corr_two[3:11].reshape(128, 128), doubled).reshape(8, 16, 128)
    rows = wide[:, 0:8, :].reshape(64, 128)
    spread[pl.ds(0, 64, stride=2), :] = rows
    spread[pl.ds(1, 64, stride=2), :] = rows

    def third(x, carry):
        c = relax(
            corr_next[x, 0:16, 0:128],
            inv[x, 0:16, 0:128],
            res[x, 0:16, 0:128],
            coef[x, 0:16, 0:128],
            (yz_c[x - 1, 0:16, 0:128] + yz_c[x + 1, 0:16, 0:128]) + 2.0 * yz_c[x, 0:16, 0:128],
            (yz_kc[x - 1, 0:16, 0:128] + yz_kc[x + 1, 0:16, 0:128]) + 2.0 * yz_kc[x, 0:16, 0:128],
        )
        block = x - 6
        base[block] = full[1, x, 0:16, :] + (c + spread[pl.ds(pl.multiple_of(16 * (block // 2), 16), 16), :])
        return carry

    lax.fori_loop(6, 22, third, 0, unroll=4)


def coarse_levels(tables, plane, base, out):
    found = jnp.dot(tables[0:576, :], jnp.concatenate(split(plane[...]), axis=1), preferred_element_type=F32)
    found = found[:, 0:128] + found[:, 128:256]
    windows = jnp.concatenate([found[192 * level : 192 * level + 192, :] for level in range(3)], axis=1)
    both = select_lanes(windows, tables[576:960, 0:256])
    corr = smooth_small(both[:, 0:128].reshape(12, 16, 128), both[:, 128:256].reshape(12, 16, 128), 4)
    wide = select_lanes(corr[4:8].reshape(64, 128), tables[960:1088, 0:384])
    wide = jnp.concatenate([wide[:, 128 * level : 128 * level + 128] for level in range(3)], axis=0)
    out[...] = base[...] + select_rows(tables[1088:1344, 0:192], wide).reshape(16, 16, 128)


VMEM = pl.BlockSpec(memory_space=pltpu.VMEM)
SMEM = pl.BlockSpec(memory_space=pltpu.SMEM)
HBM = pl.BlockSpec(memory_space=pltpu.HBM)


def call(kernel, outs, ins, scratch=(), first=VMEM, rest=VMEM, flops=1000000, grant=32):
    moved = 4 * sum(x.size for x in ins)
    return pl.pallas_call(
        kernel,
        out_shape=[out if isinstance(out, jax.ShapeDtypeStruct) else jax.ShapeDtypeStruct(out, F32) for out in outs],
        in_specs=[first] + [rest] * (len(ins) - 1),
        out_specs=[VMEM] * len(outs),
        scratch_shapes=[pltpu.VMEM(shape, F32) if isinstance(shape, tuple) else shape for shape in scratch],
        compiler_params=pltpu.CompilerParams(vmem_limit_bytes=grant * 1024 * 1024),
        cost_estimate=pl.CostEstimate(flops=flops, bytes_accessed=moved, transcendentals=0),
        name=kernel.__name__,
    )(*ins)


def swap(axis, to_up, to_down):
    count = lax.axis_size(axis)
    up = [(i, i + 1) for i in range(count - 1)]
    down = [(i + 1, i) for i in range(count - 1)]
    return lax.ppermute(to_up, axis, up), lax.ppermute(to_down, axis, down)


def on_device(right, iterate, phase, table):
    block = (16, 16, 128)
    fields, to_up, to_down = call(
        send_x,
        [(3, *block), (15, 16, 128), (15, 16, 128)],
        [table, phase, iterate, right],
        scratch=[pltpu.SMEM((4,), F32), pltpu.VMEM(block, jnp.int32), pltpu.SemaphoreType.DMA((4,))],
        first=HBM,
        rest=HBM,
        grant=60,
    )
    from_down, from_up = swap("gx", to_up, to_down)
    (held,) = call(hold, [(3, *block)], [fields], flops=30000000)
    from_down, from_up, fields = lax.optimization_barrier((from_down, from_up, held))
    ext, to_up, to_down = call(pack_y, [(3, 28, 16, 128), (28, 16, 128), (28, 16, 128)], [fields, from_down, from_up])
    from_down, from_up = swap("gy", to_up, to_down)
    planes = (3, 28, 32, 128)
    full, to_up, to_down, inner = call(
        pack_z,
        [planes, (32, 512), (32, 512), (16, 128)],
        [ext, from_down, from_up],
        scratch=[(3, 28, 16, 128), (128, 128)],
    )
    from_down, from_up = swap("gz", to_up, to_down)
    place = jnp.stack([lax.axis_index("gx"), lax.axis_index("gy")]).astype(jnp.int32)
    xy, tables = call(
        bands_xy,
        [planes, jax.ShapeDtypeStruct((1344, 512), BF16)],
        [place, full],
        scratch=[planes],
        first=SMEM,
        flops=30000000,
    )
    from_down, from_up, xy, tables = lax.optimization_barrier((from_down, from_up, xy, tables))
    z_sides = [from_down, from_up]
    count = lax.axis_size("gx") * lax.axis_size("gy")
    (chunks,) = call(own_cells, [(count, 16, 128)], [to_up, to_down, *z_sides, inner], scratch=[(256, 128)])
    plane = lax.all_to_all(chunks, ("gx", "gy"), 0, 0, tiled=True)
    wide = (28, 32, 256)
    coef, res, inv = call(
        fine_residual,
        [wide] * 3,
        [full, xy, *z_sides],
        scratch=[(2, 28, 32, 128), wide, (28, 32, 128)],
        flops=30000000,
    )
    (base,) = call(
        fine_sweeps,
        [block],
        [full, coef, res, inv],
        scratch=[wide, wide, wide, wide, (2, 896, 128), (128, 128)],
        flops=60000000,
    )
    (out,) = call(coarse_levels, [block], [tables, plane.reshape(count * 16, 128), base], flops=30000000)
    return out


def solution(mesh):
    placed = (P("gx", "gy", "gz"), P("gx", "gy", "gz"), P("gx", "gy", "gz"), P())
    return jax.shard_map(on_device, mesh=mesh, in_specs=placed, out_specs=P("gx", "gy", "gz"), check_vma=False)
```

```python
import jax
import jax.numpy as jnp
from jax import lax
from jax.experimental import pallas as pl
from jax.experimental.pallas import tpu as pltpu
from jax.sharding import PartitionSpec as P

HALO = (6, 5, 4)
ROWS = (0, 6, 11, 15)
OMEGA = 2.0 / 3.0
F32 = jnp.float32
BF16 = jnp.bfloat16


def iota(shape, dim):
    return lax.broadcasted_iota(jnp.int32, shape, dim)


def ones_where(cond, scale=1.0):
    return jnp.where(cond, F32(scale), F32(0.0)).astype(BF16)


def split(x):
    high = x.astype(BF16)
    rest = x - high.astype(F32)
    middle = rest.astype(BF16)
    return high, middle, (rest - middle.astype(F32)).astype(BF16)


def select_rows(pattern, x):
    high, middle, low = [jnp.dot(pattern, part, preferred_element_type=F32) for part in split(x)]
    return high + (middle + low)


def select_lanes(x, pattern):
    high, middle, low = [jnp.dot(part, pattern, preferred_element_type=F32) for part in split(x)]
    return high + (middle + low)


def band_matrix(size):
    apart = jnp.abs(iota((size, size), 0) - iota((size, size), 1))
    return jnp.where(apart == 0, 2.0, jnp.where((apart == 1) | (apart == size - 1), 1.0, 0.0)).astype(BF16)


def band_z(fields, matrix):
    shape = fields[0].shape
    rows = fields[0].size // shape[-1]
    found = select_lanes(jnp.concatenate([f.reshape(rows, shape[-1]) for f in fields], axis=0), matrix)
    return [found[rows * at : rows * at + rows].reshape(shape) for at in range(len(fields))]


def band(x, axis):
    return (pltpu.roll(x, 1, axis) + pltpu.roll(x, x.shape[axis] - 1, axis)) + 2.0 * x


def band_x(x):
    up = jnp.concatenate([x[1:], x[:1]], axis=0)
    down = jnp.concatenate([x[-1:], x[:-1]], axis=0)
    return (up + down) + 2.0 * x


def damped_inverse(coef, diagonal):
    inside = coef > 0.0
    return jnp.where(inside, OMEGA / jnp.where(inside, diagonal, 1.0), 0.0)


def relax(corr, inverse, residual, coef, tu_corr, tu_product):
    return corr * (1.0 / 3.0) + inverse * (residual - 2.0 * (coef * corr) + 0.125 * (coef * tu_corr + tu_product))


def smooth_small(residual, coef, sweeps, bands_z):
    inverse = damped_inverse(coef, 6.0 * coef + 0.125 * bands_z([band_x(band(coef, 1))])[0])
    corr = inverse * residual
    for _ in range(sweeps - 1):
        tu = bands_z([band_x(band(f, 1)) for f in (corr, coef * corr)])
        corr = relax(corr, inverse, residual, coef, *tu)
    return corr


def send_x(table, phase, iterate, right, fields, to_up, to_down, values, phases, sems):
    copies = [
        pltpu.make_async_copy(table, values, sems.at[0]),
        pltpu.make_async_copy(phase, phases, sems.at[1]),
        pltpu.make_async_copy(iterate, fields.at[1], sems.at[2]),
        pltpu.make_async_copy(right, fields.at[2], sems.at[3]),
    ]
    for copy in copies:
        copy.start()
    for copy in copies:
        copy.wait()
    p = phases[...]
    k = jnp.zeros(p.shape, F32)
    for index in range(4):
        k = jnp.where(p == index, values[index], k)
    fields[0] = k
    for field in range(3):
        h, a, b = HALO[field], ROWS[field], ROWS[field + 1]
        to_up[a:b] = fields[field, 16 - h : 16]
        to_down[a:b] = fields[field, 0:h]


def hold(fields, held):
    held[...] = fields[...]


def pack_y(fields, from_down, from_up, ext, to_up, to_down):
    for field in range(3):
        h, a, b = HALO[field], ROWS[field], ROWS[field + 1]
        if h < 6:
            ext[field, 0 : 6 - h] = jnp.zeros((6 - h, 16, 128), F32)
            ext[field, 22 + h : 28] = jnp.zeros((6 - h, 16, 128), F32)
        ext[field, 6 - h : 6] = from_down[a:b]
        ext[field, 6:22] = fields[field]
        ext[field, 22 : 22 + h] = from_up[a:b]
        to_up[:, a:b, :] = ext[field, :, 16 - h : 16, :]
        to_down[:, a:b, :] = ext[field, :, 0:h, :]
    to_up[:, 15:16, :] = jnp.zeros((28, 1, 128), F32)
    to_down[:, 15:16, :] = jnp.zeros((28, 1, 128), F32)


def sum_quads(quads, q, sums):
    for at, f in enumerate(sums):
        f = f + pltpu.roll(f, 15, 0)
        f = f + pltpu.roll(f, 14, 0)
        for tile in range(f.shape[1] // 128):
            start = 64 * (at * (f.shape[1] // 128) + tile) + 16 * q
            quads[pl.ds(pl.multiple_of(start, 16), 16), :] = f[:, 128 * tile : 128 * tile + 128]


def read_quads(quads):
    count = quads.shape[0] // 64
    return jnp.concatenate([quads[pl.ds(64 * at, 16, stride=4), :] for at in range(count)], axis=1)


def pack_z(ext, from_down, from_up, full, to_up, to_down, inner, in_y, quads):
    for field in range(3):
        h, a, b = HALO[field], ROWS[field], ROWS[field + 1]
        full[field, :, 0:16, :] = ext[field]
        full[field, :, 16 : 16 + h, :] = from_up[:, a:b, :]
        full[field, :, 16 + h : 32 - h, :] = jnp.zeros((28, 16 - 2 * h, 128), F32)
        full[field, :, 32 - h : 32, :] = from_down[:, a:b, :]

    def bands_y(x, carry):
        k = full[0, x]
        v = full[1, x]
        for at, f in enumerate((k, v, k * v)):
            in_y[at, x] = band(f, 0)[0:16, :]
        return carry

    lax.fori_loop(5, 23, bands_y, 0, unroll=2)

    matrix = band_matrix(128)

    def quad(q, carry):
        sums = [None, None]
        xs = [6 + 4 * q + j for j in range(4)]
        all_tu = band_z(
            [(in_y[at, x - 1] + in_y[at, x + 1]) + 2.0 * in_y[at, x] for x in xs for at in range(3)], matrix
        )
        for j, x in enumerate(xs):
            tu = all_tu[3 * j : 3 * j + 3]
            k = full[0, x, 0:16, :]
            v = full[1, x, 0:16, :]
            diagonal = 6.0 * k + 0.125 * tu[0]
            res = full[2, x, 0:16, :] - (v * diagonal + 2.0 * (k * v) - 0.125 * (k * tu[1] + tu[2]))
            sums = [f if j == 0 else total + f for total, f in zip(sums, (res, k))]
        sum_quads(quads, q, sums)
        return carry

    lax.fori_loop(0, 4, quad, 0)
    source = iota((256, 128), 0)
    lane = iota((256, 128), 1)
    coarse = (source & 127) >> 2
    base = 64 + (source >> 7) * 16
    scale = jnp.where(source < 128, F32(0.25), F32(1.0 / 64.0))
    upper = (lane == base + coarse - 16) & (coarse >= 16) & (coarse <= 30)
    lower = (lane == base + coarse) & (coarse >= 1) & (coarse <= 15)
    stay = (lane == (source >> 7) * 64 + 16 + coarse) & (coarse >= 1) & (coarse <= 30)
    place = jnp.concatenate([jnp.where(found, scale, 0.0) for found in (upper, lower, stay)], axis=1).astype(BF16)
    level3 = select_lanes(read_quads(quads), place)
    inner[...] = level3[:, 256:384]
    lane = iota((32, 128), 1)

    for group in range(4):
        up = jnp.zeros((32, 128), F32)
        down = jnp.zeros((32, 128), F32)
        for x in range(8 * group, min(8 * group + 8, 28)):
            first = 16 * (x - 8 * group)
            for field in range(3):
                h, a, b = HALO[field], ROWS[field], ROWS[field + 1]
                cells = full[field, x]
                mine = (lane >= first + a) & (lane < first + b)
                up = jnp.where(mine, pltpu.roll(cells, (first + a + h) % 128, 1), up)
                down = jnp.where(mine, rolled(cells, first + a), down)
        to_up[:, 128 * group : 128 * group + 128] = up
        to_down[:, 128 * group : 128 * group + 128] = down
    to_up[0:16, 384:512] += level3[:, 0:128]
    to_down[0:16, 384:512] += level3[:, 128:256]


def rolled(x, shift):
    shift = shift % x.shape[1]
    return pltpu.roll(x, shift, 1) if shift else x


def bands_xy(place, full, xy, tables, bands):
    row = iota((192, 512), 0)
    cell = iota((192, 512), 1)
    cell_x = (cell >> 6) * 4 + ((cell >> 2) & 3)
    cell_y = ((cell >> 4) & 3) * 4 + (cell & 3)
    for level in range(3):
        at_x = place[0] * (4 >> level) - 4 + (row >> 4)
        at_y = place[1] * (4 >> level) - 4 + (row & 15)
        found = ((cell_x >> level) == at_x) & ((cell_y >> level) == at_y)
        tables[192 * level : 192 * level + 192, :] = ones_where(found)
    source = iota((128, 256), 0)
    lane = iota((128, 256), 1)
    is_coef = source >> 6
    for level, start in enumerate((0, 64, 96)):
        scale = jnp.where(is_coef == 1, F32(0.125**level), F32(0.5**level))
        found = lane == is_coef * 128 + start + ((source & 63) >> level)
        at = 576 + 128 * level
        tables[at : at + 128, 0:256] = jnp.where(found, scale, 0.0).astype(BF16)
    source = iota((128, 128), 0)
    lane = iota((128, 128), 1)
    row = iota((256, 64), 0)
    found = iota((256, 64), 1)
    for level, start in enumerate((16, 72, 100)):
        shift = level + 2
        tables[960:1088, 128 * level : 128 * level + 128] = ones_where(source == start + (lane >> shift))
        at = ((row >> 4) >> shift) * 16 + 4 + ((row & 15) >> shift)
        tables[1088:1344, 64 * level : 64 * level + 64] = ones_where(found == at)

    def in_y(x, carry):
        k = full[0, x]
        v = full[1, x]
        bands[0, x] = band(k, 0)
        bands[1, x] = band(v, 0)
        bands[2, x] = band(k * v, 0)
        return carry

    lax.fori_loop(0, 28, in_y, 0, unroll=2)

    def in_x(x, carry):
        for field in range(3):
            xy[field, x] = (bands[field, x - 1] + bands[field, x + 1]) + 2.0 * bands[field, x]
        return carry

    lax.fori_loop(1, 27, in_x, 0, unroll=2)
    for field in range(3):
        for x in (0, 27):
            xy[field, x] = jnp.zeros((32, 128), F32)


def end_cells(lower_k, lower_v, lower_right, upper_k, upper_v, upper_right):
    position = iota((32, 512), 1) & 15
    k = jnp.where(position < 6, lower_k, jnp.where(position < 12, upper_k, 0.0))
    v = jnp.where(position < 6, lower_v, upper_v)
    right = jnp.where(position < 6, lower_right, upper_right)[0:16, :]
    tu = []
    for f in (k, v, k * v):
        f = band(f, 0)[0:16, :]
        f = f + pltpu.roll(f, 16, 1)
        tu.append(band(f + pltpu.roll(f, 512 - 16, 1), 1))
    k, v = k[0:16, :], v[0:16, :]
    diagonal = 6.0 * k + 0.125 * tu[0]
    return right - (v * diagonal + 2.0 * (k * v) - 0.125 * (k * tu[1] + tu[2])), k


def own_cells(sent_up, sent_down, from_down, from_up, inner, chunks, quads):
    def moved(f, shift):
        return pltpu.roll(f, shift % 512, 1)

    low, first, last, high = from_down[...], sent_down[...], sent_up[...], from_up[...]
    found = [
        end_cells(low, moved(low, -5), moved(low, -9), moved(first, 6), first, moved(first, -5)),
        end_cells(last, moved(last, -5), moved(last, -9), moved(high, 6), high, moved(high, -5)),
    ]
    rows = []
    for f in (found[0][0], found[1][0], found[0][1], found[1][1]):
        f = f[:, 0:384]
        f = f + pltpu.roll(f, 15, 0)
        rows.append(f + pltpu.roll(f, 14, 0))
    source = iota((384, 128), 0)
    x = (source >> 4) - 6
    z = (source & 15) - 2
    place = (x >= 0) & (x < 16) & (z >= 0) & (z < 8) & (iota((384, 128), 1) == (x >> 2) * 32 + (z >> 2))
    ends = select_lanes(jnp.concatenate(rows, axis=0), ones_where(place))
    ends = [0.25 * ends[0:16], 0.25 * ends[16:32], ends[32:48] / 64.0, ends[48:64] / 64.0]
    for q in range(4):
        for at in range(4):
            start = 64 * at + 16 * q
            quads[start : start + 16, :] = rolled(ends[at], -32 * q)
    lane = iota((16, 128), 1)
    mine = inner[...]
    for at, target in enumerate((15, 47, 79, 111)):
        cells = pltpu.roll(quads[pl.ds(64 * at, 16, stride=4), :], target, 1)
        mine = jnp.where((lane == target) | (lane == target + 1), cells, mine)
    low = from_down[0:16, 384:512]
    high = from_up[0:16, 384:512]
    mine = jnp.where(lane < 15, pltpu.roll(low, 64, 1), mine)
    mine = jnp.where((lane >= 64) & (lane < 79), pltpu.roll(low, 112, 1), mine)
    mine = jnp.where((lane >= 49) & (lane < 64), pltpu.roll(high, 112, 1), mine)
    mine = jnp.where(lane >= 113, pltpu.roll(high, 32, 1), mine)
    chunks[...] = jnp.broadcast_to(mine[None], chunks.shape)


def fine_residual(full, xy, from_down, from_up, coef, res, inv, side, sides_kv, product):
    lane = iota((32, 128), 1)

    for x in range(28):
        group, first = 128 * (x // 8), 16 * (x % 8)
        up = from_up[:, group : group + 128]
        down = from_down[:, group : group + 128]
        tiles = []
        for field in range(3):
            h, a = HALO[field], ROWS[field]
            tile = jnp.where(lane >= 128 - h, rolled(down, 128 - h - first - a), 0.0)
            tiles.append(jnp.where(lane < h, rolled(up, -first - a), tile))
        coef[x, :, 0:128] = full[0, x]
        coef[x, :, 128:256] = tiles[0]
        side[0, x] = tiles[1]
        side[1, x] = tiles[2]
        sides_kv[x, :, 0:128] = band(tiles[0], 0)
        sides_kv[x, :, 128:256] = band(tiles[1], 0)
        product[x] = band(tiles[0] * tiles[1], 0)

    for x in (0, 1, 26, 27):
        res[x] = jnp.zeros((32, 256), F32)

    def over_x(ref, x):
        return (ref[x - 1] + ref[x + 1]) + 2.0 * ref[x]

    matrix = band_matrix(256)

    def cells(step, carry):
        xs = [2 + 8 * step + j for j in range(8)]
        wanted = []
        for x in xs:
            sides = over_x(sides_kv, x)
            wanted += [
                jnp.concatenate([xy[0, x], sides[:, 0:128]], axis=1),
                jnp.concatenate([xy[1, x], sides[:, 128:256]], axis=1),
                jnp.concatenate([xy[2, x], over_x(product, x)], axis=1),
            ]
        found = band_z(wanted, matrix)
        for j, x in enumerate(xs):
            tu_k, tu_v, tu_kv = found[3 * j : 3 * j + 3]
            k = coef[x]
            v = jnp.concatenate([full[1, x], side[0, x]], axis=1)
            diagonal = 6.0 * k + 0.125 * tu_k
            applied = v * diagonal + 2.0 * (k * v) - 0.125 * (k * tu_v + tu_kv)
            res[x] = jnp.concatenate([full[2, x], side[1, x]], axis=1) - applied
            inv[x] = damped_inverse(k, diagonal)
        return carry

    lax.fori_loop(0, 3, cells, 0)


def fine_sweeps(full, coef, res, inv, base, corr, corr_next, yz_c, yz_kc, pairs, spread):
    def over_x(ref, x):
        return (ref[x - 1] + ref[x + 1]) + 2.0 * ref[x]

    matrix = band_matrix(256)

    def bands_of(xs, ref):
        wanted = []
        for x in xs:
            c = ref[x]
            wanted += [band(c, 0), band(coef[x] * c, 0)]
        found = band_z(wanted, matrix)
        for j, x in enumerate(xs):
            yz_c[x] = found[2 * j]
            yz_kc[x] = found[2 * j + 1]

    def first_sweep(step, carry):
        xs = [4 + 4 * step + j for j in range(4)]
        for x in xs:
            corr[x] = inv[x] * res[x]
        bands_of(xs, corr)
        return carry

    lax.fori_loop(0, 5, first_sweep, 0)

    def second(x, carry):
        corr_next[x] = relax(corr[x], inv[x], res[x], coef[x], over_x(yz_c, x), over_x(yz_kc, x))
        return carry

    lax.fori_loop(5, 23, second, 0, unroll=3)

    def second_bands(step, carry):
        bands_of([5 + 3 * step + j for j in range(3)], corr_next)
        return carry

    lax.fori_loop(0, 6, second_bands, 0)

    halves = ones_where((iota((256, 128), 0) >> 1) == iota((256, 128), 1))

    def pair(x, carry):
        for at, ref in enumerate((res, coef)):
            f = ref[2 * x] + ref[2 * x + 1]
            for tile in range(2):
                place = pl.ds(pl.multiple_of(448 * at + 32 * x, 32), 32)
                pairs[tile, place, :] = f[:, 128 * tile : 128 * tile + 128]
        return carry

    lax.fori_loop(0, 14, pair, 0, unroll=2)
    sums = [pairs[tile, pl.ds(0, 448, stride=2), :] + pairs[tile, pl.ds(1, 448, stride=2), :] for tile in range(2)]
    sums = select_lanes(jnp.concatenate(sums, axis=1), halves).reshape(2, 14, 16, 128)
    small = band_matrix(128)
    corr_two = smooth_small(0.5 * sums[0], 0.125 * sums[1], 3, lambda fields: band_z(fields, small))
    doubled = ones_where(iota((128, 128), 0) == (iota((128, 128), 1) >> 1))
    wide = select_lanes(corr_two[3:11].reshape(128, 128), doubled).reshape(8, 16, 128)
    rows = wide[:, 0:8, :].reshape(64, 128)
    spread[pl.ds(0, 64, stride=2), :] = rows
    spread[pl.ds(1, 64, stride=2), :] = rows

    def third(x, carry):
        c = relax(
            corr_next[x, 0:16, 0:128],
            inv[x, 0:16, 0:128],
            res[x, 0:16, 0:128],
            coef[x, 0:16, 0:128],
            (yz_c[x - 1, 0:16, 0:128] + yz_c[x + 1, 0:16, 0:128]) + 2.0 * yz_c[x, 0:16, 0:128],
            (yz_kc[x - 1, 0:16, 0:128] + yz_kc[x + 1, 0:16, 0:128]) + 2.0 * yz_kc[x, 0:16, 0:128],
        )
        block = x - 6
        base[block] = full[1, x, 0:16, :] + (c + spread[pl.ds(pl.multiple_of(16 * (block // 2), 16), 16), :])
        return carry

    lax.fori_loop(6, 22, third, 0, unroll=4)


def rolled_bands(fields):
    return [band(f, 2) for f in fields]


def coarse_levels(tables, plane, base, out):
    found = jnp.dot(tables[0:576, :], jnp.concatenate(split(plane[...]), axis=1), preferred_element_type=F32)
    found = found[:, 0:128] + (found[:, 128:256] + found[:, 256:384])
    windows = jnp.concatenate([found[192 * level : 192 * level + 192, :] for level in range(3)], axis=1)
    both = select_lanes(windows, tables[576:960, 0:256])
    corr = smooth_small(both[:, 0:128].reshape(12, 16, 128), both[:, 128:256].reshape(12, 16, 128), 4, rolled_bands)
    wide = select_lanes(corr[4:8].reshape(64, 128), tables[960:1088, 0:384])
    wide = jnp.concatenate([wide[:, 128 * level : 128 * level + 128] for level in range(3)], axis=0)
    out[...] = base[...] + select_rows(tables[1088:1344, 0:192], wide).reshape(16, 16, 128)


VMEM = pl.BlockSpec(memory_space=pltpu.VMEM)
SMEM = pl.BlockSpec(memory_space=pltpu.SMEM)
HBM = pl.BlockSpec(memory_space=pltpu.HBM)


def call(kernel, outs, ins, scratch=(), first=VMEM, rest=VMEM, flops=1000000, grant=32):
    moved = 4 * sum(x.size for x in ins)
    return pl.pallas_call(
        kernel,
        out_shape=[out if isinstance(out, jax.ShapeDtypeStruct) else jax.ShapeDtypeStruct(out, F32) for out in outs],
        in_specs=[first] + [rest] * (len(ins) - 1),
        out_specs=[VMEM] * len(outs),
        scratch_shapes=[pltpu.VMEM(shape, F32) if isinstance(shape, tuple) else shape for shape in scratch],
        compiler_params=pltpu.CompilerParams(vmem_limit_bytes=grant * 1024 * 1024),
        cost_estimate=pl.CostEstimate(flops=flops, bytes_accessed=moved, transcendentals=0),
        name=kernel.__name__,
    )(*ins)


def swap(axis, to_up, to_down):
    count = lax.axis_size(axis)
    up = [(i, i + 1) for i in range(count - 1)]
    down = [(i + 1, i) for i in range(count - 1)]
    return lax.ppermute(to_up, axis, up), lax.ppermute(to_down, axis, down)


def on_device(right, iterate, phase, table):
    block = (16, 16, 128)
    fields, to_up, to_down = call(
        send_x,
        [(3, *block), (15, 16, 128), (15, 16, 128)],
        [table, phase, iterate, right],
        scratch=[pltpu.SMEM((4,), F32), pltpu.VMEM(block, jnp.int32), pltpu.SemaphoreType.DMA((4,))],
        first=HBM,
        rest=HBM,
        grant=60,
    )
    from_down, from_up = swap("gx", to_up, to_down)
    (held,) = call(hold, [(3, *block)], [fields], flops=30000000)
    from_down, from_up, fields = lax.optimization_barrier((from_down, from_up, held))
    ext, to_up, to_down = call(pack_y, [(3, 28, 16, 128), (28, 16, 128), (28, 16, 128)], [fields, from_down, from_up])
    from_down, from_up = swap("gy", to_up, to_down)
    planes = (3, 28, 32, 128)
    full, to_up, to_down, inner = call(
        pack_z,
        [planes, (32, 512), (32, 512), (16, 128)],
        [ext, from_down, from_up],
        scratch=[(3, 28, 16, 128), (128, 128)],
    )
    from_down, from_up = swap("gz", to_up, to_down)
    place = jnp.stack([lax.axis_index("gx"), lax.axis_index("gy")]).astype(jnp.int32)
    xy, tables = call(
        bands_xy,
        [planes, jax.ShapeDtypeStruct((1344, 512), BF16)],
        [place, full],
        scratch=[planes],
        first=SMEM,
        flops=30000000,
    )
    from_down, from_up, xy, tables = lax.optimization_barrier((from_down, from_up, xy, tables))
    z_sides = [from_down, from_up]
    count = lax.axis_size("gx") * lax.axis_size("gy")
    (chunks,) = call(own_cells, [(count, 16, 128)], [to_up, to_down, *z_sides, inner], scratch=[(256, 128)])
    plane = lax.all_to_all(chunks, ("gx", "gy"), 0, 0, tiled=True)
    wide = (28, 32, 256)
    coef, res, inv = call(
        fine_residual,
        [wide] * 3,
        [full, xy, *z_sides],
        scratch=[(2, 28, 32, 128), wide, (28, 32, 128)],
        flops=30000000,
    )
    (base,) = call(
        fine_sweeps,
        [block],
        [full, coef, res, inv],
        scratch=[wide, wide, wide, wide, (2, 896, 128), (128, 128)],
        flops=60000000,
    )
    (out,) = call(coarse_levels, [block], [tables, plane.reshape(count * 16, 128), base], flops=30000000)
    return out


def solution(mesh):
    placed = (P("gx", "gy", "gz"), P("gx", "gy", "gz"), P("gx", "gy", "gz"), P())
    return jax.shard_map(on_device, mesh=mesh, in_specs=placed, out_specs=P("gx", "gy", "gz"), check_vma=False)
```

```python
import jax
import jax.numpy as jnp
from jax import lax
from jax.experimental import pallas as pl
from jax.experimental.pallas import tpu as pltpu
from jax.sharding import PartitionSpec as P

HALO = (6, 5, 4)
ROWS = (0, 6, 11, 15)
OMEGA = 2.0 / 3.0
F32 = jnp.float32
BF16 = jnp.bfloat16


def iota(shape, dim):
    return lax.broadcasted_iota(jnp.int32, shape, dim)


def ones_where(cond, scale=1.0):
    return jnp.where(cond, F32(scale), F32(0.0)).astype(BF16)


def split(x):
    high = x.astype(BF16)
    rest = x - high.astype(F32)
    middle = rest.astype(BF16)
    return high, middle, (rest - middle.astype(F32)).astype(BF16)


def select_rows(pattern, x):
    high, middle, low = [jnp.dot(pattern, part, preferred_element_type=F32) for part in split(x)]
    return high + (middle + low)


def select_lanes(x, pattern):
    high, middle, low = [jnp.dot(part, pattern, preferred_element_type=F32) for part in split(x)]
    return high + (middle + low)


def band_matrix(size):
    apart = jnp.abs(iota((size, size), 0) - iota((size, size), 1))
    return jnp.where(apart == 0, 2.0, jnp.where((apart == 1) | (apart == size - 1), 1.0, 0.0)).astype(BF16)


def band_z(fields, matrix):
    shape = fields[0].shape
    rows = fields[0].size // shape[-1]
    found = select_lanes(jnp.concatenate([f.reshape(rows, shape[-1]) for f in fields], axis=0), matrix)
    return [found[rows * at : rows * at + rows].reshape(shape) for at in range(len(fields))]


def band(x, axis):
    return (pltpu.roll(x, 1, axis) + pltpu.roll(x, x.shape[axis] - 1, axis)) + 2.0 * x


def band_x(x):
    up = jnp.concatenate([x[1:], x[:1]], axis=0)
    down = jnp.concatenate([x[-1:], x[:-1]], axis=0)
    return (up + down) + 2.0 * x


def damped_inverse(coef, diagonal):
    inside = coef > 0.0
    return jnp.where(inside, OMEGA / jnp.where(inside, diagonal, 1.0), 0.0)


def relax(corr, inverse, residual, coef, tu_corr, tu_product):
    return corr * (1.0 / 3.0) + inverse * (residual - 2.0 * (coef * corr) + 0.125 * (coef * tu_corr + tu_product))


def smooth_small(residual, coef, sweeps, bands_z):
    inverse = damped_inverse(coef, 6.0 * coef + 0.125 * bands_z([band_x(band(coef, 1))])[0])
    corr = inverse * residual
    for _ in range(sweeps - 1):
        tu = bands_z([band_x(band(f, 1)) for f in (corr, coef * corr)])
        corr = relax(corr, inverse, residual, coef, *tu)
    return corr


def send_x(table, phase, iterate, right, fields, to_up, to_down, values, phases, sems):
    copies = [
        pltpu.make_async_copy(table, values, sems.at[0]),
        pltpu.make_async_copy(phase, phases, sems.at[1]),
        pltpu.make_async_copy(iterate, fields.at[1], sems.at[2]),
        pltpu.make_async_copy(right, fields.at[2], sems.at[3]),
    ]
    for copy in copies:
        copy.start()
    for copy in copies:
        copy.wait()
    p = phases[...]
    k = jnp.zeros(p.shape, F32)
    for index in range(4):
        k = jnp.where(p == index, values[index], k)
    fields[0] = k
    for field in range(3):
        h, a, b = HALO[field], ROWS[field], ROWS[field + 1]
        to_up[a:b] = fields[field, 16 - h : 16]
        to_down[a:b] = fields[field, 0:h]


def hold(fields, held):
    held[...] = fields[...]


def pack_y(fields, from_down, from_up, ext, to_up, to_down):
    for field in range(3):
        h, a, b = HALO[field], ROWS[field], ROWS[field + 1]
        if h < 6:
            ext[field, 0 : 6 - h] = jnp.zeros((6 - h, 16, 128), F32)
            ext[field, 22 + h : 28] = jnp.zeros((6 - h, 16, 128), F32)
        ext[field, 6 - h : 6] = from_down[a:b]
        ext[field, 6:22] = fields[field]
        ext[field, 22 : 22 + h] = from_up[a:b]
        to_up[:, a:b, :] = ext[field, :, 16 - h : 16, :]
        to_down[:, a:b, :] = ext[field, :, 0:h, :]
    to_up[:, 15:16, :] = jnp.zeros((28, 1, 128), F32)
    to_down[:, 15:16, :] = jnp.zeros((28, 1, 128), F32)


def sum_quads(quads, q, sums):
    for at, f in enumerate(sums):
        f = f + pltpu.roll(f, 15, 0)
        f = f + pltpu.roll(f, 14, 0)
        for tile in range(f.shape[1] // 128):
            start = 64 * (at * (f.shape[1] // 128) + tile) + 16 * q
            quads[pl.ds(pl.multiple_of(start, 16), 16), :] = f[:, 128 * tile : 128 * tile + 128]


def read_quads(quads):
    count = quads.shape[0] // 64
    return jnp.concatenate([quads[pl.ds(64 * at, 16, stride=4), :] for at in range(count)], axis=1)


def pack_lanes(cells_of, rows, to_up, to_down, at):
    lane = iota((rows, 128), 1)
    for group in range(4):
        up = jnp.zeros((rows, 128), F32)
        down = jnp.zeros((rows, 128), F32)
        for x in range(8 * group, min(8 * group + 8, 28)):
            first = 16 * (x - 8 * group)
            for field in range(3):
                h, a, b = HALO[field], ROWS[field], ROWS[field + 1]
                cells = cells_of(field, x)
                mine = (lane >= first + a) & (lane < first + b)
                up = jnp.where(mine, pltpu.roll(cells, (first + a + h) % 128, 1), up)
                down = jnp.where(mine, rolled(cells, first + a), down)
        to_up[at : at + rows, 128 * group : 128 * group + 128] = up
        to_down[at : at + rows, 128 * group : 128 * group + 128] = down


def own_rows(ext, up, down, xz):
    pack_lanes(lambda field, x: ext[field, x], 16, up, down, 0)
    matrix = band_matrix(128)

    def bands(step, carry):
        xs = [6 + 4 * step + j for j in range(4)]
        wanted = []
        for x in xs:
            around = [(ext[0, x + d], ext[1, x + d]) for d in (-1, 0, 1)]
            for low, here, high in zip(*[(k, v, k * v) for k, v in around]):
                wanted.append((low + high) + 2.0 * here)
        for at, f in enumerate(band_z(wanted, matrix)):
            xz[at % 3, xs[at // 3] - 6] = f
        return carry

    lax.fori_loop(0, 4, bands, 0)


def pack_z(ext, from_down, from_up, up_rows, down_rows, xz, full, to_up, to_down, inner, edges, quads):
    for field in range(3):
        h, a, b = HALO[field], ROWS[field], ROWS[field + 1]
        full[field, :, 0:16, :] = ext[field]
        full[field, :, 16 : 16 + h, :] = from_up[:, a:b, :]
        full[field, :, 16 + h : 32 - h, :] = jnp.zeros((28, 16 - 2 * h, 128), F32)
        full[field, :, 32 - h : 32, :] = from_down[:, a:b, :]
    edges[:, 24:32, :] = jnp.zeros((6, 8, 128), F32)
    for at, (source, row_k, row_v) in enumerate(((from_down, 5, 10), (from_up, 0, 6))):
        k = source[:, row_k, :]
        v = source[:, row_v, :]
        for place, f in enumerate((k, v, k * v)):
            edges[3 * at + place, 0:28, :] = f
    matrix = band_matrix(128)
    for at, f in enumerate(band_z([band(edges[at], 0) for at in range(6)], matrix)):
        edges[at] = f
    row = iota((16, 128), 0)

    def quad(q, carry):
        sums = [None, None]
        for j in range(4):
            x = 6 + 4 * q + j
            tu = []
            for at in range(3):
                f = xz[at, 4 * q + j]
                below = jnp.where(row == 0, edges[at, pl.ds(x, 1), :], pltpu.roll(f, 1, 0))
                above = jnp.where(row == 15, edges[3 + at, pl.ds(x, 1), :], pltpu.roll(f, 15, 0))
                tu.append((below + above) + 2.0 * f)
            k = ext[0, x]
            v = ext[1, x]
            diagonal = 6.0 * k + 0.125 * tu[0]
            res = ext[2, x] - (v * diagonal + 2.0 * (k * v) - 0.125 * (k * tu[1] + tu[2]))
            sums = [f if j == 0 else total + f for total, f in zip(sums, (res, k))]
        sum_quads(quads, q, sums)
        return carry

    lax.fori_loop(0, 4, quad, 0)
    source = iota((256, 128), 0)
    lane = iota((256, 128), 1)
    coarse = (source & 127) >> 2
    base = 64 + (source >> 7) * 16
    scale = jnp.where(source < 128, F32(0.25), F32(1.0 / 64.0))
    upper = (lane == base + coarse - 16) & (coarse >= 16) & (coarse <= 30)
    lower = (lane == base + coarse) & (coarse >= 1) & (coarse <= 15)
    stay = (lane == (source >> 7) * 64 + 16 + coarse) & (coarse >= 1) & (coarse <= 30)
    place = jnp.concatenate([jnp.where(found, scale, 0.0) for found in (upper, lower, stay)], axis=1).astype(BF16)
    level3 = select_lanes(read_quads(quads), place)
    inner[...] = level3[:, 256:384]
    to_up[0:16, :] = up_rows[...]
    to_down[0:16, :] = down_rows[...]
    pack_lanes(lambda field, x: full[field, x, 16:32, :], 16, to_up, to_down, 16)
    to_up[0:16, 384:512] += level3[:, 0:128]
    to_down[0:16, 384:512] += level3[:, 128:256]


def rolled(x, shift):
    shift = shift % x.shape[1]
    return pltpu.roll(x, shift, 1) if shift else x


def bands_xy(place, full, xy, tables, bands):
    row = iota((192, 512), 0)
    cell = iota((192, 512), 1)
    cell_x = (cell >> 6) * 4 + ((cell >> 2) & 3)
    cell_y = ((cell >> 4) & 3) * 4 + (cell & 3)
    for level in range(3):
        at_x = place[0] * (4 >> level) - 4 + (row >> 4)
        at_y = place[1] * (4 >> level) - 4 + (row & 15)
        found = ((cell_x >> level) == at_x) & ((cell_y >> level) == at_y)
        tables[192 * level : 192 * level + 192, :] = ones_where(found)
    source = iota((128, 256), 0)
    lane = iota((128, 256), 1)
    is_coef = source >> 6
    for level, start in enumerate((0, 64, 96)):
        scale = jnp.where(is_coef == 1, F32(0.125**level), F32(0.5**level))
        found = lane == is_coef * 128 + start + ((source & 63) >> level)
        at = 576 + 128 * level
        tables[at : at + 128, 0:256] = jnp.where(found, scale, 0.0).astype(BF16)
    source = iota((128, 128), 0)
    lane = iota((128, 128), 1)
    for level, start in enumerate((16, 72, 100)):
        found = source == start + (lane >> (level + 2))
        tables[960:1088, 128 * level : 128 * level + 128] = ones_where(found)

    def in_y(x, carry):
        k = full[0, x]
        v = full[1, x]
        bands[0, x] = band(k, 0)
        bands[1, x] = band(v, 0)
        bands[2, x] = band(k * v, 0)
        return carry

    lax.fori_loop(0, 28, in_y, 0, unroll=2)

    def in_x(x, carry):
        for field in range(3):
            xy[field, x] = (bands[field, x - 1] + bands[field, x + 1]) + 2.0 * bands[field, x]
        return carry

    lax.fori_loop(1, 27, in_x, 0, unroll=2)
    for field in range(3):
        for x in (0, 27):
            xy[field, x] = jnp.zeros((32, 128), F32)


def end_cells(lower_k, lower_v, lower_right, upper_k, upper_v, upper_right):
    position = iota((32, 512), 1) & 15
    k = jnp.where(position < 6, lower_k, jnp.where(position < 12, upper_k, 0.0))
    v = jnp.where(position < 6, lower_v, upper_v)
    right = jnp.where(position < 6, lower_right, upper_right)[0:16, :]
    tu = []
    for f in (k, v, k * v):
        f = band(f, 0)[0:16, :]
        f = f + pltpu.roll(f, 16, 1)
        tu.append(band(f + pltpu.roll(f, 512 - 16, 1), 1))
    k, v = k[0:16, :], v[0:16, :]
    diagonal = 6.0 * k + 0.125 * tu[0]
    return right - (v * diagonal + 2.0 * (k * v) - 0.125 * (k * tu[1] + tu[2])), k


def own_cells(sent_up, sent_down, from_down, from_up, inner, chunks, quads):
    def moved(f, shift):
        return pltpu.roll(f, shift % 512, 1)

    low, first, last, high = from_down[...], sent_down[...], sent_up[...], from_up[...]
    found = [
        end_cells(low, moved(low, -5), moved(low, -9), moved(first, 6), first, moved(first, -5)),
        end_cells(last, moved(last, -5), moved(last, -9), moved(high, 6), high, moved(high, -5)),
    ]
    rows = []
    for f in (found[0][0], found[1][0], found[0][1], found[1][1]):
        f = f[:, 0:384]
        f = f + pltpu.roll(f, 15, 0)
        rows.append(f + pltpu.roll(f, 14, 0))
    source = iota((384, 128), 0)
    x = (source >> 4) - 6
    z = (source & 15) - 2
    place = (x >= 0) & (x < 16) & (z >= 0) & (z < 8) & (iota((384, 128), 1) == (x >> 2) * 32 + (z >> 2))
    ends = select_lanes(jnp.concatenate(rows, axis=0), ones_where(place))
    ends = [0.25 * ends[0:16], 0.25 * ends[16:32], ends[32:48] / 64.0, ends[48:64] / 64.0]
    for q in range(4):
        for at in range(4):
            start = 64 * at + 16 * q
            quads[start : start + 16, :] = rolled(ends[at], -32 * q)
    lane = iota((16, 128), 1)
    mine = inner[...]
    for at, target in enumerate((15, 47, 79, 111)):
        cells = pltpu.roll(quads[pl.ds(64 * at, 16, stride=4), :], target, 1)
        mine = jnp.where((lane == target) | (lane == target + 1), cells, mine)
    low = from_down[0:16, 384:512]
    high = from_up[0:16, 384:512]
    mine = jnp.where(lane < 15, pltpu.roll(low, 64, 1), mine)
    mine = jnp.where((lane >= 64) & (lane < 79), pltpu.roll(low, 112, 1), mine)
    mine = jnp.where((lane >= 49) & (lane < 64), pltpu.roll(high, 112, 1), mine)
    mine = jnp.where(lane >= 113, pltpu.roll(high, 32, 1), mine)
    chunks[...] = jnp.broadcast_to(mine[None], chunks.shape)


def fine_residual(full, xy, from_down, from_up, coef, res, inv, side, sides_kv, product):
    lane = iota((32, 128), 1)

    for x in range(28):
        group, first = 128 * (x // 8), 16 * (x % 8)
        up = from_up[:, group : group + 128]
        down = from_down[:, group : group + 128]
        tiles = []
        for field in range(3):
            h, a = HALO[field], ROWS[field]
            tile = jnp.where(lane >= 128 - h, rolled(down, 128 - h - first - a), 0.0)
            tiles.append(jnp.where(lane < h, rolled(up, -first - a), tile))
        coef[x, :, 0:128] = full[0, x]
        coef[x, :, 128:256] = tiles[0]
        side[0, x] = tiles[1]
        side[1, x] = tiles[2]
        sides_kv[x, :, 0:128] = band(tiles[0], 0)
        sides_kv[x, :, 128:256] = band(tiles[1], 0)
        product[x] = band(tiles[0] * tiles[1], 0)

    for x in (0, 1, 26, 27):
        res[x] = jnp.zeros((32, 256), F32)

    def over_x(ref, x):
        return (ref[x - 1] + ref[x + 1]) + 2.0 * ref[x]

    matrix = band_matrix(256)

    def cells(step, carry):
        xs = [2 + 8 * step + j for j in range(8)]
        wanted = []
        for x in xs:
            sides = over_x(sides_kv, x)
            wanted += [
                jnp.concatenate([xy[0, x], sides[:, 0:128]], axis=1),
                jnp.concatenate([xy[1, x], sides[:, 128:256]], axis=1),
                jnp.concatenate([xy[2, x], over_x(product, x)], axis=1),
            ]
        found = band_z(wanted, matrix)
        for j, x in enumerate(xs):
            tu_k, tu_v, tu_kv = found[3 * j : 3 * j + 3]
            k = coef[x]
            v = jnp.concatenate([full[1, x], side[0, x]], axis=1)
            diagonal = 6.0 * k + 0.125 * tu_k
            applied = v * diagonal + 2.0 * (k * v) - 0.125 * (k * tu_v + tu_kv)
            res[x] = jnp.concatenate([full[2, x], side[1, x]], axis=1) - applied
            inv[x] = damped_inverse(k, diagonal)
        return carry

    lax.fori_loop(0, 3, cells, 0)


def fine_sweeps(full, coef, res, inv, base, corr, corr_next, yz_c, yz_kc, pairs, spread):
    def over_x(ref, x):
        return (ref[x - 1] + ref[x + 1]) + 2.0 * ref[x]

    matrix = band_matrix(256)

    def bands_of(xs, ref):
        wanted = []
        for x in xs:
            c = ref[x]
            wanted += [band(c, 0), band(coef[x] * c, 0)]
        found = band_z(wanted, matrix)
        for j, x in enumerate(xs):
            yz_c[x] = found[2 * j]
            yz_kc[x] = found[2 * j + 1]

    def first_sweep(step, carry):
        xs = [4 + 4 * step + j for j in range(4)]
        for x in xs:
            corr[x] = inv[x] * res[x]
        bands_of(xs, corr)
        return carry

    lax.fori_loop(0, 5, first_sweep, 0)

    def second(x, carry):
        corr_next[x] = relax(corr[x], inv[x], res[x], coef[x], over_x(yz_c, x), over_x(yz_kc, x))
        return carry

    lax.fori_loop(5, 23, second, 0, unroll=3)

    def second_bands(step, carry):
        bands_of([5 + 3 * step + j for j in range(3)], corr_next)
        return carry

    lax.fori_loop(0, 6, second_bands, 0)

    halves = ones_where((iota((256, 128), 0) >> 1) == iota((256, 128), 1))

    def pair(x, carry):
        for at, ref in enumerate((res, coef)):
            f = ref[2 * x] + ref[2 * x + 1]
            for tile in range(2):
                place = pl.ds(pl.multiple_of(448 * at + 32 * x, 32), 32)
                pairs[tile, place, :] = f[:, 128 * tile : 128 * tile + 128]
        return carry

    lax.fori_loop(0, 14, pair, 0, unroll=2)
    sums = [pairs[tile, pl.ds(0, 448, stride=2), :] + pairs[tile, pl.ds(1, 448, stride=2), :] for tile in range(2)]
    sums = select_lanes(jnp.concatenate(sums, axis=1), halves).reshape(2, 14, 16, 128)
    small = band_matrix(128)
    corr_two = smooth_small(0.5 * sums[0], 0.125 * sums[1], 3, lambda fields: band_z(fields, small))
    doubled = ones_where(iota((128, 128), 0) == (iota((128, 128), 1) >> 1))
    wide = select_lanes(corr_two[3:11].reshape(128, 128), doubled).reshape(8, 16, 128)
    rows = wide[:, 0:8, :].reshape(64, 128)
    spread[pl.ds(0, 64, stride=2), :] = rows
    spread[pl.ds(1, 64, stride=2), :] = rows

    def third(x, carry):
        c = relax(
            corr_next[x, 0:16, 0:128],
            inv[x, 0:16, 0:128],
            res[x, 0:16, 0:128],
            coef[x, 0:16, 0:128],
            (yz_c[x - 1, 0:16, 0:128] + yz_c[x + 1, 0:16, 0:128]) + 2.0 * yz_c[x, 0:16, 0:128],
            (yz_kc[x - 1, 0:16, 0:128] + yz_kc[x + 1, 0:16, 0:128]) + 2.0 * yz_kc[x, 0:16, 0:128],
        )
        block = x - 6
        base[block] = full[1, x, 0:16, :] + (c + spread[pl.ds(pl.multiple_of(16 * (block // 2), 16), 16), :])
        return carry

    lax.fori_loop(6, 22, third, 0, unroll=4)


def rolled_bands(fields):
    return [band(f, 2) for f in fields]


def coarse_levels(tables, plane, base, out, spread):
    found = jnp.dot(tables[0:576, :], jnp.concatenate(split(plane[...]), axis=1), preferred_element_type=F32)
    found = found[:, 0:128] + (found[:, 128:256] + found[:, 256:384])
    windows = jnp.concatenate([found[192 * level : 192 * level + 192, :] for level in range(3)], axis=1)
    both = select_lanes(windows, tables[576:960, 0:256])
    corr = smooth_small(both[:, 0:128].reshape(12, 16, 128), both[:, 128:256].reshape(12, 16, 128), 4, rolled_bands)
    wide = select_lanes(corr[4:8].reshape(64, 128), tables[960:1088, 0:384])
    for x in range(4):
        level4 = wide[16 * (x // 2) : 16 * (x // 2) + 16, 128:256]
        level4 = jnp.concatenate([jnp.broadcast_to(level4[y : y + 1], (2, 128)) for y in (4, 5)], axis=0)
        rows = wide[16 * x + 4 : 16 * x + 8, 0:128] + (level4 + wide[4:5, 256:384])
        for y in range(4):
            spread[pl.ds(16 * x + y, 4, stride=4), :] = rows
    for x in range(16):
        start = 16 * (x // 4)
        out[x] = base[x] + spread[start : start + 16, :]


VMEM = pl.BlockSpec(memory_space=pltpu.VMEM)
SMEM = pl.BlockSpec(memory_space=pltpu.SMEM)
HBM = pl.BlockSpec(memory_space=pltpu.HBM)


def call(kernel, outs, ins, scratch=(), first=VMEM, rest=VMEM, flops=1000000, grant=32):
    moved = 4 * sum(x.size for x in ins)
    return pl.pallas_call(
        kernel,
        out_shape=[out if isinstance(out, jax.ShapeDtypeStruct) else jax.ShapeDtypeStruct(out, F32) for out in outs],
        in_specs=[first] + [rest] * (len(ins) - 1),
        out_specs=[VMEM] * len(outs),
        scratch_shapes=[pltpu.VMEM(shape, F32) if isinstance(shape, tuple) else shape for shape in scratch],
        compiler_params=pltpu.CompilerParams(vmem_limit_bytes=grant * 1024 * 1024),
        cost_estimate=pl.CostEstimate(flops=flops, bytes_accessed=moved, transcendentals=0),
        name=kernel.__name__,
    )(*ins)


def swap(axis, to_up, to_down):
    count = lax.axis_size(axis)
    up = [(i, i + 1) for i in range(count - 1)]
    down = [(i + 1, i) for i in range(count - 1)]
    return lax.ppermute(to_up, axis, up), lax.ppermute(to_down, axis, down)


def on_device(right, iterate, phase, table):
    block = (16, 16, 128)
    fields, to_up, to_down = call(
        send_x,
        [(3, *block), (15, 16, 128), (15, 16, 128)],
        [table, phase, iterate, right],
        scratch=[pltpu.SMEM((4,), F32), pltpu.VMEM(block, jnp.int32), pltpu.SemaphoreType.DMA((4,))],
        first=HBM,
        rest=HBM,
        grant=60,
    )
    from_down, from_up = swap("gx", to_up, to_down)
    (held,) = call(hold, [(3, *block)], [fields], flops=30000000)
    from_down, from_up, fields = lax.optimization_barrier((from_down, from_up, held))
    ext, to_up, to_down = call(pack_y, [(3, 28, 16, 128), (28, 16, 128), (28, 16, 128)], [fields, from_down, from_up])
    from_down, from_up = swap("gy", to_up, to_down)
    planes = (3, 28, 32, 128)
    mine = call(own_rows, [(16, 512), (16, 512), (3, *block)], [ext], flops=30000000)
    from_down, from_up, *mine = lax.optimization_barrier((from_down, from_up, *mine))
    full, to_up, to_down, inner = call(
        pack_z,
        [planes, (32, 512), (32, 512), (16, 128)],
        [ext, from_down, from_up, *mine],
        scratch=[(6, 32, 128), (128, 128)],
    )
    from_down, from_up = swap("gz", to_up, to_down)
    place = jnp.stack([lax.axis_index("gx"), lax.axis_index("gy")]).astype(jnp.int32)
    xy, tables = call(
        bands_xy,
        [planes, jax.ShapeDtypeStruct((1088, 512), BF16)],
        [place, full],
        scratch=[planes],
        first=SMEM,
        flops=30000000,
    )
    from_down, from_up, xy, tables = lax.optimization_barrier((from_down, from_up, xy, tables))
    z_sides = [from_down, from_up]
    count = lax.axis_size("gx") * lax.axis_size("gy")
    (chunks,) = call(own_cells, [(count, 16, 128)], [to_up, to_down, *z_sides, inner], scratch=[(256, 128)])
    plane = lax.all_to_all(chunks, ("gx", "gy"), 0, 0, tiled=True)
    wide = (28, 32, 256)
    coef, res, inv = call(
        fine_residual,
        [wide] * 3,
        [full, xy, *z_sides],
        scratch=[(2, 28, 32, 128), wide, (28, 32, 128)],
        flops=30000000,
    )
    (base,) = call(
        fine_sweeps,
        [block],
        [full, coef, res, inv],
        scratch=[wide, wide, wide, wide, (2, 896, 128), (128, 128)],
        flops=60000000,
    )
    (out,) = call(coarse_levels, [block], [tables, plane.reshape(count * 16, 128), base], scratch=[(64, 128)])
    return out


def solution(mesh):
    placed = (P("gx", "gy", "gz"), P("gx", "gy", "gz"), P("gx", "gy", "gz"), P())
    return jax.shard_map(on_device, mesh=mesh, in_specs=placed, out_specs=P("gx", "gy", "gz"), check_vma=False)
```

```python
import jax
import jax.numpy as jnp
from jax import lax
from jax.experimental import pallas as pl
from jax.experimental.pallas import tpu as pltpu
from jax.sharding import PartitionSpec as P

HALO = (6, 5, 4)
ROWS = (0, 6, 11, 15)
OMEGA = 2.0 / 3.0
F32 = jnp.float32
BF16 = jnp.bfloat16


def iota(shape, dim):
    return lax.broadcasted_iota(jnp.int32, shape, dim)


def ones_where(cond, scale=1.0):
    return jnp.where(cond, F32(scale), F32(0.0)).astype(BF16)


def split(x):
    high = x.astype(BF16)
    rest = x - high.astype(F32)
    middle = rest.astype(BF16)
    return high, middle, (rest - middle.astype(F32)).astype(BF16)


def select_rows(pattern, x):
    high, middle, low = [jnp.dot(pattern, part, preferred_element_type=F32) for part in split(x)]
    return high + (middle + low)


def select_lanes(x, pattern):
    high, middle, low = [jnp.dot(part, pattern, preferred_element_type=F32) for part in split(x)]
    return high + (middle + low)


def band_matrix(size):
    apart = jnp.abs(iota((size, size), 0) - iota((size, size), 1))
    return jnp.where(apart == 0, 2.0, jnp.where((apart == 1) | (apart == size - 1), 1.0, 0.0)).astype(BF16)


def band_z(fields, matrix):
    shape = fields[0].shape
    rows = fields[0].size // shape[-1]
    found = select_lanes(jnp.concatenate([f.reshape(rows, shape[-1]) for f in fields], axis=0), matrix)
    return [found[rows * at : rows * at + rows].reshape(shape) for at in range(len(fields))]


def band(x, axis):
    return (pltpu.roll(x, 1, axis) + pltpu.roll(x, x.shape[axis] - 1, axis)) + 2.0 * x


def band_x(x):
    up = jnp.concatenate([x[1:], x[:1]], axis=0)
    down = jnp.concatenate([x[-1:], x[:-1]], axis=0)
    return (up + down) + 2.0 * x


def damped_inverse(coef, diagonal):
    inside = coef > 0.0
    return jnp.where(inside, OMEGA / jnp.where(inside, diagonal, 1.0), 0.0)


def relax(corr, inverse, residual, coef, tu_corr, tu_product):
    return corr * (1.0 / 3.0) + inverse * (residual - 2.0 * (coef * corr) + 0.125 * (coef * tu_corr + tu_product))


def smooth_small(residual, coef, sweeps, bands_z):
    inverse = damped_inverse(coef, 6.0 * coef + 0.125 * bands_z([band_x(band(coef, 1))])[0])
    corr = inverse * residual
    for _ in range(sweeps - 1):
        tu = bands_z([band_x(band(f, 1)) for f in (corr, coef * corr)])
        corr = relax(corr, inverse, residual, coef, *tu)
    return corr


def send_x(table, phase, iterate, right, fields, to_up, to_down, values, phases, sems):
    copies = [
        pltpu.make_async_copy(table, values, sems.at[0]),
        pltpu.make_async_copy(phase, phases, sems.at[1]),
        pltpu.make_async_copy(iterate, fields.at[1], sems.at[2]),
        pltpu.make_async_copy(right, fields.at[2], sems.at[3]),
    ]
    for copy in copies:
        copy.start()
    for copy in copies:
        copy.wait()
    p = phases[...]
    k = jnp.zeros(p.shape, F32)
    for index in range(4):
        k = jnp.where(p == index, values[index], k)
    fields[0] = k
    for field in range(3):
        h, a, b = HALO[field], ROWS[field], ROWS[field + 1]
        to_up[a:b] = fields[field, 16 - h : 16]
        to_down[a:b] = fields[field, 0:h]


def hold(fields, held):
    held[...] = fields[...]


def by_parity(place, body, first, second):
    odd = (place[1] & 1) == 1

    @pl.when(odd)
    def _():
        body(second, first)

    @pl.when(jnp.logical_not(odd))
    def _():
        body(first, second)


def pack_y(place, fields, from_down, from_up, ext, to_first, to_second):
    for field in range(3):
        h, a, b = HALO[field], ROWS[field], ROWS[field + 1]
        if h < 6:
            ext[field, 0 : 6 - h] = jnp.zeros((6 - h, 16, 128), F32)
            ext[field, 22 + h : 28] = jnp.zeros((6 - h, 16, 128), F32)
        ext[field, 6 - h : 6] = from_down[a:b]
        ext[field, 6:22] = fields[field]
        ext[field, 22 : 22 + h] = from_up[a:b]

    def rows(to_down, to_up):
        for field in range(3):
            h, a, b = HALO[field], ROWS[field], ROWS[field + 1]
            to_up[:, a:b, :] = ext[field, :, 16 - h : 16, :]
            to_down[:, a:b, :] = ext[field, :, 0:h, :]

    by_parity(place, rows, to_first, to_second)
    to_first[:, 15:16, :] = jnp.zeros((28, 1, 128), F32)
    to_second[:, 15:16, :] = jnp.zeros((28, 1, 128), F32)


def sum_quads(quads, q, sums):
    for at, f in enumerate(sums):
        f = f + pltpu.roll(f, 15, 0)
        f = f + pltpu.roll(f, 14, 0)
        for tile in range(f.shape[1] // 128):
            start = 64 * (at * (f.shape[1] // 128) + tile) + 16 * q
            quads[pl.ds(pl.multiple_of(start, 16), 16), :] = f[:, 128 * tile : 128 * tile + 128]


def read_quads(quads):
    count = quads.shape[0] // 64
    return jnp.concatenate([quads[pl.ds(64 * at, 16, stride=4), :] for at in range(count)], axis=1)


def pack_lanes(cells_of, rows, to_up, to_down, at):
    lane = iota((rows, 128), 1)
    for group in range(4):
        up = jnp.zeros((rows, 128), F32)
        down = jnp.zeros((rows, 128), F32)
        for x in range(8 * group, min(8 * group + 8, 28)):
            first = 16 * (x - 8 * group)
            for field in range(3):
                h, a, b = HALO[field], ROWS[field], ROWS[field + 1]
                cells = cells_of(field, x)
                mine = (lane >= first + a) & (lane < first + b)
                up = jnp.where(mine, pltpu.roll(cells, (first + a + h) % 128, 1), up)
                down = jnp.where(mine, rolled(cells, first + a), down)
        to_up[at : at + rows, 128 * group : 128 * group + 128] = up
        to_down[at : at + rows, 128 * group : 128 * group + 128] = down


def own_rows(ext, up, down, xz):
    pack_lanes(lambda field, x: ext[field, x], 16, up, down, 0)
    matrix = band_matrix(128)

    def bands(step, carry):
        xs = [6 + 4 * step + j for j in range(4)]
        wanted = []
        for x in xs:
            around = [(ext[0, x + d], ext[1, x + d]) for d in (-1, 0, 1)]
            for low, here, high in zip(*[(k, v, k * v) for k, v in around]):
                wanted.append((low + high) + 2.0 * here)
        for at, f in enumerate(band_z(wanted, matrix)):
            xz[at % 3, xs[at // 3] - 6] = f
        return carry

    lax.fori_loop(0, 4, bands, 0)


def pack_z(place, ext, from_first, from_second, up_rows, down_rows, xz, full, to_up, to_down, inner, edges, quads):
    edges[:, 24:32, :] = jnp.zeros((6, 8, 128), F32)
    for field in range(3):
        h = HALO[field]
        full[field, :, 0:16, :] = ext[field]
        full[field, :, 16 + h : 32 - h, :] = jnp.zeros((28, 16 - 2 * h, 128), F32)

    def rows(from_down, from_up):
        for field in range(3):
            h, a, b = HALO[field], ROWS[field], ROWS[field + 1]
            full[field, :, 16 : 16 + h, :] = from_up[:, a:b, :]
            full[field, :, 32 - h : 32, :] = from_down[:, a:b, :]
        for at, (source, row_k, row_v) in enumerate(((from_down, 5, 10), (from_up, 0, 6))):
            k = source[:, row_k, :]
            v = source[:, row_v, :]
            for number, f in enumerate((k, v, k * v)):
                edges[3 * at + number, 0:28, :] = f

    by_parity(place, rows, from_first, from_second)
    matrix = band_matrix(128)
    for at, f in enumerate(band_z([band(edges[at], 0) for at in range(6)], matrix)):
        edges[at] = f
    row = iota((16, 128), 0)

    def quad(q, carry):
        sums = [None, None]
        for j in range(4):
            x = 6 + 4 * q + j
            tu = []
            for at in range(3):
                f = xz[at, 4 * q + j]
                below = jnp.where(row == 0, edges[at, pl.ds(x, 1), :], pltpu.roll(f, 1, 0))
                above = jnp.where(row == 15, edges[3 + at, pl.ds(x, 1), :], pltpu.roll(f, 15, 0))
                tu.append((below + above) + 2.0 * f)
            k = ext[0, x]
            v = ext[1, x]
            diagonal = 6.0 * k + 0.125 * tu[0]
            res = ext[2, x] - (v * diagonal + 2.0 * (k * v) - 0.125 * (k * tu[1] + tu[2]))
            sums = [f if j == 0 else total + f for total, f in zip(sums, (res, k))]
        sum_quads(quads, q, sums)
        return carry

    lax.fori_loop(0, 4, quad, 0)
    source = iota((256, 128), 0)
    lane = iota((256, 128), 1)
    coarse = (source & 127) >> 2
    base = 64 + (source >> 7) * 16
    scale = jnp.where(source < 128, F32(0.25), F32(1.0 / 64.0))
    upper = (lane == base + coarse - 16) & (coarse >= 16) & (coarse <= 30)
    lower = (lane == base + coarse) & (coarse >= 1) & (coarse <= 15)
    stay = (lane == (source >> 7) * 64 + 16 + coarse) & (coarse >= 1) & (coarse <= 30)
    place = jnp.concatenate([jnp.where(found, scale, 0.0) for found in (upper, lower, stay)], axis=1).astype(BF16)
    level3 = select_lanes(read_quads(quads), place)
    inner[...] = level3[:, 256:384]
    to_up[0:16, :] = up_rows[...]
    to_down[0:16, :] = down_rows[...]
    pack_lanes(lambda field, x: full[field, x, 16:32, :], 16, to_up, to_down, 16)
    to_up[0:16, 384:512] += level3[:, 0:128]
    to_down[0:16, 384:512] += level3[:, 128:256]


def rolled(x, shift):
    shift = shift % x.shape[1]
    return pltpu.roll(x, shift, 1) if shift else x


def bands_xy(place, full, xy, tables, bands):
    row = iota((192, 512), 0)
    cell = iota((192, 512), 1)
    cell_x = (cell >> 6) * 4 + ((cell >> 2) & 3)
    cell_y = ((cell >> 4) & 3) * 4 + (cell & 3)
    for level in range(3):
        at_x = place[0] * (4 >> level) - 4 + (row >> 4)
        at_y = place[1] * (4 >> level) - 4 + (row & 15)
        found = ((cell_x >> level) == at_x) & ((cell_y >> level) == at_y)
        tables[192 * level : 192 * level + 192, :] = ones_where(found)
    source = iota((128, 256), 0)
    lane = iota((128, 256), 1)
    is_coef = source >> 6
    for level, start in enumerate((0, 64, 96)):
        scale = jnp.where(is_coef == 1, F32(0.125**level), F32(0.5**level))
        found = lane == is_coef * 128 + start + ((source & 63) >> level)
        at = 576 + 128 * level
        tables[at : at + 128, 0:256] = jnp.where(found, scale, 0.0).astype(BF16)
    source = iota((128, 128), 0)
    lane = iota((128, 128), 1)
    for level, start in enumerate((16, 72, 100)):
        found = source == start + (lane >> (level + 2))
        tables[960:1088, 128 * level : 128 * level + 128] = ones_where(found)

    def in_y(x, carry):
        k = full[0, x]
        v = full[1, x]
        bands[0, x] = band(k, 0)
        bands[1, x] = band(v, 0)
        bands[2, x] = band(k * v, 0)
        return carry

    lax.fori_loop(0, 28, in_y, 0, unroll=2)

    def in_x(x, carry):
        for field in range(3):
            xy[field, x] = (bands[field, x - 1] + bands[field, x + 1]) + 2.0 * bands[field, x]
        return carry

    lax.fori_loop(1, 27, in_x, 0, unroll=2)
    for field in range(3):
        for x in (0, 27):
            xy[field, x] = jnp.zeros((32, 128), F32)


def end_cells(lower_k, lower_v, lower_right, upper_k, upper_v, upper_right):
    position = iota((32, 512), 1) & 15
    k = jnp.where(position < 6, lower_k, jnp.where(position < 12, upper_k, 0.0))
    v = jnp.where(position < 6, lower_v, upper_v)
    right = jnp.where(position < 6, lower_right, upper_right)[0:16, :]
    tu = []
    for f in (k, v, k * v):
        f = band(f, 0)[0:16, :]
        f = f + pltpu.roll(f, 16, 1)
        tu.append(band(f + pltpu.roll(f, 512 - 16, 1), 1))
    k, v = k[0:16, :], v[0:16, :]
    diagonal = 6.0 * k + 0.125 * tu[0]
    return right - (v * diagonal + 2.0 * (k * v) - 0.125 * (k * tu[1] + tu[2])), k


def own_cells(sent_up, sent_down, from_down, from_up, inner, chunks, quads):
    def moved(f, shift):
        return pltpu.roll(f, shift % 512, 1)

    low, first, last, high = from_down[...], sent_down[...], sent_up[...], from_up[...]
    found = [
        end_cells(low, moved(low, -5), moved(low, -9), moved(first, 6), first, moved(first, -5)),
        end_cells(last, moved(last, -5), moved(last, -9), moved(high, 6), high, moved(high, -5)),
    ]
    rows = []
    for f in (found[0][0], found[1][0], found[0][1], found[1][1]):
        f = f[:, 0:384]
        f = f + pltpu.roll(f, 15, 0)
        rows.append(f + pltpu.roll(f, 14, 0))
    source = iota((384, 128), 0)
    x = (source >> 4) - 6
    z = (source & 15) - 2
    place = (x >= 0) & (x < 16) & (z >= 0) & (z < 8) & (iota((384, 128), 1) == (x >> 2) * 32 + (z >> 2))
    ends = select_lanes(jnp.concatenate(rows, axis=0), ones_where(place))
    ends = [0.25 * ends[0:16], 0.25 * ends[16:32], ends[32:48] / 64.0, ends[48:64] / 64.0]
    for q in range(4):
        for at in range(4):
            start = 64 * at + 16 * q
            quads[start : start + 16, :] = rolled(ends[at], -32 * q)
    lane = iota((16, 128), 1)
    mine = inner[...]
    for at, target in enumerate((15, 47, 79, 111)):
        cells = pltpu.roll(quads[pl.ds(64 * at, 16, stride=4), :], target, 1)
        mine = jnp.where((lane == target) | (lane == target + 1), cells, mine)
    low = from_down[0:16, 384:512]
    high = from_up[0:16, 384:512]
    mine = jnp.where(lane < 15, pltpu.roll(low, 64, 1), mine)
    mine = jnp.where((lane >= 64) & (lane < 79), pltpu.roll(low, 112, 1), mine)
    mine = jnp.where((lane >= 49) & (lane < 64), pltpu.roll(high, 112, 1), mine)
    mine = jnp.where(lane >= 113, pltpu.roll(high, 32, 1), mine)
    chunks[...] = jnp.broadcast_to(mine[None], chunks.shape)


def fine_residual(full, xy, from_down, from_up, coef, res, inv, side, sides_kv, product):
    lane = iota((32, 128), 1)

    for x in range(28):
        group, first = 128 * (x // 8), 16 * (x % 8)
        up = from_up[:, group : group + 128]
        down = from_down[:, group : group + 128]
        tiles = []
        for field in range(3):
            h, a = HALO[field], ROWS[field]
            tile = jnp.where(lane >= 128 - h, rolled(down, 128 - h - first - a), 0.0)
            tiles.append(jnp.where(lane < h, rolled(up, -first - a), tile))
        coef[x, :, 0:128] = full[0, x]
        coef[x, :, 128:256] = tiles[0]
        side[0, x] = tiles[1]
        side[1, x] = tiles[2]
        sides_kv[x, :, 0:128] = band(tiles[0], 0)
        sides_kv[x, :, 128:256] = band(tiles[1], 0)
        product[x] = band(tiles[0] * tiles[1], 0)

    for x in (0, 1, 26, 27):
        res[x] = jnp.zeros((32, 256), F32)

    def over_x(ref, x):
        return (ref[x - 1] + ref[x + 1]) + 2.0 * ref[x]

    matrix = band_matrix(256)

    def cells(step, carry):
        xs = [2 + 8 * step + j for j in range(8)]
        wanted = []
        for x in xs:
            sides = over_x(sides_kv, x)
            wanted += [
                jnp.concatenate([xy[0, x], sides[:, 0:128]], axis=1),
                jnp.concatenate([xy[1, x], sides[:, 128:256]], axis=1),
                jnp.concatenate([xy[2, x], over_x(product, x)], axis=1),
            ]
        found = band_z(wanted, matrix)
        for j, x in enumerate(xs):
            tu_k, tu_v, tu_kv = found[3 * j : 3 * j + 3]
            k = coef[x]
            v = jnp.concatenate([full[1, x], side[0, x]], axis=1)
            diagonal = 6.0 * k + 0.125 * tu_k
            applied = v * diagonal + 2.0 * (k * v) - 0.125 * (k * tu_v + tu_kv)
            res[x] = jnp.concatenate([full[2, x], side[1, x]], axis=1) - applied
            inv[x] = damped_inverse(k, diagonal)
        return carry

    lax.fori_loop(0, 3, cells, 0)


def fine_sweeps(full, coef, res, inv, base, corr, corr_next, yz_c, yz_kc, pairs, spread):
    def over_x(ref, x):
        return (ref[x - 1] + ref[x + 1]) + 2.0 * ref[x]

    matrix = band_matrix(256)

    def bands_of(xs, ref):
        wanted = []
        for x in xs:
            c = ref[x]
            wanted += [band(c, 0), band(coef[x] * c, 0)]
        found = band_z(wanted, matrix)
        for j, x in enumerate(xs):
            yz_c[x] = found[2 * j]
            yz_kc[x] = found[2 * j + 1]

    def first_sweep(step, carry):
        xs = [4 + 4 * step + j for j in range(4)]
        for x in xs:
            corr[x] = inv[x] * res[x]
        bands_of(xs, corr)
        return carry

    lax.fori_loop(0, 5, first_sweep, 0)

    def second(x, carry):
        corr_next[x] = relax(corr[x], inv[x], res[x], coef[x], over_x(yz_c, x), over_x(yz_kc, x))
        return carry

    lax.fori_loop(5, 23, second, 0, unroll=3)

    def second_bands(step, carry):
        bands_of([5 + 3 * step + j for j in range(3)], corr_next)
        return carry

    lax.fori_loop(0, 6, second_bands, 0)

    halves = ones_where((iota((256, 128), 0) >> 1) == iota((256, 128), 1))

    def pair(x, carry):
        for at, ref in enumerate((res, coef)):
            f = ref[2 * x] + ref[2 * x + 1]
            for tile in range(2):
                place = pl.ds(pl.multiple_of(448 * at + 32 * x, 32), 32)
                pairs[tile, place, :] = f[:, 128 * tile : 128 * tile + 128]
        return carry

    lax.fori_loop(0, 14, pair, 0, unroll=2)
    sums = [pairs[tile, pl.ds(0, 448, stride=2), :] + pairs[tile, pl.ds(1, 448, stride=2), :] for tile in range(2)]
    sums = select_lanes(jnp.concatenate(sums, axis=1), halves).reshape(2, 14, 16, 128)
    small = band_matrix(128)
    corr_two = smooth_small(0.5 * sums[0], 0.125 * sums[1], 3, lambda fields: band_z(fields, small))
    doubled = ones_where(iota((128, 128), 0) == (iota((128, 128), 1) >> 1))
    wide = select_lanes(corr_two[3:11].reshape(128, 128), doubled).reshape(8, 16, 128)
    rows = wide[:, 0:8, :].reshape(64, 128)
    spread[pl.ds(0, 64, stride=2), :] = rows
    spread[pl.ds(1, 64, stride=2), :] = rows

    def third(x, carry):
        c = relax(
            corr_next[x, 0:16, 0:128],
            inv[x, 0:16, 0:128],
            res[x, 0:16, 0:128],
            coef[x, 0:16, 0:128],
            (yz_c[x - 1, 0:16, 0:128] + yz_c[x + 1, 0:16, 0:128]) + 2.0 * yz_c[x, 0:16, 0:128],
            (yz_kc[x - 1, 0:16, 0:128] + yz_kc[x + 1, 0:16, 0:128]) + 2.0 * yz_kc[x, 0:16, 0:128],
        )
        block = x - 6
        base[block] = full[1, x, 0:16, :] + (c + spread[pl.ds(pl.multiple_of(16 * (block // 2), 16), 16), :])
        return carry

    lax.fori_loop(6, 22, third, 0, unroll=4)


def rolled_bands(fields):
    return [band(f, 2) for f in fields]


def coarse_levels(tables, plane, base, out, spread):
    found = jnp.dot(tables[0:576, :], jnp.concatenate(split(plane[...]), axis=1), preferred_element_type=F32)
    found = found[:, 0:128] + (found[:, 128:256] + found[:, 256:384])
    windows = jnp.concatenate([found[192 * level : 192 * level + 192, :] for level in range(3)], axis=1)
    both = select_lanes(windows, tables[576:960, 0:256])
    corr = smooth_small(both[:, 0:128].reshape(12, 16, 128), both[:, 128:256].reshape(12, 16, 128), 4, rolled_bands)
    wide = select_lanes(corr[4:8].reshape(64, 128), tables[960:1088, 0:384])
    for x in range(4):
        level4 = wide[16 * (x // 2) : 16 * (x // 2) + 16, 128:256]
        level4 = jnp.concatenate([jnp.broadcast_to(level4[y : y + 1], (2, 128)) for y in (4, 5)], axis=0)
        rows = wide[16 * x + 4 : 16 * x + 8, 0:128] + (level4 + wide[4:5, 256:384])
        for y in range(4):
            spread[pl.ds(16 * x + y, 4, stride=4), :] = rows
    for x in range(16):
        start = 16 * (x // 4)
        out[x] = base[x] + spread[start : start + 16, :]


VMEM = pl.BlockSpec(memory_space=pltpu.VMEM)
SMEM = pl.BlockSpec(memory_space=pltpu.SMEM)
HBM = pl.BlockSpec(memory_space=pltpu.HBM)


def call(kernel, outs, ins, scratch=(), first=VMEM, rest=VMEM, flops=1000000, grant=32):
    moved = 4 * sum(x.size for x in ins)
    return pl.pallas_call(
        kernel,
        out_shape=[out if isinstance(out, jax.ShapeDtypeStruct) else jax.ShapeDtypeStruct(out, F32) for out in outs],
        in_specs=[first] + [rest] * (len(ins) - 1),
        out_specs=[VMEM] * len(outs),
        scratch_shapes=[pltpu.VMEM(shape, F32) if isinstance(shape, tuple) else shape for shape in scratch],
        compiler_params=pltpu.CompilerParams(vmem_limit_bytes=grant * 1024 * 1024),
        cost_estimate=pl.CostEstimate(flops=flops, bytes_accessed=moved, transcendentals=0),
        name=kernel.__name__,
    )(*ins)


def neighbour_pairs(count):
    for start in (1, 0):
        lower = range(start, count - 1, 2)
        yield [(i, i + 1) for i in lower] + [(i + 1, i) for i in lower]


def swap(axis, to_up, to_down):
    count = lax.axis_size(axis)
    up = [(i, i + 1) for i in range(count - 1)]
    down = [(i + 1, i) for i in range(count - 1)]
    return lax.ppermute(to_up, axis, up), lax.ppermute(to_down, axis, down)


def on_device(right, iterate, phase, table):
    block = (16, 16, 128)
    place = jnp.stack([lax.axis_index("gx"), lax.axis_index("gy")]).astype(jnp.int32)
    fields, to_up, to_down = call(
        send_x,
        [(3, *block), (15, 16, 128), (15, 16, 128)],
        [table, phase, iterate, right],
        scratch=[pltpu.SMEM((4,), F32), pltpu.VMEM(block, jnp.int32), pltpu.SemaphoreType.DMA((4,))],
        first=HBM,
        rest=HBM,
        grant=60,
    )
    from_down, from_up = swap("gx", to_up, to_down)
    (held,) = call(hold, [(3, *block)], [fields], flops=30000000)
    from_down, from_up, fields, place = lax.optimization_barrier((from_down, from_up, held, place))
    ext, *sent = call(
        pack_y,
        [(3, 28, 16, 128), (28, 16, 128), (28, 16, 128)],
        [place, fields, from_down, from_up],
        first=SMEM,
    )
    found = [lax.ppermute(rows, "gy", pairs) for rows, pairs in zip(sent, neighbour_pairs(lax.axis_size("gy")))]
    planes = (3, 28, 32, 128)
    mine = call(own_rows, [(16, 512), (16, 512), (3, *block)], [ext], flops=30000000)
    *found, up_rows, down_rows, xz = lax.optimization_barrier((*found, *mine))
    full, to_up, to_down, inner = call(
        pack_z,
        [planes, (32, 512), (32, 512), (16, 128)],
        [place, ext, *found, up_rows, down_rows, xz],
        scratch=[(6, 32, 128), (128, 128)],
        first=SMEM,
    )
    from_down, from_up = swap("gz", to_up, to_down)
    xy, tables = call(
        bands_xy,
        [planes, jax.ShapeDtypeStruct((1088, 512), BF16)],
        [place, full],
        scratch=[planes],
        first=SMEM,
        flops=30000000,
    )
    from_down, from_up, xy, tables = lax.optimization_barrier((from_down, from_up, xy, tables))
    z_sides = [from_down, from_up]
    count = lax.axis_size("gx") * lax.axis_size("gy")
    (chunks,) = call(own_cells, [(count, 16, 128)], [to_up, to_down, *z_sides, inner], scratch=[(256, 128)])
    plane = lax.all_to_all(chunks, ("gx", "gy"), 0, 0, tiled=True)
    wide = (28, 32, 256)
    coef, res, inv = call(
        fine_residual,
        [wide] * 3,
        [full, xy, *z_sides],
        scratch=[(2, 28, 32, 128), wide, (28, 32, 128)],
        flops=30000000,
    )
    (base,) = call(
        fine_sweeps,
        [block],
        [full, coef, res, inv],
        scratch=[wide, wide, wide, wide, (2, 896, 128), (128, 128)],
        flops=60000000,
    )
    (out,) = call(coarse_levels, [block], [tables, plane.reshape(count * 16, 128), base], scratch=[(64, 128)])
    return out


def solution(mesh):
    placed = (P("gx", "gy", "gz"), P("gx", "gy", "gz"), P("gx", "gy", "gz"), P())
    return jax.shard_map(on_device, mesh=mesh, in_specs=placed, out_specs=P("gx", "gy", "gz"), check_vma=False)
```

```python
import jax
import jax.numpy as jnp
from jax import lax
from jax.experimental import pallas as pl
from jax.experimental.pallas import tpu as pltpu
from jax.sharding import PartitionSpec as P

HALO = (6, 5, 4)
ROWS = (0, 6, 11, 15)
OMEGA = 2.0 / 3.0
F32 = jnp.float32
BF16 = jnp.bfloat16


def iota(shape, dim):
    return lax.broadcasted_iota(jnp.int32, shape, dim)


def ones_where(cond, scale=1.0):
    return jnp.where(cond, F32(scale), F32(0.0)).astype(BF16)


def split(x):
    high = x.astype(BF16)
    rest = x - high.astype(F32)
    middle = rest.astype(BF16)
    return high, middle, (rest - middle.astype(F32)).astype(BF16)


def select_rows(pattern, x):
    high, middle, low = [jnp.dot(pattern, part, preferred_element_type=F32) for part in split(x)]
    return high + (middle + low)


def select_lanes(x, pattern):
    high, middle, low = [jnp.dot(part, pattern, preferred_element_type=F32) for part in split(x)]
    return high + (middle + low)


def band_matrix(size):
    apart = jnp.abs(iota((size, size), 0) - iota((size, size), 1))
    return jnp.where(apart == 0, 2.0, jnp.where((apart == 1) | (apart == size - 1), 1.0, 0.0)).astype(BF16)


def band_z(fields, matrix):
    shape = fields[0].shape
    rows = fields[0].size // shape[-1]
    found = select_lanes(jnp.concatenate([f.reshape(rows, shape[-1]) for f in fields], axis=0), matrix)
    return [found[rows * at : rows * at + rows].reshape(shape) for at in range(len(fields))]


def band(x, axis):
    return (pltpu.roll(x, 1, axis) + pltpu.roll(x, x.shape[axis] - 1, axis)) + 2.0 * x


def band_x(x):
    up = jnp.concatenate([x[1:], x[:1]], axis=0)
    down = jnp.concatenate([x[-1:], x[:-1]], axis=0)
    return (up + down) + 2.0 * x


def damped_inverse(coef, diagonal):
    inside = coef > 0.0
    return jnp.where(inside, OMEGA / jnp.where(inside, diagonal, 1.0), 0.0)


def relax(corr, inverse, residual, coef, tu_corr, tu_product):
    return corr * (1.0 / 3.0) + inverse * (residual - 2.0 * (coef * corr) + 0.125 * (coef * tu_corr + tu_product))


def smooth_small(residual, coef, sweeps, bands_z):
    inverse = damped_inverse(coef, 6.0 * coef + 0.125 * bands_z([band_x(band(coef, 1))])[0])
    corr = inverse * residual
    for _ in range(sweeps - 1):
        tu = bands_z([band_x(band(f, 1)) for f in (corr, coef * corr)])
        corr = relax(corr, inverse, residual, coef, *tu)
    return corr


def send_x(table, phase, iterate, right, fields, to_up, to_down, values, phases, sems):
    copies = [
        pltpu.make_async_copy(table, values, sems.at[0]),
        pltpu.make_async_copy(phase, phases, sems.at[1]),
        pltpu.make_async_copy(iterate, fields.at[1], sems.at[2]),
        pltpu.make_async_copy(right, fields.at[2], sems.at[3]),
    ]
    for copy in copies:
        copy.start()
    for copy in copies:
        copy.wait()
    p = phases[...]
    k = jnp.zeros(p.shape, F32)
    for index in range(4):
        k = jnp.where(p == index, values[index], k)
    fields[0] = k
    for field in range(3):
        h, a, b = HALO[field], ROWS[field], ROWS[field + 1]
        to_up[a:b] = fields[field, 16 - h : 16]
        to_down[a:b] = fields[field, 0:h]


def hold(fields, held):
    held[...] = fields[...]


def by_parity(body, first, second):
    odd = (lax.axis_index("gy") & 1) == 1

    @pl.when(odd)
    def _():
        body(second, first)

    @pl.when(jnp.logical_not(odd))
    def _():
        body(first, second)


def pack_y(fields, from_down, from_up, ext, to_first, to_second):
    for field in range(3):
        h, a, b = HALO[field], ROWS[field], ROWS[field + 1]
        if h < 6:
            ext[field, 0 : 6 - h] = jnp.zeros((6 - h, 16, 128), F32)
            ext[field, 22 + h : 28] = jnp.zeros((6 - h, 16, 128), F32)
        ext[field, 6 - h : 6] = from_down[a:b]
        ext[field, 6:22] = fields[field]
        ext[field, 22 : 22 + h] = from_up[a:b]

    def rows(to_down, to_up):
        for field in range(3):
            h, a, b = HALO[field], ROWS[field], ROWS[field + 1]
            to_up[:, a:b, :] = ext[field, :, 16 - h : 16, :]
            to_down[:, a:b, :] = ext[field, :, 0:h, :]

    by_parity(rows, to_first, to_second)
    to_first[:, 15:16, :] = jnp.zeros((28, 1, 128), F32)
    to_second[:, 15:16, :] = jnp.zeros((28, 1, 128), F32)


def sum_quads(quads, q, sums):
    for at, f in enumerate(sums):
        f = f + pltpu.roll(f, 15, 0)
        f = f + pltpu.roll(f, 14, 0)
        for tile in range(f.shape[1] // 128):
            start = 64 * (at * (f.shape[1] // 128) + tile) + 16 * q
            quads[pl.ds(pl.multiple_of(start, 16), 16), :] = f[:, 128 * tile : 128 * tile + 128]


def read_quads(quads):
    count = quads.shape[0] // 64
    return jnp.concatenate([quads[pl.ds(64 * at, 16, stride=4), :] for at in range(count)], axis=1)


def pack_lanes(cells_of, rows, to_up, to_down, at):
    lane = iota((rows, 128), 1)
    for group in range(4):
        up = jnp.zeros((rows, 128), F32)
        down = jnp.zeros((rows, 128), F32)
        for x in range(8 * group, min(8 * group + 8, 28)):
            first = 16 * (x - 8 * group)
            for field in range(3):
                h, a, b = HALO[field], ROWS[field], ROWS[field + 1]
                cells = cells_of(field, x)
                mine = (lane >= first + a) & (lane < first + b)
                up = jnp.where(mine, pltpu.roll(cells, (first + a + h) % 128, 1), up)
                down = jnp.where(mine, rolled(cells, first + a), down)
        to_up[at : at + rows, 128 * group : 128 * group + 128] = up
        to_down[at : at + rows, 128 * group : 128 * group + 128] = down


def own_rows(ext, up, down, xz):
    pack_lanes(lambda field, x: ext[field, x], 16, up, down, 0)
    matrix = band_matrix(128)

    def bands(step, carry):
        xs = [6 + 4 * step + j for j in range(4)]
        wanted = []
        for x in xs:
            around = [(ext[0, x + d], ext[1, x + d]) for d in (-1, 0, 1)]
            for low, here, high in zip(*[(k, v, k * v) for k, v in around]):
                wanted.append((low + high) + 2.0 * here)
        for at, f in enumerate(band_z(wanted, matrix)):
            xz[at % 3, xs[at // 3] - 6] = f
        return carry

    lax.fori_loop(0, 4, bands, 0)


def pack_z(ext, from_first, from_second, up_rows, down_rows, xz, full, to_up, to_down, inner, edges, quads):
    edges[:, 24:32, :] = jnp.zeros((6, 8, 128), F32)
    for field in range(3):
        h = HALO[field]
        full[field, :, 0:16, :] = ext[field]
        full[field, :, 16 + h : 32 - h, :] = jnp.zeros((28, 16 - 2 * h, 128), F32)

    def rows(from_down, from_up):
        for field in range(3):
            h, a, b = HALO[field], ROWS[field], ROWS[field + 1]
            full[field, :, 16 : 16 + h, :] = from_up[:, a:b, :]
            full[field, :, 32 - h : 32, :] = from_down[:, a:b, :]
        for at, (source, row_k, row_v) in enumerate(((from_down, 5, 10), (from_up, 0, 6))):
            k = source[:, row_k, :]
            v = source[:, row_v, :]
            for number, f in enumerate((k, v, k * v)):
                edges[3 * at + number, 0:28, :] = f

    by_parity(rows, from_first, from_second)
    matrix = band_matrix(128)
    for at, f in enumerate(band_z([band(edges[at], 0) for at in range(6)], matrix)):
        edges[at] = f
    row = iota((16, 128), 0)

    def quad(q, carry):
        sums = [None, None]
        for j in range(4):
            x = 6 + 4 * q + j
            tu = []
            for at in range(3):
                f = xz[at, 4 * q + j]
                below = jnp.where(row == 0, edges[at, pl.ds(x, 1), :], pltpu.roll(f, 1, 0))
                above = jnp.where(row == 15, edges[3 + at, pl.ds(x, 1), :], pltpu.roll(f, 15, 0))
                tu.append((below + above) + 2.0 * f)
            k = ext[0, x]
            v = ext[1, x]
            diagonal = 6.0 * k + 0.125 * tu[0]
            res = ext[2, x] - (v * diagonal + 2.0 * (k * v) - 0.125 * (k * tu[1] + tu[2]))
            sums = [f if j == 0 else total + f for total, f in zip(sums, (res, k))]
        sum_quads(quads, q, sums)
        return carry

    lax.fori_loop(0, 4, quad, 0)
    source = iota((256, 128), 0)
    lane = iota((256, 128), 1)
    coarse = (source & 127) >> 2
    base = 64 + (source >> 7) * 16
    scale = jnp.where(source < 128, F32(0.25), F32(1.0 / 64.0))
    upper = (lane == base + coarse - 16) & (coarse >= 16) & (coarse <= 30)
    lower = (lane == base + coarse) & (coarse >= 1) & (coarse <= 15)
    stay = (lane == (source >> 7) * 64 + 16 + coarse) & (coarse >= 1) & (coarse <= 30)
    place = jnp.concatenate([jnp.where(found, scale, 0.0) for found in (upper, lower, stay)], axis=1).astype(BF16)
    level3 = select_lanes(read_quads(quads), place)
    inner[...] = level3[:, 256:384]
    to_up[0:16, :] = up_rows[...]
    to_down[0:16, :] = down_rows[...]
    pack_lanes(lambda field, x: full[field, x, 16:32, :], 16, to_up, to_down, 16)
    to_up[0:16, 384:512] += level3[:, 0:128]
    to_down[0:16, 384:512] += level3[:, 128:256]


def rolled(x, shift):
    shift = shift % x.shape[1]
    return pltpu.roll(x, shift, 1) if shift else x


def bands_xy(full, xy, tables, bands):
    row = iota((192, 512), 0)
    cell = iota((192, 512), 1)
    cell_x = (cell >> 6) * 4 + ((cell >> 2) & 3)
    cell_y = ((cell >> 4) & 3) * 4 + (cell & 3)
    for level in range(3):
        at_x = lax.axis_index("gx") * (4 >> level) - 4 + (row >> 4)
        at_y = lax.axis_index("gy") * (4 >> level) - 4 + (row & 15)
        found = ((cell_x >> level) == at_x) & ((cell_y >> level) == at_y)
        tables[192 * level : 192 * level + 192, :] = ones_where(found)
    source = iota((128, 256), 0)
    lane = iota((128, 256), 1)
    is_coef = source >> 6
    for level, start in enumerate((0, 64, 96)):
        scale = jnp.where(is_coef == 1, F32(0.125**level), F32(0.5**level))
        found = lane == is_coef * 128 + start + ((source & 63) >> level)
        at = 576 + 128 * level
        tables[at : at + 128, 0:256] = jnp.where(found, scale, 0.0).astype(BF16)
    source = iota((128, 128), 0)
    lane = iota((128, 128), 1)
    for level, start in enumerate((16, 72, 100)):
        found = source == start + (lane >> (level + 2))
        tables[960:1088, 128 * level : 128 * level + 128] = ones_where(found)

    def in_y(x, carry):
        k = full[0, x]
        v = full[1, x]
        bands[0, x] = band(k, 0)
        bands[1, x] = band(v, 0)
        bands[2, x] = band(k * v, 0)
        return carry

    lax.fori_loop(0, 28, in_y, 0, unroll=2)

    def in_x(x, carry):
        for field in range(3):
            xy[field, x] = (bands[field, x - 1] + bands[field, x + 1]) + 2.0 * bands[field, x]
        return carry

    lax.fori_loop(1, 27, in_x, 0, unroll=2)
    for field in range(3):
        for x in (0, 27):
            xy[field, x] = jnp.zeros((32, 128), F32)


def end_cells(lower_k, lower_v, lower_right, upper_k, upper_v, upper_right):
    position = iota((32, 512), 1) & 15
    k = jnp.where(position < 6, lower_k, jnp.where(position < 12, upper_k, 0.0))
    v = jnp.where(position < 6, lower_v, upper_v)
    right = jnp.where(position < 6, lower_right, upper_right)[0:16, :]
    tu = []
    for f in (k, v, k * v):
        f = band(f, 0)[0:16, :]
        f = f + pltpu.roll(f, 16, 1)
        tu.append(band(f + pltpu.roll(f, 512 - 16, 1), 1))
    k, v = k[0:16, :], v[0:16, :]
    diagonal = 6.0 * k + 0.125 * tu[0]
    return right - (v * diagonal + 2.0 * (k * v) - 0.125 * (k * tu[1] + tu[2])), k


def own_cells(sent_up, sent_down, from_down, from_up, inner, chunks, quads):
    def moved(f, shift):
        return pltpu.roll(f, shift % 512, 1)

    low, first, last, high = from_down[...], sent_down[...], sent_up[...], from_up[...]
    found = [
        end_cells(low, moved(low, -5), moved(low, -9), moved(first, 6), first, moved(first, -5)),
        end_cells(last, moved(last, -5), moved(last, -9), moved(high, 6), high, moved(high, -5)),
    ]
    rows = []
    for f in (found[0][0], found[1][0], found[0][1], found[1][1]):
        f = f[:, 0:384]
        f = f + pltpu.roll(f, 15, 0)
        rows.append(f + pltpu.roll(f, 14, 0))
    source = iota((384, 128), 0)
    x = (source >> 4) - 6
    z = (source & 15) - 2
    place = (x >= 0) & (x < 16) & (z >= 0) & (z < 8) & (iota((384, 128), 1) == (x >> 2) * 32 + (z >> 2))
    ends = select_lanes(jnp.concatenate(rows, axis=0), ones_where(place))
    ends = [0.25 * ends[0:16], 0.25 * ends[16:32], ends[32:48] / 64.0, ends[48:64] / 64.0]
    for q in range(4):
        for at in range(4):
            start = 64 * at + 16 * q
            quads[start : start + 16, :] = rolled(ends[at], -32 * q)
    lane = iota((16, 128), 1)
    mine = inner[...]
    for at, target in enumerate((15, 47, 79, 111)):
        cells = pltpu.roll(quads[pl.ds(64 * at, 16, stride=4), :], target, 1)
        mine = jnp.where((lane == target) | (lane == target + 1), cells, mine)
    low = from_down[0:16, 384:512]
    high = from_up[0:16, 384:512]
    mine = jnp.where(lane < 15, pltpu.roll(low, 64, 1), mine)
    mine = jnp.where((lane >= 64) & (lane < 79), pltpu.roll(low, 112, 1), mine)
    mine = jnp.where((lane >= 49) & (lane < 64), pltpu.roll(high, 112, 1), mine)
    mine = jnp.where(lane >= 113, pltpu.roll(high, 32, 1), mine)
    chunks[...] = jnp.broadcast_to(mine[None], chunks.shape)


def fine_residual(full, xy, from_down, from_up, coef, res, inv, side, sides_kv, product):
    lane = iota((32, 128), 1)

    for x in range(28):
        group, first = 128 * (x // 8), 16 * (x % 8)
        up = from_up[:, group : group + 128]
        down = from_down[:, group : group + 128]
        tiles = []
        for field in range(3):
            h, a = HALO[field], ROWS[field]
            tile = jnp.where(lane >= 128 - h, rolled(down, 128 - h - first - a), 0.0)
            tiles.append(jnp.where(lane < h, rolled(up, -first - a), tile))
        coef[x, :, 0:128] = full[0, x]
        coef[x, :, 128:256] = tiles[0]
        side[0, x] = tiles[1]
        side[1, x] = tiles[2]
        sides_kv[x, :, 0:128] = band(tiles[0], 0)
        sides_kv[x, :, 128:256] = band(tiles[1], 0)
        product[x] = band(tiles[0] * tiles[1], 0)

    for x in (0, 1, 26, 27):
        res[x] = jnp.zeros((32, 256), F32)

    def over_x(ref, x):
        return (ref[x - 1] + ref[x + 1]) + 2.0 * ref[x]

    matrix = band_matrix(256)

    def cells(step, carry):
        xs = [2 + 8 * step + j for j in range(8)]
        wanted = []
        for x in xs:
            sides = over_x(sides_kv, x)
            wanted += [
                jnp.concatenate([xy[0, x], sides[:, 0:128]], axis=1),
                jnp.concatenate([xy[1, x], sides[:, 128:256]], axis=1),
                jnp.concatenate([xy[2, x], over_x(product, x)], axis=1),
            ]
        found = band_z(wanted, matrix)
        for j, x in enumerate(xs):
            tu_k, tu_v, tu_kv = found[3 * j : 3 * j + 3]
            k = coef[x]
            v = jnp.concatenate([full[1, x], side[0, x]], axis=1)
            diagonal = 6.0 * k + 0.125 * tu_k
            applied = v * diagonal + 2.0 * (k * v) - 0.125 * (k * tu_v + tu_kv)
            res[x] = jnp.concatenate([full[2, x], side[1, x]], axis=1) - applied
            inv[x] = damped_inverse(k, diagonal)
        return carry

    lax.fori_loop(0, 3, cells, 0)


def fine_sweeps(full, coef, res, inv, base, corr, corr_next, yz_c, yz_kc, pairs, spread):
    def over_x(ref, x):
        return (ref[x - 1] + ref[x + 1]) + 2.0 * ref[x]

    matrix = band_matrix(256)

    def bands_of(xs, ref):
        wanted = []
        for x in xs:
            c = ref[x]
            wanted += [band(c, 0), band(coef[x] * c, 0)]
        found = band_z(wanted, matrix)
        for j, x in enumerate(xs):
            yz_c[x] = found[2 * j]
            yz_kc[x] = found[2 * j + 1]

    def first_sweep(step, carry):
        xs = [4 + 4 * step + j for j in range(4)]
        for x in xs:
            corr[x] = inv[x] * res[x]
        bands_of(xs, corr)
        return carry

    lax.fori_loop(0, 5, first_sweep, 0)

    def second(x, carry):
        corr_next[x] = relax(corr[x], inv[x], res[x], coef[x], over_x(yz_c, x), over_x(yz_kc, x))
        return carry

    lax.fori_loop(5, 23, second, 0, unroll=3)

    def second_bands(step, carry):
        bands_of([5 + 3 * step + j for j in range(3)], corr_next)
        return carry

    lax.fori_loop(0, 6, second_bands, 0)

    halves = ones_where((iota((256, 128), 0) >> 1) == iota((256, 128), 1))

    def pair(x, carry):
        for at, ref in enumerate((res, coef)):
            f = ref[2 * x] + ref[2 * x + 1]
            for tile in range(2):
                place = pl.ds(pl.multiple_of(448 * at + 32 * x, 32), 32)
                pairs[tile, place, :] = f[:, 128 * tile : 128 * tile + 128]
        return carry

    lax.fori_loop(0, 14, pair, 0, unroll=2)
    sums = [pairs[tile, pl.ds(0, 448, stride=2), :] + pairs[tile, pl.ds(1, 448, stride=2), :] for tile in range(2)]
    sums = select_lanes(jnp.concatenate(sums, axis=1), halves).reshape(2, 14, 16, 128)
    small = band_matrix(128)
    corr_two = smooth_small(0.5 * sums[0], 0.125 * sums[1], 3, lambda fields: band_z(fields, small))
    doubled = ones_where(iota((128, 128), 0) == (iota((128, 128), 1) >> 1))
    wide = select_lanes(corr_two[3:11].reshape(128, 128), doubled).reshape(8, 16, 128)
    rows = wide[:, 0:8, :].reshape(64, 128)
    spread[pl.ds(0, 64, stride=2), :] = rows
    spread[pl.ds(1, 64, stride=2), :] = rows

    def third(x, carry):
        c = relax(
            corr_next[x, 0:16, 0:128],
            inv[x, 0:16, 0:128],
            res[x, 0:16, 0:128],
            coef[x, 0:16, 0:128],
            (yz_c[x - 1, 0:16, 0:128] + yz_c[x + 1, 0:16, 0:128]) + 2.0 * yz_c[x, 0:16, 0:128],
            (yz_kc[x - 1, 0:16, 0:128] + yz_kc[x + 1, 0:16, 0:128]) + 2.0 * yz_kc[x, 0:16, 0:128],
        )
        block = x - 6
        base[block] = full[1, x, 0:16, :] + (c + spread[pl.ds(pl.multiple_of(16 * (block // 2), 16), 16), :])
        return carry

    lax.fori_loop(6, 22, third, 0, unroll=4)


def rolled_bands(fields):
    return [band(f, 2) for f in fields]


def coarse_levels(tables, plane, base, out, spread):
    found = jnp.dot(tables[0:576, :], jnp.concatenate(split(plane[...]), axis=1), preferred_element_type=F32)
    found = found[:, 0:128] + (found[:, 128:256] + found[:, 256:384])
    windows = jnp.concatenate([found[192 * level : 192 * level + 192, :] for level in range(3)], axis=1)
    both = select_lanes(windows, tables[576:960, 0:256])
    corr = smooth_small(both[:, 0:128].reshape(12, 16, 128), both[:, 128:256].reshape(12, 16, 128), 4, rolled_bands)
    wide = select_lanes(corr[4:8].reshape(64, 128), tables[960:1088, 0:384])
    for x in range(4):
        level4 = wide[16 * (x // 2) : 16 * (x // 2) + 16, 128:256]
        level4 = jnp.concatenate([jnp.broadcast_to(level4[y : y + 1], (2, 128)) for y in (4, 5)], axis=0)
        rows = wide[16 * x + 4 : 16 * x + 8, 0:128] + (level4 + wide[4:5, 256:384])
        for y in range(4):
            spread[pl.ds(16 * x + y, 4, stride=4), :] = rows
    for x in range(16):
        start = 16 * (x // 4)
        out[x] = base[x] + spread[start : start + 16, :]


VMEM = pl.BlockSpec(memory_space=pltpu.VMEM)
HBM = pl.BlockSpec(memory_space=pltpu.HBM)


def call(kernel, outs, ins, scratch=(), first=VMEM, rest=VMEM, flops=1000000, grant=32):
    moved = 4 * sum(x.size for x in ins)
    return pl.pallas_call(
        kernel,
        out_shape=[out if isinstance(out, jax.ShapeDtypeStruct) else jax.ShapeDtypeStruct(out, F32) for out in outs],
        in_specs=[first] + [rest] * (len(ins) - 1),
        out_specs=[VMEM] * len(outs),
        scratch_shapes=[pltpu.VMEM(shape, F32) if isinstance(shape, tuple) else shape for shape in scratch],
        compiler_params=pltpu.CompilerParams(vmem_limit_bytes=grant * 1024 * 1024),
        cost_estimate=pl.CostEstimate(flops=flops, bytes_accessed=moved, transcendentals=0),
        name=kernel.__name__,
    )(*ins)


def neighbour_pairs(count):
    for start in (1, 0):
        lower = range(start, count - 1, 2)
        yield [(i, i + 1) for i in lower] + [(i + 1, i) for i in lower]


def swap(axis, to_up, to_down):
    count = lax.axis_size(axis)
    up = [(i, i + 1) for i in range(count - 1)]
    down = [(i + 1, i) for i in range(count - 1)]
    return lax.ppermute(to_up, axis, up), lax.ppermute(to_down, axis, down)


def on_device(right, iterate, phase, table):
    block = (16, 16, 128)
    fields, to_up, to_down = call(
        send_x,
        [(3, *block), (15, 16, 128), (15, 16, 128)],
        [table, phase, iterate, right],
        scratch=[pltpu.SMEM((4,), F32), pltpu.VMEM(block, jnp.int32), pltpu.SemaphoreType.DMA((4,))],
        first=HBM,
        rest=HBM,
        grant=60,
    )
    from_down, from_up = swap("gx", to_up, to_down)
    (held,) = call(hold, [(3, *block)], [fields], flops=30000000)
    from_down, from_up, fields = lax.optimization_barrier((from_down, from_up, held))
    ext, *sent = call(
        pack_y,
        [(3, 28, 16, 128), (28, 16, 128), (28, 16, 128)],
        [fields, from_down, from_up],
    )
    found = [lax.ppermute(rows, "gy", pairs) for rows, pairs in zip(sent, neighbour_pairs(lax.axis_size("gy")))]
    planes = (3, 28, 32, 128)
    mine = call(own_rows, [(16, 512), (16, 512), (3, *block)], [ext], flops=30000000)
    *found, up_rows, down_rows, xz = lax.optimization_barrier((*found, *mine))
    full, to_up, to_down, inner = call(
        pack_z,
        [planes, (32, 512), (32, 512), (16, 128)],
        [ext, *found, up_rows, down_rows, xz],
        scratch=[(6, 32, 128), (128, 128)],
    )
    from_down, from_up = swap("gz", to_up, to_down)
    xy, tables = call(
        bands_xy,
        [planes, jax.ShapeDtypeStruct((1088, 512), BF16)],
        [full],
        scratch=[planes],
        flops=30000000,
    )
    from_down, from_up, xy, tables = lax.optimization_barrier((from_down, from_up, xy, tables))
    z_sides = [from_down, from_up]
    count = lax.axis_size("gx") * lax.axis_size("gy")
    (chunks,) = call(own_cells, [(count, 16, 128)], [to_up, to_down, *z_sides, inner], scratch=[(256, 128)])
    plane = lax.all_to_all(chunks, ("gx", "gy"), 0, 0, tiled=True)
    wide = (28, 32, 256)
    coef, res, inv = call(
        fine_residual,
        [wide] * 3,
        [full, xy, *z_sides],
        scratch=[(2, 28, 32, 128), wide, (28, 32, 128)],
        flops=30000000,
    )
    (base,) = call(
        fine_sweeps,
        [block],
        [full, coef, res, inv],
        scratch=[wide, wide, wide, wide, (2, 896, 128), (128, 128)],
        flops=60000000,
    )
    (out,) = call(coarse_levels, [block], [tables, plane.reshape(count * 16, 128), base], scratch=[(64, 128)])
    return out


def solution(mesh):
    placed = (P("gx", "gy", "gz"), P("gx", "gy", "gz"), P("gx", "gy", "gz"), P())
    return jax.shard_map(on_device, mesh=mesh, in_specs=placed, out_specs=P("gx", "gy", "gz"), check_vma=False)
```

```python
import jax
import jax.numpy as jnp
from jax import lax
from jax.experimental import pallas as pl
from jax.experimental.pallas import tpu as pltpu
from jax.sharding import PartitionSpec as P

HALO = (6, 5, 4)
ROWS = (0, 6, 11, 15)
OMEGA = 2.0 / 3.0
F32 = jnp.float32
BF16 = jnp.bfloat16


def iota(shape, dim):
    return lax.broadcasted_iota(jnp.int32, shape, dim)


def ones_where(cond, scale=1.0):
    return jnp.where(cond, F32(scale), F32(0.0)).astype(BF16)


def split(x):
    high = x.astype(BF16)
    rest = x - high.astype(F32)
    middle = rest.astype(BF16)
    return high, middle, (rest - middle.astype(F32)).astype(BF16)


def select_rows(pattern, x):
    high, middle, low = [jnp.dot(pattern, part, preferred_element_type=F32) for part in split(x)]
    return high + (middle + low)


def select_lanes(x, pattern):
    high, middle, low = [jnp.dot(part, pattern, preferred_element_type=F32) for part in split(x)]
    return high + (middle + low)


def band_matrix(size):
    apart = jnp.abs(iota((size, size), 0) - iota((size, size), 1))
    return jnp.where(apart == 0, 2.0, jnp.where((apart == 1) | (apart == size - 1), 1.0, 0.0)).astype(BF16)


def band_z(fields, matrix):
    shape = fields[0].shape
    rows = fields[0].size // shape[-1]
    found = select_lanes(jnp.concatenate([f.reshape(rows, shape[-1]) for f in fields], axis=0), matrix)
    return [found[rows * at : rows * at + rows].reshape(shape) for at in range(len(fields))]


def band(x, axis):
    return (pltpu.roll(x, 1, axis) + pltpu.roll(x, x.shape[axis] - 1, axis)) + 2.0 * x


def band_x(x):
    up = jnp.concatenate([x[1:], x[:1]], axis=0)
    down = jnp.concatenate([x[-1:], x[:-1]], axis=0)
    return (up + down) + 2.0 * x


def damped_inverse(coef, diagonal):
    inside = coef > 0.0
    return jnp.where(inside, OMEGA / jnp.where(inside, diagonal, 1.0), 0.0)


def relax(corr, inverse, residual, coef, tu_corr, tu_product):
    return corr * (1.0 / 3.0) + inverse * (residual - 2.0 * (coef * corr) + 0.125 * (coef * tu_corr + tu_product))


def smooth_small(residual, coef, sweeps):
    inverse = damped_inverse(coef, 6.0 * coef + 0.125 * band(band_x(band(coef, 1)), 2))
    corr = inverse * residual
    for _ in range(sweeps - 1):
        tu = [band(band_x(band(f, 1)), 2) for f in (corr, coef * corr)]
        corr = relax(corr, inverse, residual, coef, *tu)
    return corr


def send_x(table, phase, iterate, right, fields, to_up, to_down, values, phases, sems):
    copies = [
        pltpu.make_async_copy(table, values, sems.at[0]),
        pltpu.make_async_copy(phase, phases, sems.at[1]),
        pltpu.make_async_copy(iterate, fields.at[1], sems.at[2]),
        pltpu.make_async_copy(right, fields.at[2], sems.at[3]),
    ]
    for copy in copies:
        copy.start()
    for copy in copies:
        copy.wait()
    p = phases[...]
    k = jnp.zeros(p.shape, F32)
    for index in range(4):
        k = jnp.where(p == index, values[index], k)
    fields[0] = k
    for field in range(3):
        h, a, b = HALO[field], ROWS[field], ROWS[field + 1]
        to_up[a:b] = fields[field, 16 - h : 16]
        to_down[a:b] = fields[field, 0:h]


def hold(fields, held):
    held[...] = fields[...]


def by_parity(body, first, second):
    odd = (lax.axis_index("gy") & 1) == 1

    @pl.when(odd)
    def _():
        body(second, first)

    @pl.when(jnp.logical_not(odd))
    def _():
        body(first, second)


def pack_y(fields, from_down, from_up, ext, to_first, to_second):
    for field in range(3):
        h, a, b = HALO[field], ROWS[field], ROWS[field + 1]
        if h < 6:
            ext[field, 0 : 6 - h] = jnp.zeros((6 - h, 16, 128), F32)
            ext[field, 22 + h : 28] = jnp.zeros((6 - h, 16, 128), F32)
        ext[field, 6 - h : 6] = from_down[a:b]
        ext[field, 6:22] = fields[field]
        ext[field, 22 : 22 + h] = from_up[a:b]

    def rows(to_down, to_up):
        for field in range(3):
            h, a, b = HALO[field], ROWS[field], ROWS[field + 1]
            to_up[:, a:b, :] = ext[field, :, 16 - h : 16, :]
            to_down[:, a:b, :] = ext[field, :, 0:h, :]

    by_parity(rows, to_first, to_second)
    to_first[:, 15:16, :] = jnp.zeros((28, 1, 128), F32)
    to_second[:, 15:16, :] = jnp.zeros((28, 1, 128), F32)


def sum_quads(quads, q, sums):
    for at, f in enumerate(sums):
        f = f + pltpu.roll(f, 15, 0)
        f = f + pltpu.roll(f, 14, 0)
        for tile in range(f.shape[1] // 128):
            start = 64 * (at * (f.shape[1] // 128) + tile) + 16 * q
            quads[pl.ds(pl.multiple_of(start, 16), 16), :] = f[:, 128 * tile : 128 * tile + 128]


def read_quads(quads):
    count = quads.shape[0] // 64
    return jnp.concatenate([quads[pl.ds(64 * at, 16, stride=4), :] for at in range(count)], axis=1)


def pack_lanes(cells_of, rows, to_up, to_down, at):
    lane = iota((rows, 128), 1)
    for group in range(4):
        up = jnp.zeros((rows, 128), F32)
        down = jnp.zeros((rows, 128), F32)
        for x in range(8 * group, min(8 * group + 8, 28)):
            first = 16 * (x - 8 * group)
            for field in range(3):
                h, a, b = HALO[field], ROWS[field], ROWS[field + 1]
                cells = cells_of(field, x)
                mine = (lane >= first + a) & (lane < first + b)
                up = jnp.where(mine, pltpu.roll(cells, (first + a + h) % 128, 1), up)
                down = jnp.where(mine, rolled(cells, first + a), down)
        to_up[at : at + rows, 128 * group : 128 * group + 128] = up
        to_down[at : at + rows, 128 * group : 128 * group + 128] = down


def own_rows(ext, up, down, xz, level3_lanes):
    pack_lanes(lambda field, x: ext[field, x], 16, up, down, 0)
    matrix = band_matrix(128)

    def bands(step, carry):
        xs = [6 + 4 * step + j for j in range(4)]
        wanted = []
        for x in xs:
            around = [(ext[0, x + d], ext[1, x + d]) for d in (-1, 0, 1)]
            for low, here, high in zip(*[(k, v, k * v) for k, v in around]):
                wanted.append((low + high) + 2.0 * here)
        for at, f in enumerate(band_z(wanted, matrix)):
            xz[at % 3, xs[at // 3] - 6] = f
        return carry

    lax.fori_loop(0, 4, bands, 0)
    source = iota((256, 128), 0)
    lane = iota((256, 128), 1)
    coarse = (source & 127) >> 2
    base = 64 + (source >> 7) * 16
    scale = jnp.where(source < 128, F32(0.25), F32(1.0 / 64.0))
    upper = (lane == base + coarse - 16) & (coarse >= 16) & (coarse <= 30)
    lower = (lane == base + coarse) & (coarse >= 1) & (coarse <= 15)
    stay = (lane == (source >> 7) * 64 + 16 + coarse) & (coarse >= 1) & (coarse <= 30)
    for at, found in enumerate((upper, lower, stay)):
        level3_lanes[:, 128 * at : 128 * at + 128] = jnp.where(found, scale, 0.0).astype(BF16)


def pack_z(ext, from_first, from_second, up_rows, down_rows, xz, level3_lanes, full, to_up, to_down, inner, edges, quads):
    edges[:, 24:32, :] = jnp.zeros((6, 8, 128), F32)
    for field in range(3):
        h = HALO[field]
        full[field, :, 0:16, :] = ext[field]
        full[field, :, 16 + h : 32 - h, :] = jnp.zeros((28, 16 - 2 * h, 128), F32)

    def rows(from_down, from_up):
        for field in range(3):
            h, a, b = HALO[field], ROWS[field], ROWS[field + 1]
            full[field, :, 16 : 16 + h, :] = from_up[:, a:b, :]
            full[field, :, 32 - h : 32, :] = from_down[:, a:b, :]
        for at, (source, row_k, row_v) in enumerate(((from_down, 5, 10), (from_up, 0, 6))):
            k = source[:, row_k, :]
            v = source[:, row_v, :]
            for number, f in enumerate((k, v, k * v)):
                edges[3 * at + number, 0:28, :] = f

    by_parity(rows, from_first, from_second)
    for at in range(6):
        edges[at] = band(band(edges[at], 0), 1)
    row = iota((16, 128), 0)

    def quad(q, carry):
        sums = [None, None]
        for j in range(4):
            x = 6 + 4 * q + j
            tu = []
            for at in range(3):
                f = xz[at, 4 * q + j]
                below = jnp.where(row == 0, edges[at, pl.ds(x, 1), :], pltpu.roll(f, 1, 0))
                above = jnp.where(row == 15, edges[3 + at, pl.ds(x, 1), :], pltpu.roll(f, 15, 0))
                tu.append((below + above) + 2.0 * f)
            k = ext[0, x]
            v = ext[1, x]
            diagonal = 6.0 * k + 0.125 * tu[0]
            res = ext[2, x] - (v * diagonal + 2.0 * (k * v) - 0.125 * (k * tu[1] + tu[2]))
            sums = [f if j == 0 else total + f for total, f in zip(sums, (res, k))]
        sum_quads(quads, q, sums)
        return carry

    lax.fori_loop(0, 4, quad, 0)
    level3 = select_lanes(read_quads(quads), level3_lanes[...])
    inner[...] = level3[:, 256:384]
    to_up[0:16, :] = up_rows[...]
    to_down[0:16, :] = down_rows[...]
    pack_lanes(lambda field, x: full[field, x, 16:32, :], 16, to_up, to_down, 16)
    to_up[0:16, 384:512] += level3[:, 0:128]
    to_down[0:16, 384:512] += level3[:, 128:256]


def rolled(x, shift):
    shift = shift % x.shape[1]
    return pltpu.roll(x, shift, 1) if shift else x


def bands_xy(full, xy, tables, end_lanes, bands):
    row = iota((192, 512), 0)
    cell = iota((192, 512), 1)
    cell_x = (cell >> 6) * 4 + ((cell >> 2) & 3)
    cell_y = ((cell >> 4) & 3) * 4 + (cell & 3)
    for level in range(3):
        at_x = lax.axis_index("gx") * (4 >> level) - 4 + (row >> 4)
        at_y = lax.axis_index("gy") * (4 >> level) - 4 + (row & 15)
        found = ((cell_x >> level) == at_x) & ((cell_y >> level) == at_y)
        tables[192 * level : 192 * level + 192, :] = ones_where(found)
    source = iota((128, 256), 0)
    lane = iota((128, 256), 1)
    is_coef = source >> 6
    for level, start in enumerate((0, 64, 96)):
        scale = jnp.where(is_coef == 1, F32(0.125**level), F32(0.5**level))
        found = lane == is_coef * 128 + start + ((source & 63) >> level)
        at = 576 + 128 * level
        tables[at : at + 128, 0:256] = jnp.where(found, scale, 0.0).astype(BF16)
    source = iota((128, 128), 0)
    lane = iota((128, 128), 1)
    for level, start in enumerate((16, 72, 100)):
        found = source == start + (lane >> (level + 2))
        tables[960:1088, 128 * level : 128 * level + 128] = ones_where(found)

    source = iota((384, 128), 0)
    x = (source >> 4) - 6
    z = (source & 15) - 2
    place = (x >= 0) & (x < 16) & (z >= 0) & (z < 8) & (iota((384, 128), 1) == (x >> 2) * 32 + (z >> 2))
    end_lanes[...] = ones_where(place)

    def in_y(x, carry):
        k = full[0, x]
        v = full[1, x]
        bands[0, x] = band(k, 0)
        bands[1, x] = band(v, 0)
        bands[2, x] = band(k * v, 0)
        return carry

    lax.fori_loop(0, 28, in_y, 0, unroll=2)

    def in_x(x, carry):
        for field in range(3):
            xy[field, x - 2] = (bands[field, x - 1] + bands[field, x + 1]) + 2.0 * bands[field, x]
        return carry

    lax.fori_loop(2, 26, in_x, 0, unroll=2)


def end_cells(lower_k, lower_v, lower_right, upper_k, upper_v, upper_right):
    position = iota((32, 512), 1) & 15
    k = jnp.where(position < 6, lower_k, jnp.where(position < 12, upper_k, 0.0))
    v = jnp.where(position < 6, lower_v, upper_v)
    right = jnp.where(position < 6, lower_right, upper_right)[0:16, :]
    tu = []
    for f in (k, v, k * v):
        f = band(f, 0)[0:16, :]
        f = f + pltpu.roll(f, 16, 1)
        tu.append(band(f + pltpu.roll(f, 512 - 16, 1), 1))
    k, v = k[0:16, :], v[0:16, :]
    diagonal = 6.0 * k + 0.125 * tu[0]
    return right - (v * diagonal + 2.0 * (k * v) - 0.125 * (k * tu[1] + tu[2])), k


def own_cells(sent_up, sent_down, from_down, from_up, inner, end_lanes, chunks, quads):
    def moved(f, shift):
        return pltpu.roll(f, shift % 512, 1)

    low, first, last, high = from_down[...], sent_down[...], sent_up[...], from_up[...]
    found = [
        end_cells(low, moved(low, -5), moved(low, -9), moved(first, 6), first, moved(first, -5)),
        end_cells(last, moved(last, -5), moved(last, -9), moved(high, 6), high, moved(high, -5)),
    ]
    rows = []
    for f in (found[0][0], found[1][0], found[0][1], found[1][1]):
        f = f[:, 0:384]
        f = f + pltpu.roll(f, 15, 0)
        rows.append(f + pltpu.roll(f, 14, 0))
    ends = select_lanes(jnp.concatenate(rows, axis=0), end_lanes[...])
    ends = [0.25 * ends[0:16], 0.25 * ends[16:32], ends[32:48] / 64.0, ends[48:64] / 64.0]
    for q in range(4):
        for at in range(4):
            start = 64 * at + 16 * q
            quads[start : start + 16, :] = rolled(ends[at], -32 * q)
    lane = iota((16, 128), 1)
    mine = inner[...]
    for at, target in enumerate((15, 47, 79, 111)):
        cells = pltpu.roll(quads[pl.ds(64 * at, 16, stride=4), :], target, 1)
        mine = jnp.where((lane == target) | (lane == target + 1), cells, mine)
    low = from_down[0:16, 384:512]
    high = from_up[0:16, 384:512]
    mine = jnp.where(lane < 15, pltpu.roll(low, 64, 1), mine)
    mine = jnp.where((lane >= 64) & (lane < 79), pltpu.roll(low, 112, 1), mine)
    mine = jnp.where((lane >= 49) & (lane < 64), pltpu.roll(high, 112, 1), mine)
    mine = jnp.where(lane >= 113, pltpu.roll(high, 32, 1), mine)
    chunks[...] = jnp.broadcast_to(mine[None], chunks.shape)


def fine_residual(full, xy, from_down, from_up, coef, res, inv, side, sides_kv, product):
    lane = iota((32, 128), 1)

    for x in range(28):
        group, first = 128 * (x // 8), 16 * (x % 8)
        up = from_up[:, group : group + 128]
        down = from_down[:, group : group + 128]
        tiles = []
        for field in range(3):
            h, a = HALO[field], ROWS[field]
            tile = jnp.where(lane >= 128 - h, rolled(down, 128 - h - first - a), 0.0)
            tiles.append(jnp.where(lane < h, rolled(up, -first - a), tile))
        coef[x, :, 0:128] = full[0, x]
        coef[x, :, 128:256] = tiles[0]
        side[0, x] = tiles[1]
        side[1, x] = tiles[2]
        sides_kv[x, :, 0:128] = band(tiles[0], 0)
        sides_kv[x, :, 128:256] = band(tiles[1], 0)
        product[x] = band(tiles[0] * tiles[1], 0)

    for x in (0, 1, 26, 27):
        res[x] = jnp.zeros((32, 256), F32)

    def over_x(ref, x):
        return (ref[x - 1] + ref[x + 1]) + 2.0 * ref[x]

    matrix = band_matrix(256)

    def cells(step, carry):
        xs = [2 + 8 * step + j for j in range(8)]
        wanted = []
        for x in xs:
            sides = over_x(sides_kv, x)
            wanted += [
                jnp.concatenate([xy[0, x - 2], sides[:, 0:128]], axis=1),
                jnp.concatenate([xy[1, x - 2], sides[:, 128:256]], axis=1),
                jnp.concatenate([xy[2, x - 2], over_x(product, x)], axis=1),
            ]
        found = band_z(wanted, matrix)
        for j, x in enumerate(xs):
            tu_k, tu_v, tu_kv = found[3 * j : 3 * j + 3]
            k = coef[x]
            v = jnp.concatenate([full[1, x], side[0, x]], axis=1)
            diagonal = 6.0 * k + 0.125 * tu_k
            applied = v * diagonal + 2.0 * (k * v) - 0.125 * (k * tu_v + tu_kv)
            res[x] = jnp.concatenate([full[2, x], side[1, x]], axis=1) - applied
            inv[x] = damped_inverse(k, diagonal)
        return carry

    lax.fori_loop(0, 3, cells, 0)


def fine_sweeps(full, coef, res, inv, base, corr, corr_next, yz_c, yz_kc, pairs, spread):
    def over_x(ref, x):
        return (ref[x - 1] + ref[x + 1]) + 2.0 * ref[x]

    def bands_of(xs, ref):
        wanted = []
        for x in xs:
            c = ref[x]
            wanted += [band(c, 0), band(coef[x] * c, 0)]
        found = [band(f, 1) for f in wanted]
        for j, x in enumerate(xs):
            yz_c[x] = found[2 * j]
            yz_kc[x] = found[2 * j + 1]

    def first_sweep(step, carry):
        xs = [4 + 4 * step + j for j in range(4)]
        for x in xs:
            corr[x] = inv[x] * res[x]
        bands_of(xs, corr)
        return carry

    lax.fori_loop(0, 5, first_sweep, 0)

    def second(x, carry):
        corr_next[x] = relax(corr[x], inv[x], res[x], coef[x], over_x(yz_c, x), over_x(yz_kc, x))
        return carry

    lax.fori_loop(5, 23, second, 0, unroll=3)

    def second_bands(step, carry):
        bands_of([5 + 3 * step + j for j in range(3)], corr_next)
        return carry

    lax.fori_loop(0, 6, second_bands, 0)

    halves = ones_where((iota((256, 128), 0) >> 1) == iota((256, 128), 1))

    def pair(x, carry):
        for at, ref in enumerate((res, coef)):
            f = ref[2 * x] + ref[2 * x + 1]
            for tile in range(2):
                place = pl.ds(pl.multiple_of(448 * at + 32 * x, 32), 32)
                pairs[tile, place, :] = f[:, 128 * tile : 128 * tile + 128]
        return carry

    lax.fori_loop(0, 14, pair, 0, unroll=2)
    sums = [pairs[tile, pl.ds(0, 448, stride=2), :] + pairs[tile, pl.ds(1, 448, stride=2), :] for tile in range(2)]
    sums = select_lanes(jnp.concatenate(sums, axis=1), halves).reshape(2, 14, 16, 128)
    corr_two = smooth_small(0.5 * sums[0], 0.125 * sums[1], 3)
    doubled = ones_where(iota((128, 128), 0) == (iota((128, 128), 1) >> 1))
    wide = select_lanes(corr_two[3:11].reshape(128, 128), doubled).reshape(8, 16, 128)
    rows = wide[:, 0:8, :].reshape(64, 128)
    spread[pl.ds(0, 64, stride=2), :] = rows
    spread[pl.ds(1, 64, stride=2), :] = rows

    def third(x, carry):
        c = relax(
            corr_next[x, 0:16, 0:128],
            inv[x, 0:16, 0:128],
            res[x, 0:16, 0:128],
            coef[x, 0:16, 0:128],
            (yz_c[x - 1, 0:16, 0:128] + yz_c[x + 1, 0:16, 0:128]) + 2.0 * yz_c[x, 0:16, 0:128],
            (yz_kc[x - 1, 0:16, 0:128] + yz_kc[x + 1, 0:16, 0:128]) + 2.0 * yz_kc[x, 0:16, 0:128],
        )
        block = x - 6
        base[block] = full[1, x, 0:16, :] + (c + spread[pl.ds(pl.multiple_of(16 * (block // 2), 16), 16), :])
        return carry

    lax.fori_loop(6, 22, third, 0, unroll=4)


def coarse_levels(tables, plane, base, out, spread):
    found = jnp.dot(tables[0:576, :], jnp.concatenate(split(plane[...]), axis=1), preferred_element_type=F32)
    found = found[:, 0:128] + (found[:, 128:256] + found[:, 256:384])
    windows = jnp.concatenate([found[192 * level : 192 * level + 192, :] for level in range(3)], axis=1)
    both = select_lanes(windows, tables[576:960, 0:256])
    corr = smooth_small(both[:, 0:128].reshape(12, 16, 128), both[:, 128:256].reshape(12, 16, 128), 4)
    wide = select_lanes(corr[4:8].reshape(64, 128), tables[960:1088, 0:384])
    for x in range(4):
        level4 = wide[16 * (x // 2) : 16 * (x // 2) + 16, 128:256]
        level4 = jnp.concatenate([jnp.broadcast_to(level4[y : y + 1], (2, 128)) for y in (4, 5)], axis=0)
        rows = wide[16 * x + 4 : 16 * x + 8, 0:128] + (level4 + wide[4:5, 256:384])
        for y in range(4):
            spread[pl.ds(16 * x + y, 4, stride=4), :] = rows
    for x in range(16):
        start = 16 * (x // 4)
        out[x] = base[x] + spread[start : start + 16, :]


VMEM = pl.BlockSpec(memory_space=pltpu.VMEM)
HBM = pl.BlockSpec(memory_space=pltpu.HBM)


def call(kernel, outs, ins, scratch=(), first=VMEM, rest=VMEM, flops=1000000, grant=32):
    moved = 4 * sum(x.size for x in ins)
    return pl.pallas_call(
        kernel,
        out_shape=[out if isinstance(out, jax.ShapeDtypeStruct) else jax.ShapeDtypeStruct(out, F32) for out in outs],
        in_specs=[first] + [rest] * (len(ins) - 1),
        out_specs=[VMEM] * len(outs),
        scratch_shapes=[pltpu.VMEM(shape, F32) if isinstance(shape, tuple) else shape for shape in scratch],
        compiler_params=pltpu.CompilerParams(vmem_limit_bytes=grant * 1024 * 1024),
        cost_estimate=pl.CostEstimate(flops=flops, bytes_accessed=moved, transcendentals=0),
        name=kernel.__name__,
    )(*ins)


def neighbour_pairs(count):
    for start in (1, 0):
        lower = range(start, count - 1, 2)
        yield [(i, i + 1) for i in lower] + [(i + 1, i) for i in lower]


def swap(axis, to_up, to_down):
    count = lax.axis_size(axis)
    up = [(i, i + 1) for i in range(count - 1)]
    down = [(i + 1, i) for i in range(count - 1)]
    return lax.ppermute(to_up, axis, up), lax.ppermute(to_down, axis, down)


def on_device(right, iterate, phase, table):
    block = (16, 16, 128)
    fields, to_up, to_down = call(
        send_x,
        [(3, *block), (15, 16, 128), (15, 16, 128)],
        [table, phase, iterate, right],
        scratch=[pltpu.SMEM((4,), F32), pltpu.VMEM(block, jnp.int32), pltpu.SemaphoreType.DMA((4,))],
        first=HBM,
        rest=HBM,
        grant=60,
    )
    from_down, from_up = swap("gx", to_up, to_down)
    (held,) = call(hold, [(3, *block)], [fields], flops=30000000)
    from_down, from_up, fields = lax.optimization_barrier((from_down, from_up, held))
    ext, *sent = call(
        pack_y,
        [(3, 28, 16, 128), (28, 16, 128), (28, 16, 128)],
        [fields, from_down, from_up],
    )
    found = [lax.ppermute(rows, "gy", pairs) for rows, pairs in zip(sent, neighbour_pairs(lax.axis_size("gy")))]
    planes = (3, 28, 32, 128)
    mine = call(
        own_rows,
        [(16, 512), (16, 512), (3, *block), jax.ShapeDtypeStruct((256, 384), BF16)],
        [ext],
        flops=30000000,
    )
    *found, up_rows, down_rows, xz, level3_lanes = lax.optimization_barrier((*found, *mine))
    full, to_up, to_down, inner = call(
        pack_z,
        [planes, (32, 512), (32, 512), (16, 128)],
        [ext, *found, up_rows, down_rows, xz, level3_lanes],
        scratch=[(6, 32, 128), (128, 128)],
    )
    from_down, from_up = swap("gz", to_up, to_down)
    xy, tables, end_lanes = call(
        bands_xy,
        [(3, 24, 32, 128), jax.ShapeDtypeStruct((1088, 512), BF16), jax.ShapeDtypeStruct((384, 128), BF16)],
        [full],
        scratch=[planes],
        flops=30000000,
    )
    from_down, from_up, xy, tables, end_lanes = lax.optimization_barrier((from_down, from_up, xy, tables, end_lanes))
    z_sides = [from_down, from_up]
    count = lax.axis_size("gx") * lax.axis_size("gy")
    (chunks,) = call(own_cells, [(count, 16, 128)], [to_up, to_down, *z_sides, inner, end_lanes], scratch=[(256, 128)])
    plane = lax.all_to_all(chunks, ("gx", "gy"), 0, 0, tiled=True)
    wide = (28, 32, 256)
    coef, res, inv = call(
        fine_residual,
        [wide] * 3,
        [full, xy, *z_sides],
        scratch=[(2, 28, 32, 128), wide, (28, 32, 128)],
        flops=30000000,
    )
    (base,) = call(
        fine_sweeps,
        [block],
        [full, coef, res, inv],
        scratch=[wide, wide, wide, wide, (2, 896, 128), (128, 128)],
        flops=60000000,
    )
    (out,) = call(coarse_levels, [block], [tables, plane.reshape(count * 16, 128), base], scratch=[(64, 128)])
    return out


def solution(mesh):
    placed = (P("gx", "gy", "gz"), P("gx", "gy", "gz"), P("gx", "gy", "gz"), P())
    return jax.shard_map(on_device, mesh=mesh, in_specs=placed, out_specs=P("gx", "gy", "gz"), check_vma=False)
```

```python
import jax
import jax.numpy as jnp
from jax import lax
from jax.experimental import pallas as pl
from jax.experimental.pallas import tpu as pltpu
from jax.sharding import PartitionSpec as P

HALO = (6, 5, 4)
ROWS = (0, 6, 11, 15)
OMEGA = 2.0 / 3.0
F32 = jnp.float32
BF16 = jnp.bfloat16


def iota(shape, dim):
    return lax.broadcasted_iota(jnp.int32, shape, dim)


def ones_where(cond, scale=1.0):
    return jnp.where(cond, F32(scale), F32(0.0)).astype(BF16)


def split(x):
    high = x.astype(BF16)
    rest = x - high.astype(F32)
    middle = rest.astype(BF16)
    return high, middle, (rest - middle.astype(F32)).astype(BF16)


def select_rows(pattern, x):
    high, middle, low = [jnp.dot(pattern, part, preferred_element_type=F32) for part in split(x)]
    return high + (middle + low)


def select_lanes(x, pattern):
    high, middle, low = [jnp.dot(part, pattern, preferred_element_type=F32) for part in split(x)]
    return high + (middle + low)


def band_matrix(size):
    apart = jnp.abs(iota((size, size), 0) - iota((size, size), 1))
    return jnp.where(apart == 0, 2.0, jnp.where((apart == 1) | (apart == size - 1), 1.0, 0.0)).astype(BF16)


def band_z(fields, matrix):
    shape = fields[0].shape
    rows = fields[0].size // shape[-1]
    found = select_lanes(jnp.concatenate([f.reshape(rows, shape[-1]) for f in fields], axis=0), matrix)
    return [found[rows * at : rows * at + rows].reshape(shape) for at in range(len(fields))]


def band(x, axis):
    return (pltpu.roll(x, 1, axis) + pltpu.roll(x, x.shape[axis] - 1, axis)) + 2.0 * x


def band_x(x):
    up = jnp.concatenate([x[1:], x[:1]], axis=0)
    down = jnp.concatenate([x[-1:], x[:-1]], axis=0)
    return (up + down) + 2.0 * x


def damped_inverse(coef, diagonal):
    inside = coef > 0.0
    return jnp.where(inside, OMEGA / jnp.where(inside, diagonal, 1.0), 0.0)


def relax(corr, inverse, residual, coef, tu_corr, tu_product):
    return corr * (1.0 / 3.0) + inverse * (residual - 2.0 * (coef * corr) + 0.125 * (coef * tu_corr + tu_product))


def smooth_small(residual, coef, sweeps):
    inverse = damped_inverse(coef, 6.0 * coef + 0.125 * band(band_x(band(coef, 1)), 2))
    corr = inverse * residual
    for _ in range(sweeps - 1):
        tu = [band(band_x(band(f, 1)), 2) for f in (corr, coef * corr)]
        corr = relax(corr, inverse, residual, coef, *tu)
    return corr


def send_x(table, phase, iterate, right, fields, to_up, to_down, values, phases, sems):
    copies = [
        pltpu.make_async_copy(table, values, sems.at[0]),
        pltpu.make_async_copy(phase, phases, sems.at[1]),
        pltpu.make_async_copy(iterate, fields.at[1], sems.at[2]),
        pltpu.make_async_copy(right, fields.at[2], sems.at[3]),
    ]
    for copy in copies:
        copy.start()
    for copy in copies:
        copy.wait()
    p = phases[...]
    k = jnp.zeros(p.shape, F32)
    for index in range(4):
        k = jnp.where(p == index, values[index], k)
    fields[0] = k
    for field in range(3):
        h, a, b = HALO[field], ROWS[field], ROWS[field + 1]
        to_up[a:b] = fields[field, 16 - h : 16]
        to_down[a:b] = fields[field, 0:h]


def hold(fields, held):
    held[...] = fields[...]


def by_parity(body, first, second):
    odd = (lax.axis_index("gy") & 1) == 1

    @pl.when(odd)
    def _():
        body(second, first)

    @pl.when(jnp.logical_not(odd))
    def _():
        body(first, second)


def pack_y(fields, from_down, from_up, ext, to_first, to_second):
    for field in range(3):
        h, a, b = HALO[field], ROWS[field], ROWS[field + 1]
        if h < 6:
            ext[field, 0 : 6 - h] = jnp.zeros((6 - h, 16, 128), F32)
            ext[field, 22 + h : 28] = jnp.zeros((6 - h, 16, 128), F32)
        ext[field, 6 - h : 6] = from_down[a:b]
        ext[field, 6:22] = fields[field]
        ext[field, 22 : 22 + h] = from_up[a:b]

    def rows(to_down, to_up):
        for field in range(3):
            h, a, b = HALO[field], ROWS[field], ROWS[field + 1]
            to_up[:, a:b, :] = ext[field, :, 16 - h : 16, :]
            to_down[:, a:b, :] = ext[field, :, 0:h, :]

    by_parity(rows, to_first, to_second)
    to_first[:, 15:16, :] = jnp.zeros((28, 1, 128), F32)
    to_second[:, 15:16, :] = jnp.zeros((28, 1, 128), F32)


def sum_quads(quads, q, sums):
    for at, f in enumerate(sums):
        f = f + pltpu.roll(f, 15, 0)
        f = f + pltpu.roll(f, 14, 0)
        for tile in range(f.shape[1] // 128):
            start = 64 * (at * (f.shape[1] // 128) + tile) + 16 * q
            quads[pl.ds(pl.multiple_of(start, 16), 16), :] = f[:, 128 * tile : 128 * tile + 128]


def read_quads(quads):
    count = quads.shape[0] // 64
    return jnp.concatenate([quads[pl.ds(64 * at, 16, stride=4), :] for at in range(count)], axis=1)


def pack_lanes(cells_of, rows, to_up, to_down, at):
    lane = iota((rows, 128), 1)
    for group in range(4):
        up = jnp.zeros((rows, 128), F32)
        down = jnp.zeros((rows, 128), F32)
        for x in range(8 * group, min(8 * group + 8, 28)):
            first = 16 * (x - 8 * group)
            for field in range(3):
                h, a, b = HALO[field], ROWS[field], ROWS[field + 1]
                cells = cells_of(field, x)
                mine = (lane >= first + a) & (lane < first + b)
                up = jnp.where(mine, pltpu.roll(cells, (first + a + h) % 128, 1), up)
                down = jnp.where(mine, rolled(cells, first + a), down)
        to_up[at : at + rows, 128 * group : 128 * group + 128] = up
        to_down[at : at + rows, 128 * group : 128 * group + 128] = down


def own_rows(ext, up, down, xz, level3_lanes):
    pack_lanes(lambda field, x: ext[field, x], 16, up, down, 0)
    matrix = band_matrix(128)

    def bands(step, carry):
        xs = [6 + 4 * step + j for j in range(4)]
        wanted = []
        for x in xs:
            around = [(ext[0, x + d], ext[1, x + d]) for d in (-1, 0, 1)]
            for low, here, high in zip(*[(k, v, k * v) for k, v in around]):
                wanted.append((low + high) + 2.0 * here)
        for at, f in enumerate(band_z(wanted, matrix)):
            xz[at % 3, xs[at // 3] - 6] = f
        return carry

    lax.fori_loop(0, 4, bands, 0)
    source = iota((256, 128), 0)
    lane = iota((256, 128), 1)
    coarse = (source & 127) >> 2
    is_coef = source >> 7
    scale = jnp.where(source < 128, F32(0.25), F32(1.0 / 64.0))
    upper = jnp.where(coarse >= 28, coarse - 28, jnp.where(coarse >= 24, (coarse >> 1) - 9, (coarse >> 2) + 1))
    lower = jnp.where(coarse <= 3, coarse - 1, jnp.where(coarse <= 7, (coarse >> 1) + 1, (coarse >> 2) + 3))
    found = (
        (lane == 64 + 16 * is_coef + upper) & (coarse >= 16) & (coarse <= 30),
        (lane == 64 + 16 * is_coef + lower) & (coarse >= 1) & (coarse <= 15),
        (lane == 40 * is_coef + 4 + coarse) & (coarse >= 1) & (coarse <= 30),
    )
    for at, here in enumerate(found):
        level3_lanes[:, 128 * at : 128 * at + 128] = jnp.where(here, scale, 0.0).astype(BF16)


def pack_z(ext, from_first, from_second, up_rows, down_rows, xz, level3_lanes, full, to_up, to_down, inner, edges, quads):
    edges[:, 24:32, :] = jnp.zeros((6, 8, 128), F32)
    for field in range(3):
        h = HALO[field]
        full[field, :, 0:16, :] = ext[field]
        full[field, :, 16 + h : 32 - h, :] = jnp.zeros((28, 16 - 2 * h, 128), F32)

    def rows(from_down, from_up):
        for field in range(3):
            h, a, b = HALO[field], ROWS[field], ROWS[field + 1]
            full[field, :, 16 : 16 + h, :] = from_up[:, a:b, :]
            full[field, :, 32 - h : 32, :] = from_down[:, a:b, :]
        for at, (source, row_k, row_v) in enumerate(((from_down, 5, 10), (from_up, 0, 6))):
            k = source[:, row_k, :]
            v = source[:, row_v, :]
            for number, f in enumerate((k, v, k * v)):
                edges[3 * at + number, 0:28, :] = f

    by_parity(rows, from_first, from_second)
    for at in range(6):
        edges[at] = band(band(edges[at], 0), 1)
    row = iota((16, 128), 0)

    def quad(q, carry):
        sums = [None, None]
        for j in range(4):
            x = 6 + 4 * q + j
            tu = []
            for at in range(3):
                f = xz[at, 4 * q + j]
                below = jnp.where(row == 0, edges[at, pl.ds(x, 1), :], pltpu.roll(f, 1, 0))
                above = jnp.where(row == 15, edges[3 + at, pl.ds(x, 1), :], pltpu.roll(f, 15, 0))
                tu.append((below + above) + 2.0 * f)
            k = ext[0, x]
            v = ext[1, x]
            diagonal = 6.0 * k + 0.125 * tu[0]
            res = ext[2, x] - (v * diagonal + 2.0 * (k * v) - 0.125 * (k * tu[1] + tu[2]))
            sums = [f if j == 0 else total + f for total, f in zip(sums, (res, k))]
        sum_quads(quads, q, sums)
        return carry

    lax.fori_loop(0, 4, quad, 0)
    level3 = select_lanes(read_quads(quads), level3_lanes[...])
    inner[...] = level3[:, 256:384]
    to_up[0:16, :] = up_rows[...]
    to_down[0:16, :] = down_rows[...]
    pack_lanes(lambda field, x: full[field, x, 16:32, :], 16, to_up, to_down, 16)
    to_up[0:16, 384:512] += level3[:, 0:128]
    to_down[0:16, 384:512] += level3[:, 128:256]


def rolled(x, shift):
    shift = shift % x.shape[1]
    return pltpu.roll(x, shift, 1) if shift else x


def bands_xy(full, xy, tables, end_lanes, bands):
    row = iota((192, 512), 0)
    cell = iota((192, 512), 1)
    cell_x = (cell >> 6) * 4 + ((cell >> 2) & 3)
    cell_y = ((cell >> 4) & 3) * 4 + (cell & 3)
    for level in range(3):
        at_x = lax.axis_index("gx") * (4 >> level) - 4 + (row >> 4)
        at_y = lax.axis_index("gy") * (4 >> level) - 4 + (row & 15)
        found = ((cell_x >> level) == at_x) & ((cell_y >> level) == at_y)
        tables[192 * level : 192 * level + 192, :] = ones_where(found)
    source = iota((128, 256), 0)
    lane = iota((128, 256), 1)
    is_coef = jnp.where(source < 80, jnp.where(source >= 40, 1, 0), jnp.where(source >= 88, 1, 0))
    cell = jnp.where(source < 80, source - 40 * is_coef - 4, source - 80 - 8 * is_coef)
    inner = source < 80
    pairs = (source >= 80) & (source < 96) & (cell < 4)
    fours = (source >= 80) & (source < 96) & (cell >= 4)
    pair = jnp.where(cell < 2, cell - 4, cell + 16)
    four = jnp.where(cell < 6, cell - 8, cell + 4)
    targets = (
        jnp.where(inner, cell + 16, -1),
        jnp.where(inner, 64 + 8 + (cell >> 1), jnp.where(pairs, 64 + 8 + pair, -1)),
        jnp.where(inner, 96 + 4 + (cell >> 2), jnp.where(pairs, 96 + 4 + (pair >> 1), jnp.where(fours, 96 + 4 + four, -1))),
    )
    for level, target in enumerate(targets):
        scale = jnp.where(is_coef == 1, F32(0.125**level), F32(0.5**level))
        found = (target >= 0) & (lane == is_coef * 128 + target)
        at = 576 + 128 * level
        tables[at : at + 128, 0:256] = jnp.where(found, scale, 0.0).astype(BF16)
    source = iota((128, 128), 0)
    lane = iota((128, 128), 1)
    for level, start in enumerate((16, 72, 100)):
        found = source == start + (lane >> (level + 2))
        tables[960:1088, 128 * level : 128 * level + 128] = ones_where(found)

    source = iota((384, 128), 0)
    x = (source >> 4) - 6
    z = (source & 15) - 2
    place = (x >= 0) & (x < 16) & (z >= 0) & (z < 8) & (iota((384, 128), 1) == (x >> 2) * 32 + (z >> 2))
    end_lanes[...] = ones_where(place)

    def in_y(x, carry):
        k = full[0, x]
        v = full[1, x]
        bands[0, x] = band(k, 0)
        bands[1, x] = band(v, 0)
        bands[2, x] = band(k * v, 0)
        return carry

    lax.fori_loop(0, 28, in_y, 0, unroll=2)

    def in_x(x, carry):
        for field in range(3):
            xy[field, x - 2] = (bands[field, x - 1] + bands[field, x + 1]) + 2.0 * bands[field, x]
        return carry

    lax.fori_loop(2, 26, in_x, 0, unroll=2)


def end_cells(lower_k, lower_v, lower_right, upper_k, upper_v, upper_right):
    position = iota((32, 512), 1) & 15
    k = jnp.where(position < 6, lower_k, jnp.where(position < 12, upper_k, 0.0))
    v = jnp.where(position < 6, lower_v, upper_v)
    right = jnp.where(position < 6, lower_right, upper_right)[0:16, :]
    tu = []
    for f in (k, v, k * v):
        f = band(f, 0)[0:16, :]
        f = f + pltpu.roll(f, 16, 1)
        tu.append(band(f + pltpu.roll(f, 512 - 16, 1), 1))
    k, v = k[0:16, :], v[0:16, :]
    diagonal = 6.0 * k + 0.125 * tu[0]
    return right - (v * diagonal + 2.0 * (k * v) - 0.125 * (k * tu[1] + tu[2])), k


def own_cells(sent_up, sent_down, from_down, from_up, inner, end_lanes, chunks, quads):
    def moved(f, shift):
        return pltpu.roll(f, shift % 512, 1)

    low, first, last, high = from_down[...], sent_down[...], sent_up[...], from_up[...]
    found = [
        end_cells(low, moved(low, -5), moved(low, -9), moved(first, 6), first, moved(first, -5)),
        end_cells(last, moved(last, -5), moved(last, -9), moved(high, 6), high, moved(high, -5)),
    ]
    rows = []
    for f in (found[0][0], found[1][0], found[0][1], found[1][1]):
        f = f[:, 0:384]
        f = f + pltpu.roll(f, 15, 0)
        rows.append(f + pltpu.roll(f, 14, 0))
    ends = select_lanes(jnp.concatenate(rows, axis=0), end_lanes[...])
    ends = [0.25 * ends[0:16], 0.25 * ends[16:32], ends[32:48] / 64.0, ends[48:64] / 64.0]
    for q in range(4):
        for at in range(4):
            start = 64 * at + 16 * q
            quads[start : start + 16, :] = rolled(ends[at], -32 * q)
    lane = iota((16, 128), 1)
    mine = inner[...]
    for at, target in enumerate((3, 35, 43, 75)):
        cells = pltpu.roll(quads[pl.ds(64 * at, 16, stride=4), :], target, 1)
        mine = jnp.where((lane == target) | (lane == target + 1), cells, mine)
    low = from_down[0:16, 384:512]
    high = from_up[0:16, 384:512]
    for cells, moves in (
        (low, ((64, 0, 3), (67, 80, 2), (69, 84, 2), (80, 40, 3), (83, 88, 2), (85, 92, 2))),
        (high, ((64, 37, 3), (67, 82, 2), (69, 86, 2), (80, 77, 3), (83, 90, 2), (85, 94, 2))),
    ):
        for at, target, count in moves:
            mine = jnp.where((lane >= target) & (lane < target + count), rolled(cells, target - at), mine)
    lane = iota((4, 128), 1)
    for part in range(3):
        rest = rolled(mine, 96 - 32 * part)[12:16]
        tile = jnp.where(lane < 96, mine[4 * part : 4 * part + 4], rest)
        chunks[:, part] = jnp.broadcast_to(tile[None], (chunks.shape[0], 4, 128))


def fine_residual(full, xy, from_down, from_up, coef, res, inv, side, sides_kv, product):
    lane = iota((32, 128), 1)

    for x in range(28):
        group, first = 128 * (x // 8), 16 * (x % 8)
        up = from_up[:, group : group + 128]
        down = from_down[:, group : group + 128]
        tiles = []
        for field in range(3):
            h, a = HALO[field], ROWS[field]
            tile = jnp.where(lane >= 128 - h, rolled(down, 128 - h - first - a), 0.0)
            tiles.append(jnp.where(lane < h, rolled(up, -first - a), tile))
        coef[x, :, 0:128] = full[0, x]
        coef[x, :, 128:256] = tiles[0]
        side[0, x] = tiles[1]
        side[1, x] = tiles[2]
        sides_kv[x, :, 0:128] = band(tiles[0], 0)
        sides_kv[x, :, 128:256] = band(tiles[1], 0)
        product[x] = band(tiles[0] * tiles[1], 0)

    for x in (0, 1, 26, 27):
        res[x] = jnp.zeros((32, 256), F32)

    def over_x(ref, x):
        return (ref[x - 1] + ref[x + 1]) + 2.0 * ref[x]

    matrix = band_matrix(256)

    def cells(step, carry):
        xs = [2 + 8 * step + j for j in range(8)]
        wanted = []
        for x in xs:
            sides = over_x(sides_kv, x)
            wanted += [
                jnp.concatenate([xy[0, x - 2], sides[:, 0:128]], axis=1),
                jnp.concatenate([xy[1, x - 2], sides[:, 128:256]], axis=1),
                jnp.concatenate([xy[2, x - 2], over_x(product, x)], axis=1),
            ]
        found = band_z(wanted, matrix)
        for j, x in enumerate(xs):
            tu_k, tu_v, tu_kv = found[3 * j : 3 * j + 3]
            k = coef[x]
            v = jnp.concatenate([full[1, x], side[0, x]], axis=1)
            diagonal = 6.0 * k + 0.125 * tu_k
            applied = v * diagonal + 2.0 * (k * v) - 0.125 * (k * tu_v + tu_kv)
            res[x] = jnp.concatenate([full[2, x], side[1, x]], axis=1) - applied
            inv[x] = damped_inverse(k, diagonal)
        return carry

    lax.fori_loop(0, 3, cells, 0)


def fine_sweeps(full, coef, res, inv, base, corr, corr_next, yz_c, yz_kc, pairs, spread):
    def over_x(ref, x):
        return (ref[x - 1] + ref[x + 1]) + 2.0 * ref[x]

    def bands_of(xs, ref):
        wanted = []
        for x in xs:
            c = ref[x]
            wanted += [band(c, 0), band(coef[x] * c, 0)]
        found = [band(f, 1) for f in wanted]
        for j, x in enumerate(xs):
            yz_c[x] = found[2 * j]
            yz_kc[x] = found[2 * j + 1]

    def first_sweep(step, carry):
        xs = [4 + 4 * step + j for j in range(4)]
        for x in xs:
            corr[x] = inv[x] * res[x]
        bands_of(xs, corr)
        return carry

    lax.fori_loop(0, 5, first_sweep, 0)

    def second(x, carry):
        corr_next[x] = relax(corr[x], inv[x], res[x], coef[x], over_x(yz_c, x), over_x(yz_kc, x))
        return carry

    lax.fori_loop(5, 23, second, 0, unroll=3)

    def second_bands(step, carry):
        bands_of([5 + 3 * step + j for j in range(3)], corr_next)
        return carry

    lax.fori_loop(0, 6, second_bands, 0)

    halves = ones_where((iota((256, 128), 0) >> 1) == iota((256, 128), 1))

    def pair(x, carry):
        for at, ref in enumerate((res, coef)):
            f = ref[2 * x] + ref[2 * x + 1]
            for tile in range(2):
                place = pl.ds(pl.multiple_of(448 * at + 32 * x, 32), 32)
                pairs[tile, place, :] = f[:, 128 * tile : 128 * tile + 128]
        return carry

    lax.fori_loop(0, 14, pair, 0, unroll=2)
    sums = [pairs[tile, pl.ds(0, 448, stride=2), :] + pairs[tile, pl.ds(1, 448, stride=2), :] for tile in range(2)]
    sums = select_lanes(jnp.concatenate(sums, axis=1), halves).reshape(2, 14, 16, 128)
    corr_two = smooth_small(0.5 * sums[0], 0.125 * sums[1], 3)
    doubled = ones_where(iota((128, 128), 0) == (iota((128, 128), 1) >> 1))
    wide = select_lanes(corr_two[3:11].reshape(128, 128), doubled).reshape(8, 16, 128)
    rows = wide[:, 0:8, :].reshape(64, 128)
    spread[pl.ds(0, 64, stride=2), :] = rows
    spread[pl.ds(1, 64, stride=2), :] = rows

    def third(x, carry):
        c = relax(
            corr_next[x, 0:16, 0:128],
            inv[x, 0:16, 0:128],
            res[x, 0:16, 0:128],
            coef[x, 0:16, 0:128],
            (yz_c[x - 1, 0:16, 0:128] + yz_c[x + 1, 0:16, 0:128]) + 2.0 * yz_c[x, 0:16, 0:128],
            (yz_kc[x - 1, 0:16, 0:128] + yz_kc[x + 1, 0:16, 0:128]) + 2.0 * yz_kc[x, 0:16, 0:128],
        )
        block = x - 6
        base[block] = full[1, x, 0:16, :] + (c + spread[pl.ds(pl.multiple_of(16 * (block // 2), 16), 16), :])
        return carry

    lax.fori_loop(6, 22, third, 0, unroll=4)


def coarse_levels(tables, plane, base, out, columns, spread):
    lane = iota((plane.shape[0], 4, 128), 2)
    parts = [plane[:, part] for part in range(3)]
    for part in range(3):
        columns[:, 4 * part : 4 * part + 4, :] = parts[part]
    rest = [pltpu.roll(parts[part], 32 + 32 * part, 2) for part in range(3)]
    columns[:, 12:16, :] = jnp.where(lane < 32, rest[0], jnp.where(lane < 64, rest[1], rest[2]))
    columns = columns[...].reshape(plane.shape[0] * 16, 128)
    found = jnp.dot(tables[0:576, :], jnp.concatenate(split(columns), axis=1), preferred_element_type=F32)
    found = found[:, 0:128] + (found[:, 128:256] + found[:, 256:384])
    windows = jnp.concatenate([found[192 * level : 192 * level + 192, :] for level in range(3)], axis=1)
    both = select_lanes(windows, tables[576:960, 0:256])
    corr = smooth_small(both[:, 0:128].reshape(12, 16, 128), both[:, 128:256].reshape(12, 16, 128), 4)
    wide = select_lanes(corr[4:8].reshape(64, 128), tables[960:1088, 0:384])
    for x in range(4):
        level4 = wide[16 * (x // 2) : 16 * (x // 2) + 16, 128:256]
        level4 = jnp.concatenate([jnp.broadcast_to(level4[y : y + 1], (2, 128)) for y in (4, 5)], axis=0)
        rows = wide[16 * x + 4 : 16 * x + 8, 0:128] + (level4 + wide[4:5, 256:384])
        for y in range(4):
            spread[pl.ds(16 * x + y, 4, stride=4), :] = rows
    for x in range(16):
        start = 16 * (x // 4)
        out[x] = base[x] + spread[start : start + 16, :]


VMEM = pl.BlockSpec(memory_space=pltpu.VMEM)
HBM = pl.BlockSpec(memory_space=pltpu.HBM)


def call(kernel, outs, ins, scratch=(), first=VMEM, rest=VMEM, flops=1000000, grant=32):
    moved = 4 * sum(x.size for x in ins)
    return pl.pallas_call(
        kernel,
        out_shape=[out if isinstance(out, jax.ShapeDtypeStruct) else jax.ShapeDtypeStruct(out, F32) for out in outs],
        in_specs=[first] + [rest] * (len(ins) - 1),
        out_specs=[VMEM] * len(outs),
        scratch_shapes=[pltpu.VMEM(shape, F32) if isinstance(shape, tuple) else shape for shape in scratch],
        compiler_params=pltpu.CompilerParams(vmem_limit_bytes=grant * 1024 * 1024),
        cost_estimate=pl.CostEstimate(flops=flops, bytes_accessed=moved, transcendentals=0),
        name=kernel.__name__,
    )(*ins)


def neighbour_pairs(count):
    for start in (1, 0):
        lower = range(start, count - 1, 2)
        yield [(i, i + 1) for i in lower] + [(i + 1, i) for i in lower]


def swap(axis, to_up, to_down):
    count = lax.axis_size(axis)
    up = [(i, i + 1) for i in range(count - 1)]
    down = [(i + 1, i) for i in range(count - 1)]
    return lax.ppermute(to_up, axis, up), lax.ppermute(to_down, axis, down)


def on_device(right, iterate, phase, table):
    block = (16, 16, 128)
    fields, to_up, to_down = call(
        send_x,
        [(3, *block), (15, 16, 128), (15, 16, 128)],
        [table, phase, iterate, right],
        scratch=[pltpu.SMEM((4,), F32), pltpu.VMEM(block, jnp.int32), pltpu.SemaphoreType.DMA((4,))],
        first=HBM,
        rest=HBM,
        grant=60,
    )
    from_down, from_up = swap("gx", to_up, to_down)
    (held,) = call(hold, [(3, *block)], [fields], flops=30000000)
    from_down, from_up, fields = lax.optimization_barrier((from_down, from_up, held))
    ext, *sent = call(
        pack_y,
        [(3, 28, 16, 128), (28, 16, 128), (28, 16, 128)],
        [fields, from_down, from_up],
    )
    found = [lax.ppermute(rows, "gy", pairs) for rows, pairs in zip(sent, neighbour_pairs(lax.axis_size("gy")))]
    planes = (3, 28, 32, 128)
    mine = call(
        own_rows,
        [(16, 512), (16, 512), (3, *block), jax.ShapeDtypeStruct((256, 384), BF16)],
        [ext],
        flops=30000000,
    )
    *found, up_rows, down_rows, xz, level3_lanes = lax.optimization_barrier((*found, *mine))
    full, to_up, to_down, inner = call(
        pack_z,
        [planes, (32, 512), (32, 512), (16, 128)],
        [ext, *found, up_rows, down_rows, xz, level3_lanes],
        scratch=[(6, 32, 128), (128, 128)],
    )
    from_down, from_up = swap("gz", to_up, to_down)
    xy, tables, end_lanes = call(
        bands_xy,
        [(3, 24, 32, 128), jax.ShapeDtypeStruct((1088, 512), BF16), jax.ShapeDtypeStruct((384, 128), BF16)],
        [full],
        scratch=[planes],
        flops=30000000,
    )
    from_down, from_up, xy, tables, end_lanes = lax.optimization_barrier((from_down, from_up, xy, tables, end_lanes))
    z_sides = [from_down, from_up]
    count = lax.axis_size("gx") * lax.axis_size("gy")
    (chunks,) = call(own_cells, [(count, 3, 4, 128)], [to_up, to_down, *z_sides, inner, end_lanes], scratch=[(256, 128)])
    plane = lax.all_to_all(chunks, ("gx", "gy"), 0, 0, tiled=True)
    wide = (28, 32, 256)
    coef, res, inv = call(
        fine_residual,
        [wide] * 3,
        [full, xy, *z_sides],
        scratch=[(2, 28, 32, 128), wide, (28, 32, 128)],
        flops=30000000,
    )
    (base,) = call(
        fine_sweeps,
        [block],
        [full, coef, res, inv],
        scratch=[wide, wide, wide, wide, (2, 896, 128), (128, 128)],
        flops=60000000,
    )
    (out,) = call(coarse_levels, [block], [tables, plane, base], scratch=[(count, 16, 128), (64, 128)])
    return out


def solution(mesh):
    placed = (P("gx", "gy", "gz"), P("gx", "gy", "gz"), P("gx", "gy", "gz"), P())
    return jax.shard_map(on_device, mesh=mesh, in_specs=placed, out_specs=P("gx", "gy", "gz"), check_vma=False)
```

```python
import jax
import jax.numpy as jnp
from jax import lax
from jax.experimental import pallas as pl
from jax.experimental.pallas import tpu as pltpu
from jax.sharding import PartitionSpec as P

HALO = (6, 5, 4)
ROWS = (0, 6, 11, 15)
OMEGA = 2.0 / 3.0
F32 = jnp.float32
BF16 = jnp.bfloat16


def iota(shape, dim):
    return lax.broadcasted_iota(jnp.int32, shape, dim)


def ones_where(cond, scale=1.0):
    return jnp.where(cond, F32(scale), F32(0.0)).astype(BF16)


def split(x):
    high = x.astype(BF16)
    rest = x - high.astype(F32)
    middle = rest.astype(BF16)
    return high, middle, (rest - middle.astype(F32)).astype(BF16)


def select_rows(pattern, x):
    high, middle, low = [jnp.dot(pattern, part, preferred_element_type=F32) for part in split(x)]
    return high + (middle + low)


def select_lanes(x, pattern):
    high, middle, low = [jnp.dot(part, pattern, preferred_element_type=F32) for part in split(x)]
    return high + (middle + low)


def band_matrix(size):
    apart = jnp.abs(iota((size, size), 0) - iota((size, size), 1))
    return jnp.where(apart == 0, 2.0, jnp.where((apart == 1) | (apart == size - 1), 1.0, 0.0)).astype(BF16)


def band_z(fields, matrix):
    shape = fields[0].shape
    rows = fields[0].size // shape[-1]
    found = select_lanes(jnp.concatenate([f.reshape(rows, shape[-1]) for f in fields], axis=0), matrix)
    return [found[rows * at : rows * at + rows].reshape(shape) for at in range(len(fields))]


def band(x, axis):
    return (pltpu.roll(x, 1, axis) + pltpu.roll(x, x.shape[axis] - 1, axis)) + 2.0 * x


def band_x(x):
    up = jnp.concatenate([x[1:], x[:1]], axis=0)
    down = jnp.concatenate([x[-1:], x[:-1]], axis=0)
    return (up + down) + 2.0 * x


def damped_inverse(coef, diagonal):
    inside = coef > 0.0
    return jnp.where(inside, OMEGA / jnp.where(inside, diagonal, 1.0), 0.0)


def relax(corr, inverse, residual, coef, tu_corr, tu_product):
    return corr * (1.0 / 3.0) + inverse * (residual - 2.0 * (coef * corr) + 0.125 * (coef * tu_corr + tu_product))


def smooth_small(residual, coef, sweeps):
    inverse = damped_inverse(coef, 6.0 * coef + 0.125 * band(band_x(band(coef, 1)), 2))
    corr = inverse * residual
    for _ in range(sweeps - 1):
        tu = [band(band_x(band(f, 1)), 2) for f in (corr, coef * corr)]
        corr = relax(corr, inverse, residual, coef, *tu)
    return corr


def send_x(table, phase, iterate, right, fields, to_up, to_down, values, phases, sems):
    copies = [
        pltpu.make_async_copy(table, values, sems.at[0]),
        pltpu.make_async_copy(phase, phases, sems.at[1]),
        pltpu.make_async_copy(iterate, fields.at[1], sems.at[2]),
        pltpu.make_async_copy(right, fields.at[2], sems.at[3]),
    ]
    for copy in copies:
        copy.start()
    for copy in copies:
        copy.wait()
    p = phases[...]
    k = jnp.zeros(p.shape, F32)
    for index in range(4):
        k = jnp.where(p == index, values[index], k)
    fields[0] = k
    for field in range(3):
        h, a, b = HALO[field], ROWS[field], ROWS[field + 1]
        to_up[a:b] = fields[field, 16 - h : 16]
        to_down[a:b] = fields[field, 0:h]


def hold(fields, held):
    held[...] = fields[...]


def by_parity(body, first, second):
    odd = (lax.axis_index("gy") & 1) == 1

    @pl.when(odd)
    def _():
        body(second, first)

    @pl.when(jnp.logical_not(odd))
    def _():
        body(first, second)


def pack_y(fields, from_down, from_up, ext, to_first, to_second):
    for field in range(3):
        h, a, b = HALO[field], ROWS[field], ROWS[field + 1]
        if h < 6:
            ext[field, 0 : 6 - h] = jnp.zeros((6 - h, 16, 128), F32)
            ext[field, 22 + h : 28] = jnp.zeros((6 - h, 16, 128), F32)
        ext[field, 6 - h : 6] = from_down[a:b]
        ext[field, 6:22] = fields[field]
        ext[field, 22 : 22 + h] = from_up[a:b]

    def rows(to_down, to_up):
        for field in range(3):
            h, a, b = HALO[field], ROWS[field], ROWS[field + 1]
            to_up[:, a:b, :] = ext[field, :, 16 - h : 16, :]
            to_down[:, a:b, :] = ext[field, :, 0:h, :]

    by_parity(rows, to_first, to_second)
    to_first[:, 15:16, :] = jnp.zeros((28, 1, 128), F32)
    to_second[:, 15:16, :] = jnp.zeros((28, 1, 128), F32)


def sum_quads(quads, q, sums):
    for at, f in enumerate(sums):
        f = f + pltpu.roll(f, 15, 0)
        f = f + pltpu.roll(f, 14, 0)
        for tile in range(f.shape[1] // 128):
            start = 64 * (at * (f.shape[1] // 128) + tile) + 16 * q
            quads[pl.ds(pl.multiple_of(start, 16), 16), :] = f[:, 128 * tile : 128 * tile + 128]


def read_quads(quads):
    count = quads.shape[0] // 64
    return jnp.concatenate([quads[pl.ds(64 * at, 16, stride=4), :] for at in range(count)], axis=1)


def pack_lanes(cells_of, rows, to_up, to_down, at):
    lane = iota((rows, 128), 1)
    for group in range(4):
        up = jnp.zeros((rows, 128), F32)
        down = jnp.zeros((rows, 128), F32)
        for x in range(8 * group, min(8 * group + 8, 28)):
            first = 16 * (x - 8 * group)
            for field in range(3):
                h, a, b = HALO[field], ROWS[field], ROWS[field + 1]
                if not 6 - h <= x < 22 + h:
                    continue
                cells = cells_of(field, x)
                mine = (lane >= first + a) & (lane < first + b)
                up = jnp.where(mine, pltpu.roll(cells, (first + a + h) % 128, 1), up)
                down = jnp.where(mine, rolled(cells, first + a), down)
        to_up[at : at + rows, 128 * group : 128 * group + 128] = up
        to_down[at : at + rows, 128 * group : 128 * group + 128] = down


def own_rows(ext, up, down, xz, level3_lanes):
    pack_lanes(lambda field, x: ext[field, x], 16, up, down, 0)
    matrix = band_matrix(128)

    def bands(step, carry):
        xs = [6 + 4 * step + j for j in range(4)]
        wanted = []
        for x in xs:
            around = [(ext[0, x + d], ext[1, x + d]) for d in (-1, 0, 1)]
            for low, here, high in zip(*[(k, v, k * v) for k, v in around]):
                wanted.append((low + high) + 2.0 * here)
        for at, f in enumerate(band_z(wanted, matrix)):
            xz[at % 3, xs[at // 3] - 6] = f
        return carry

    lax.fori_loop(0, 4, bands, 0)
    source = iota((256, 128), 0)
    lane = iota((256, 128), 1)
    coarse = (source & 127) >> 2
    is_coef = source >> 7
    scale = jnp.where(source < 128, F32(0.25), F32(1.0 / 64.0))
    upper = jnp.where(coarse >= 28, coarse - 28, jnp.where(coarse >= 24, (coarse >> 1) - 9, (coarse >> 2) + 1))
    lower = jnp.where(coarse <= 3, coarse - 1, jnp.where(coarse <= 7, (coarse >> 1) + 1, (coarse >> 2) + 3))
    found = (
        (lane == 64 + 16 * is_coef + upper) & (coarse >= 16) & (coarse <= 30),
        (lane == 64 + 16 * is_coef + lower) & (coarse >= 1) & (coarse <= 15),
        (lane == 40 * is_coef + 4 + coarse) & (coarse >= 1) & (coarse <= 30),
    )
    for at, here in enumerate(found):
        level3_lanes[:, 128 * at : 128 * at + 128] = jnp.where(here, scale, 0.0).astype(BF16)


def pack_z(ext, from_first, from_second, up_rows, down_rows, xz, level3_lanes, beyond, to_up, to_down, inner, edges, quads):
    edges[:, 24:32, :] = jnp.zeros((6, 8, 128), F32)
    for field in range(3):
        h = HALO[field]
        beyond[field, :, h : 16 - h, :] = jnp.zeros((28, 16 - 2 * h, 128), F32)

    def rows(from_down, from_up):
        for field in range(3):
            h, a, b = HALO[field], ROWS[field], ROWS[field + 1]
            beyond[field, :, 0:h, :] = from_up[:, a:b, :]
            beyond[field, :, 16 - h : 16, :] = from_down[:, a:b, :]
        for at, (source, row_k, row_v) in enumerate(((from_down, 5, 10), (from_up, 0, 6))):
            k = source[:, row_k, :]
            v = source[:, row_v, :]
            for number, f in enumerate((k, v, k * v)):
                edges[3 * at + number, 0:28, :] = f

    by_parity(rows, from_first, from_second)
    for at in range(6):
        edges[at] = band(band(edges[at], 0), 1)
    row = iota((16, 128), 0)

    def quad(q, carry):
        sums = [None, None]
        for j in range(4):
            x = 6 + 4 * q + j
            tu = []
            for at in range(3):
                f = xz[at, 4 * q + j]
                below = jnp.where(row == 0, edges[at, pl.ds(x, 1), :], pltpu.roll(f, 1, 0))
                above = jnp.where(row == 15, edges[3 + at, pl.ds(x, 1), :], pltpu.roll(f, 15, 0))
                tu.append((below + above) + 2.0 * f)
            k = ext[0, x]
            v = ext[1, x]
            diagonal = 6.0 * k + 0.125 * tu[0]
            res = ext[2, x] - (v * diagonal + 2.0 * (k * v) - 0.125 * (k * tu[1] + tu[2]))
            sums = [f if j == 0 else total + f for total, f in zip(sums, (res, k))]
        sum_quads(quads, q, sums)
        return carry

    lax.fori_loop(0, 4, quad, 0)
    level3 = select_lanes(read_quads(quads), level3_lanes[...])
    inner[...] = level3[:, 256:384]
    to_up[0:16, :] = up_rows[...]
    to_down[0:16, :] = down_rows[...]
    pack_lanes(lambda field, x: beyond[field, x], 16, to_up, to_down, 16)
    to_up[0:16, 384:512] += level3[:, 0:128]
    to_down[0:16, 384:512] += level3[:, 128:256]


def rolled(x, shift):
    shift = shift % x.shape[1]
    return pltpu.roll(x, shift, 1) if shift else x


def all_rows(ext, beyond, field, x):
    return jnp.concatenate([ext[field, x], beyond[field, x]], axis=0)


def bands_xy(ext, beyond, xy, tables, end_lanes, bands):
    row = iota((192, 512), 0)
    cell = iota((192, 512), 1)
    cell_x = (cell >> 6) * 4 + ((cell >> 2) & 3)
    cell_y = ((cell >> 4) & 3) * 4 + (cell & 3)
    for level in range(3):
        at_x = lax.axis_index("gx") * (4 >> level) - 4 + (row >> 4)
        at_y = lax.axis_index("gy") * (4 >> level) - 4 + (row & 15)
        found = ((cell_x >> level) == at_x) & ((cell_y >> level) == at_y)
        tables[192 * level : 192 * level + 192, :] = ones_where(found)
    source = iota((128, 256), 0)
    lane = iota((128, 256), 1)
    is_coef = jnp.where(source < 80, jnp.where(source >= 40, 1, 0), jnp.where(source >= 88, 1, 0))
    cell = jnp.where(source < 80, source - 40 * is_coef - 4, source - 80 - 8 * is_coef)
    inner = source < 80
    pairs = (source >= 80) & (source < 96) & (cell < 4)
    fours = (source >= 80) & (source < 96) & (cell >= 4)
    pair = jnp.where(cell < 2, cell - 4, cell + 16)
    four = jnp.where(cell < 6, cell - 8, cell + 4)
    targets = (
        jnp.where(inner, cell + 16, -1),
        jnp.where(inner, 64 + 8 + (cell >> 1), jnp.where(pairs, 64 + 8 + pair, -1)),
        jnp.where(inner, 96 + 4 + (cell >> 2), jnp.where(pairs, 96 + 4 + (pair >> 1), jnp.where(fours, 96 + 4 + four, -1))),
    )
    for level, target in enumerate(targets):
        scale = jnp.where(is_coef == 1, F32(0.125**level), F32(0.5**level))
        found = (target >= 0) & (lane == is_coef * 128 + target)
        at = 576 + 128 * level
        tables[at : at + 128, 0:256] = jnp.where(found, scale, 0.0).astype(BF16)
    source = iota((128, 128), 0)
    lane = iota((128, 128), 1)
    for level, start in enumerate((16, 72, 100)):
        found = source == start + (lane >> (level + 2))
        tables[960:1088, 128 * level : 128 * level + 128] = ones_where(found)

    source = iota((384, 128), 0)
    x = (source >> 4) - 6
    z = (source & 15) - 2
    place = (x >= 0) & (x < 16) & (z >= 0) & (z < 8) & (iota((384, 128), 1) == (x >> 2) * 32 + (z >> 2))
    end_lanes[...] = ones_where(place)

    def in_y(x, carry):
        k, v = [all_rows(ext, beyond, field, x) for field in range(2)]
        bands[0, x] = band(k, 0)
        bands[1, x] = band(v, 0)
        bands[2, x] = band(k * v, 0)
        return carry

    lax.fori_loop(0, 28, in_y, 0, unroll=2)

    def in_x(x, carry):
        for field in range(3):
            xy[field, x - 2] = (bands[field, x - 1] + bands[field, x + 1]) + 2.0 * bands[field, x]
        return carry

    lax.fori_loop(2, 26, in_x, 0, unroll=2)


def end_cells(lower_k, lower_v, lower_right, upper_k, upper_v, upper_right):
    position = iota((32, 384), 1) & 15
    k = jnp.where(position < 6, lower_k, jnp.where(position < 12, upper_k, 0.0))
    v = jnp.where(position < 6, lower_v, upper_v)
    right = jnp.where(position < 6, lower_right, upper_right)[0:16, :]
    tu = []
    for f in (k, v, k * v):
        f = band(f, 0)[0:16, :]
        f = f + pltpu.roll(f, 16, 1)
        tu.append(band(f + pltpu.roll(f, 384 - 16, 1), 1))
    k, v = k[0:16, :], v[0:16, :]
    diagonal = 6.0 * k + 0.125 * tu[0]
    return right - (v * diagonal + 2.0 * (k * v) - 0.125 * (k * tu[1] + tu[2])), k


def own_cells(sent_up, sent_down, from_down, from_up, inner, end_lanes, chunks, quads):
    def moved(f, shift):
        return pltpu.roll(f, shift % 384, 1)

    low, first, last, high = [ref[:, 0:384] for ref in (from_down, sent_down, sent_up, from_up)]
    found = [
        end_cells(low, moved(low, -5), moved(low, -9), moved(first, 6), first, moved(first, -5)),
        end_cells(last, moved(last, -5), moved(last, -9), moved(high, 6), high, moved(high, -5)),
    ]
    rows = []
    for f in (found[0][0], found[1][0], found[0][1], found[1][1]):
        f = f + pltpu.roll(f, 15, 0)
        rows.append(f + pltpu.roll(f, 14, 0))
    ends = select_lanes(jnp.concatenate(rows, axis=0), end_lanes[...])
    ends = [0.25 * ends[0:16], 0.25 * ends[16:32], ends[32:48] / 64.0, ends[48:64] / 64.0]
    for q in range(4):
        for at in range(4):
            start = 64 * at + 16 * q
            quads[start : start + 16, :] = rolled(ends[at], -32 * q)
    lane = iota((16, 128), 1)
    mine = inner[...]
    for at, target in enumerate((3, 35, 43, 75)):
        cells = pltpu.roll(quads[pl.ds(64 * at, 16, stride=4), :], target, 1)
        mine = jnp.where((lane == target) | (lane == target + 1), cells, mine)
    low = from_down[0:16, 384:512]
    high = from_up[0:16, 384:512]
    for cells, moves in (
        (low, ((64, 0, 3), (67, 80, 2), (69, 84, 2), (80, 40, 3), (83, 88, 2), (85, 92, 2))),
        (high, ((64, 37, 3), (67, 82, 2), (69, 86, 2), (80, 77, 3), (83, 90, 2), (85, 94, 2))),
    ):
        for at, target, count in moves:
            mine = jnp.where((lane >= target) & (lane < target + count), rolled(cells, target - at), mine)
    lane = iota((4, 128), 1)
    for part in range(3):
        rest = rolled(mine, 96 - 32 * part)[12:16]
        tile = jnp.where(lane < 96, mine[4 * part : 4 * part + 4], rest)
        chunks[:, part] = jnp.broadcast_to(tile[None], (chunks.shape[0], 4, 128))


def fine_residual(ext, beyond, xy, from_down, from_up, coef, res, inv, side, sides_kv, product):
    lane = iota((32, 128), 1)

    for x in range(28):
        group, first = 128 * (x // 8), 16 * (x % 8)
        up = from_up[:, group : group + 128]
        down = from_down[:, group : group + 128]
        tiles = []
        for field in range(3):
            h, a = HALO[field], ROWS[field]
            tile = jnp.where(lane >= 128 - h, rolled(down, 128 - h - first - a), 0.0)
            tiles.append(jnp.where(lane < h, rolled(up, -first - a), tile))
        coef[x, :, 0:128] = all_rows(ext, beyond, 0, x)
        coef[x, :, 128:256] = tiles[0]
        side[0, x] = tiles[1]
        side[1, x] = tiles[2]
        sides_kv[x, :, 0:128] = band(tiles[0], 0)
        sides_kv[x, :, 128:256] = band(tiles[1], 0)
        product[x] = band(tiles[0] * tiles[1], 0)

    for x in (0, 1, 26, 27):
        res[x] = jnp.zeros((32, 256), F32)

    def over_x(ref, x):
        return (ref[x - 1] + ref[x + 1]) + 2.0 * ref[x]

    matrix = band_matrix(256)

    def cells(step, carry):
        xs = [2 + 8 * step + j for j in range(8)]
        wanted = []
        for x in xs:
            sides = over_x(sides_kv, x)
            wanted += [
                jnp.concatenate([xy[0, x - 2], sides[:, 0:128]], axis=1),
                jnp.concatenate([xy[1, x - 2], sides[:, 128:256]], axis=1),
                jnp.concatenate([xy[2, x - 2], over_x(product, x)], axis=1),
            ]
        found = band_z(wanted, matrix)
        for j, x in enumerate(xs):
            tu_k, tu_v, tu_kv = found[3 * j : 3 * j + 3]
            k = coef[x]
            v = jnp.concatenate([all_rows(ext, beyond, 1, x), side[0, x]], axis=1)
            diagonal = 6.0 * k + 0.125 * tu_k
            applied = v * diagonal + 2.0 * (k * v) - 0.125 * (k * tu_v + tu_kv)
            res[x] = jnp.concatenate([all_rows(ext, beyond, 2, x), side[1, x]], axis=1) - applied
            inv[x] = damped_inverse(k, diagonal)
        return carry

    lax.fori_loop(0, 3, cells, 0)


def fine_sweeps(ext, coef, res, inv, base, corr, corr_next, yz_c, yz_kc, pairs, spread):
    def over_x(ref, x):
        return (ref[x - 1] + ref[x + 1]) + 2.0 * ref[x]

    def bands_of(xs, ref):
        wanted = []
        for x in xs:
            c = ref[x]
            wanted += [band(c, 0), band(coef[x] * c, 0)]
        found = [band(f, 1) for f in wanted]
        for j, x in enumerate(xs):
            yz_c[x] = found[2 * j]
            yz_kc[x] = found[2 * j + 1]

    def first_sweep(step, carry):
        xs = [4 + 4 * step + j for j in range(4)]
        for x in xs:
            corr[x] = inv[x] * res[x]
        bands_of(xs, corr)
        return carry

    lax.fori_loop(0, 5, first_sweep, 0)

    def second(x, carry):
        corr_next[x] = relax(corr[x], inv[x], res[x], coef[x], over_x(yz_c, x), over_x(yz_kc, x))
        return carry

    lax.fori_loop(5, 23, second, 0, unroll=3)

    def second_bands(step, carry):
        bands_of([5 + 3 * step + j for j in range(3)], corr_next)
        return carry

    lax.fori_loop(0, 6, second_bands, 0)

    halves = ones_where((iota((256, 128), 0) >> 1) == iota((256, 128), 1))

    def pair(x, carry):
        for at, ref in enumerate((res, coef)):
            f = ref[2 * x] + ref[2 * x + 1]
            for tile in range(2):
                place = pl.ds(pl.multiple_of(448 * at + 32 * x, 32), 32)
                pairs[tile, place, :] = f[:, 128 * tile : 128 * tile + 128]
        return carry

    lax.fori_loop(0, 14, pair, 0, unroll=2)
    sums = [pairs[tile, pl.ds(0, 448, stride=2), :] + pairs[tile, pl.ds(1, 448, stride=2), :] for tile in range(2)]
    sums = select_lanes(jnp.concatenate(sums, axis=1), halves).reshape(2, 14, 16, 128)
    corr_two = smooth_small(0.5 * sums[0], 0.125 * sums[1], 3)
    doubled = ones_where(iota((128, 128), 0) == (iota((128, 128), 1) >> 1))
    wide = select_lanes(corr_two[3:11].reshape(128, 128), doubled).reshape(8, 16, 128)
    rows = wide[:, 0:8, :].reshape(64, 128)
    spread[pl.ds(0, 64, stride=2), :] = rows
    spread[pl.ds(1, 64, stride=2), :] = rows

    def third(x, carry):
        c = relax(
            corr_next[x, 0:16, 0:128],
            inv[x, 0:16, 0:128],
            res[x, 0:16, 0:128],
            coef[x, 0:16, 0:128],
            (yz_c[x - 1, 0:16, 0:128] + yz_c[x + 1, 0:16, 0:128]) + 2.0 * yz_c[x, 0:16, 0:128],
            (yz_kc[x - 1, 0:16, 0:128] + yz_kc[x + 1, 0:16, 0:128]) + 2.0 * yz_kc[x, 0:16, 0:128],
        )
        block = x - 6
        base[block] = ext[1, x] + (c + spread[pl.ds(pl.multiple_of(16 * (block // 2), 16), 16), :])
        return carry

    lax.fori_loop(6, 22, third, 0, unroll=4)


def coarse_levels(tables, plane, base, out, columns, spread):
    lane = iota((plane.shape[0], 4, 128), 2)
    parts = [plane[:, part] for part in range(3)]
    for part in range(3):
        columns[:, 4 * part : 4 * part + 4, :] = parts[part]
    rest = [pltpu.roll(parts[part], 32 + 32 * part, 2) for part in range(3)]
    columns[:, 12:16, :] = jnp.where(lane < 32, rest[0], jnp.where(lane < 64, rest[1], rest[2]))
    columns = columns[...].reshape(plane.shape[0] * 16, 128)
    found = jnp.dot(tables[0:576, :], jnp.concatenate(split(columns), axis=1), preferred_element_type=F32)
    found = found[:, 0:128] + (found[:, 128:256] + found[:, 256:384])
    windows = jnp.concatenate([found[192 * level : 192 * level + 192, :] for level in range(3)], axis=1)
    both = select_lanes(windows, tables[576:960, 0:256])
    corr = smooth_small(both[:, 0:128].reshape(12, 16, 128), both[:, 128:256].reshape(12, 16, 128), 4)
    wide = select_lanes(corr[4:8].reshape(64, 128), tables[960:1088, 0:384])
    for x in range(4):
        level4 = wide[16 * (x // 2) : 16 * (x // 2) + 16, 128:256]
        level4 = jnp.concatenate([jnp.broadcast_to(level4[y : y + 1], (2, 128)) for y in (4, 5)], axis=0)
        rows = wide[16 * x + 4 : 16 * x + 8, 0:128] + (level4 + wide[4:5, 256:384])
        for y in range(4):
            spread[pl.ds(16 * x + y, 4, stride=4), :] = rows
    for x in range(16):
        start = 16 * (x // 4)
        out[x] = base[x] + spread[start : start + 16, :]


VMEM = pl.BlockSpec(memory_space=pltpu.VMEM)
HBM = pl.BlockSpec(memory_space=pltpu.HBM)


def call(kernel, outs, ins, scratch=(), first=VMEM, rest=VMEM, flops=1000000, grant=32):
    moved = 4 * sum(x.size for x in ins)
    return pl.pallas_call(
        kernel,
        out_shape=[out if isinstance(out, jax.ShapeDtypeStruct) else jax.ShapeDtypeStruct(out, F32) for out in outs],
        in_specs=[first] + [rest] * (len(ins) - 1),
        out_specs=[VMEM] * len(outs),
        scratch_shapes=[pltpu.VMEM(shape, F32) if isinstance(shape, tuple) else shape for shape in scratch],
        compiler_params=pltpu.CompilerParams(vmem_limit_bytes=grant * 1024 * 1024),
        cost_estimate=pl.CostEstimate(flops=flops, bytes_accessed=moved, transcendentals=0),
        name=kernel.__name__,
    )(*ins)


def neighbour_pairs(count):
    for start in (1, 0):
        lower = range(start, count - 1, 2)
        yield [(i, i + 1) for i in lower] + [(i + 1, i) for i in lower]


def swap(axis, to_up, to_down):
    count = lax.axis_size(axis)
    up = [(i, i + 1) for i in range(count - 1)]
    down = [(i + 1, i) for i in range(count - 1)]
    return lax.ppermute(to_up, axis, up), lax.ppermute(to_down, axis, down)


def on_device(right, iterate, phase, table):
    block = (16, 16, 128)
    fields, to_up, to_down = call(
        send_x,
        [(3, *block), (15, 16, 128), (15, 16, 128)],
        [table, phase, iterate, right],
        scratch=[pltpu.SMEM((4,), F32), pltpu.VMEM(block, jnp.int32), pltpu.SemaphoreType.DMA((4,))],
        first=HBM,
        rest=HBM,
        grant=60,
    )
    from_down, from_up = swap("gx", to_up, to_down)
    (held,) = call(hold, [(3, *block)], [fields], flops=30000000)
    from_down, from_up, fields = lax.optimization_barrier((from_down, from_up, held))
    ext, *sent = call(
        pack_y,
        [(3, 28, 16, 128), (28, 16, 128), (28, 16, 128)],
        [fields, from_down, from_up],
    )
    found = [lax.ppermute(rows, "gy", pairs) for rows, pairs in zip(sent, neighbour_pairs(lax.axis_size("gy")))]
    planes = (3, 28, 32, 128)
    mine = call(
        own_rows,
        [(16, 512), (16, 512), (3, *block), jax.ShapeDtypeStruct((256, 384), BF16)],
        [ext],
        flops=30000000,
    )
    *found, up_rows, down_rows, xz, level3_lanes = lax.optimization_barrier((*found, *mine))
    beyond, to_up, to_down, inner = call(
        pack_z,
        [(3, 28, 16, 128), (32, 512), (32, 512), (16, 128)],
        [ext, *found, up_rows, down_rows, xz, level3_lanes],
        scratch=[(6, 32, 128), (128, 128)],
    )
    from_down, from_up = swap("gz", to_up, to_down)
    xy, tables, end_lanes = call(
        bands_xy,
        [(3, 24, 32, 128), jax.ShapeDtypeStruct((1088, 512), BF16), jax.ShapeDtypeStruct((384, 128), BF16)],
        [ext, beyond],
        scratch=[planes],
        flops=30000000,
    )
    from_down, from_up, xy, tables, end_lanes = lax.optimization_barrier((from_down, from_up, xy, tables, end_lanes))
    z_sides = [from_down, from_up]
    count = lax.axis_size("gx") * lax.axis_size("gy")
    (chunks,) = call(own_cells, [(count, 3, 4, 128)], [to_up, to_down, *z_sides, inner, end_lanes], scratch=[(256, 128)])
    plane = lax.all_to_all(chunks, ("gx", "gy"), 0, 0, tiled=True)
    wide = (28, 32, 256)
    coef, res, inv = call(
        fine_residual,
        [wide] * 3,
        [ext, beyond, xy, *z_sides],
        scratch=[(2, 28, 32, 128), wide, (28, 32, 128)],
        flops=30000000,
    )
    (base,) = call(
        fine_sweeps,
        [block],
        [ext, coef, res, inv],
        scratch=[wide, wide, wide, wide, (2, 896, 128), (128, 128)],
        flops=60000000,
    )
    (out,) = call(coarse_levels, [block], [tables, plane, base], scratch=[(count, 16, 128), (64, 128)])
    return out


def solution(mesh):
    placed = (P("gx", "gy", "gz"), P("gx", "gy", "gz"), P("gx", "gy", "gz"), P())
    return jax.shard_map(on_device, mesh=mesh, in_specs=placed, out_specs=P("gx", "gy", "gz"), check_vma=False)
```

```python
import jax
import jax.numpy as jnp
from jax import lax
from jax.experimental import pallas as pl
from jax.experimental.pallas import tpu as pltpu
from jax.sharding import PartitionSpec as P

HALO = (6, 5, 4)
ROWS = (0, 6, 11, 15)
OMEGA = 2.0 / 3.0
F32 = jnp.float32
BF16 = jnp.bfloat16


def iota(shape, dim):
    return lax.broadcasted_iota(jnp.int32, shape, dim)


def ones_where(cond, scale=1.0):
    return jnp.where(cond, F32(scale), F32(0.0)).astype(BF16)


def split(x):
    high = x.astype(BF16)
    rest = x - high.astype(F32)
    middle = rest.astype(BF16)
    return high, middle, (rest - middle.astype(F32)).astype(BF16)


def select_rows(pattern, x):
    high, middle, low = [jnp.dot(pattern, part, preferred_element_type=F32) for part in split(x)]
    return high + (middle + low)


def select_lanes(x, pattern):
    high, middle, low = [jnp.dot(part, pattern, preferred_element_type=F32) for part in split(x)]
    return high + (middle + low)


def band_matrix(size):
    apart = jnp.abs(iota((size, size), 0) - iota((size, size), 1))
    return jnp.where(apart == 0, 2.0, jnp.where((apart == 1) | (apart == size - 1), 1.0, 0.0)).astype(BF16)


def band_z(fields, matrix):
    shape = fields[0].shape
    rows = fields[0].size // shape[-1]
    found = select_lanes(jnp.concatenate([f.reshape(rows, shape[-1]) for f in fields], axis=0), matrix)
    return [found[rows * at : rows * at + rows].reshape(shape) for at in range(len(fields))]


def band(x, axis):
    return (pltpu.roll(x, 1, axis) + pltpu.roll(x, x.shape[axis] - 1, axis)) + 2.0 * x


def damped_inverse(coef, diagonal):
    inside = coef > 0.0
    return jnp.where(inside, OMEGA / jnp.where(inside, diagonal, 1.0), 0.0)


def relax(corr, inverse, residual, coef, tu_corr, tu_product):
    return corr * (1.0 / 3.0) + inverse * (residual - 2.0 * (coef * corr) + 0.125 * (coef * tu_corr + tu_product))


def sum_x(x):
    return (x[:-2] + x[2:]) + 2.0 * x[1:-1]


def smooth_small(residual, coef, sweeps, first, last):
    low, high = first - sweeps + 1, last + sweeps - 1
    tu = band(band(sum_x(coef[low - 1 : high + 1]), 1), 2)
    coef = coef[low:high]
    residual = residual[low:high]
    inverse = damped_inverse(coef, 6.0 * coef + 0.125 * tu)
    corr = inverse * residual
    for _ in range(sweeps - 1):
        tu = [band(band(sum_x(f), 1), 2) for f in (corr, coef * corr)]
        corr, inverse, residual, coef = [f[1:-1] for f in (corr, inverse, residual, coef)]
        corr = relax(corr, inverse, residual, coef, *tu)
    return corr


def send_x(table, phase, iterate, right, fields, to_up, to_down, values, phases, sems):
    copies = [
        pltpu.make_async_copy(table, values, sems.at[0]),
        pltpu.make_async_copy(phase, phases, sems.at[1]),
        pltpu.make_async_copy(iterate, fields.at[1], sems.at[2]),
        pltpu.make_async_copy(right, fields.at[2], sems.at[3]),
    ]
    for copy in copies:
        copy.start()
    for copy in copies:
        copy.wait()
    p = phases[...]
    k = jnp.zeros(p.shape, F32)
    for index in range(4):
        k = jnp.where(p == index, values[index], k)
    fields[0] = k
    for field in range(3):
        h, a, b = HALO[field], ROWS[field], ROWS[field + 1]
        to_up[a:b] = fields[field, 16 - h : 16]
        to_down[a:b] = fields[field, 0:h]


def hold(fields, held):
    held[...] = fields[...]


def by_parity(body, first, second):
    odd = (lax.axis_index("gy") & 1) == 1

    @pl.when(odd)
    def _():
        body(second, first)

    @pl.when(jnp.logical_not(odd))
    def _():
        body(first, second)


def pack_y(fields, from_down, from_up, ext, to_first, to_second):
    for field in range(3):
        h, a, b = HALO[field], ROWS[field], ROWS[field + 1]
        if h < 6:
            ext[field, 0 : 6 - h] = jnp.zeros((6 - h, 16, 128), F32)
            ext[field, 22 + h : 28] = jnp.zeros((6 - h, 16, 128), F32)
        ext[field, 6 - h : 6] = from_down[a:b]
        ext[field, 6:22] = fields[field]
        ext[field, 22 : 22 + h] = from_up[a:b]

    def rows(to_down, to_up):
        for field in range(3):
            h, a, b = HALO[field], ROWS[field], ROWS[field + 1]
            to_up[:, a:b, :] = ext[field, :, 16 - h : 16, :]
            to_down[:, a:b, :] = ext[field, :, 0:h, :]

    by_parity(rows, to_first, to_second)
    to_first[:, 15:16, :] = jnp.zeros((28, 1, 128), F32)
    to_second[:, 15:16, :] = jnp.zeros((28, 1, 128), F32)


def sum_quads(quads, q, sums):
    for at, f in enumerate(sums):
        f = f + pltpu.roll(f, 15, 0)
        f = f + pltpu.roll(f, 14, 0)
        for tile in range(f.shape[1] // 128):
            start = 64 * (at * (f.shape[1] // 128) + tile) + 16 * q
            quads[pl.ds(pl.multiple_of(start, 16), 16), :] = f[:, 128 * tile : 128 * tile + 128]


def read_quads(quads):
    count = quads.shape[0] // 64
    return jnp.concatenate([quads[pl.ds(64 * at, 16, stride=4), :] for at in range(count)], axis=1)


def pack_lanes(cells_of, rows, to_up, to_down, at):
    lane = iota((rows, 128), 1)
    for group in range(4):
        up = jnp.zeros((rows, 128), F32)
        down = jnp.zeros((rows, 128), F32)
        for x in range(8 * group, min(8 * group + 8, 28)):
            first = 16 * (x - 8 * group)
            for field in range(3):
                h, a, b = HALO[field], ROWS[field], ROWS[field + 1]
                if not 6 - h <= x < 22 + h:
                    continue
                cells = cells_of(field, x)
                mine = (lane >= first + a) & (lane < first + b)
                up = jnp.where(mine, pltpu.roll(cells, (first + a + h) % 128, 1), up)
                down = jnp.where(mine, rolled(cells, first + a), down)
        to_up[at : at + rows, 128 * group : 128 * group + 128] = up
        to_down[at : at + rows, 128 * group : 128 * group + 128] = down


def own_rows(ext, up, down, xz, level3_lanes):
    pack_lanes(lambda field, x: ext[field, x], 16, up, down, 0)
    matrix = band_matrix(128)

    def bands(step, carry):
        xs = [6 + 4 * step + j for j in range(4)]
        wanted = []
        for x in xs:
            around = [(ext[0, x + d], ext[1, x + d]) for d in (-1, 0, 1)]
            for low, here, high in zip(*[(k, v, k * v) for k, v in around]):
                wanted.append((low + high) + 2.0 * here)
        for at, f in enumerate(band_z(wanted, matrix)):
            xz[at % 3, xs[at // 3] - 6] = f
        return carry

    lax.fori_loop(0, 4, bands, 0)
    source = iota((256, 128), 0)
    lane = iota((256, 128), 1)
    coarse = (source & 127) >> 2
    is_coef = source >> 7
    scale = jnp.where(source < 128, F32(0.25), F32(1.0 / 64.0))
    upper = jnp.where(coarse >= 28, coarse - 28, jnp.where(coarse >= 24, (coarse >> 1) - 9, (coarse >> 2) + 1))
    lower = jnp.where(coarse <= 3, coarse - 1, jnp.where(coarse <= 7, (coarse >> 1) + 1, (coarse >> 2) + 3))
    found = (
        (lane == 64 + 16 * is_coef + upper) & (coarse >= 16) & (coarse <= 30),
        (lane == 64 + 16 * is_coef + lower) & (coarse >= 1) & (coarse <= 15),
        (lane == 40 * is_coef + 4 + coarse) & (coarse >= 1) & (coarse <= 30),
    )
    for at, here in enumerate(found):
        level3_lanes[:, 128 * at : 128 * at + 128] = jnp.where(here, scale, 0.0).astype(BF16)


def pack_z(ext, from_first, from_second, up_rows, down_rows, xz, level3_lanes, beyond, to_up, to_down, inner, edges, quads):
    edges[:, 24:32, :] = jnp.zeros((6, 8, 128), F32)
    for field in range(3):
        h = HALO[field]
        beyond[field, :, h : 16 - h, :] = jnp.zeros((28, 16 - 2 * h, 128), F32)

    def rows(from_down, from_up):
        for field in range(3):
            h, a, b = HALO[field], ROWS[field], ROWS[field + 1]
            beyond[field, :, 0:h, :] = from_up[:, a:b, :]
            beyond[field, :, 16 - h : 16, :] = from_down[:, a:b, :]
        for at, (source, row_k, row_v) in enumerate(((from_down, 5, 10), (from_up, 0, 6))):
            k = source[:, row_k, :]
            v = source[:, row_v, :]
            for number, f in enumerate((k, v, k * v)):
                edges[3 * at + number, 0:28, :] = f

    by_parity(rows, from_first, from_second)
    for at in range(6):
        edges[at] = band(band(edges[at], 0), 1)
    row = iota((16, 128), 0)

    def quad(q, carry):
        sums = [None, None]
        for j in range(4):
            x = 6 + 4 * q + j
            tu = []
            for at in range(3):
                f = xz[at, 4 * q + j]
                below = jnp.where(row == 0, edges[at, pl.ds(x, 1), :], pltpu.roll(f, 1, 0))
                above = jnp.where(row == 15, edges[3 + at, pl.ds(x, 1), :], pltpu.roll(f, 15, 0))
                tu.append((below + above) + 2.0 * f)
            k = ext[0, x]
            v = ext[1, x]
            diagonal = 6.0 * k + 0.125 * tu[0]
            res = ext[2, x] - (v * diagonal + 2.0 * (k * v) - 0.125 * (k * tu[1] + tu[2]))
            sums = [f if j == 0 else total + f for total, f in zip(sums, (res, k))]
        sum_quads(quads, q, sums)
        return carry

    lax.fori_loop(0, 4, quad, 0)
    level3 = select_lanes(read_quads(quads), level3_lanes[...])
    inner[...] = level3[:, 256:384]
    to_up[0:16, :] = up_rows[...]
    to_down[0:16, :] = down_rows[...]
    pack_lanes(lambda field, x: beyond[field, x], 16, to_up, to_down, 16)
    to_up[0:16, 384:512] += level3[:, 0:128]
    to_down[0:16, 384:512] += level3[:, 128:256]


def rolled(x, shift):
    shift = shift % x.shape[1]
    return pltpu.roll(x, shift, 1) if shift else x


def all_rows(ext, beyond, field, x):
    return jnp.concatenate([ext[field, x], beyond[field, x]], axis=0)


def bands_xy(ext, beyond, xy, tables, end_lanes, bands):
    row = iota((192, 512), 0)
    cell = iota((192, 512), 1)
    cell_x = (cell >> 6) * 4 + ((cell >> 2) & 3)
    cell_y = ((cell >> 4) & 3) * 4 + (cell & 3)
    for level in range(3):
        at_x = lax.axis_index("gx") * (4 >> level) - 4 + (row >> 4)
        at_y = lax.axis_index("gy") * (4 >> level) - 4 + (row & 15)
        found = ((cell_x >> level) == at_x) & ((cell_y >> level) == at_y)
        tables[192 * level : 192 * level + 192, :] = ones_where(found)
    source = iota((128, 256), 0)
    lane = iota((128, 256), 1)
    is_coef = jnp.where(source < 80, jnp.where(source >= 40, 1, 0), jnp.where(source >= 88, 1, 0))
    cell = jnp.where(source < 80, source - 40 * is_coef - 4, source - 80 - 8 * is_coef)
    inner = source < 80
    pairs = (source >= 80) & (source < 96) & (cell < 4)
    fours = (source >= 80) & (source < 96) & (cell >= 4)
    pair = jnp.where(cell < 2, cell - 4, cell + 16)
    four = jnp.where(cell < 6, cell - 8, cell + 4)
    targets = (
        jnp.where(inner, cell + 16, -1),
        jnp.where(inner, 64 + 8 + (cell >> 1), jnp.where(pairs, 64 + 8 + pair, -1)),
        jnp.where(inner, 96 + 4 + (cell >> 2), jnp.where(pairs, 96 + 4 + (pair >> 1), jnp.where(fours, 96 + 4 + four, -1))),
    )
    for level, target in enumerate(targets):
        scale = jnp.where(is_coef == 1, F32(0.125**level), F32(0.5**level))
        found = (target >= 0) & (lane == is_coef * 128 + target)
        at = 576 + 128 * level
        tables[at : at + 128, 0:256] = jnp.where(found, scale, 0.0).astype(BF16)
    source = iota((128, 128), 0)
    lane = iota((128, 128), 1)
    for level, start in enumerate((16, 72, 100)):
        found = source == start + (lane >> (level + 2))
        tables[960:1088, 128 * level : 128 * level + 128] = ones_where(found)

    source = iota((384, 128), 0)
    x = (source >> 4) - 6
    z = (source & 15) - 2
    place = (x >= 0) & (x < 16) & (z >= 0) & (z < 8) & (iota((384, 128), 1) == (x >> 2) * 32 + (z >> 2))
    end_lanes[...] = ones_where(place)

    def in_y(x, carry):
        k, v = [all_rows(ext, beyond, field, x) for field in range(2)]
        bands[0, x] = band(k, 0)
        bands[1, x] = band(v, 0)
        bands[2, x] = band(k * v, 0)
        return carry

    lax.fori_loop(0, 28, in_y, 0, unroll=2)

    def in_x(x, carry):
        for field in range(3):
            xy[field, x - 2] = (bands[field, x - 1] + bands[field, x + 1]) + 2.0 * bands[field, x]
        return carry

    lax.fori_loop(2, 26, in_x, 0, unroll=2)


def end_cells(lower_k, lower_v, lower_right, upper_k, upper_v, upper_right):
    position = iota((32, 384), 1) & 15
    k = jnp.where(position < 6, lower_k, jnp.where(position < 12, upper_k, 0.0))
    v = jnp.where(position < 6, lower_v, upper_v)
    right = jnp.where(position < 6, lower_right, upper_right)[0:16, :]
    tu = []
    for f in (k, v, k * v):
        f = band(f, 0)[0:16, :]
        f = f + pltpu.roll(f, 16, 1)
        tu.append(band(f + pltpu.roll(f, 384 - 16, 1), 1))
    k, v = k[0:16, :], v[0:16, :]
    diagonal = 6.0 * k + 0.125 * tu[0]
    return right - (v * diagonal + 2.0 * (k * v) - 0.125 * (k * tu[1] + tu[2])), k


def own_cells(sent_up, sent_down, from_down, from_up, inner, end_lanes, chunks, quads):
    def moved(f, shift):
        return pltpu.roll(f, shift % 384, 1)

    low, first, last, high = [ref[:, 0:384] for ref in (from_down, sent_down, sent_up, from_up)]
    found = [
        end_cells(low, moved(low, -5), moved(low, -9), moved(first, 6), first, moved(first, -5)),
        end_cells(last, moved(last, -5), moved(last, -9), moved(high, 6), high, moved(high, -5)),
    ]
    rows = []
    for f in (found[0][0], found[1][0], found[0][1], found[1][1]):
        f = f + pltpu.roll(f, 15, 0)
        rows.append(f + pltpu.roll(f, 14, 0))
    ends = select_lanes(jnp.concatenate(rows, axis=0), end_lanes[...])
    ends = [0.25 * ends[0:16], 0.25 * ends[16:32], ends[32:48] / 64.0, ends[48:64] / 64.0]
    for q in range(4):
        for at in range(4):
            start = 64 * at + 16 * q
            quads[start : start + 16, :] = rolled(ends[at], -32 * q)
    lane = iota((16, 128), 1)
    mine = inner[...]
    for at, target in enumerate((3, 35, 43, 75)):
        cells = pltpu.roll(quads[pl.ds(64 * at, 16, stride=4), :], target, 1)
        mine = jnp.where((lane == target) | (lane == target + 1), cells, mine)
    low = from_down[0:16, 384:512]
    high = from_up[0:16, 384:512]
    for cells, moves in (
        (low, ((64, 0, 3), (67, 80, 2), (69, 84, 2), (80, 40, 3), (83, 88, 2), (85, 92, 2))),
        (high, ((64, 37, 3), (67, 82, 2), (69, 86, 2), (80, 77, 3), (83, 90, 2), (85, 94, 2))),
    ):
        for at, target, count in moves:
            mine = jnp.where((lane >= target) & (lane < target + count), rolled(cells, target - at), mine)
    lane = iota((4, 128), 1)
    for part in range(3):
        rest = rolled(mine, 96 - 32 * part)[12:16]
        tile = jnp.where(lane < 96, mine[4 * part : 4 * part + 4], rest)
        chunks[:, part] = jnp.broadcast_to(tile[None], (chunks.shape[0], 4, 128))


def fine_residual(ext, beyond, xy, from_down, from_up, coef, res, inv, side, sides_kv, product):
    lane = iota((32, 128), 1)

    for x in range(28):
        group, first = 128 * (x // 8), 16 * (x % 8)
        up = from_up[:, group : group + 128]
        down = from_down[:, group : group + 128]
        tiles = []
        for field in range(3):
            h, a = HALO[field], ROWS[field]
            tile = jnp.where(lane >= 128 - h, rolled(down, 128 - h - first - a), 0.0)
            tiles.append(jnp.where(lane < h, rolled(up, -first - a), tile))
        coef[x, :, 0:128] = all_rows(ext, beyond, 0, x)
        coef[x, :, 128:256] = tiles[0]
        side[0, x] = tiles[1]
        side[1, x] = tiles[2]
        sides_kv[x, :, 0:128] = band(tiles[0], 0)
        sides_kv[x, :, 128:256] = band(tiles[1], 0)
        product[x] = band(tiles[0] * tiles[1], 0)

    for x in (0, 1, 26, 27):
        res[x] = jnp.zeros((32, 256), F32)

    def over_x(ref, x):
        return (ref[x - 1] + ref[x + 1]) + 2.0 * ref[x]

    matrix = band_matrix(256)

    def cells(step, carry):
        xs = [2 + 8 * step + j for j in range(8)]
        wanted = []
        for x in xs:
            sides = over_x(sides_kv, x)
            wanted += [
                jnp.concatenate([xy[0, x - 2], sides[:, 0:128]], axis=1),
                jnp.concatenate([xy[1, x - 2], sides[:, 128:256]], axis=1),
                jnp.concatenate([xy[2, x - 2], over_x(product, x)], axis=1),
            ]
        found = band_z(wanted, matrix)
        for j, x in enumerate(xs):
            tu_k, tu_v, tu_kv = found[3 * j : 3 * j + 3]
            k = coef[x]
            v = jnp.concatenate([all_rows(ext, beyond, 1, x), side[0, x]], axis=1)
            diagonal = 6.0 * k + 0.125 * tu_k
            applied = v * diagonal + 2.0 * (k * v) - 0.125 * (k * tu_v + tu_kv)
            res[x] = jnp.concatenate([all_rows(ext, beyond, 2, x), side[1, x]], axis=1) - applied
            inv[x] = damped_inverse(k, diagonal)
        return carry

    lax.fori_loop(0, 3, cells, 0)


def fine_sweeps(ext, coef, res, inv, base, corr, corr_next, yz_c, yz_kc, pairs, spread):
    def over_x(ref, x):
        return (ref[x - 1] + ref[x + 1]) + 2.0 * ref[x]

    def bands_of(xs, ref):
        wanted = []
        for x in xs:
            c = ref[x]
            wanted += [band(c, 0), band(coef[x] * c, 0)]
        found = [band(f, 1) for f in wanted]
        for j, x in enumerate(xs):
            yz_c[x] = found[2 * j]
            yz_kc[x] = found[2 * j + 1]

    def first_sweep(step, carry):
        xs = [4 + 4 * step + j for j in range(4)]
        for x in xs:
            corr[x] = inv[x] * res[x]
        bands_of(xs, corr)
        return carry

    lax.fori_loop(0, 5, first_sweep, 0)

    def second(x, carry):
        corr_next[x] = relax(corr[x], inv[x], res[x], coef[x], over_x(yz_c, x), over_x(yz_kc, x))
        return carry

    lax.fori_loop(5, 23, second, 0, unroll=3)

    def second_bands(step, carry):
        bands_of([5 + 3 * step + j for j in range(3)], corr_next)
        return carry

    lax.fori_loop(0, 6, second_bands, 0)

    halves = ones_where((iota((256, 128), 0) >> 1) == iota((256, 128), 1))

    def pair(x, carry):
        for at, ref in enumerate((res, coef)):
            f = ref[2 * x] + ref[2 * x + 1]
            for tile in range(2):
                place = pl.ds(pl.multiple_of(448 * at + 32 * x, 32), 32)
                pairs[tile, place, :] = f[:, 128 * tile : 128 * tile + 128]
        return carry

    lax.fori_loop(0, 14, pair, 0, unroll=2)
    sums = [pairs[tile, pl.ds(0, 448, stride=2), :] + pairs[tile, pl.ds(1, 448, stride=2), :] for tile in range(2)]
    sums = select_lanes(jnp.concatenate(sums, axis=1), halves).reshape(2, 14, 16, 128)
    corr_two = smooth_small(0.5 * sums[0], 0.125 * sums[1], 3, 3, 11)
    doubled = ones_where(iota((128, 128), 0) == (iota((128, 128), 1) >> 1))
    wide = select_lanes(corr_two.reshape(128, 128), doubled).reshape(8, 16, 128)
    rows = wide[:, 0:8, :].reshape(64, 128)
    spread[pl.ds(0, 64, stride=2), :] = rows
    spread[pl.ds(1, 64, stride=2), :] = rows

    def third(x, carry):
        c = relax(
            corr_next[x, 0:16, 0:128],
            inv[x, 0:16, 0:128],
            res[x, 0:16, 0:128],
            coef[x, 0:16, 0:128],
            (yz_c[x - 1, 0:16, 0:128] + yz_c[x + 1, 0:16, 0:128]) + 2.0 * yz_c[x, 0:16, 0:128],
            (yz_kc[x - 1, 0:16, 0:128] + yz_kc[x + 1, 0:16, 0:128]) + 2.0 * yz_kc[x, 0:16, 0:128],
        )
        block = x - 6
        base[block] = ext[1, x] + (c + spread[pl.ds(pl.multiple_of(16 * (block // 2), 16), 16), :])
        return carry

    lax.fori_loop(6, 22, third, 0, unroll=4)


def coarse_levels(tables, plane, base, out, columns, spread):
    lane = iota((plane.shape[0], 4, 128), 2)
    parts = [plane[:, part] for part in range(3)]
    for part in range(3):
        columns[:, 4 * part : 4 * part + 4, :] = parts[part]
    rest = [pltpu.roll(parts[part], 32 + 32 * part, 2) for part in range(3)]
    columns[:, 12:16, :] = jnp.where(lane < 32, rest[0], jnp.where(lane < 64, rest[1], rest[2]))
    columns = columns[...].reshape(plane.shape[0] * 16, 128)
    found = jnp.dot(tables[0:576, :], jnp.concatenate(split(columns), axis=1), preferred_element_type=F32)
    found = found[:, 0:128] + (found[:, 128:256] + found[:, 256:384])
    windows = jnp.concatenate([found[192 * level : 192 * level + 192, :] for level in range(3)], axis=1)
    both = select_lanes(windows, tables[576:960, 0:256])
    corr = smooth_small(both[:, 0:128].reshape(12, 16, 128), both[:, 128:256].reshape(12, 16, 128), 4, 4, 8)
    wide = select_lanes(corr.reshape(64, 128), tables[960:1088, 0:384])
    for x in range(4):
        level4 = wide[16 * (x // 2) : 16 * (x // 2) + 16, 128:256]
        level4 = jnp.concatenate([jnp.broadcast_to(level4[y : y + 1], (2, 128)) for y in (4, 5)], axis=0)
        rows = wide[16 * x + 4 : 16 * x + 8, 0:128] + (level4 + wide[4:5, 256:384])
        for y in range(4):
            spread[pl.ds(16 * x + y, 4, stride=4), :] = rows
    for x in range(16):
        start = 16 * (x // 4)
        out[x] = base[x] + spread[start : start + 16, :]


VMEM = pl.BlockSpec(memory_space=pltpu.VMEM)
HBM = pl.BlockSpec(memory_space=pltpu.HBM)


def call(kernel, outs, ins, scratch=(), first=VMEM, rest=VMEM, flops=1000000, grant=32):
    moved = 4 * sum(x.size for x in ins)
    return pl.pallas_call(
        kernel,
        out_shape=[out if isinstance(out, jax.ShapeDtypeStruct) else jax.ShapeDtypeStruct(out, F32) for out in outs],
        in_specs=[first] + [rest] * (len(ins) - 1),
        out_specs=[VMEM] * len(outs),
        scratch_shapes=[pltpu.VMEM(shape, F32) if isinstance(shape, tuple) else shape for shape in scratch],
        compiler_params=pltpu.CompilerParams(vmem_limit_bytes=grant * 1024 * 1024),
        cost_estimate=pl.CostEstimate(flops=flops, bytes_accessed=moved, transcendentals=0),
        name=kernel.__name__,
    )(*ins)


def neighbour_pairs(count):
    for start in (1, 0):
        lower = range(start, count - 1, 2)
        yield [(i, i + 1) for i in lower] + [(i + 1, i) for i in lower]


def swap(axis, to_up, to_down):
    count = lax.axis_size(axis)
    up = [(i, i + 1) for i in range(count - 1)]
    down = [(i + 1, i) for i in range(count - 1)]
    return lax.ppermute(to_up, axis, up), lax.ppermute(to_down, axis, down)


def on_device(right, iterate, phase, table):
    block = (16, 16, 128)
    fields, to_up, to_down = call(
        send_x,
        [(3, *block), (15, 16, 128), (15, 16, 128)],
        [table, phase, iterate, right],
        scratch=[pltpu.SMEM((4,), F32), pltpu.VMEM(block, jnp.int32), pltpu.SemaphoreType.DMA((4,))],
        first=HBM,
        rest=HBM,
        grant=60,
    )
    from_down, from_up = swap("gx", to_up, to_down)
    (held,) = call(hold, [(3, *block)], [fields], flops=30000000)
    from_down, from_up, fields = lax.optimization_barrier((from_down, from_up, held))
    ext, *sent = call(
        pack_y,
        [(3, 28, 16, 128), (28, 16, 128), (28, 16, 128)],
        [fields, from_down, from_up],
    )
    found = [lax.ppermute(rows, "gy", pairs) for rows, pairs in zip(sent, neighbour_pairs(lax.axis_size("gy")))]
    planes = (3, 28, 32, 128)
    mine = call(
        own_rows,
        [(16, 512), (16, 512), (3, *block), jax.ShapeDtypeStruct((256, 384), BF16)],
        [ext],
        flops=30000000,
    )
    *found, up_rows, down_rows, xz, level3_lanes = lax.optimization_barrier((*found, *mine))
    beyond, to_up, to_down, inner = call(
        pack_z,
        [(3, 28, 16, 128), (32, 512), (32, 512), (16, 128)],
        [ext, *found, up_rows, down_rows, xz, level3_lanes],
        scratch=[(6, 32, 128), (128, 128)],
    )
    from_down, from_up = swap("gz", to_up, to_down)
    xy, tables, end_lanes = call(
        bands_xy,
        [(3, 24, 32, 128), jax.ShapeDtypeStruct((1088, 512), BF16), jax.ShapeDtypeStruct((384, 128), BF16)],
        [ext, beyond],
        scratch=[planes],
        flops=30000000,
    )
    from_down, from_up, xy, tables, end_lanes = lax.optimization_barrier((from_down, from_up, xy, tables, end_lanes))
    z_sides = [from_down, from_up]
    count = lax.axis_size("gx") * lax.axis_size("gy")
    (chunks,) = call(own_cells, [(count, 3, 4, 128)], [to_up, to_down, *z_sides, inner, end_lanes], scratch=[(256, 128)])
    plane = lax.all_to_all(chunks, ("gx", "gy"), 0, 0, tiled=True)
    wide = (28, 32, 256)
    coef, res, inv = call(
        fine_residual,
        [wide] * 3,
        [ext, beyond, xy, *z_sides],
        scratch=[(2, 28, 32, 128), wide, (28, 32, 128)],
        flops=30000000,
    )
    (base,) = call(
        fine_sweeps,
        [block],
        [ext, coef, res, inv],
        scratch=[wide, wide, wide, wide, (2, 896, 128), (128, 128)],
        flops=60000000,
    )
    (out,) = call(coarse_levels, [block], [tables, plane, base], scratch=[(count, 16, 128), (64, 128)])
    return out


def solution(mesh):
    placed = (P("gx", "gy", "gz"), P("gx", "gy", "gz"), P("gx", "gy", "gz"), P())
    return jax.shard_map(on_device, mesh=mesh, in_specs=placed, out_specs=P("gx", "gy", "gz"), check_vma=False)
```

```python
import jax
import jax.numpy as jnp
from jax import lax
from jax.experimental import pallas as pl
from jax.experimental.pallas import tpu as pltpu
from jax.sharding import PartitionSpec as P

HALO = (6, 5, 4)
ROWS = (0, 6, 11, 15)
OMEGA = 2.0 / 3.0
F32 = jnp.float32
BF16 = jnp.bfloat16


def iota(shape, dim):
    return lax.broadcasted_iota(jnp.int32, shape, dim)


def ones_where(cond, scale=1.0):
    return jnp.where(cond, F32(scale), F32(0.0)).astype(BF16)


def split(x):
    high = x.astype(BF16)
    rest = x - high.astype(F32)
    middle = rest.astype(BF16)
    return high, middle, (rest - middle.astype(F32)).astype(BF16)


def select_rows(pattern, x):
    high, middle, low = [jnp.dot(pattern, part, preferred_element_type=F32) for part in split(x)]
    return high + (middle + low)


def select_lanes(x, pattern):
    high, middle, low = [jnp.dot(part, pattern, preferred_element_type=F32) for part in split(x)]
    return high + (middle + low)


def band_matrix(size):
    apart = jnp.abs(iota((size, size), 0) - iota((size, size), 1))
    return jnp.where(apart == 0, 2.0, jnp.where((apart == 1) | (apart == size - 1), 1.0, 0.0)).astype(BF16)


def band_z(fields, matrix):
    shape = fields[0].shape
    rows = fields[0].size // shape[-1]
    found = select_lanes(jnp.concatenate([f.reshape(rows, shape[-1]) for f in fields], axis=0), matrix)
    return [found[rows * at : rows * at + rows].reshape(shape) for at in range(len(fields))]


def band(x, axis):
    return (pltpu.roll(x, 1, axis) + pltpu.roll(x, x.shape[axis] - 1, axis)) + 2.0 * x


def damped_inverse(coef, diagonal):
    inside = coef > 0.0
    return jnp.where(inside, OMEGA / jnp.where(inside, diagonal, 1.0), 0.0)


def relax(corr, inverse, residual, coef, tu_corr, tu_product):
    return corr * (1.0 / 3.0) + inverse * (residual - 2.0 * (coef * corr) + 0.125 * (coef * tu_corr + tu_product))


def sum_x(x):
    return (x[:-2] + x[2:]) + 2.0 * x[1:-1]


def smooth_small(residual, coef, sweeps, first, last):
    low, high = first - sweeps + 1, last + sweeps - 1
    tu = band(band(sum_x(coef[low - 1 : high + 1]), 1), 2)
    coef = coef[low:high]
    residual = residual[low:high]
    inverse = damped_inverse(coef, 6.0 * coef + 0.125 * tu)
    corr = inverse * residual
    for _ in range(sweeps - 1):
        tu = [band(band(sum_x(f), 1), 2) for f in (corr, coef * corr)]
        corr, inverse, residual, coef = [f[1:-1] for f in (corr, inverse, residual, coef)]
        corr = relax(corr, inverse, residual, coef, *tu)
    return corr


def lookup(phase, values):
    k = jnp.zeros(phase.shape, F32)
    for index in range(4):
        k = jnp.where(phase == index, values[index], k)
    return k


def fetch(pairs, sems):
    copies = [pltpu.make_async_copy(source, target, sems.at[at]) for at, (source, target) in enumerate(pairs)]
    for copy in copies:
        copy.start()
    for copy in copies:
        copy.wait()


def send_x(table, phase, iterate, right, to_up, to_down, values, upper, lower, sems):
    fetch(
        [
            (table, values),
            (phase.at[10:16], upper),
            (phase.at[0:6], lower),
            (iterate.at[11:16], to_up.at[6:11]),
            (iterate.at[0:5], to_down.at[6:11]),
            (right.at[12:16], to_up.at[11:15]),
            (right.at[0:4], to_down.at[11:15]),
        ],
        sems,
    )
    to_up[0:6] = lookup(upper[...], values)
    to_down[0:6] = lookup(lower[...], values)


def hold(table, phase, iterate, right, fields, values, phases, sems):
    fetch([(table, values), (phase, phases), (iterate, fields.at[1]), (right, fields.at[2])], sems)
    fields[0] = lookup(phases[...], values)


def by_parity(body, first, second):
    odd = (lax.axis_index("gy") & 1) == 1

    @pl.when(odd)
    def _():
        body(second, first)

    @pl.when(jnp.logical_not(odd))
    def _():
        body(first, second)


def pack_y(fields, from_down, from_up, ext, to_first, to_second):
    for field in range(3):
        h, a, b = HALO[field], ROWS[field], ROWS[field + 1]
        if h < 6:
            ext[field, 0 : 6 - h] = jnp.zeros((6 - h, 16, 128), F32)
            ext[field, 22 + h : 28] = jnp.zeros((6 - h, 16, 128), F32)
        ext[field, 6 - h : 6] = from_down[a:b]
        ext[field, 6:22] = fields[field]
        ext[field, 22 : 22 + h] = from_up[a:b]

    def rows(to_down, to_up):
        for field in range(3):
            h, a, b = HALO[field], ROWS[field], ROWS[field + 1]
            to_up[:, a:b, :] = ext[field, :, 16 - h : 16, :]
            to_down[:, a:b, :] = ext[field, :, 0:h, :]

    by_parity(rows, to_first, to_second)
    to_first[:, 15:16, :] = jnp.zeros((28, 1, 128), F32)
    to_second[:, 15:16, :] = jnp.zeros((28, 1, 128), F32)


def sum_quads(quads, q, sums):
    for at, f in enumerate(sums):
        f = f + pltpu.roll(f, 15, 0)
        f = f + pltpu.roll(f, 14, 0)
        for tile in range(f.shape[1] // 128):
            start = 64 * (at * (f.shape[1] // 128) + tile) + 16 * q
            quads[pl.ds(pl.multiple_of(start, 16), 16), :] = f[:, 128 * tile : 128 * tile + 128]


def read_quads(quads):
    count = quads.shape[0] // 64
    return jnp.concatenate([quads[pl.ds(64 * at, 16, stride=4), :] for at in range(count)], axis=1)


def pack_lanes(cells_of, rows, to_up, to_down, at):
    lane = iota((rows, 128), 1)
    for group in range(4):
        up = jnp.zeros((rows, 128), F32)
        down = jnp.zeros((rows, 128), F32)
        for x in range(8 * group, min(8 * group + 8, 28)):
            first = 16 * (x - 8 * group)
            for field in range(3):
                h, a, b = HALO[field], ROWS[field], ROWS[field + 1]
                if not 6 - h <= x < 22 + h:
                    continue
                cells = cells_of(field, x)
                mine = (lane >= first + a) & (lane < first + b)
                up = jnp.where(mine, pltpu.roll(cells, (first + a + h) % 128, 1), up)
                down = jnp.where(mine, rolled(cells, first + a), down)
        to_up[at : at + rows, 128 * group : 128 * group + 128] = up
        to_down[at : at + rows, 128 * group : 128 * group + 128] = down


def own_rows(ext, up, down, xz, level3_lanes):
    pack_lanes(lambda field, x: ext[field, x], 16, up, down, 0)
    matrix = band_matrix(128)

    def bands(step, carry):
        xs = [6 + 4 * step + j for j in range(4)]
        wanted = []
        for x in xs:
            around = [(ext[0, x + d], ext[1, x + d]) for d in (-1, 0, 1)]
            for low, here, high in zip(*[(k, v, k * v) for k, v in around]):
                wanted.append((low + high) + 2.0 * here)
        for at, f in enumerate(band_z(wanted, matrix)):
            xz[at % 3, xs[at // 3] - 6] = f
        return carry

    lax.fori_loop(0, 4, bands, 0)
    source = iota((256, 128), 0)
    lane = iota((256, 128), 1)
    coarse = (source & 127) >> 2
    is_coef = source >> 7
    scale = jnp.where(source < 128, F32(0.25), F32(1.0 / 64.0))
    upper = jnp.where(coarse >= 28, coarse - 28, jnp.where(coarse >= 24, (coarse >> 1) - 9, (coarse >> 2) + 1))
    lower = jnp.where(coarse <= 3, coarse - 1, jnp.where(coarse <= 7, (coarse >> 1) + 1, (coarse >> 2) + 3))
    found = (
        (lane == 64 + 16 * is_coef + upper) & (coarse >= 16) & (coarse <= 30),
        (lane == 64 + 16 * is_coef + lower) & (coarse >= 1) & (coarse <= 15),
        (lane == 40 * is_coef + 4 + coarse) & (coarse >= 1) & (coarse <= 30),
    )
    for at, here in enumerate(found):
        level3_lanes[:, 128 * at : 128 * at + 128] = jnp.where(here, scale, 0.0).astype(BF16)


def pack_z(ext, from_first, from_second, up_rows, down_rows, xz, level3_lanes, beyond, to_up, to_down, inner, edges, quads):
    edges[:, 24:32, :] = jnp.zeros((6, 8, 128), F32)
    for field in range(3):
        h = HALO[field]
        beyond[field, :, h : 16 - h, :] = jnp.zeros((28, 16 - 2 * h, 128), F32)

    def rows(from_down, from_up):
        for field in range(3):
            h, a, b = HALO[field], ROWS[field], ROWS[field + 1]
            beyond[field, :, 0:h, :] = from_up[:, a:b, :]
            beyond[field, :, 16 - h : 16, :] = from_down[:, a:b, :]
        for at, (source, row_k, row_v) in enumerate(((from_down, 5, 10), (from_up, 0, 6))):
            k = source[:, row_k, :]
            v = source[:, row_v, :]
            for number, f in enumerate((k, v, k * v)):
                edges[3 * at + number, 0:28, :] = f

    by_parity(rows, from_first, from_second)
    for at in range(6):
        edges[at] = band(band(edges[at], 0), 1)
    row = iota((16, 128), 0)

    def quad(q, carry):
        sums = [None, None]
        for j in range(4):
            x = 6 + 4 * q + j
            tu = []
            for at in range(3):
                f = xz[at, 4 * q + j]
                below = jnp.where(row == 0, edges[at, pl.ds(x, 1), :], pltpu.roll(f, 1, 0))
                above = jnp.where(row == 15, edges[3 + at, pl.ds(x, 1), :], pltpu.roll(f, 15, 0))
                tu.append((below + above) + 2.0 * f)
            k = ext[0, x]
            v = ext[1, x]
            diagonal = 6.0 * k + 0.125 * tu[0]
            res = ext[2, x] - (v * diagonal + 2.0 * (k * v) - 0.125 * (k * tu[1] + tu[2]))
            sums = [f if j == 0 else total + f for total, f in zip(sums, (res, k))]
        sum_quads(quads, q, sums)
        return carry

    lax.fori_loop(0, 4, quad, 0)
    level3 = select_lanes(read_quads(quads), level3_lanes[...])
    inner[...] = level3[:, 256:384]
    to_up[0:16, :] = up_rows[...]
    to_down[0:16, :] = down_rows[...]
    pack_lanes(lambda field, x: beyond[field, x], 16, to_up, to_down, 16)
    to_up[0:16, 384:512] += level3[:, 0:128]
    to_down[0:16, 384:512] += level3[:, 128:256]


def rolled(x, shift):
    shift = shift % x.shape[1]
    return pltpu.roll(x, shift, 1) if shift else x


def all_rows(ext, beyond, field, x):
    return jnp.concatenate([ext[field, x], beyond[field, x]], axis=0)


def bands_xy(ext, beyond, xy, tables, end_lanes, bands):
    row = iota((192, 512), 0)
    cell = iota((192, 512), 1)
    cell_x = (cell >> 6) * 4 + ((cell >> 2) & 3)
    cell_y = ((cell >> 4) & 3) * 4 + (cell & 3)
    for level in range(3):
        at_x = lax.axis_index("gx") * (4 >> level) - 4 + (row >> 4)
        at_y = lax.axis_index("gy") * (4 >> level) - 4 + (row & 15)
        found = ((cell_x >> level) == at_x) & ((cell_y >> level) == at_y)
        tables[192 * level : 192 * level + 192, :] = ones_where(found)
    source = iota((128, 256), 0)
    lane = iota((128, 256), 1)
    is_coef = jnp.where(source < 80, jnp.where(source >= 40, 1, 0), jnp.where(source >= 88, 1, 0))
    cell = jnp.where(source < 80, source - 40 * is_coef - 4, source - 80 - 8 * is_coef)
    inner = source < 80
    pairs = (source >= 80) & (source < 96) & (cell < 4)
    fours = (source >= 80) & (source < 96) & (cell >= 4)
    pair = jnp.where(cell < 2, cell - 4, cell + 16)
    four = jnp.where(cell < 6, cell - 8, cell + 4)
    targets = (
        jnp.where(inner, cell + 16, -1),
        jnp.where(inner, 64 + 8 + (cell >> 1), jnp.where(pairs, 64 + 8 + pair, -1)),
        jnp.where(inner, 96 + 4 + (cell >> 2), jnp.where(pairs, 96 + 4 + (pair >> 1), jnp.where(fours, 96 + 4 + four, -1))),
    )
    for level, target in enumerate(targets):
        scale = jnp.where(is_coef == 1, F32(0.125**level), F32(0.5**level))
        found = (target >= 0) & (lane == is_coef * 128 + target)
        at = 576 + 128 * level
        tables[at : at + 128, 0:256] = jnp.where(found, scale, 0.0).astype(BF16)
    source = iota((128, 128), 0)
    lane = iota((128, 128), 1)
    for level, start in enumerate((16, 72, 100)):
        found = source == start + (lane >> (level + 2))
        tables[960:1088, 128 * level : 128 * level + 128] = ones_where(found)

    source = iota((384, 128), 0)
    x = (source >> 4) - 6
    z = (source & 15) - 2
    place = (x >= 0) & (x < 16) & (z >= 0) & (z < 8) & (iota((384, 128), 1) == (x >> 2) * 32 + (z >> 2))
    end_lanes[...] = ones_where(place)

    def in_y(x, carry):
        k, v = [all_rows(ext, beyond, field, x) for field in range(2)]
        bands[0, x] = band(k, 0)
        bands[1, x] = band(v, 0)
        bands[2, x] = band(k * v, 0)
        return carry

    lax.fori_loop(0, 28, in_y, 0, unroll=2)

    def in_x(x, carry):
        for field in range(3):
            xy[field, x - 2] = (bands[field, x - 1] + bands[field, x + 1]) + 2.0 * bands[field, x]
        return carry

    lax.fori_loop(2, 26, in_x, 0, unroll=2)


def end_cells(lower_k, lower_v, lower_right, upper_k, upper_v, upper_right):
    position = iota((32, 384), 1) & 15
    k = jnp.where(position < 6, lower_k, jnp.where(position < 12, upper_k, 0.0))
    v = jnp.where(position < 6, lower_v, upper_v)
    right = jnp.where(position < 6, lower_right, upper_right)[0:16, :]
    tu = []
    for f in (k, v, k * v):
        f = band(f, 0)[0:16, :]
        f = f + pltpu.roll(f, 16, 1)
        tu.append(band(f + pltpu.roll(f, 384 - 16, 1), 1))
    k, v = k[0:16, :], v[0:16, :]
    diagonal = 6.0 * k + 0.125 * tu[0]
    return right - (v * diagonal + 2.0 * (k * v) - 0.125 * (k * tu[1] + tu[2])), k


def own_cells(sent_up, sent_down, from_down, from_up, inner, end_lanes, chunks, quads):
    def moved(f, shift):
        return pltpu.roll(f, shift % 384, 1)

    low, first, last, high = [ref[:, 0:384] for ref in (from_down, sent_down, sent_up, from_up)]
    found = [
        end_cells(low, moved(low, -5), moved(low, -9), moved(first, 6), first, moved(first, -5)),
        end_cells(last, moved(last, -5), moved(last, -9), moved(high, 6), high, moved(high, -5)),
    ]
    rows = []
    for f in (found[0][0], found[1][0], found[0][1], found[1][1]):
        f = f + pltpu.roll(f, 15, 0)
        rows.append(f + pltpu.roll(f, 14, 0))
    ends = select_lanes(jnp.concatenate(rows, axis=0), end_lanes[...])
    ends = [0.25 * ends[0:16], 0.25 * ends[16:32], ends[32:48] / 64.0, ends[48:64] / 64.0]
    for q in range(4):
        for at in range(4):
            start = 64 * at + 16 * q
            quads[start : start + 16, :] = rolled(ends[at], -32 * q)
    lane = iota((16, 128), 1)
    mine = inner[...]
    for at, target in enumerate((3, 35, 43, 75)):
        cells = pltpu.roll(quads[pl.ds(64 * at, 16, stride=4), :], target, 1)
        mine = jnp.where((lane == target) | (lane == target + 1), cells, mine)
    low = from_down[0:16, 384:512]
    high = from_up[0:16, 384:512]
    for cells, moves in (
        (low, ((64, 0, 3), (67, 80, 2), (69, 84, 2), (80, 40, 3), (83, 88, 2), (85, 92, 2))),
        (high, ((64, 37, 3), (67, 82, 2), (69, 86, 2), (80, 77, 3), (83, 90, 2), (85, 94, 2))),
    ):
        for at, target, count in moves:
            mine = jnp.where((lane >= target) & (lane < target + count), rolled(cells, target - at), mine)
    lane = iota((4, 128), 1)
    for part in range(3):
        rest = rolled(mine, 96 - 32 * part)[12:16]
        tile = jnp.where(lane < 96, mine[4 * part : 4 * part + 4], rest)
        chunks[:, part] = jnp.broadcast_to(tile[None], (chunks.shape[0], 4, 128))


def fine_residual(ext, beyond, xy, from_down, from_up, coef, res, inv, side, sides_kv, product):
    lane = iota((32, 128), 1)

    for x in range(28):
        group, first = 128 * (x // 8), 16 * (x % 8)
        up = from_up[:, group : group + 128]
        down = from_down[:, group : group + 128]
        tiles = []
        for field in range(3):
            h, a = HALO[field], ROWS[field]
            tile = jnp.where(lane >= 128 - h, rolled(down, 128 - h - first - a), 0.0)
            tiles.append(jnp.where(lane < h, rolled(up, -first - a), tile))
        coef[x, :, 0:128] = all_rows(ext, beyond, 0, x)
        coef[x, :, 128:256] = tiles[0]
        side[0, x] = tiles[1]
        side[1, x] = tiles[2]
        sides_kv[x, :, 0:128] = band(tiles[0], 0)
        sides_kv[x, :, 128:256] = band(tiles[1], 0)
        product[x] = band(tiles[0] * tiles[1], 0)

    for x in (0, 1, 26, 27):
        res[x] = jnp.zeros((32, 256), F32)

    def over_x(ref, x):
        return (ref[x - 1] + ref[x + 1]) + 2.0 * ref[x]

    matrix = band_matrix(256)

    def cells(step, carry):
        xs = [2 + 8 * step + j for j in range(8)]
        wanted = []
        for x in xs:
            sides = over_x(sides_kv, x)
            wanted += [
                jnp.concatenate([xy[0, x - 2], sides[:, 0:128]], axis=1),
                jnp.concatenate([xy[1, x - 2], sides[:, 128:256]], axis=1),
                jnp.concatenate([xy[2, x - 2], over_x(product, x)], axis=1),
            ]
        found = band_z(wanted, matrix)
        for j, x in enumerate(xs):
            tu_k, tu_v, tu_kv = found[3 * j : 3 * j + 3]
            k = coef[x]
            v = jnp.concatenate([all_rows(ext, beyond, 1, x), side[0, x]], axis=1)
            diagonal = 6.0 * k + 0.125 * tu_k
            applied = v * diagonal + 2.0 * (k * v) - 0.125 * (k * tu_v + tu_kv)
            res[x] = jnp.concatenate([all_rows(ext, beyond, 2, x), side[1, x]], axis=1) - applied
            inv[x] = damped_inverse(k, diagonal)
        return carry

    lax.fori_loop(0, 3, cells, 0)


def fine_sweeps(ext, coef, res, inv, base, corr, corr_next, yz_c, yz_kc, pairs, spread):
    def over_x(ref, x):
        return (ref[x - 1] + ref[x + 1]) + 2.0 * ref[x]

    def bands_of(xs, ref):
        wanted = []
        for x in xs:
            c = ref[x]
            wanted += [band(c, 0), band(coef[x] * c, 0)]
        found = [band(f, 1) for f in wanted]
        for j, x in enumerate(xs):
            yz_c[x] = found[2 * j]
            yz_kc[x] = found[2 * j + 1]

    def first_sweep(step, carry):
        xs = [4 + 4 * step + j for j in range(4)]
        for x in xs:
            corr[x] = inv[x] * res[x]
        bands_of(xs, corr)
        return carry

    lax.fori_loop(0, 5, first_sweep, 0)

    def second(x, carry):
        corr_next[x] = relax(corr[x], inv[x], res[x], coef[x], over_x(yz_c, x), over_x(yz_kc, x))
        return carry

    lax.fori_loop(5, 23, second, 0, unroll=3)

    def second_bands(step, carry):
        bands_of([5 + 3 * step + j for j in range(3)], corr_next)
        return carry

    lax.fori_loop(0, 6, second_bands, 0)

    halves = ones_where((iota((256, 128), 0) >> 1) == iota((256, 128), 1))

    def pair(x, carry):
        for at, ref in enumerate((res, coef)):
            f = ref[2 * x] + ref[2 * x + 1]
            for tile in range(2):
                place = pl.ds(pl.multiple_of(448 * at + 32 * x, 32), 32)
                pairs[tile, place, :] = f[:, 128 * tile : 128 * tile + 128]
        return carry

    lax.fori_loop(0, 14, pair, 0, unroll=2)
    sums = [pairs[tile, pl.ds(0, 448, stride=2), :] + pairs[tile, pl.ds(1, 448, stride=2), :] for tile in range(2)]
    sums = select_lanes(jnp.concatenate(sums, axis=1), halves).reshape(2, 14, 16, 128)
    corr_two = smooth_small(0.5 * sums[0], 0.125 * sums[1], 3, 3, 11)
    doubled = ones_where(iota((128, 128), 0) == (iota((128, 128), 1) >> 1))
    wide = select_lanes(corr_two.reshape(128, 128), doubled).reshape(8, 16, 128)
    rows = wide[:, 0:8, :].reshape(64, 128)
    spread[pl.ds(0, 64, stride=2), :] = rows
    spread[pl.ds(1, 64, stride=2), :] = rows

    def third(x, carry):
        c = relax(
            corr_next[x, 0:16, 0:128],
            inv[x, 0:16, 0:128],
            res[x, 0:16, 0:128],
            coef[x, 0:16, 0:128],
            (yz_c[x - 1, 0:16, 0:128] + yz_c[x + 1, 0:16, 0:128]) + 2.0 * yz_c[x, 0:16, 0:128],
            (yz_kc[x - 1, 0:16, 0:128] + yz_kc[x + 1, 0:16, 0:128]) + 2.0 * yz_kc[x, 0:16, 0:128],
        )
        block = x - 6
        base[block] = ext[1, x] + (c + spread[pl.ds(pl.multiple_of(16 * (block // 2), 16), 16), :])
        return carry

    lax.fori_loop(6, 22, third, 0, unroll=4)


def coarse_levels(tables, plane, base, out, columns, spread):
    lane = iota((plane.shape[0], 4, 128), 2)
    parts = [plane[:, part] for part in range(3)]
    for part in range(3):
        columns[:, 4 * part : 4 * part + 4, :] = parts[part]
    rest = [pltpu.roll(parts[part], 32 + 32 * part, 2) for part in range(3)]
    columns[:, 12:16, :] = jnp.where(lane < 32, rest[0], jnp.where(lane < 64, rest[1], rest[2]))
    columns = columns[...].reshape(plane.shape[0] * 16, 128)
    found = jnp.dot(tables[0:576, :], jnp.concatenate(split(columns), axis=1), preferred_element_type=F32)
    found = found[:, 0:128] + (found[:, 128:256] + found[:, 256:384])
    windows = jnp.concatenate([found[192 * level : 192 * level + 192, :] for level in range(3)], axis=1)
    both = select_lanes(windows, tables[576:960, 0:256])
    corr = smooth_small(both[:, 0:128].reshape(12, 16, 128), both[:, 128:256].reshape(12, 16, 128), 4, 4, 8)
    wide = select_lanes(corr.reshape(64, 128), tables[960:1088, 0:384])
    for x in range(4):
        level4 = wide[16 * (x // 2) : 16 * (x // 2) + 16, 128:256]
        level4 = jnp.concatenate([jnp.broadcast_to(level4[y : y + 1], (2, 128)) for y in (4, 5)], axis=0)
        rows = wide[16 * x + 4 : 16 * x + 8, 0:128] + (level4 + wide[4:5, 256:384])
        for y in range(4):
            spread[pl.ds(16 * x + y, 4, stride=4), :] = rows
    for x in range(16):
        start = 16 * (x // 4)
        out[x] = base[x] + spread[start : start + 16, :]


VMEM = pl.BlockSpec(memory_space=pltpu.VMEM)
HBM = pl.BlockSpec(memory_space=pltpu.HBM)


def call(kernel, outs, ins, scratch=(), first=VMEM, rest=VMEM, flops=1000000, grant=32):
    moved = 4 * sum(x.size for x in ins)
    return pl.pallas_call(
        kernel,
        out_shape=[out if isinstance(out, jax.ShapeDtypeStruct) else jax.ShapeDtypeStruct(out, F32) for out in outs],
        in_specs=[first] + [rest] * (len(ins) - 1),
        out_specs=[VMEM] * len(outs),
        scratch_shapes=[pltpu.VMEM(shape, F32) if isinstance(shape, tuple) else shape for shape in scratch],
        compiler_params=pltpu.CompilerParams(vmem_limit_bytes=grant * 1024 * 1024),
        cost_estimate=pl.CostEstimate(flops=flops, bytes_accessed=moved, transcendentals=0),
        name=kernel.__name__,
    )(*ins)


def neighbour_pairs(count):
    for start in (1, 0):
        lower = range(start, count - 1, 2)
        yield [(i, i + 1) for i in lower] + [(i + 1, i) for i in lower]


def swap(axis, to_up, to_down):
    count = lax.axis_size(axis)
    up = [(i, i + 1) for i in range(count - 1)]
    down = [(i + 1, i) for i in range(count - 1)]
    return lax.ppermute(to_up, axis, up), lax.ppermute(to_down, axis, down)


def on_device(right, iterate, phase, table):
    block = (16, 16, 128)
    inputs = [table, phase, iterate, right]
    values = pltpu.SMEM((4,), F32)
    edge = pltpu.VMEM((6, 16, 128), jnp.int32)
    to_up, to_down = call(
        send_x,
        [(15, 16, 128), (15, 16, 128)],
        inputs,
        scratch=[values, edge, edge, pltpu.SemaphoreType.DMA((7,))],
        first=HBM,
        rest=HBM,
        grant=60,
    )
    from_down, from_up = swap("gx", to_up, to_down)
    (held,) = call(
        hold,
        [(3, *block)],
        inputs,
        scratch=[values, pltpu.VMEM(block, jnp.int32), pltpu.SemaphoreType.DMA((4,))],
        first=HBM,
        rest=HBM,
        flops=30000000,
        grant=60,
    )
    from_down, from_up, fields = lax.optimization_barrier((from_down, from_up, held))
    ext, *sent = call(
        pack_y,
        [(3, 28, 16, 128), (28, 16, 128), (28, 16, 128)],
        [fields, from_down, from_up],
    )
    found = [lax.ppermute(rows, "gy", pairs) for rows, pairs in zip(sent, neighbour_pairs(lax.axis_size("gy")))]
    planes = (3, 28, 32, 128)
    mine = call(
        own_rows,
        [(16, 512), (16, 512), (3, *block), jax.ShapeDtypeStruct((256, 384), BF16)],
        [ext],
        flops=30000000,
    )
    *found, up_rows, down_rows, xz, level3_lanes = lax.optimization_barrier((*found, *mine))
    beyond, to_up, to_down, inner = call(
        pack_z,
        [(3, 28, 16, 128), (32, 512), (32, 512), (16, 128)],
        [ext, *found, up_rows, down_rows, xz, level3_lanes],
        scratch=[(6, 32, 128), (128, 128)],
    )
    from_down, from_up = swap("gz", to_up, to_down)
    xy, tables, end_lanes = call(
        bands_xy,
        [(3, 24, 32, 128), jax.ShapeDtypeStruct((1088, 512), BF16), jax.ShapeDtypeStruct((384, 128), BF16)],
        [ext, beyond],
        scratch=[planes],
        flops=30000000,
    )
    from_down, from_up, xy, tables, end_lanes = lax.optimization_barrier((from_down, from_up, xy, tables, end_lanes))
    z_sides = [from_down, from_up]
    count = lax.axis_size("gx") * lax.axis_size("gy")
    (chunks,) = call(own_cells, [(count, 3, 4, 128)], [to_up, to_down, *z_sides, inner, end_lanes], scratch=[(256, 128)])
    plane = lax.all_to_all(chunks, ("gx", "gy"), 0, 0, tiled=True)
    wide = (28, 32, 256)
    coef, res, inv = call(
        fine_residual,
        [wide] * 3,
        [ext, beyond, xy, *z_sides],
        scratch=[(2, 28, 32, 128), wide, (28, 32, 128)],
        flops=30000000,
    )
    (base,) = call(
        fine_sweeps,
        [block],
        [ext, coef, res, inv],
        scratch=[wide, wide, wide, wide, (2, 896, 128), (128, 128)],
        flops=60000000,
    )
    (out,) = call(coarse_levels, [block], [tables, plane, base], scratch=[(count, 16, 128), (64, 128)])
    return out


def solution(mesh):
    placed = (P("gx", "gy", "gz"), P("gx", "gy", "gz"), P("gx", "gy", "gz"), P())
    return jax.shard_map(on_device, mesh=mesh, in_specs=placed, out_specs=P("gx", "gy", "gz"), check_vma=False)
```

```python
import jax
import jax.numpy as jnp
from jax import lax
from jax.experimental import pallas as pl
from jax.experimental.pallas import tpu as pltpu
from jax.sharding import PartitionSpec as P

HALO = (6, 5, 4)
ROWS = (0, 6, 11, 15)
OMEGA = 2.0 / 3.0
F32 = jnp.float32
BF16 = jnp.bfloat16


def iota(shape, dim):
    return lax.broadcasted_iota(jnp.int32, shape, dim)


def ones_where(cond, scale=1.0):
    return jnp.where(cond, F32(scale), F32(0.0)).astype(BF16)


def split(x):
    high = x.astype(BF16)
    rest = x - high.astype(F32)
    middle = rest.astype(BF16)
    return high, middle, (rest - middle.astype(F32)).astype(BF16)


def select_rows(pattern, x):
    high, middle, low = [jnp.dot(pattern, part, preferred_element_type=F32) for part in split(x)]
    return high + (middle + low)


def select_lanes(x, pattern):
    high, middle, low = [jnp.dot(part, pattern, preferred_element_type=F32) for part in split(x)]
    return high + (middle + low)


def band_matrix(size):
    apart = jnp.abs(iota((size, size), 0) - iota((size, size), 1))
    return jnp.where(apart == 0, 2.0, jnp.where((apart == 1) | (apart == size - 1), 1.0, 0.0)).astype(BF16)


def band_z(fields, matrix):
    shape = fields[0].shape
    rows = fields[0].size // shape[-1]
    found = select_lanes(jnp.concatenate([f.reshape(rows, shape[-1]) for f in fields], axis=0), matrix)
    return [found[rows * at : rows * at + rows].reshape(shape) for at in range(len(fields))]


def band(x, axis):
    return (pltpu.roll(x, 1, axis) + pltpu.roll(x, x.shape[axis] - 1, axis)) + 2.0 * x


def damped_inverse(coef, diagonal):
    inside = coef > 0.0
    return jnp.where(inside, OMEGA / jnp.where(inside, diagonal, 1.0), 0.0)


def relax(corr, inverse, residual, coef, tu_corr, tu_product):
    return corr * (1.0 / 3.0) + inverse * (residual - 2.0 * (coef * corr) + 0.125 * (coef * tu_corr + tu_product))


def sum_x(x):
    return (x[:-2] + x[2:]) + 2.0 * x[1:-1]


def smooth_small(residual, coef, sweeps, first, last):
    low, high = first - sweeps + 1, last + sweeps - 1
    tu = band(band(sum_x(coef[low - 1 : high + 1]), 1), 2)
    coef = coef[low:high]
    residual = residual[low:high]
    inverse = damped_inverse(coef, 6.0 * coef + 0.125 * tu)
    corr = inverse * residual
    for _ in range(sweeps - 1):
        tu = [band(band(sum_x(f), 1), 2) for f in (corr, coef * corr)]
        corr, inverse, residual, coef = [f[1:-1] for f in (corr, inverse, residual, coef)]
        corr = relax(corr, inverse, residual, coef, *tu)
    return corr


def lookup(phase, values):
    k = jnp.zeros(phase.shape, F32)
    for index in range(4):
        k = jnp.where(phase == index, values[index], k)
    return k


def fetch(pairs, sems):
    copies = [pltpu.make_async_copy(source, target, sems.at[at]) for at, (source, target) in enumerate(pairs)]
    for copy in copies:
        copy.start()
    for copy in copies:
        copy.wait()


def send_x(table, phase, iterate, right, to_up, to_down, values, upper, lower, sems):
    fetch(
        [
            (table, values),
            (phase.at[10:16], upper),
            (phase.at[0:6], lower),
            (iterate.at[11:16], to_up.at[6:11]),
            (iterate.at[0:5], to_down.at[6:11]),
            (right.at[12:16], to_up.at[11:15]),
            (right.at[0:4], to_down.at[11:15]),
        ],
        sems,
    )
    to_up[0:6] = lookup(upper[...], values)
    to_down[0:6] = lookup(lower[...], values)


def hold(table, phase, iterate, right, fields, values, phases, sems):
    fetch([(table, values), (phase, phases), (iterate, fields.at[1]), (right, fields.at[2])], sems)
    fields[0] = lookup(phases[...], values)


def near(fields, held):
    held[...] = fields[...]


def by_parity(body, first, second):
    odd = (lax.axis_index("gy") & 1) == 1

    @pl.when(odd)
    def _():
        body(second, first)

    @pl.when(jnp.logical_not(odd))
    def _():
        body(first, second)


def pack_y(fields, from_down, from_up, ext, to_first, to_second):
    for field in range(3):
        h, a, b = HALO[field], ROWS[field], ROWS[field + 1]
        if h < 6:
            ext[field, 0 : 6 - h] = jnp.zeros((6 - h, 16, 128), F32)
            ext[field, 22 + h : 28] = jnp.zeros((6 - h, 16, 128), F32)
        ext[field, 6 - h : 6] = from_down[a:b]
        ext[field, 6:22] = fields[field]
        ext[field, 22 : 22 + h] = from_up[a:b]

    def rows(to_down, to_up):
        for field in range(3):
            h, a, b = HALO[field], ROWS[field], ROWS[field + 1]
            to_up[:, a:b, :] = ext[field, :, 16 - h : 16, :]
            to_down[:, a:b, :] = ext[field, :, 0:h, :]

    by_parity(rows, to_first, to_second)
    to_first[:, 15:16, :] = jnp.zeros((28, 1, 128), F32)
    to_second[:, 15:16, :] = jnp.zeros((28, 1, 128), F32)


def sum_quads(quads, q, sums):
    for at, f in enumerate(sums):
        f = f + pltpu.roll(f, 15, 0)
        f = f + pltpu.roll(f, 14, 0)
        for tile in range(f.shape[1] // 128):
            start = 64 * (at * (f.shape[1] // 128) + tile) + 16 * q
            quads[pl.ds(pl.multiple_of(start, 16), 16), :] = f[:, 128 * tile : 128 * tile + 128]


def read_quads(quads):
    count = quads.shape[0] // 64
    return jnp.concatenate([quads[pl.ds(64 * at, 16, stride=4), :] for at in range(count)], axis=1)


def pack_lanes(cells_of, rows, to_up, to_down, at):
    lane = iota((rows, 128), 1)
    for group in range(4):
        up = jnp.zeros((rows, 128), F32)
        down = jnp.zeros((rows, 128), F32)
        for x in range(8 * group, min(8 * group + 8, 28)):
            first = 16 * (x - 8 * group)
            for field in range(3):
                h, a, b = HALO[field], ROWS[field], ROWS[field + 1]
                if not 6 - h <= x < 22 + h:
                    continue
                cells = cells_of(field, x)
                mine = (lane >= first + a) & (lane < first + b)
                up = jnp.where(mine, pltpu.roll(cells, (first + a + h) % 128, 1), up)
                down = jnp.where(mine, rolled(cells, first + a), down)
        to_up[at : at + rows, 128 * group : 128 * group + 128] = up
        to_down[at : at + rows, 128 * group : 128 * group + 128] = down


def own_rows(ext, up, down, xz, level3_lanes):
    pack_lanes(lambda field, x: ext[field, x], 16, up, down, 0)
    matrix = band_matrix(128)

    def bands(step, carry):
        xs = [6 + 4 * step + j for j in range(4)]
        wanted = []
        for x in xs:
            around = [(ext[0, x + d], ext[1, x + d]) for d in (-1, 0, 1)]
            for low, here, high in zip(*[(k, v, k * v) for k, v in around]):
                wanted.append((low + high) + 2.0 * here)
        for at, f in enumerate(band_z(wanted, matrix)):
            xz[at % 3, xs[at // 3] - 6] = f
        return carry

    lax.fori_loop(0, 4, bands, 0)
    source = iota((256, 128), 0)
    lane = iota((256, 128), 1)
    coarse = (source & 127) >> 2
    is_coef = source >> 7
    scale = jnp.where(source < 128, F32(0.25), F32(1.0 / 64.0))
    upper = jnp.where(coarse >= 28, coarse - 28, jnp.where(coarse >= 24, (coarse >> 1) - 9, (coarse >> 2) + 1))
    lower = jnp.where(coarse <= 3, coarse - 1, jnp.where(coarse <= 7, (coarse >> 1) + 1, (coarse >> 2) + 3))
    found = (
        (lane == 64 + 16 * is_coef + upper) & (coarse >= 16) & (coarse <= 30),
        (lane == 64 + 16 * is_coef + lower) & (coarse >= 1) & (coarse <= 15),
        (lane == 40 * is_coef + 4 + coarse) & (coarse >= 1) & (coarse <= 30),
    )
    for at, here in enumerate(found):
        level3_lanes[:, 128 * at : 128 * at + 128] = jnp.where(here, scale, 0.0).astype(BF16)


def pack_z(ext, from_first, from_second, up_rows, down_rows, xz, level3_lanes, beyond, to_up, to_down, inner, edges, quads):
    edges[:, 24:32, :] = jnp.zeros((6, 8, 128), F32)
    for field in range(3):
        h = HALO[field]
        beyond[field, :, h : 16 - h, :] = jnp.zeros((28, 16 - 2 * h, 128), F32)

    def rows(from_down, from_up):
        for field in range(3):
            h, a, b = HALO[field], ROWS[field], ROWS[field + 1]
            beyond[field, :, 0:h, :] = from_up[:, a:b, :]
            beyond[field, :, 16 - h : 16, :] = from_down[:, a:b, :]
        for at, (source, row_k, row_v) in enumerate(((from_down, 5, 10), (from_up, 0, 6))):
            k = source[:, row_k, :]
            v = source[:, row_v, :]
            for number, f in enumerate((k, v, k * v)):
                edges[3 * at + number, 0:28, :] = f

    by_parity(rows, from_first, from_second)
    for at in range(6):
        edges[at] = band(band(edges[at], 0), 1)
    row = iota((16, 128), 0)

    def quad(q, carry):
        sums = [None, None]
        for j in range(4):
            x = 6 + 4 * q + j
            tu = []
            for at in range(3):
                f = xz[at, 4 * q + j]
                below = jnp.where(row == 0, edges[at, pl.ds(x, 1), :], pltpu.roll(f, 1, 0))
                above = jnp.where(row == 15, edges[3 + at, pl.ds(x, 1), :], pltpu.roll(f, 15, 0))
                tu.append((below + above) + 2.0 * f)
            k = ext[0, x]
            v = ext[1, x]
            diagonal = 6.0 * k + 0.125 * tu[0]
            res = ext[2, x] - (v * diagonal + 2.0 * (k * v) - 0.125 * (k * tu[1] + tu[2]))
            sums = [f if j == 0 else total + f for total, f in zip(sums, (res, k))]
        sum_quads(quads, q, sums)
        return carry

    lax.fori_loop(0, 4, quad, 0)
    level3 = select_lanes(read_quads(quads), level3_lanes[...])
    inner[...] = level3[:, 256:384]
    to_up[0:16, :] = up_rows[...]
    to_down[0:16, :] = down_rows[...]
    pack_lanes(lambda field, x: beyond[field, x], 16, to_up, to_down, 16)
    to_up[0:16, 384:512] += level3[:, 0:128]
    to_down[0:16, 384:512] += level3[:, 128:256]


def rolled(x, shift):
    shift = shift % x.shape[1]
    return pltpu.roll(x, shift, 1) if shift else x


def all_rows(ext, beyond, field, x):
    return jnp.concatenate([ext[field, x], beyond[field, x]], axis=0)


def bands_xy(ext, beyond, xy, tables, end_lanes, bands):
    row = iota((192, 512), 0)
    cell = iota((192, 512), 1)
    cell_x = (cell >> 6) * 4 + ((cell >> 2) & 3)
    cell_y = ((cell >> 4) & 3) * 4 + (cell & 3)
    for level in range(3):
        at_x = lax.axis_index("gx") * (4 >> level) - 4 + (row >> 4)
        at_y = lax.axis_index("gy") * (4 >> level) - 4 + (row & 15)
        found = ((cell_x >> level) == at_x) & ((cell_y >> level) == at_y)
        tables[192 * level : 192 * level + 192, :] = ones_where(found)
    source = iota((128, 256), 0)
    lane = iota((128, 256), 1)
    is_coef = jnp.where(source < 80, jnp.where(source >= 40, 1, 0), jnp.where(source >= 88, 1, 0))
    cell = jnp.where(source < 80, source - 40 * is_coef - 4, source - 80 - 8 * is_coef)
    inner = source < 80
    pairs = (source >= 80) & (source < 96) & (cell < 4)
    fours = (source >= 80) & (source < 96) & (cell >= 4)
    pair = jnp.where(cell < 2, cell - 4, cell + 16)
    four = jnp.where(cell < 6, cell - 8, cell + 4)
    targets = (
        jnp.where(inner, cell + 16, -1),
        jnp.where(inner, 64 + 8 + (cell >> 1), jnp.where(pairs, 64 + 8 + pair, -1)),
        jnp.where(inner, 96 + 4 + (cell >> 2), jnp.where(pairs, 96 + 4 + (pair >> 1), jnp.where(fours, 96 + 4 + four, -1))),
    )
    for level, target in enumerate(targets):
        scale = jnp.where(is_coef == 1, F32(0.125**level), F32(0.5**level))
        found = (target >= 0) & (lane == is_coef * 128 + target)
        at = 576 + 128 * level
        tables[at : at + 128, 0:256] = jnp.where(found, scale, 0.0).astype(BF16)
    source = iota((128, 128), 0)
    lane = iota((128, 128), 1)
    for level, start in enumerate((16, 72, 100)):
        found = source == start + (lane >> (level + 2))
        tables[960:1088, 128 * level : 128 * level + 128] = ones_where(found)

    source = iota((384, 128), 0)
    x = (source >> 4) - 6
    z = (source & 15) - 2
    place = (x >= 0) & (x < 16) & (z >= 0) & (z < 8) & (iota((384, 128), 1) == (x >> 2) * 32 + (z >> 2))
    end_lanes[...] = ones_where(place)

    def in_y(x, carry):
        k, v = [all_rows(ext, beyond, field, x) for field in range(2)]
        bands[0, x] = band(k, 0)
        bands[1, x] = band(v, 0)
        bands[2, x] = band(k * v, 0)
        return carry

    lax.fori_loop(0, 28, in_y, 0, unroll=2)

    def in_x(x, carry):
        for field in range(3):
            xy[field, x - 2] = (bands[field, x - 1] + bands[field, x + 1]) + 2.0 * bands[field, x]
        return carry

    lax.fori_loop(2, 26, in_x, 0, unroll=2)


def end_cells(lower_k, lower_v, lower_right, upper_k, upper_v, upper_right):
    position = iota((32, 384), 1) & 15
    k = jnp.where(position < 6, lower_k, jnp.where(position < 12, upper_k, 0.0))
    v = jnp.where(position < 6, lower_v, upper_v)
    right = jnp.where(position < 6, lower_right, upper_right)[0:16, :]
    tu = []
    for f in (k, v, k * v):
        f = band(f, 0)[0:16, :]
        f = f + pltpu.roll(f, 16, 1)
        tu.append(band(f + pltpu.roll(f, 384 - 16, 1), 1))
    k, v = k[0:16, :], v[0:16, :]
    diagonal = 6.0 * k + 0.125 * tu[0]
    return right - (v * diagonal + 2.0 * (k * v) - 0.125 * (k * tu[1] + tu[2])), k


def own_cells(sent_up, sent_down, from_down, from_up, inner, end_lanes, chunks, quads):
    def moved(f, shift):
        return pltpu.roll(f, shift % 384, 1)

    low, first, last, high = [ref[:, 0:384] for ref in (from_down, sent_down, sent_up, from_up)]
    found = [
        end_cells(low, moved(low, -5), moved(low, -9), moved(first, 6), first, moved(first, -5)),
        end_cells(last, moved(last, -5), moved(last, -9), moved(high, 6), high, moved(high, -5)),
    ]
    rows = []
    for f in (found[0][0], found[1][0], found[0][1], found[1][1]):
        f = f + pltpu.roll(f, 15, 0)
        rows.append(f + pltpu.roll(f, 14, 0))
    ends = select_lanes(jnp.concatenate(rows, axis=0), end_lanes[...])
    ends = [0.25 * ends[0:16], 0.25 * ends[16:32], ends[32:48] / 64.0, ends[48:64] / 64.0]
    for q in range(4):
        for at in range(4):
            start = 64 * at + 16 * q
            quads[start : start + 16, :] = rolled(ends[at], -32 * q)
    lane = iota((16, 128), 1)
    mine = inner[...]
    for at, target in enumerate((3, 35, 43, 75)):
        cells = pltpu.roll(quads[pl.ds(64 * at, 16, stride=4), :], target, 1)
        mine = jnp.where((lane == target) | (lane == target + 1), cells, mine)
    low = from_down[0:16, 384:512]
    high = from_up[0:16, 384:512]
    for cells, moves in (
        (low, ((64, 0, 3), (67, 80, 2), (69, 84, 2), (80, 40, 3), (83, 88, 2), (85, 92, 2))),
        (high, ((64, 37, 3), (67, 82, 2), (69, 86, 2), (80, 77, 3), (83, 90, 2), (85, 94, 2))),
    ):
        for at, target, count in moves:
            mine = jnp.where((lane >= target) & (lane < target + count), rolled(cells, target - at), mine)
    lane = iota((4, 128), 1)
    for part in range(3):
        rest = rolled(mine, 96 - 32 * part)[12:16]
        tile = jnp.where(lane < 96, mine[4 * part : 4 * part + 4], rest)
        chunks[:, part] = jnp.broadcast_to(tile[None], (chunks.shape[0], 4, 128))


def fine_residual(ext, beyond, xy, from_down, from_up, coef, res, inv, side, sides_kv, product):
    lane = iota((32, 128), 1)

    for x in range(28):
        group, first = 128 * (x // 8), 16 * (x % 8)
        up = from_up[:, group : group + 128]
        down = from_down[:, group : group + 128]
        tiles = []
        for field in range(3):
            h, a = HALO[field], ROWS[field]
            tile = jnp.where(lane >= 128 - h, rolled(down, 128 - h - first - a), 0.0)
            tiles.append(jnp.where(lane < h, rolled(up, -first - a), tile))
        coef[x, :, 0:128] = all_rows(ext, beyond, 0, x)
        coef[x, :, 128:256] = tiles[0]
        side[0, x] = tiles[1]
        side[1, x] = tiles[2]
        sides_kv[x, :, 0:128] = band(tiles[0], 0)
        sides_kv[x, :, 128:256] = band(tiles[1], 0)
        product[x] = band(tiles[0] * tiles[1], 0)

    for x in (0, 1, 26, 27):
        res[x] = jnp.zeros((32, 256), F32)

    def over_x(ref, x):
        return (ref[x - 1] + ref[x + 1]) + 2.0 * ref[x]

    matrix = band_matrix(256)

    def cells(step, carry):
        xs = [2 + 8 * step + j for j in range(8)]
        wanted = []
        for x in xs:
            sides = over_x(sides_kv, x)
            wanted += [
                jnp.concatenate([xy[0, x - 2], sides[:, 0:128]], axis=1),
                jnp.concatenate([xy[1, x - 2], sides[:, 128:256]], axis=1),
                jnp.concatenate([xy[2, x - 2], over_x(product, x)], axis=1),
            ]
        found = band_z(wanted, matrix)
        for j, x in enumerate(xs):
            tu_k, tu_v, tu_kv = found[3 * j : 3 * j + 3]
            k = coef[x]
            v = jnp.concatenate([all_rows(ext, beyond, 1, x), side[0, x]], axis=1)
            diagonal = 6.0 * k + 0.125 * tu_k
            applied = v * diagonal + 2.0 * (k * v) - 0.125 * (k * tu_v + tu_kv)
            res[x] = jnp.concatenate([all_rows(ext, beyond, 2, x), side[1, x]], axis=1) - applied
            inv[x] = damped_inverse(k, diagonal)
        return carry

    lax.fori_loop(0, 3, cells, 0)


def fine_sweeps(ext, coef, res, inv, base, corr, corr_next, yz_c, yz_kc, pairs, spread):
    def over_x(ref, x):
        return (ref[x - 1] + ref[x + 1]) + 2.0 * ref[x]

    def bands_of(xs, ref):
        wanted = []
        for x in xs:
            c = ref[x]
            wanted += [band(c, 0), band(coef[x] * c, 0)]
        found = [band(f, 1) for f in wanted]
        for j, x in enumerate(xs):
            yz_c[x] = found[2 * j]
            yz_kc[x] = found[2 * j + 1]

    def first_sweep(step, carry):
        xs = [4 + 4 * step + j for j in range(4)]
        for x in xs:
            corr[x] = inv[x] * res[x]
        bands_of(xs, corr)
        return carry

    lax.fori_loop(0, 5, first_sweep, 0)

    def second(x, carry):
        corr_next[x] = relax(corr[x], inv[x], res[x], coef[x], over_x(yz_c, x), over_x(yz_kc, x))
        return carry

    lax.fori_loop(5, 23, second, 0, unroll=3)

    def second_bands(step, carry):
        bands_of([5 + 3 * step + j for j in range(3)], corr_next)
        return carry

    lax.fori_loop(0, 6, second_bands, 0)

    halves = ones_where((iota((256, 128), 0) >> 1) == iota((256, 128), 1))

    def pair(x, carry):
        for at, ref in enumerate((res, coef)):
            f = ref[2 * x] + ref[2 * x + 1]
            for tile in range(2):
                place = pl.ds(pl.multiple_of(448 * at + 32 * x, 32), 32)
                pairs[tile, place, :] = f[:, 128 * tile : 128 * tile + 128]
        return carry

    lax.fori_loop(0, 14, pair, 0, unroll=2)
    sums = [pairs[tile, pl.ds(0, 448, stride=2), :] + pairs[tile, pl.ds(1, 448, stride=2), :] for tile in range(2)]
    sums = select_lanes(jnp.concatenate(sums, axis=1), halves).reshape(2, 14, 16, 128)
    corr_two = smooth_small(0.5 * sums[0], 0.125 * sums[1], 3, 3, 11)
    doubled = ones_where(iota((128, 128), 0) == (iota((128, 128), 1) >> 1))
    wide = select_lanes(corr_two.reshape(128, 128), doubled).reshape(8, 16, 128)
    rows = wide[:, 0:8, :].reshape(64, 128)
    spread[pl.ds(0, 64, stride=2), :] = rows
    spread[pl.ds(1, 64, stride=2), :] = rows

    def third(x, carry):
        c = relax(
            corr_next[x, 0:16, 0:128],
            inv[x, 0:16, 0:128],
            res[x, 0:16, 0:128],
            coef[x, 0:16, 0:128],
            (yz_c[x - 1, 0:16, 0:128] + yz_c[x + 1, 0:16, 0:128]) + 2.0 * yz_c[x, 0:16, 0:128],
            (yz_kc[x - 1, 0:16, 0:128] + yz_kc[x + 1, 0:16, 0:128]) + 2.0 * yz_kc[x, 0:16, 0:128],
        )
        block = x - 6
        base[block] = ext[1, x] + (c + spread[pl.ds(pl.multiple_of(16 * (block // 2), 16), 16), :])
        return carry

    lax.fori_loop(6, 22, third, 0, unroll=4)


def coarse_levels(tables, plane, base, out, columns, spread):
    lane = iota((plane.shape[0], 4, 128), 2)
    parts = [plane[:, part] for part in range(3)]
    for part in range(3):
        columns[:, 4 * part : 4 * part + 4, :] = parts[part]
    rest = [pltpu.roll(parts[part], 32 + 32 * part, 2) for part in range(3)]
    columns[:, 12:16, :] = jnp.where(lane < 32, rest[0], jnp.where(lane < 64, rest[1], rest[2]))
    columns = columns[...].reshape(plane.shape[0] * 16, 128)
    found = jnp.dot(tables[0:576, :], jnp.concatenate(split(columns), axis=1), preferred_element_type=F32)
    found = found[:, 0:128] + (found[:, 128:256] + found[:, 256:384])
    windows = jnp.concatenate([found[192 * level : 192 * level + 192, :] for level in range(3)], axis=1)
    both = select_lanes(windows, tables[576:960, 0:256])
    corr = smooth_small(both[:, 0:128].reshape(12, 16, 128), both[:, 128:256].reshape(12, 16, 128), 4, 4, 8)
    wide = select_lanes(corr.reshape(64, 128), tables[960:1088, 0:384])
    for x in range(4):
        level4 = wide[16 * (x // 2) : 16 * (x // 2) + 16, 128:256]
        level4 = jnp.concatenate([jnp.broadcast_to(level4[y : y + 1], (2, 128)) for y in (4, 5)], axis=0)
        rows = wide[16 * x + 4 : 16 * x + 8, 0:128] + (level4 + wide[4:5, 256:384])
        for y in range(4):
            spread[pl.ds(16 * x + y, 4, stride=4), :] = rows
    for x in range(16):
        start = 16 * (x // 4)
        out[x] = base[x] + spread[start : start + 16, :]


VMEM = pl.BlockSpec(memory_space=pltpu.VMEM)
HBM = pl.BlockSpec(memory_space=pltpu.HBM)


def call(kernel, outs, ins, scratch=(), first=VMEM, rest=VMEM, flops=1000000, grant=32):
    moved = 4 * sum(x.size for x in ins)
    return pl.pallas_call(
        kernel,
        out_shape=[out if isinstance(out, jax.ShapeDtypeStruct) else jax.ShapeDtypeStruct(out, F32) for out in outs],
        in_specs=[first] + [rest] * (len(ins) - 1),
        out_specs=[VMEM] * len(outs),
        scratch_shapes=[pltpu.VMEM(shape, F32) if isinstance(shape, tuple) else shape for shape in scratch],
        compiler_params=pltpu.CompilerParams(vmem_limit_bytes=grant * 1024 * 1024),
        cost_estimate=pl.CostEstimate(flops=flops, bytes_accessed=moved, transcendentals=0),
        name=kernel.__name__,
    )(*ins)


def neighbour_pairs(count):
    for start in (1, 0):
        lower = range(start, count - 1, 2)
        yield [(i, i + 1) for i in lower] + [(i + 1, i) for i in lower]


def swap(axis, to_up, to_down):
    count = lax.axis_size(axis)
    up = [(i, i + 1) for i in range(count - 1)]
    down = [(i + 1, i) for i in range(count - 1)]
    return lax.ppermute(to_up, axis, up), lax.ppermute(to_down, axis, down)


def on_device(right, iterate, phase, table):
    block = (16, 16, 128)
    inputs = [table, phase, iterate, right]
    values = pltpu.SMEM((4,), F32)
    edge = pltpu.VMEM((6, 16, 128), jnp.int32)
    to_up, to_down = call(
        send_x,
        [(15, 16, 128), (15, 16, 128)],
        inputs,
        scratch=[values, edge, edge, pltpu.SemaphoreType.DMA((7,))],
        first=HBM,
        rest=HBM,
        grant=60,
    )
    from_down, from_up = swap("gx", to_up, to_down)
    (held,) = call(
        hold,
        [(3, *block)],
        inputs,
        scratch=[values, pltpu.VMEM(block, jnp.int32), pltpu.SemaphoreType.DMA((4,))],
        first=HBM,
        rest=HBM,
        flops=30000000,
        grant=60,
    )
    (held,) = call(near, [(3, *block)], [held], flops=30000000)
    from_down, from_up, fields = lax.optimization_barrier((from_down, from_up, held))
    ext, *sent = call(
        pack_y,
        [(3, 28, 16, 128), (28, 16, 128), (28, 16, 128)],
        [fields, from_down, from_up],
    )
    found = [lax.ppermute(rows, "gy", pairs) for rows, pairs in zip(sent, neighbour_pairs(lax.axis_size("gy")))]
    planes = (3, 28, 32, 128)
    mine = call(
        own_rows,
        [(16, 512), (16, 512), (3, *block), jax.ShapeDtypeStruct((256, 384), BF16)],
        [ext],
        flops=30000000,
    )
    *found, up_rows, down_rows, xz, level3_lanes = lax.optimization_barrier((*found, *mine))
    beyond, to_up, to_down, inner = call(
        pack_z,
        [(3, 28, 16, 128), (32, 512), (32, 512), (16, 128)],
        [ext, *found, up_rows, down_rows, xz, level3_lanes],
        scratch=[(6, 32, 128), (128, 128)],
    )
    from_down, from_up = swap("gz", to_up, to_down)
    xy, tables, end_lanes = call(
        bands_xy,
        [(3, 24, 32, 128), jax.ShapeDtypeStruct((1088, 512), BF16), jax.ShapeDtypeStruct((384, 128), BF16)],
        [ext, beyond],
        scratch=[planes],
        flops=30000000,
    )
    from_down, from_up, xy, tables, end_lanes = lax.optimization_barrier((from_down, from_up, xy, tables, end_lanes))
    z_sides = [from_down, from_up]
    count = lax.axis_size("gx") * lax.axis_size("gy")
    (chunks,) = call(own_cells, [(count, 3, 4, 128)], [to_up, to_down, *z_sides, inner, end_lanes], scratch=[(256, 128)])
    plane = lax.all_to_all(chunks, ("gx", "gy"), 0, 0, tiled=True)
    wide = (28, 32, 256)
    coef, res, inv = call(
        fine_residual,
        [wide] * 3,
        [ext, beyond, xy, *z_sides],
        scratch=[(2, 28, 32, 128), wide, (28, 32, 128)],
        flops=30000000,
    )
    (base,) = call(
        fine_sweeps,
        [block],
        [ext, coef, res, inv],
        scratch=[wide, wide, wide, wide, (2, 896, 128), (128, 128)],
        flops=60000000,
    )
    (out,) = call(coarse_levels, [block], [tables, plane, base], scratch=[(count, 16, 128), (64, 128)])
    return out


def solution(mesh):
    placed = (P("gx", "gy", "gz"), P("gx", "gy", "gz"), P("gx", "gy", "gz"), P())
    return jax.shard_map(on_device, mesh=mesh, in_specs=placed, out_specs=P("gx", "gy", "gz"), check_vma=False)
```
